32 devices in a mesh: band: 2 (over x), feed: 16 (over z, y, core).
Axes of the slice: x: 2, y: 2, z: 4, core: 2. Of those that a mesh axis runs over, the one named last changes fastest.
Arguments:
- samples: int32 [8192, 16, 519], P(('band', 'feed')), parts along dimension 0, may hold values from 0 to 255
- gains: int32 [2, 32, 4096], P(None, 'band', 'feed'), parts along dimension 1, may hold values from -2048 to 2047
- feed_slot: int32 [4096], replicated, may hold values from 0 to 4095, each once
Outputs:
- visibility: float32 [8192, 2, 4096], P(('band', 'feed')), parts along dimension 0
The draws below stay inside these ranges and needn't reach their ends.
There are 2 independent parts, one for each index of `band`. The reference program is written for one: setup_inputs(seed, part) draws one part's arguments, and reference() takes and returns one part's arrays. A program takes and returns all parts, laid end to end along the dimension named above; an argument that names none is the same for every part. Nothing has to cross between parts.
Inputs may be any that keep to these rules, and one draw needn't show every extreme that they name: `samples`: each word is 16 times the in-phase level plus the quadrature level, both offset by 8. `feed_slot`: every slot appears once.
All inputs are finite; a program needn't handle non-finite values.
Results may differ from the reference program's by a relative error of at most 0.0026.
Values may be sent and summed in bfloat16 or wider, within the bound.
No kernel may reach another device: no remote copies, remote signals or barrier semaphores. Data moves between devices by JAX's collectives and lax.ppermute only.
A program may use at most 128 MiB of HBM per device.

```python
import math
import jax
import jax.numpy as jnp
from jax import lax

INPUTS = 4096
CH = 16
TAPS = 8
SPECTRA = 512
ROWS = 256
QUARTS = 1
NFRAME = 519
N_FEED = 16


def place_ends(entries, own_key, smallest, top_value):
    longest = entries.shape.index(max(entries.shape))
    spots = []
    for shift in (0, 1):
        where = [jax.random.randint(jax.random.fold_in(own_key, axis), (), 0, length) for axis, length in enumerate(entries.shape)]
        where[longest] = (where[longest] + shift) % entries.shape[longest]
        spots.append(tuple(where))
    return entries.at[spots[0]].set(smallest).at[spots[1]].set(top_value)


def setup_inputs(seed: int = 0, part: int = 0) -> dict:
    streams_of = jax.random.split(jax.random.key(seed), 4)
    part_splits = jax.random.split(jax.random.fold_in(streams_of[3], part), 4)
    return {
        "samples": place_ends(jax.random.randint(part_splits[0], (INPUTS, CH, NFRAME), 0, 256), jax.random.fold_in(part_splits[0], 1), 0, 255).astype(jnp.int32),
        "gains": place_ends(jax.random.randint(part_splits[1], (2, CH, INPUTS), -2048, 2048), jax.random.fold_in(part_splits[1], 1), -2048, 2047).astype(jnp.int32),
        "feed_slot": jax.random.permutation(streams_of[2], INPUTS).astype(jnp.int32),
    }


def filter_taps():
    length = TAPS * CH
    place = jnp.arange(length).astype(jnp.float32)
    window = 0.5 - 0.5 * jnp.cos(2.0 * math.pi * place / (length - 1))
    return (jnp.sinc((place - 0.5 * (length - 1)) / CH) * window).reshape(TAPS, CH)

def dft_table():
    index = jnp.arange(CH, dtype=jnp.int32)
    phase = index[:, None] * index[None, :] % CH
    angle = phase.astype(jnp.float32) * (2.0 * math.pi / CH)
    cosine = jnp.cos(angle) / math.sqrt(CH)
    sine = jnp.sin(angle) / math.sqrt(CH)
    upper = jnp.stack([cosine, sine], axis=1)
    lower = jnp.stack([-sine, cosine], axis=1)
    return jnp.stack([upper, lower], axis=0)

def channelize(words, scales, blocks):
    inphase = (words // 16 - 8).astype(jnp.float32) * 0.125
    quadrature = (words % 16 - 8).astype(jnp.float32) * 0.125
    voltage = jnp.stack([inphase, quadrature], axis=1)
    taps = filter_taps()
    count = words.shape[2] - TAPS + 1
    filtered = taps[0][None, None, :, None] * voltage[:, :, :, 0:count]
    for tap in range(1, TAPS):
        filtered = filtered + taps[tap][None, None, :, None] * voltage[:, :, :, tap:tap + count]
    split = filtered.reshape(filtered.shape[0], 2, CH, blocks, count // blocks)
    channels = jnp.einsum('pcqk,nqkat->canpt', dft_table(), split, precision=lax.Precision.HIGHEST)
    gain = scales.astype(jnp.float32) * (1.0 / 2048.0)
    gain_real = gain[0][:, None, :, None]
    gain_imag = gain[1][:, None, :, None]
    real = channels[:, :, :, 0]
    imag = channels[:, :, :, 1]
    weighted = jnp.stack([gain_real * real - gain_imag * imag, gain_real * imag + gain_imag * real], axis=3)
    return weighted.astype(jnp.bfloat16)

def reference(samples, gains, feed_slot):
    width = INPUTS // N_FEED

    def one_tile(first):
        words = lax.dynamic_slice_in_dim(samples, first, width, 0)
        scales = lax.dynamic_slice_in_dim(gains, first, width, 2)
        return channelize(words, scales, 1)[:, 0]
    firsts = jnp.arange(N_FEED, dtype=jnp.int32) * width
    tiles = lax.map(one_tile, firsts)
    weighted = jnp.transpose(tiles, (1, 0, 2, 3, 4)).reshape(CH, INPUTS, 2 * SPECTRA)
    span = QUARTS * ROWS

    def one_channel(channel_block):
        ordered = jnp.take(channel_block, feed_slot, axis=0)
        feed_rows = ordered[:span]
        real = feed_rows[:, :SPECTRA]
        imag = feed_rows[:, SPECTRA:]
        left_side = jnp.stack([feed_rows, jnp.concatenate([imag, -real], axis=1)], axis=1)
        left_side = left_side.reshape(2 * span, 2 * SPECTRA)
        product = jnp.dot(left_side, ordered.T, preferred_element_type=jnp.float32)
        return product.reshape(span, 2, INPUTS) * (1.0 / SPECTRA)
    visibility = lax.map(one_channel, weighted)
    return visibility.reshape(N_FEED * ROWS, 2, INPUTS)
```

```python
import functools
import math

import jax
import jax.numpy as jnp
import numpy as np
from jax import lax
from jax.experimental import pallas as pl
from jax.experimental.pallas import tpu as pltpu
from jax.sharding import PartitionSpec as P

TAPS = 8
ROWS = 256
LANES = 128


def filter_taps(ch):
    length = TAPS * ch
    place = np.arange(length, dtype=np.float64)
    window = 0.5 - 0.5 * np.cos(2.0 * math.pi * place / (length - 1))
    return (np.sinc((place - 0.5 * (length - 1)) / ch) * window).reshape(TAPS, ch)


def twiddle(value, turn):
    real, imag = value
    if turn == 0:
        return value
    if turn == 0.25:
        return imag, -real
    half = math.sqrt(0.5)
    if turn == 0.125:
        return half * (real + imag), half * (imag - real)
    if turn == 0.375:
        return half * (imag - real), -half * (real + imag)
    c, s = math.cos(2.0 * math.pi * turn), math.sin(2.0 * math.pi * turn)
    return c * real + s * imag, c * imag - s * real


def fft(values):
    count = len(values)
    if count == 1:
        return values
    even, odd = fft(values[0::2]), fft(values[1::2])
    low, high = [], []
    for index in range(count // 2):
        real, imag = twiddle(odd[index], index / count)
        low.append((even[index][0] + real, even[index][1] + imag))
        high.append((even[index][0] - real, even[index][1] - imag))
    return low + high


def channel_kernel(taps, *refs):
    *samples_refs, gains_ref, out_ref, filtered = refs
    ch, block, width = out_ref.shape
    spectra = width // 2
    padded = len(samples_refs) * LANES
    for k in range(ch):
        words = jnp.concatenate(
            [ref[pl.ds(k, block, stride=ch), :] for ref in samples_refs], axis=1
        )
        levels = ((words >> 4) - 8, (words & 15) - 8)
        for part in range(2):
            value = levels[part].astype(jnp.float32)
            shifted = [value] + [pltpu.roll(value, padded - t, 1) for t in range(1, TAPS // 2)]
            near = float(taps[0, k]) * shifted[0]
            far = float(taps[TAPS // 2, k]) * shifted[0]
            for t in range(1, TAPS // 2):
                near = near + float(taps[t, k]) * shifted[t]
                far = far + float(taps[t + TAPS // 2, k]) * shifted[t]
            total = near + pltpu.roll(far, padded - TAPS // 2, 1)
            filtered[2 * k + part] = total[:, :spectra]
    for row in range(0, block, 8):
        gains = gains_ref[row : row + 8, :]
        for lane in range(0, spectra, LANES):
            spot = (slice(row, row + 8), slice(lane, lane + LANES))
            values = [(filtered[2 * k][spot], filtered[2 * k + 1][spot]) for k in range(ch)]
            for c, (real, imag) in enumerate(fft(values)):
                gain_real = gains[:, c : c + 1]
                gain_imag = gains[:, ch + c : ch + c + 1]
                out_ref[c, row : row + 8, lane : lane + LANES] = (
                    gain_real * real - gain_imag * imag
                ).astype(out_ref.dtype)
                out_ref[c, row : row + 8, spectra + lane : spectra + lane + LANES] = (
                    gain_real * imag + gain_imag * real
                ).astype(out_ref.dtype)


def channelize(samples, gains):
    count, ch, frames = samples.shape
    spectra = frames - TAPS + 1
    block = 16
    pieces = pl.cdiv(frames, LANES)
    scale = 0.125 / math.sqrt(ch) / 2048.0
    taps = (filter_taps(ch) * scale).astype(np.float32)
    return pl.pallas_call(
        functools.partial(channel_kernel, taps),
        grid=(count // block,),
        in_specs=[
            pl.BlockSpec((block * ch, LANES), functools.partial(lambda piece, i: (i, piece), piece))
            for piece in range(pieces)
        ]
        + [pl.BlockSpec((block, 2 * ch), lambda i: (i, 0))],
        out_specs=pl.BlockSpec((ch, block, 2 * spectra), lambda i: (0, i, 0)),
        out_shape=jax.ShapeDtypeStruct((ch, count, 2 * spectra), jnp.bfloat16),
        scratch_shapes=[pltpu.VMEM((2 * ch, block, spectra), jnp.float32)],
        compiler_params=pltpu.CompilerParams(vmem_limit_bytes=32 << 20),
        name="channelize",
    )(*[samples.reshape(count * ch, frames)] * pieces, gains)


def correlate_kernel(scale, slot_ref, row_ref, data_ref, out_ref, products, tile):
    feeds, width = data_ref.shape
    spectra = width // 2
    rows = row_ref.shape[0]
    pieces = 2 * rows // LANES
    step = 256
    picked = jnp.zeros((rows, width), jnp.float32)
    for first in range(0, feeds, 512):
        place = lax.broadcasted_iota(jnp.int32, (rows, 512), 1) + first
        choice = jnp.where(row_ref[...] == place, 1.0, 0.0).astype(jnp.bfloat16)
        picked = picked + jnp.dot(
            choice, data_ref[first : first + 512, :], preferred_element_type=jnp.float32
        )
    left = jnp.concatenate(
        [
            picked,
            jnp.concatenate([picked[:, spectra:], -picked[:, :spectra]], axis=1),
        ],
        axis=0,
    ).astype(jnp.bfloat16)

    @pl.loop(0, feeds // step)
    def _(i):
        first = pl.multiple_of(i * step, step)
        result = lax.dot_general(
            data_ref[pl.ds(first, step), :],
            left,
            (((1,), (1,)), ((), ())),
            preferred_element_type=jnp.float32,
        )
        for piece in range(pieces):
            products[pl.ds(first * pieces + piece, step, stride=pieces), :] = (
                result[:, piece * LANES : (piece + 1) * LANES] * scale
            )

    lines = 2 * (feeds // LANES)

    @pl.loop(0, feeds // LANES)
    def _(j):
        @pl.loop(0, LANES, unroll=16)
        def _(i):
            slot = slot_ref[j * LANES + i]
            tile[pl.ds(pl.multiple_of(i * pieces, pieces), pieces), :] = products[
                pl.ds(pl.multiple_of(slot * pieces, pieces), pieces), :
            ]

        for piece in range(pieces):
            part, first = divmod(piece * LANES, rows)
            turned = tile[pl.ds(piece, LANES, stride=pieces), :].T
            out_ref[pl.ds(first * lines + 2 * j + part, LANES, stride=lines), :] = turned


def correlate(data, feed_slot, first, rows):
    feeds, width = data.shape
    row_slots = lax.dynamic_slice_in_dim(feed_slot, first, rows, 0).reshape(rows, 1)
    lines = 2 * (feeds // LANES)
    out = pl.pallas_call(
        functools.partial(correlate_kernel, 2.0 / width),
        in_specs=[
            pl.BlockSpec(memory_space=pltpu.SMEM),
            pl.BlockSpec(memory_space=pltpu.VMEM),
            pl.BlockSpec(memory_space=pltpu.VMEM),
        ],
        out_specs=pl.BlockSpec(memory_space=pltpu.VMEM),
        out_shape=jax.ShapeDtypeStruct((rows * lines, LANES), jnp.float32),
        scratch_shapes=[
            pltpu.VMEM((feeds * 2 * rows // LANES, LANES), jnp.float32),
            pltpu.VMEM((LANES * 2 * rows // LANES, LANES), jnp.float32),
        ],
        compiler_params=pltpu.CompilerParams(vmem_limit_bytes=48 << 20),
        name="correlate",
    )(feed_slot, row_slots, data)
    out = out.reshape(rows, feeds // LANES, 2, LANES)
    return jnp.transpose(out, (0, 2, 1, 3)).reshape(rows, 2, feeds)


def body(samples, gains, feed_slot):
    count, ch, _ = samples.shape
    groups = lax.axis_size("feed") // ch
    first = lax.axis_index("feed") % groups * ROWS
    scales = jnp.transpose(gains, (2, 0, 1)).reshape(count, 2 * ch).astype(jnp.float32)
    spectra = channelize(samples, scales)
    width = spectra.shape[2]
    outgoing = jnp.broadcast_to(spectra[:, None], (ch, groups, count, width))
    outgoing = outgoing.reshape(ch * groups, count, width)
    moved = lax.all_to_all(outgoing, "feed", split_axis=0, concat_axis=0, tiled=True)
    return correlate(moved.reshape(-1, width), feed_slot, first, ROWS)


def solution(mesh):
    return jax.shard_map(
        body,
        mesh=mesh,
        in_specs=(P(("band", "feed"), None, None), P(None, "band", "feed"), P()),
        out_specs=P(("band", "feed"), None, None),
        check_vma=False,
    )
```

```python
import functools
import math

import jax
import jax.numpy as jnp
import numpy as np
from jax import lax
from jax.experimental import pallas as pl
from jax.experimental.pallas import tpu as pltpu
from jax.sharding import PartitionSpec as P

TAPS = 8
ROWS = 256
LANES = 128


def filter_taps(ch):
    length = TAPS * ch
    place = np.arange(length, dtype=np.float64)
    window = 0.5 - 0.5 * np.cos(2.0 * math.pi * place / (length - 1))
    return (np.sinc((place - 0.5 * (length - 1)) / ch) * window).reshape(TAPS, ch)


def twiddle(value, turn):
    real, imag = value
    if turn == 0:
        return value
    if turn == 0.25:
        return imag, -real
    half = math.sqrt(0.5)
    if turn == 0.125:
        return half * (real + imag), half * (imag - real)
    if turn == 0.375:
        return half * (imag - real), -half * (real + imag)
    c, s = math.cos(2.0 * math.pi * turn), math.sin(2.0 * math.pi * turn)
    return c * real + s * imag, c * imag - s * real


def fft(values):
    count = len(values)
    if count == 1:
        return values
    even, odd = fft(values[0::2]), fft(values[1::2])
    low, high = [], []
    for index in range(count // 2):
        real, imag = twiddle(odd[index], index / count)
        low.append((even[index][0] + real, even[index][1] + imag))
        high.append((even[index][0] - real, even[index][1] - imag))
    return low + high


def channel_kernel(taps, *refs):
    *samples_refs, gains_ref, out_ref, filtered = refs
    ch, block, width = out_ref.shape
    spectra = width // 2
    padded = len(samples_refs) * LANES
    for k in range(ch):
        words = jnp.concatenate(
            [ref[pl.ds(k, block, stride=ch), :] for ref in samples_refs], axis=1
        )
        levels = ((words >> 4) - 8, (words & 15) - 8)
        for part in range(2):
            value = levels[part].astype(jnp.float32)
            shifted = [value] + [pltpu.roll(value, padded - t, 1) for t in range(1, TAPS // 2)]
            near = float(taps[0, k]) * shifted[0]
            far = float(taps[TAPS // 2, k]) * shifted[0]
            for t in range(1, TAPS // 2):
                near = near + float(taps[t, k]) * shifted[t]
                far = far + float(taps[t + TAPS // 2, k]) * shifted[t]
            total = near + pltpu.roll(far, padded - TAPS // 2, 1)
            filtered[2 * k + part] = total[:, :spectra]
    for row in range(0, block, 8):
        gains = gains_ref[row : row + 8, :]
        for lane in range(0, spectra, LANES):
            spot = (slice(row, row + 8), slice(lane, lane + LANES))
            values = [(filtered[2 * k][spot], filtered[2 * k + 1][spot]) for k in range(ch)]
            for c, (real, imag) in enumerate(fft(values)):
                gain_real = gains[:, c : c + 1]
                gain_imag = gains[:, ch + c : ch + c + 1]
                out_ref[c, row : row + 8, lane : lane + LANES] = (
                    gain_real * real - gain_imag * imag
                ).astype(out_ref.dtype)
                out_ref[c, row : row + 8, spectra + lane : spectra + lane + LANES] = (
                    gain_real * imag + gain_imag * real
                ).astype(out_ref.dtype)


def channelize(samples, gains):
    count, ch, frames = samples.shape
    spectra = frames - TAPS + 1
    block = 16
    pieces = pl.cdiv(frames, LANES)
    scale = 0.125 / math.sqrt(ch) / 2048.0
    taps = (filter_taps(ch) * scale).astype(np.float32)
    return pl.pallas_call(
        functools.partial(channel_kernel, taps),
        grid=(count // block,),
        in_specs=[
            pl.BlockSpec((block * ch, LANES), functools.partial(lambda piece, i: (i, piece), piece))
            for piece in range(pieces)
        ]
        + [pl.BlockSpec((block, 2 * ch), lambda i: (i, 0))],
        out_specs=pl.BlockSpec((ch, block, 2 * spectra), lambda i: (0, i, 0)),
        out_shape=jax.ShapeDtypeStruct((ch, count, 2 * spectra), jnp.bfloat16),
        scratch_shapes=[pltpu.VMEM((2 * ch, block, spectra), jnp.float32)],
        compiler_params=pltpu.CompilerParams(vmem_limit_bytes=32 << 20),
        name="channelize",
    )(*[samples.reshape(count * ch, frames)] * pieces, gains)


def correlate_kernel(scale, slot_ref, row_ref, data_ref, out_ref, products, tile):
    feeds, width = data_ref.shape
    spectra = width // 2
    rows = row_ref.shape[0]
    pieces = 2 * rows // LANES
    step = 256
    picked = jnp.zeros((rows, width), jnp.float32)
    for first in range(0, feeds, 512):
        place = lax.broadcasted_iota(jnp.int32, (rows, 512), 1) + first
        choice = jnp.where(row_ref[...] == place, 1.0, 0.0).astype(jnp.bfloat16)
        picked = picked + jnp.dot(
            choice, data_ref[first : first + 512, :], preferred_element_type=jnp.float32
        )
    left = jnp.concatenate(
        [
            picked,
            jnp.concatenate([picked[:, spectra:], -picked[:, :spectra]], axis=1),
        ],
        axis=0,
    ).astype(jnp.bfloat16)

    @pl.loop(0, feeds // step)
    def _(i):
        first = pl.multiple_of(i * step, step)
        result = lax.dot_general(
            data_ref[pl.ds(first, step), :],
            left,
            (((1,), (1,)), ((), ())),
            preferred_element_type=jnp.float32,
        )
        for piece in range(pieces):
            products[pl.ds(first * pieces + piece, step, stride=pieces), :] = (
                result[:, piece * LANES : (piece + 1) * LANES] * scale
            )

    lines = 2 * (feeds // LANES)

    @pl.loop(0, feeds // LANES)
    def _(j):
        @pl.loop(0, LANES, unroll=16)
        def _(i):
            slot = slot_ref[j * LANES + i]
            tile[pl.ds(pl.multiple_of(i * pieces, pieces), pieces), :] = products[
                pl.ds(pl.multiple_of(slot * pieces, pieces), pieces), :
            ]

        for piece in range(pieces):
            part, first = divmod(piece * LANES, rows)
            turned = tile[pl.ds(piece, LANES, stride=pieces), :].T
            out_ref[pl.ds(first * lines + 2 * j + part, LANES, stride=lines), :] = turned


def correlate(data, feed_slot, first, rows):
    feeds, width = data.shape
    row_slots = lax.dynamic_slice_in_dim(feed_slot, first, rows, 0).reshape(rows, 1)
    lines = 2 * (feeds // LANES)
    out = pl.pallas_call(
        functools.partial(correlate_kernel, 2.0 / width),
        in_specs=[
            pl.BlockSpec(memory_space=pltpu.SMEM),
            pl.BlockSpec(memory_space=pltpu.VMEM),
            pl.BlockSpec(memory_space=pltpu.VMEM),
        ],
        out_specs=pl.BlockSpec(memory_space=pltpu.VMEM),
        out_shape=jax.ShapeDtypeStruct((rows * lines, LANES), jnp.float32),
        scratch_shapes=[
            pltpu.VMEM((feeds * 2 * rows // LANES, LANES), jnp.float32),
            pltpu.VMEM((LANES * 2 * rows // LANES, LANES), jnp.float32),
        ],
        compiler_params=pltpu.CompilerParams(vmem_limit_bytes=48 << 20),
        name="correlate",
    )(feed_slot, row_slots, data)
    out = out.reshape(rows, feeds // LANES, 2, LANES)
    return jnp.transpose(out, (0, 2, 1, 3)).reshape(rows, 2, feeds)


def through_spectra(samples, gains, feed_slot):
    count, ch, _ = samples.shape
    groups = lax.axis_size("feed") // ch
    first = lax.axis_index("feed") % groups * ROWS
    scales = jnp.transpose(gains, (2, 0, 1)).reshape(count, 2 * ch).astype(jnp.float32)
    spectra = channelize(samples, scales)
    width = spectra.shape[2]
    outgoing = jnp.broadcast_to(spectra[:, None], (ch, groups, count, width))
    outgoing = outgoing.reshape(ch * groups, count, width)
    moved = lax.all_to_all(outgoing, "feed", split_axis=0, concat_axis=0, tiled=True)
    return correlate(moved.reshape(-1, width), feed_slot, first, ROWS)


STEP = 8
SPAN = 16
STEPS = 8
RANGE = 14


def filter_weights(ch):
    taps = filter_taps(ch) * (0.125 / math.sqrt(ch) / 2048.0)
    weights = np.zeros((ch, 2, STEP, 2, SPAN, ch))
    angle = 2.0 * math.pi * (np.arange(ch)[:, None] * np.arange(ch)[None, :] % ch) / ch
    for spectrum in range(STEP):
        for t in range(TAPS):
            cosine, sine = taps[t] * np.cos(angle), taps[t] * np.sin(angle)
            weights[:, 0, spectrum, 0, spectrum + t] = cosine
            weights[:, 0, spectrum, 1, spectrum + t] = sine
            weights[:, 1, spectrum, 0, spectrum + t] = -sine
            weights[:, 1, spectrum, 1, spectrum + t] = cosine
    weights = weights.reshape(ch * 2 * STEP, 2, SPAN * ch)
    high = weights.astype(jnp.bfloat16)
    low = (weights - high.astype(np.float64)).astype(jnp.bfloat16)
    return np.stack([high[:, 0], high[:, 1], low[:, 0], low[:, 1]])


def spectra_of(weights_ref, levels, gains, ch, store):
    count = levels[0].shape[1]
    for b in range(STEPS):
        spot = slice(b * STEP * ch, b * STEP * ch + SPAN * ch)
        total = None
        for part in range(2):
            slab = levels[part][spot]
            for split in range(2):
                term = jnp.dot(weights_ref[2 * split + part], slab, preferred_element_type=jnp.float32)
                total = term if total is None else total + term
        for c in range(ch):
            real = total[c * 2 * STEP : c * 2 * STEP + STEP]
            imag = total[c * 2 * STEP + STEP : (c + 1) * 2 * STEP]
            gain_real, gain_imag = gains[c : c + 1], gains[ch + c : ch + c + 1]
            store(b, c, gain_real * real - gain_imag * imag, gain_real * imag + gain_imag * real)


def levels_of(words):
    return [
        ((words >> 4) - 8).astype(jnp.float32).astype(jnp.bfloat16),
        ((words & 15) - 8).astype(jnp.float32).astype(jnp.bfloat16),
    ]


def own_kernel(main_ref, next_ref, gains_ref, weights_ref, out_ref):
    ch = out_ref.shape[0]
    words = jnp.concatenate([main_ref[...], next_ref[...]], axis=0)

    def store(b, c, real, imag):
        out_ref[c, b * 2 * STEP : (b + 1) * 2 * STEP, :] = jnp.concatenate([real, imag], axis=0).astype(
            out_ref.dtype
        )

    spectra_of(weights_ref, levels_of(words), gains_ref[...], ch, store)


def own_spectra(words, gains, weights, ch, spectra):
    count = words.shape[1]
    main = STEPS * STEP * ch
    return pl.pallas_call(
        own_kernel,
        grid=(spectra // (STEPS * STEP),),
        in_specs=[
            pl.BlockSpec((main, count), lambda i: (i, 0)),
            pl.BlockSpec((STEP * ch, count), lambda i: ((i + 1) * STEPS, 0)),
            pl.BlockSpec(gains.shape, lambda i: (0, 0)),
            pl.BlockSpec(weights.shape, lambda i: (0, 0, 0)),
        ],
        out_specs=pl.BlockSpec((ch, 2 * STEPS * STEP, count), lambda i: (0, i, 0)),
        out_shape=jax.ShapeDtypeStruct((ch, 2 * spectra, count), jnp.bfloat16),
        compiler_params=pltpu.CompilerParams(vmem_limit_bytes=40 << 20),
        name="own_spectra",
    )(words, words, gains, weights)


def select_kernel(last_rows, slots_ref, words_ref, parts_ref, *outs):
    step = pl.program_id(0)
    count = words_ref.shape[1]
    words = words_ref[...].astype(jnp.float32).astype(jnp.bfloat16)
    for index, out_ref in enumerate(outs):
        rows = out_ref.shape[1]
        place = lax.broadcasted_iota(jnp.int32, (count, rows), 0)
        choice = jnp.where(slots_ref[index : index + 1, :] == place, 1.0, 0.0).astype(jnp.bfloat16)
        out_ref[...] = jnp.dot(words, choice, preferred_element_type=jnp.float32).astype(out_ref.dtype)

        @pl.when(step == pl.num_programs(0) - 1)
        def _():
            extra = parts_ref.shape[0]
            out_ref[last_rows : last_rows + extra, :] = jnp.dot(
                parts_ref[...], choice, preferred_element_type=jnp.float32
            ).astype(out_ref.dtype)
            left = out_ref.shape[0] - last_rows - extra
            out_ref[last_rows + extra :, :] = jnp.zeros((left, rows), out_ref.dtype)


def select_rows(words, gains, slots, total):
    lines, count = words.shape
    pieces, rows = slots.shape
    block = total // STEPS
    parts = jnp.concatenate([gains >> 4, gains & 15], axis=0).astype(jnp.bfloat16)
    return pl.pallas_call(
        functools.partial(select_kernel, lines - (STEPS - 1) * block),
        grid=(STEPS,),
        in_specs=[
            pl.BlockSpec((pieces, rows), lambda i: (0, 0)),
            pl.BlockSpec((block, count), lambda i: (i, 0)),
            pl.BlockSpec(parts.shape, lambda i: (0, 0)),
        ],
        out_specs=[pl.BlockSpec((block, rows), lambda i: (i, 0))] * pieces,
        out_shape=[jax.ShapeDtypeStruct((total, rows), jnp.bfloat16)] * pieces,
        compiler_params=pltpu.CompilerParams(vmem_limit_bytes=24 << 20),
        name="select_rows",
    )(slots, words, parts)


def swap(value, bit):
    pairs = [(index, index ^ bit) for index in range(lax.axis_size("feed"))]
    return lax.ppermute(value, "feed", pairs)


def side(bit):
    return lax.axis_index("feed") // bit % 2


def reduce_half(value, bit):
    size = value.shape[0] // 2
    keep = lax.dynamic_slice_in_dim(value, side(bit) * size, size, 0)
    send = lax.dynamic_slice_in_dim(value, (1 - side(bit)) * size, size, 0)
    return keep + swap(send, bit)


def gather_half(value, bit, buffer):
    size = value.shape[0]
    other = swap(value, bit)
    buffer = lax.dynamic_update_slice_in_dim(buffer, value, side(bit) * size, 0)
    return lax.dynamic_update_slice_in_dim(buffer, other, (1 - side(bit)) * size, 0)


def sum_over_feed(value):
    half = reduce_half(value, 1)
    size = half.shape[0] // 2
    left, right = half[:size], half[size:]
    left_1, right_1 = reduce_half(left, 2), reduce_half(right, 4)
    left_2, right_2 = reduce_half(left_1, 4), reduce_half(right_1, 2)
    left_3, right_3 = left_2 + swap(left_2, 8), right_2 + swap(right_2, 8)
    left_1, right_1 = gather_half(left_3, 4, left_1), gather_half(right_3, 2, right_1)
    left, right = gather_half(left_1, 2, left), gather_half(right_1, 4, right)
    return gather_half(jnp.concatenate([left, right], axis=0), 1, value)


def rows_kernel(main_ref, next_ref, parts_ref, weights_ref, own_ref, out_ref, left):
    step = pl.program_id(0)
    steps = pl.num_programs(0) // 2
    ch = left.shape[0]
    rows = main_ref.shape[1]

    @pl.when(step < steps)
    def _():
        words = jnp.concatenate([main_ref[...], next_ref[...]], axis=0).astype(jnp.float32).astype(jnp.int32)
        parts = parts_ref[...].astype(jnp.float32)
        gains = parts[: 2 * ch] * 16.0 + parts[2 * ch :]

        def store(b, c, real, imag):
            spot = pl.ds(pl.multiple_of(step * (2 * STEPS * STEP), 2 * STEPS * STEP) + b * 2 * STEP, 2 * STEP)
            left[c, spot, :rows] = jnp.concatenate([real, imag], axis=0).astype(left.dtype)
            left[c, spot, rows:] = jnp.concatenate([imag, -real], axis=0).astype(left.dtype)

        spectra_of(weights_ref, levels_of(words), gains, ch, store)

    @pl.when(step >= steps)
    def _():
        each = own_ref.shape[0]
        for index in range(each):
            products = lax.dot_general(
                own_ref[index],
                left[(step - steps) * each + index],
                (((0,), (0,)), ((), ())),
                preferred_element_type=jnp.float32,
            )
            count = products.shape[0]
            largest = jnp.maximum(jnp.max(jnp.abs(products), axis=0, keepdims=True), 2.0**-60)
            power = jnp.floor(jnp.log2(largest))
            coded = jnp.clip(jnp.round(products * jnp.exp2(RANGE - power)), -32767.0, 32767.0)
            out_ref[index, :count, :] = coded.astype(jnp.int32).astype(jnp.int16)
            line = jnp.broadcast_to(power, (out_ref.shape[1] - count, power.shape[1]))
            out_ref[index, count:, :] = line.astype(jnp.int32).astype(jnp.int16)


def row_products(words, own, weights, lines):
    ch, width, count = own.shape
    rows = words.shape[1]
    main = STEPS * STEP * ch
    steps = width // (2 * STEPS * STEP)
    each = ch // steps
    parts = words[lines : lines + 4 * ch]
    return pl.pallas_call(
        rows_kernel,
        grid=(2 * steps,),
        in_specs=[
            pl.BlockSpec((main, rows), lambda i: (jnp.minimum(i, steps - 1), 0)),
            pl.BlockSpec((STEP * ch, rows), lambda i: ((jnp.minimum(i, steps - 1) + 1) * STEPS, 0)),
            pl.BlockSpec(parts.shape, lambda i: (0, 0)),
            pl.BlockSpec(weights.shape, lambda i: (0, 0, 0)),
            pl.BlockSpec((each, width, count), lambda i: (jnp.maximum(i - steps, 0), 0, 0)),
        ],
        out_specs=pl.BlockSpec((each, count + 16, 2 * rows), lambda i: (jnp.maximum(i - steps, 0), 0, 0)),
        out_shape=jax.ShapeDtypeStruct((ch, count + 16, 2 * rows), jnp.int16),
        scratch_shapes=[pltpu.VMEM((ch, width, 2 * rows), jnp.bfloat16)],
        compiler_params=pltpu.CompilerParams(vmem_limit_bytes=40 << 20),
        name="row_products",
    )(words, words, parts, weights, own)


def finish_kernel(scale, slot_ref, coded_ref, *refs):
    out_ref, products, tile = refs[-3:]
    step = pl.program_id(0)
    sources, lines, width = coded_ref.shape
    count = lines - 16
    pieces = width // LANES
    feeds = sources * count
    columns = 2 * (feeds // LANES)
    for source in range(sources):
        power = coded_ref[source, count : count + 16, :][:1].astype(jnp.float32)
        values = coded_ref[source, :count, :].astype(jnp.float32) * (jnp.exp2(power - RANGE) * scale)
        for piece in range(pieces):
            products[pl.ds(source * count * pieces + piece, count, stride=pieces), :] = values[
                :, piece * LANES : (piece + 1) * LANES
            ]

    @pl.loop(0, feeds // LANES)
    def _(j):
        @pl.loop(0, LANES, unroll=16)
        def _(i):
            slot = slot_ref[j * LANES + i]
            tile[pl.ds(pl.multiple_of(i * pieces, pieces), pieces), :] = products[
                pl.ds(pl.multiple_of(slot * pieces, pieces), pieces), :
            ]

        for piece in range(pieces):
            turned = tile[pl.ds(piece, LANES, stride=pieces), :].T
            out_ref[pl.ds(2 * j + piece, LANES, stride=columns), :] = turned


def finish(coded, feed_slot, index, pieces, scale, before):
    sources, lines, width = coded.shape
    rows = width // 2
    feeds = sources * (lines - 16)
    columns = 2 * (feeds // LANES)
    earlier = [] if before is None else [before]
    return pl.pallas_call(
        functools.partial(finish_kernel, scale),
        grid=(1,),
        in_specs=[
            pl.BlockSpec(memory_space=pltpu.SMEM),
            pl.BlockSpec(coded.shape, lambda i: (0, 0, 0)),
        ]
        + [pl.BlockSpec(memory_space=pl.ANY)] * len(earlier),
        out_specs=pl.BlockSpec((rows * columns, LANES), lambda i: (index, 0)),
        out_shape=jax.ShapeDtypeStruct((pieces * rows * columns, LANES), jnp.float32),
        scratch_shapes=[
            pltpu.VMEM((feeds * width // LANES, LANES), jnp.float32),
            pltpu.VMEM((width, LANES), jnp.float32),
        ],
        input_output_aliases={2: 0} if earlier else {},
        compiler_params=pltpu.CompilerParams(vmem_limit_bytes=40 << 20),
        name="finish",
    )(feed_slot, coded, *earlier)


def through_rows(samples, gains, feed_slot):
    count, ch, frames = samples.shape
    spectra = frames - TAPS + 1
    pieces = ROWS // LANES
    lines = frames * ch
    unit = 16 * STEPS * 2
    total = pl.cdiv(lines + 4 * ch, unit) * unit
    words = jnp.transpose(samples, (2, 1, 0)).reshape(lines, count)
    scales = gains.reshape(2 * ch, count)
    weights = jnp.asarray(filter_weights(ch))
    slots = (feed_slot[:ROWS] - lax.axis_index("feed") * count).reshape(pieces, LANES)
    picked = select_rows(words, scales, slots, total)
    own = own_spectra(words, scales.astype(jnp.float32), weights, ch, spectra)
    out = None
    for index in range(pieces):
        rows = sum_over_feed(picked[index])
        coded = row_products(rows, own, weights, lines)
        moved = lax.all_to_all(coded, "feed", split_axis=0, concat_axis=0, tiled=True)
        out = finish(moved, feed_slot, index, pieces, 1.0 / spectra, out)
    feeds = feed_slot.shape[0]
    out = out.reshape(ROWS, feeds // LANES, 2, LANES)
    return jnp.transpose(out, (0, 2, 1, 3)).reshape(ROWS, 2, feeds)


def body(samples, gains, feed_slot):
    count, ch, frames = samples.shape
    spectra = frames - TAPS + 1
    even = count % LANES == 0 and spectra % (STEPS * STEP) == 0 and ch % STEPS == 0
    if lax.axis_size("feed") == ch == 16 and even:
        return through_rows(samples, gains, feed_slot)
    return through_spectra(samples, gains, feed_slot)


def solution(mesh):
    return jax.shard_map(
        body,
        mesh=mesh,
        in_specs=(P(("band", "feed"), None, None), P(None, "band", "feed"), P()),
        out_specs=P(("band", "feed"), None, None),
        check_vma=False,
    )
```

```python
import functools
import math

import jax
import jax.numpy as jnp
import numpy as np
from jax import lax
from jax.experimental import pallas as pl
from jax.experimental.pallas import tpu as pltpu
from jax.sharding import PartitionSpec as P

TAPS = 8
ROWS = 256
LANES = 128


def filter_taps(ch):
    length = TAPS * ch
    place = np.arange(length, dtype=np.float64)
    window = 0.5 - 0.5 * np.cos(2.0 * math.pi * place / (length - 1))
    return (np.sinc((place - 0.5 * (length - 1)) / ch) * window).reshape(TAPS, ch)


def twiddle(value, turn):
    real, imag = value
    if turn == 0:
        return value
    if turn == 0.25:
        return imag, -real
    half = math.sqrt(0.5)
    if turn == 0.125:
        return half * (real + imag), half * (imag - real)
    if turn == 0.375:
        return half * (imag - real), -half * (real + imag)
    c, s = math.cos(2.0 * math.pi * turn), math.sin(2.0 * math.pi * turn)
    return c * real + s * imag, c * imag - s * real


def fft(values):
    count = len(values)
    if count == 1:
        return values
    even, odd = fft(values[0::2]), fft(values[1::2])
    low, high = [], []
    for index in range(count // 2):
        real, imag = twiddle(odd[index], index / count)
        low.append((even[index][0] + real, even[index][1] + imag))
        high.append((even[index][0] - real, even[index][1] - imag))
    return low + high


def channel_kernel(taps, *refs):
    *samples_refs, gains_ref, out_ref, filtered = refs
    ch, block, width = out_ref.shape
    spectra = width // 2
    padded = len(samples_refs) * LANES
    for k in range(ch):
        words = jnp.concatenate(
            [ref[pl.ds(k, block, stride=ch), :] for ref in samples_refs], axis=1
        )
        levels = ((words >> 4) - 8, (words & 15) - 8)
        for part in range(2):
            value = levels[part].astype(jnp.float32)
            shifted = [value] + [pltpu.roll(value, padded - t, 1) for t in range(1, TAPS // 2)]
            near = float(taps[0, k]) * shifted[0]
            far = float(taps[TAPS // 2, k]) * shifted[0]
            for t in range(1, TAPS // 2):
                near = near + float(taps[t, k]) * shifted[t]
                far = far + float(taps[t + TAPS // 2, k]) * shifted[t]
            total = near + pltpu.roll(far, padded - TAPS // 2, 1)
            filtered[2 * k + part] = total[:, :spectra]
    for row in range(0, block, 8):
        gains = gains_ref[row : row + 8, :]
        for lane in range(0, spectra, LANES):
            spot = (slice(row, row + 8), slice(lane, lane + LANES))
            values = [(filtered[2 * k][spot], filtered[2 * k + 1][spot]) for k in range(ch)]
            for c, (real, imag) in enumerate(fft(values)):
                gain_real = gains[:, c : c + 1]
                gain_imag = gains[:, ch + c : ch + c + 1]
                out_ref[c, row : row + 8, lane : lane + LANES] = (
                    gain_real * real - gain_imag * imag
                ).astype(out_ref.dtype)
                out_ref[c, row : row + 8, spectra + lane : spectra + lane + LANES] = (
                    gain_real * imag + gain_imag * real
                ).astype(out_ref.dtype)


def channelize(samples, gains):
    count, ch, frames = samples.shape
    spectra = frames - TAPS + 1
    block = 16
    pieces = pl.cdiv(frames, LANES)
    scale = 0.125 / math.sqrt(ch) / 2048.0
    taps = (filter_taps(ch) * scale).astype(np.float32)
    return pl.pallas_call(
        functools.partial(channel_kernel, taps),
        grid=(count // block,),
        in_specs=[
            pl.BlockSpec((block * ch, LANES), functools.partial(lambda piece, i: (i, piece), piece))
            for piece in range(pieces)
        ]
        + [pl.BlockSpec((block, 2 * ch), lambda i: (i, 0))],
        out_specs=pl.BlockSpec((ch, block, 2 * spectra), lambda i: (0, i, 0)),
        out_shape=jax.ShapeDtypeStruct((ch, count, 2 * spectra), jnp.bfloat16),
        scratch_shapes=[pltpu.VMEM((2 * ch, block, spectra), jnp.float32)],
        compiler_params=pltpu.CompilerParams(vmem_limit_bytes=32 << 20),
        name="channelize",
    )(*[samples.reshape(count * ch, frames)] * pieces, gains)


def correlate_kernel(scale, slot_ref, row_ref, data_ref, out_ref, products, tile):
    feeds, width = data_ref.shape
    spectra = width // 2
    rows = row_ref.shape[0]
    pieces = 2 * rows // LANES
    step = 256
    picked = jnp.zeros((rows, width), jnp.float32)
    for first in range(0, feeds, 512):
        place = lax.broadcasted_iota(jnp.int32, (rows, 512), 1) + first
        choice = jnp.where(row_ref[...] == place, 1.0, 0.0).astype(jnp.bfloat16)
        picked = picked + jnp.dot(
            choice, data_ref[first : first + 512, :], preferred_element_type=jnp.float32
        )
    left = jnp.concatenate(
        [
            picked,
            jnp.concatenate([picked[:, spectra:], -picked[:, :spectra]], axis=1),
        ],
        axis=0,
    ).astype(jnp.bfloat16)

    @pl.loop(0, feeds // step)
    def _(i):
        first = pl.multiple_of(i * step, step)
        result = lax.dot_general(
            data_ref[pl.ds(first, step), :],
            left,
            (((1,), (1,)), ((), ())),
            preferred_element_type=jnp.float32,
        )
        for piece in range(pieces):
            products[pl.ds(first * pieces + piece, step, stride=pieces), :] = (
                result[:, piece * LANES : (piece + 1) * LANES] * scale
            )

    lines = 2 * (feeds // LANES)

    @pl.loop(0, feeds // LANES)
    def _(j):
        @pl.loop(0, LANES, unroll=16)
        def _(i):
            slot = slot_ref[j * LANES + i]
            tile[pl.ds(pl.multiple_of(i * pieces, pieces), pieces), :] = products[
                pl.ds(pl.multiple_of(slot * pieces, pieces), pieces), :
            ]

        for piece in range(pieces):
            part, first = divmod(piece * LANES, rows)
            turned = tile[pl.ds(piece, LANES, stride=pieces), :].T
            out_ref[pl.ds(first * lines + 2 * j + part, LANES, stride=lines), :] = turned


def correlate(data, feed_slot, first, rows):
    feeds, width = data.shape
    row_slots = lax.dynamic_slice_in_dim(feed_slot, first, rows, 0).reshape(rows, 1)
    lines = 2 * (feeds // LANES)
    out = pl.pallas_call(
        functools.partial(correlate_kernel, 2.0 / width),
        in_specs=[
            pl.BlockSpec(memory_space=pltpu.SMEM),
            pl.BlockSpec(memory_space=pltpu.VMEM),
            pl.BlockSpec(memory_space=pltpu.VMEM),
        ],
        out_specs=pl.BlockSpec(memory_space=pltpu.VMEM),
        out_shape=jax.ShapeDtypeStruct((rows * lines, LANES), jnp.float32),
        scratch_shapes=[
            pltpu.VMEM((feeds * 2 * rows // LANES, LANES), jnp.float32),
            pltpu.VMEM((LANES * 2 * rows // LANES, LANES), jnp.float32),
        ],
        compiler_params=pltpu.CompilerParams(vmem_limit_bytes=48 << 20),
        name="correlate",
    )(feed_slot, row_slots, data)
    out = out.reshape(rows, feeds // LANES, 2, LANES)
    return jnp.transpose(out, (0, 2, 1, 3)).reshape(rows, 2, feeds)


def through_spectra(samples, gains, feed_slot):
    count, ch, _ = samples.shape
    groups = lax.axis_size("feed") // ch
    first = lax.axis_index("feed") % groups * ROWS
    scales = jnp.transpose(gains, (2, 0, 1)).reshape(count, 2 * ch).astype(jnp.float32)
    spectra = channelize(samples, scales)
    width = spectra.shape[2]
    outgoing = jnp.broadcast_to(spectra[:, None], (ch, groups, count, width))
    outgoing = outgoing.reshape(ch * groups, count, width)
    moved = lax.all_to_all(outgoing, "feed", split_axis=0, concat_axis=0, tiled=True)
    return correlate(moved.reshape(-1, width), feed_slot, first, ROWS)


STEP = 8
SPAN = 16
STEPS = 8
RANGE = 14


def filter_weights(ch):
    taps = filter_taps(ch) * (0.125 / math.sqrt(ch) / 2048.0)
    weights = np.zeros((ch, 2, STEP, 2, SPAN, ch))
    angle = 2.0 * math.pi * (np.arange(ch)[:, None] * np.arange(ch)[None, :] % ch) / ch
    for spectrum in range(STEP):
        for t in range(TAPS):
            cosine, sine = taps[t] * np.cos(angle), taps[t] * np.sin(angle)
            weights[:, 0, spectrum, 0, spectrum + t] = cosine
            weights[:, 0, spectrum, 1, spectrum + t] = sine
            weights[:, 1, spectrum, 0, spectrum + t] = -sine
            weights[:, 1, spectrum, 1, spectrum + t] = cosine
    weights = weights.reshape(ch * 2 * STEP, 2, SPAN * ch)
    high = weights.astype(jnp.bfloat16)
    low = (weights - high.astype(np.float64)).astype(jnp.bfloat16)
    return np.stack([high[:, 0], high[:, 1], low[:, 0], low[:, 1]])


def spectra_of(weights_ref, levels, gains, ch, store):
    count = levels[0].shape[1]
    for b in range(STEPS):
        spot = slice(b * STEP * ch, b * STEP * ch + SPAN * ch)
        total = None
        for part in range(2):
            slab = levels[part][spot]
            for split in range(2):
                term = jnp.dot(weights_ref[2 * split + part], slab, preferred_element_type=jnp.float32)
                total = term if total is None else total + term
        for c in range(ch):
            real = total[c * 2 * STEP : c * 2 * STEP + STEP]
            imag = total[c * 2 * STEP + STEP : (c + 1) * 2 * STEP]
            gain_real, gain_imag = gains[c : c + 1], gains[ch + c : ch + c + 1]
            store(b, c, gain_real * real - gain_imag * imag, gain_real * imag + gain_imag * real)


def levels_of(words):
    return [
        ((words >> 4) - 8).astype(jnp.float32).astype(jnp.bfloat16),
        ((words & 15) - 8).astype(jnp.float32).astype(jnp.bfloat16),
    ]


def own_kernel(main_ref, next_ref, gains_ref, weights_ref, out_ref):
    ch = out_ref.shape[0]
    words = jnp.concatenate([main_ref[...], next_ref[...]], axis=0)

    def store(b, c, real, imag):
        out_ref[c, b * 2 * STEP : (b + 1) * 2 * STEP, :] = jnp.concatenate([real, imag], axis=0).astype(
            out_ref.dtype
        )

    spectra_of(weights_ref, levels_of(words), gains_ref[...], ch, store)


def own_spectra(words, gains, weights, ch, spectra):
    count = words.shape[1]
    main = STEPS * STEP * ch
    return pl.pallas_call(
        own_kernel,
        grid=(spectra // (STEPS * STEP),),
        in_specs=[
            pl.BlockSpec((main, count), lambda i: (i, 0)),
            pl.BlockSpec((STEP * ch, count), lambda i: ((i + 1) * STEPS, 0)),
            pl.BlockSpec(gains.shape, lambda i: (0, 0)),
            pl.BlockSpec(weights.shape, lambda i: (0, 0, 0)),
        ],
        out_specs=pl.BlockSpec((ch, 2 * STEPS * STEP, count), lambda i: (0, i, 0)),
        out_shape=jax.ShapeDtypeStruct((ch, 2 * spectra, count), jnp.bfloat16),
        compiler_params=pltpu.CompilerParams(vmem_limit_bytes=40 << 20),
        name="own_spectra",
    )(words, words, gains, weights)


def select_kernel(last_rows, slots_ref, words_ref, parts_ref, out_ref):
    step = pl.program_id(0)
    count, rows = words_ref.shape[1], out_ref.shape[1]
    words = words_ref[...].astype(jnp.float32).astype(jnp.bfloat16)
    place = lax.broadcasted_iota(jnp.int32, (count, rows), 0)
    choice = jnp.where(slots_ref[...] == place, 1.0, 0.0).astype(jnp.bfloat16)
    out_ref[...] = jnp.dot(words, choice, preferred_element_type=jnp.float32).astype(out_ref.dtype)

    @pl.when(step == pl.num_programs(0) - 1)
    def _():
        extra = parts_ref.shape[0]
        out_ref[last_rows : last_rows + extra, :] = jnp.dot(
            parts_ref[...], choice, preferred_element_type=jnp.float32
        ).astype(out_ref.dtype)
        left = out_ref.shape[0] - last_rows - extra
        out_ref[last_rows + extra :, :] = jnp.zeros((left, rows), out_ref.dtype)


def select_rows(words, gains, slots, total):
    lines, count = words.shape
    rows = slots.shape[1]
    block = total // STEPS
    parts = jnp.concatenate([gains >> 4, gains & 15], axis=0).astype(jnp.bfloat16)
    return pl.pallas_call(
        functools.partial(select_kernel, lines - (STEPS - 1) * block),
        grid=(STEPS,),
        in_specs=[
            pl.BlockSpec((1, rows), lambda i: (0, 0)),
            pl.BlockSpec((block, count), lambda i: (i, 0)),
            pl.BlockSpec(parts.shape, lambda i: (0, 0)),
        ],
        out_specs=pl.BlockSpec((block, rows), lambda i: (i, 0)),
        out_shape=jax.ShapeDtypeStruct((total, rows), jnp.bfloat16),
        compiler_params=pltpu.CompilerParams(vmem_limit_bytes=24 << 20),
        name="select_rows",
    )(slots, words, parts)


def swap(value, bit):
    pairs = [(index, index ^ bit) for index in range(lax.axis_size("feed"))]
    return lax.ppermute(value, "feed", pairs)


def side(bit):
    return lax.axis_index("feed") // bit % 2


def reduce_half(value, bit):
    size = value.shape[0] // 2
    keep = lax.dynamic_slice_in_dim(value, side(bit) * size, size, 0)
    send = lax.dynamic_slice_in_dim(value, (1 - side(bit)) * size, size, 0)
    return keep + swap(send, bit)


def gather_half(value, bit, buffer):
    size = value.shape[0]
    other = swap(value, bit)
    buffer = lax.dynamic_update_slice_in_dim(buffer, value, side(bit) * size, 0)
    return lax.dynamic_update_slice_in_dim(buffer, other, (1 - side(bit)) * size, 0)


def sum_over_feed(value):
    half = reduce_half(value, 1)
    size = half.shape[0] // 2
    left, right = half[:size], half[size:]
    left_1, right_1 = reduce_half(left, 2), reduce_half(right, 4)
    left_2, right_2 = reduce_half(left_1, 4), reduce_half(right_1, 2)
    left_3, right_3 = left_2 + swap(left_2, 8), right_2 + swap(right_2, 8)
    left_1, right_1 = gather_half(left_3, 4, left_1), gather_half(right_3, 2, right_1)
    left, right = gather_half(left_1, 2, left), gather_half(right_1, 4, right)
    return gather_half(jnp.concatenate([left, right], axis=0), 1, value)


def rows_kernel(main_ref, next_ref, parts_ref, weights_ref, own_ref, out_ref, left):
    step = pl.program_id(0)
    steps = pl.num_programs(0) // 2
    ch = left.shape[0]
    rows = main_ref.shape[1]

    @pl.when(step < steps)
    def _():
        words = jnp.concatenate([main_ref[...], next_ref[...]], axis=0).astype(jnp.float32).astype(jnp.int32)
        parts = parts_ref[...].astype(jnp.float32)
        gains = parts[: 2 * ch] * 16.0 + parts[2 * ch :]

        def store(b, c, real, imag):
            spot = pl.ds(pl.multiple_of(step * (2 * STEPS * STEP), 2 * STEPS * STEP) + b * 2 * STEP, 2 * STEP)
            left[c, spot, :rows] = jnp.concatenate([real, imag], axis=0).astype(left.dtype)
            left[c, spot, rows:] = jnp.concatenate([imag, -real], axis=0).astype(left.dtype)

        spectra_of(weights_ref, levels_of(words), gains, ch, store)

    @pl.when(step >= steps)
    def _():
        each = own_ref.shape[0]
        for index in range(each):
            products = lax.dot_general(
                own_ref[index],
                left[(step - steps) * each + index],
                (((0,), (0,)), ((), ())),
                preferred_element_type=jnp.float32,
            )
            count = products.shape[0]
            largest = jnp.maximum(jnp.max(jnp.abs(products), axis=0, keepdims=True), 2.0**-60)
            power = jnp.floor(jnp.log2(largest))
            coded = jnp.clip(jnp.round(products * jnp.exp2(RANGE - power)), -32767.0, 32767.0)
            out_ref[index, :count, :] = coded.astype(jnp.int32).astype(jnp.int16)
            line = jnp.broadcast_to(power, (out_ref.shape[1] - count, power.shape[1]))
            out_ref[index, count:, :] = line.astype(jnp.int32).astype(jnp.int16)


def row_products(words, parts, own, weights, index):
    ch, width, count = own.shape
    rows = LANES
    main = STEPS * STEP * ch
    steps = width // (2 * STEPS * STEP)
    each = ch // steps
    return pl.pallas_call(
        rows_kernel,
        grid=(2 * steps,),
        in_specs=[
            pl.BlockSpec((main, rows), lambda i: (jnp.minimum(i, steps - 1), index)),
            pl.BlockSpec((STEP * ch, rows), lambda i: ((jnp.minimum(i, steps - 1) + 1) * STEPS, index)),
            pl.BlockSpec((parts.shape[0], rows), lambda i: (0, index)),
            pl.BlockSpec(weights.shape, lambda i: (0, 0, 0)),
            pl.BlockSpec((each, width, count), lambda i: (jnp.maximum(i - steps, 0), 0, 0)),
        ],
        out_specs=pl.BlockSpec((each, count + 16, 2 * rows), lambda i: (jnp.maximum(i - steps, 0), 0, 0)),
        out_shape=jax.ShapeDtypeStruct((ch, count + 16, 2 * rows), jnp.int16),
        scratch_shapes=[pltpu.VMEM((ch, width, 2 * rows), jnp.bfloat16)],
        compiler_params=pltpu.CompilerParams(vmem_limit_bytes=40 << 20),
        name="row_products",
    )(words, words, parts, weights, own)


def finish_kernel(scale, slot_ref, coded_ref, *refs):
    out_ref, products, tile = refs[-3:]
    step = pl.program_id(0)
    sources, lines, width = coded_ref.shape
    count = lines - 16
    pieces = width // LANES
    feeds = sources * count
    columns = 2 * (feeds // LANES)
    for source in range(sources):
        power = coded_ref[source, count : count + 16, :][:1].astype(jnp.float32)
        values = coded_ref[source, :count, :].astype(jnp.float32) * (jnp.exp2(power - RANGE) * scale)
        for piece in range(pieces):
            products[pl.ds(source * count * pieces + piece, count, stride=pieces), :] = values[
                :, piece * LANES : (piece + 1) * LANES
            ]

    @pl.loop(0, feeds // LANES)
    def _(j):
        @pl.loop(0, LANES, unroll=16)
        def _(i):
            slot = slot_ref[j * LANES + i]
            tile[pl.ds(pl.multiple_of(i * pieces, pieces), pieces), :] = products[
                pl.ds(pl.multiple_of(slot * pieces, pieces), pieces), :
            ]

        for piece in range(pieces):
            turned = tile[pl.ds(piece, LANES, stride=pieces), :].T
            out_ref[pl.ds(2 * j + piece, LANES, stride=columns), :] = turned


def finish(coded, feed_slot, index, pieces, scale, before):
    sources, lines, width = coded.shape
    rows = width // 2
    feeds = sources * (lines - 16)
    columns = 2 * (feeds // LANES)
    earlier = [] if before is None else [before]
    return pl.pallas_call(
        functools.partial(finish_kernel, scale),
        grid=(1,),
        in_specs=[
            pl.BlockSpec(memory_space=pltpu.SMEM),
            pl.BlockSpec(coded.shape, lambda i: (0, 0, 0)),
        ]
        + [pl.BlockSpec(memory_space=pl.ANY)] * len(earlier),
        out_specs=pl.BlockSpec((rows * columns, LANES), lambda i: (index, 0)),
        out_shape=jax.ShapeDtypeStruct((pieces * rows * columns, LANES), jnp.float32),
        scratch_shapes=[
            pltpu.VMEM((feeds * width // LANES, LANES), jnp.float32),
            pltpu.VMEM((width, LANES), jnp.float32),
        ],
        input_output_aliases={2: 0} if earlier else {},
        compiler_params=pltpu.CompilerParams(vmem_limit_bytes=40 << 20),
        name="finish",
    )(feed_slot, coded, *earlier)


def through_rows(samples, gains, feed_slot):
    count, ch, frames = samples.shape
    spectra = frames - TAPS + 1
    pieces = ROWS // LANES
    lines = frames * ch
    unit = 16 * STEPS * 2
    total = pl.cdiv(lines + 4 * ch, unit) * unit
    words = jnp.transpose(samples, (2, 1, 0)).reshape(lines, count)
    scales = gains.reshape(2 * ch, count)
    weights = jnp.asarray(filter_weights(ch))
    slots = (feed_slot[:ROWS] - lax.axis_index("feed") * count).reshape(1, ROWS)
    picked = select_rows(words, scales, slots, total)
    own = own_spectra(words, scales.astype(jnp.float32), weights, ch, spectra)
    rows = sum_over_feed(picked)
    parts = rows[lines : lines + 4 * ch]
    out = None
    for index in range(pieces):
        coded = row_products(rows, parts, own, weights, index)
        moved = lax.all_to_all(coded, "feed", split_axis=0, concat_axis=0, tiled=True)
        out = finish(moved, feed_slot, index, pieces, 1.0 / spectra, out)
    feeds = feed_slot.shape[0]
    out = out.reshape(ROWS, feeds // LANES, 2, LANES)
    return jnp.transpose(out, (0, 2, 1, 3)).reshape(ROWS, 2, feeds)


def body(samples, gains, feed_slot):
    count, ch, frames = samples.shape
    spectra = frames - TAPS + 1
    even = count % LANES == 0 and spectra % (STEPS * STEP) == 0 and ch % STEPS == 0
    if lax.axis_size("feed") == ch == 16 and even:
        return through_rows(samples, gains, feed_slot)
    return through_spectra(samples, gains, feed_slot)


def solution(mesh):
    return jax.shard_map(
        body,
        mesh=mesh,
        in_specs=(P(("band", "feed"), None, None), P(None, "band", "feed"), P()),
        out_specs=P(("band", "feed"), None, None),
        check_vma=False,
    )
```

```python
import functools
import math

import jax
import jax.numpy as jnp
import numpy as np
from jax import lax
from jax.experimental import pallas as pl
from jax.experimental.pallas import tpu as pltpu
from jax.sharding import PartitionSpec as P

TAPS = 8
ROWS = 256
LANES = 128


def filter_taps(ch):
    length = TAPS * ch
    place = np.arange(length, dtype=np.float64)
    window = 0.5 - 0.5 * np.cos(2.0 * math.pi * place / (length - 1))
    return (np.sinc((place - 0.5 * (length - 1)) / ch) * window).reshape(TAPS, ch)


def twiddle(value, turn):
    real, imag = value
    if turn == 0:
        return value
    if turn == 0.25:
        return imag, -real
    half = math.sqrt(0.5)
    if turn == 0.125:
        return half * (real + imag), half * (imag - real)
    if turn == 0.375:
        return half * (imag - real), -half * (real + imag)
    c, s = math.cos(2.0 * math.pi * turn), math.sin(2.0 * math.pi * turn)
    return c * real + s * imag, c * imag - s * real


def fft(values):
    count = len(values)
    if count == 1:
        return values
    even, odd = fft(values[0::2]), fft(values[1::2])
    low, high = [], []
    for index in range(count // 2):
        real, imag = twiddle(odd[index], index / count)
        low.append((even[index][0] + real, even[index][1] + imag))
        high.append((even[index][0] - real, even[index][1] - imag))
    return low + high


def channel_kernel(taps, *refs):
    *samples_refs, gains_ref, out_ref, filtered = refs
    ch, block, width = out_ref.shape
    spectra = width // 2
    padded = len(samples_refs) * LANES
    for k in range(ch):
        words = jnp.concatenate(
            [ref[pl.ds(k, block, stride=ch), :] for ref in samples_refs], axis=1
        )
        levels = ((words >> 4) - 8, (words & 15) - 8)
        for part in range(2):
            value = levels[part].astype(jnp.float32)
            shifted = [value] + [pltpu.roll(value, padded - t, 1) for t in range(1, TAPS // 2)]
            near = float(taps[0, k]) * shifted[0]
            far = float(taps[TAPS // 2, k]) * shifted[0]
            for t in range(1, TAPS // 2):
                near = near + float(taps[t, k]) * shifted[t]
                far = far + float(taps[t + TAPS // 2, k]) * shifted[t]
            total = near + pltpu.roll(far, padded - TAPS // 2, 1)
            filtered[2 * k + part] = total[:, :spectra]
    for row in range(0, block, 8):
        gains = gains_ref[row : row + 8, :]
        for lane in range(0, spectra, LANES):
            spot = (slice(row, row + 8), slice(lane, lane + LANES))
            values = [(filtered[2 * k][spot], filtered[2 * k + 1][spot]) for k in range(ch)]
            for c, (real, imag) in enumerate(fft(values)):
                gain_real = gains[:, c : c + 1]
                gain_imag = gains[:, ch + c : ch + c + 1]
                out_ref[c, row : row + 8, lane : lane + LANES] = (
                    gain_real * real - gain_imag * imag
                ).astype(out_ref.dtype)
                out_ref[c, row : row + 8, spectra + lane : spectra + lane + LANES] = (
                    gain_real * imag + gain_imag * real
                ).astype(out_ref.dtype)


def channelize(samples, gains):
    count, ch, frames = samples.shape
    spectra = frames - TAPS + 1
    block = 16
    pieces = pl.cdiv(frames, LANES)
    scale = 0.125 / math.sqrt(ch) / 2048.0
    taps = (filter_taps(ch) * scale).astype(np.float32)
    return pl.pallas_call(
        functools.partial(channel_kernel, taps),
        grid=(count // block,),
        in_specs=[
            pl.BlockSpec((block * ch, LANES), functools.partial(lambda piece, i: (i, piece), piece))
            for piece in range(pieces)
        ]
        + [pl.BlockSpec((block, 2 * ch), lambda i: (i, 0))],
        out_specs=pl.BlockSpec((ch, block, 2 * spectra), lambda i: (0, i, 0)),
        out_shape=jax.ShapeDtypeStruct((ch, count, 2 * spectra), jnp.bfloat16),
        scratch_shapes=[pltpu.VMEM((2 * ch, block, spectra), jnp.float32)],
        compiler_params=pltpu.CompilerParams(vmem_limit_bytes=32 << 20),
        name="channelize",
    )(*[samples.reshape(count * ch, frames)] * pieces, gains)


def correlate_kernel(scale, slot_ref, row_ref, data_ref, out_ref, products, tile):
    feeds, width = data_ref.shape
    spectra = width // 2
    rows = row_ref.shape[0]
    pieces = 2 * rows // LANES
    step = 256
    picked = jnp.zeros((rows, width), jnp.float32)
    for first in range(0, feeds, 512):
        place = lax.broadcasted_iota(jnp.int32, (rows, 512), 1) + first
        choice = jnp.where(row_ref[...] == place, 1.0, 0.0).astype(jnp.bfloat16)
        picked = picked + jnp.dot(
            choice, data_ref[first : first + 512, :], preferred_element_type=jnp.float32
        )
    left = jnp.concatenate(
        [
            picked,
            jnp.concatenate([picked[:, spectra:], -picked[:, :spectra]], axis=1),
        ],
        axis=0,
    ).astype(jnp.bfloat16)

    @pl.loop(0, feeds // step)
    def _(i):
        first = pl.multiple_of(i * step, step)
        result = lax.dot_general(
            data_ref[pl.ds(first, step), :],
            left,
            (((1,), (1,)), ((), ())),
            preferred_element_type=jnp.float32,
        )
        for piece in range(pieces):
            products[pl.ds(first * pieces + piece, step, stride=pieces), :] = (
                result[:, piece * LANES : (piece + 1) * LANES] * scale
            )

    lines = 2 * (feeds // LANES)

    @pl.loop(0, feeds // LANES)
    def _(j):
        @pl.loop(0, LANES, unroll=16)
        def _(i):
            slot = slot_ref[j * LANES + i]
            tile[pl.ds(pl.multiple_of(i * pieces, pieces), pieces), :] = products[
                pl.ds(pl.multiple_of(slot * pieces, pieces), pieces), :
            ]

        for piece in range(pieces):
            part, first = divmod(piece * LANES, rows)
            turned = tile[pl.ds(piece, LANES, stride=pieces), :].T
            out_ref[pl.ds(first * lines + 2 * j + part, LANES, stride=lines), :] = turned


def correlate(data, feed_slot, first, rows):
    feeds, width = data.shape
    row_slots = lax.dynamic_slice_in_dim(feed_slot, first, rows, 0).reshape(rows, 1)
    lines = 2 * (feeds // LANES)
    out = pl.pallas_call(
        functools.partial(correlate_kernel, 2.0 / width),
        in_specs=[
            pl.BlockSpec(memory_space=pltpu.SMEM),
            pl.BlockSpec(memory_space=pltpu.VMEM),
            pl.BlockSpec(memory_space=pltpu.VMEM),
        ],
        out_specs=pl.BlockSpec(memory_space=pltpu.VMEM),
        out_shape=jax.ShapeDtypeStruct((rows * lines, LANES), jnp.float32),
        scratch_shapes=[
            pltpu.VMEM((feeds * 2 * rows // LANES, LANES), jnp.float32),
            pltpu.VMEM((LANES * 2 * rows // LANES, LANES), jnp.float32),
        ],
        compiler_params=pltpu.CompilerParams(vmem_limit_bytes=48 << 20),
        name="correlate",
    )(feed_slot, row_slots, data)
    out = out.reshape(rows, feeds // LANES, 2, LANES)
    return jnp.transpose(out, (0, 2, 1, 3)).reshape(rows, 2, feeds)


def through_spectra(samples, gains, feed_slot):
    count, ch, _ = samples.shape
    groups = lax.axis_size("feed") // ch
    first = lax.axis_index("feed") % groups * ROWS
    scales = jnp.transpose(gains, (2, 0, 1)).reshape(count, 2 * ch).astype(jnp.float32)
    spectra = channelize(samples, scales)
    width = spectra.shape[2]
    outgoing = jnp.broadcast_to(spectra[:, None], (ch, groups, count, width))
    outgoing = outgoing.reshape(ch * groups, count, width)
    moved = lax.all_to_all(outgoing, "feed", split_axis=0, concat_axis=0, tiled=True)
    return correlate(moved.reshape(-1, width), feed_slot, first, ROWS)


STEP = 8
SPAN = 16
STEPS = 8
RANGE = 14


def filter_weights(ch):
    taps = filter_taps(ch) * (0.125 / math.sqrt(ch) / 2048.0)
    weights = np.zeros((ch, 2, STEP, 2, SPAN, ch))
    angle = 2.0 * math.pi * (np.arange(ch)[:, None] * np.arange(ch)[None, :] % ch) / ch
    for spectrum in range(STEP):
        for t in range(TAPS):
            cosine, sine = taps[t] * np.cos(angle), taps[t] * np.sin(angle)
            weights[:, 0, spectrum, 0, spectrum + t] = cosine
            weights[:, 0, spectrum, 1, spectrum + t] = sine
            weights[:, 1, spectrum, 0, spectrum + t] = -sine
            weights[:, 1, spectrum, 1, spectrum + t] = cosine
    weights = weights.reshape(ch * 2 * STEP, 2, SPAN * ch)
    high = weights.astype(jnp.bfloat16)
    low = (weights - high.astype(np.float64)).astype(jnp.bfloat16)
    return np.stack([high[:, 0], high[:, 1], low[:, 0], low[:, 1]])


def spectra_of(weights_ref, levels, gains, ch, store):
    count = levels[0].shape[1]
    beside = max(1, 256 // count)
    for first in range(0, STEPS, beside):
        total = None
        for part in range(2):
            slabs = [levels[part][b * STEP * ch : (b * STEP + SPAN) * ch] for b in range(first, first + beside)]
            slab = jnp.concatenate(slabs, axis=1) if beside > 1 else slabs[0]
            for split in range(2):
                term = jnp.dot(weights_ref[2 * split + part], slab, preferred_element_type=jnp.float32)
                total = term if total is None else total + term
        for index in range(beside):
            mine = total[:, index * count : (index + 1) * count]
            for c in range(ch):
                real = mine[c * 2 * STEP : c * 2 * STEP + STEP]
                imag = mine[c * 2 * STEP + STEP : (c + 1) * 2 * STEP]
                gain_real, gain_imag = gains[c : c + 1], gains[ch + c : ch + c + 1]
                store(
                    first + index,
                    c,
                    gain_real * real - gain_imag * imag,
                    gain_real * imag + gain_imag * real,
                )


def levels_of(words):
    return [
        ((words >> 4) - 8).astype(jnp.float32).astype(jnp.bfloat16),
        ((words & 15) - 8).astype(jnp.float32).astype(jnp.bfloat16),
    ]


def own_kernel(main_ref, next_ref, gains_ref, weights_ref, out_ref, held):
    ch = out_ref.shape[0]
    words = jnp.concatenate([main_ref[...], next_ref[...]], axis=0)

    def store(b, c, real, imag):
        held[c, b * 2 * STEP : (b + 1) * 2 * STEP, :] = jnp.concatenate([real, imag], axis=0).astype(held.dtype)

    spectra_of(weights_ref, levels_of(words), gains_ref[...], ch, store)
    for c in range(ch):
        out_ref[c] = held[c].T


def own_spectra(words, gains, weights, ch, spectra):
    count = words.shape[1]
    main = STEPS * STEP * ch
    return pl.pallas_call(
        own_kernel,
        grid=(spectra // (STEPS * STEP),),
        in_specs=[
            pl.BlockSpec((main, count), lambda i: (i, 0)),
            pl.BlockSpec((STEP * ch, count), lambda i: ((i + 1) * STEPS, 0)),
            pl.BlockSpec(gains.shape, lambda i: (0, 0)),
            pl.BlockSpec(weights.shape, lambda i: (0, 0, 0)),
        ],
        out_specs=pl.BlockSpec((ch, count, 2 * STEPS * STEP), lambda i: (0, 0, i)),
        out_shape=jax.ShapeDtypeStruct((ch, count, 2 * spectra), jnp.bfloat16),
        scratch_shapes=[pltpu.VMEM((ch, 2 * STEPS * STEP, count), jnp.bfloat16)],
        compiler_params=pltpu.CompilerParams(vmem_limit_bytes=40 << 20),
        cost_estimate=pl.CostEstimate(
            flops=8 * spectra * ch * 2 * SPAN * ch * count,
            bytes_accessed=4 * words.size + 4 * ch * spectra * count,
            transcendentals=0,
        ),
        name="own_spectra",
    )(words, words, gains, weights)


def select_kernel(last_rows, slots_ref, words_ref, parts_ref, out_ref):
    step = pl.program_id(0)
    count, rows = words_ref.shape[1], out_ref.shape[1]
    words = words_ref[...].astype(jnp.float32).astype(jnp.bfloat16)
    place = lax.broadcasted_iota(jnp.int32, (count, rows), 0)
    choice = jnp.where(slots_ref[...] == place, 1.0, 0.0).astype(jnp.bfloat16)
    out_ref[...] = jnp.dot(words, choice, preferred_element_type=jnp.float32).astype(out_ref.dtype)

    @pl.when(step == pl.num_programs(0) - 1)
    def _():
        extra = parts_ref.shape[0]
        out_ref[last_rows : last_rows + extra, :] = jnp.dot(
            parts_ref[...], choice, preferred_element_type=jnp.float32
        ).astype(out_ref.dtype)
        left = out_ref.shape[0] - last_rows - extra
        out_ref[last_rows + extra :, :] = jnp.zeros((left, rows), out_ref.dtype)


def select_rows(words, gains, slots, total):
    lines, count = words.shape
    rows = slots.shape[1]
    block = total // STEPS
    parts = jnp.concatenate([gains >> 4, gains & 15], axis=0).astype(jnp.bfloat16)
    return pl.pallas_call(
        functools.partial(select_kernel, lines - (STEPS - 1) * block),
        grid=(STEPS,),
        in_specs=[
            pl.BlockSpec((1, rows), lambda i: (0, 0)),
            pl.BlockSpec((block, count), lambda i: (i, 0)),
            pl.BlockSpec(parts.shape, lambda i: (0, 0)),
        ],
        out_specs=pl.BlockSpec((block, rows), lambda i: (i, 0)),
        out_shape=jax.ShapeDtypeStruct((total, rows), jnp.bfloat16),
        compiler_params=pltpu.CompilerParams(vmem_limit_bytes=24 << 20),
        name="select_rows",
    )(slots, words, parts)


def swap(value, bit):
    pairs = [(index, index ^ bit) for index in range(lax.axis_size("feed"))]
    return lax.ppermute(value, "feed", pairs)


def side(bit):
    return lax.axis_index("feed") // bit % 2


def reduce_half(value, bit):
    size = value.shape[0] // 2
    keep = lax.dynamic_slice_in_dim(value, side(bit) * size, size, 0)
    send = lax.dynamic_slice_in_dim(value, (1 - side(bit)) * size, size, 0)
    return keep + swap(send, bit)


def gather_half(value, bit, buffer):
    size = value.shape[0]
    other = swap(value, bit)
    buffer = lax.dynamic_update_slice_in_dim(buffer, value, side(bit) * size, 0)
    return lax.dynamic_update_slice_in_dim(buffer, other, (1 - side(bit)) * size, 0)


def sum_over_feed(value):
    half = reduce_half(value, 1)
    size = half.shape[0] // 2
    left, right = half[:size], half[size:]
    left_1, right_1 = reduce_half(left, 2), reduce_half(right, 4)
    left_2, right_2 = reduce_half(left_1, 4), reduce_half(right_1, 2)
    left_3, right_3 = left_2 + swap(left_2, 8), right_2 + swap(right_2, 8)
    left_1, right_1 = gather_half(left_3, 4, left_1), gather_half(right_3, 2, right_1)
    left, right = gather_half(left_1, 2, left), gather_half(right_1, 4, right)
    return gather_half(jnp.concatenate([left, right], axis=0), 1, value)


def rows_kernel(main_ref, next_ref, parts_ref, weights_ref, own_ref, out_ref, left):
    step = pl.program_id(0)
    steps = pl.num_programs(0) // 2
    ch = left.shape[0]
    rows = main_ref.shape[1]

    @pl.when(step < steps)
    def _():
        words = jnp.concatenate([main_ref[...], next_ref[...]], axis=0).astype(jnp.float32).astype(jnp.int32)
        parts = parts_ref[...].astype(jnp.float32)
        gains = parts[: 2 * ch] * 16.0 + parts[2 * ch :]

        def store(b, c, real, imag):
            spot = pl.ds(pl.multiple_of(step * (2 * STEPS * STEP), 2 * STEPS * STEP) + b * 2 * STEP, 2 * STEP)
            left[c, spot, :rows] = jnp.concatenate([real, imag], axis=0).astype(left.dtype)
            left[c, spot, rows:] = jnp.concatenate([imag, -real], axis=0).astype(left.dtype)

        spectra_of(weights_ref, levels_of(words), gains, ch, store)

    @pl.when(step >= steps)
    def _():
        each = own_ref.shape[0]
        for index in range(each):
            products = jnp.dot(
                own_ref[index], left[(step - steps) * each + index], preferred_element_type=jnp.float32
            )
            count = products.shape[0]
            largest = jnp.maximum(jnp.max(jnp.abs(products), axis=0, keepdims=True), 2.0**-60)
            power = jnp.floor(jnp.log2(largest))
            coded = jnp.clip(jnp.round(products * jnp.exp2(RANGE - power)), -32767.0, 32767.0)
            out_ref[index, :count, :] = coded.astype(jnp.int32).astype(jnp.int16)
            line = jnp.broadcast_to(power, (out_ref.shape[1] - count, power.shape[1]))
            out_ref[index, count:, :] = line.astype(jnp.int32).astype(jnp.int16)


def row_products(words, parts, own, weights, index):
    ch, count, width = own.shape
    rows = LANES
    main = STEPS * STEP * ch
    steps = width // (2 * STEPS * STEP)
    each = ch // steps
    return pl.pallas_call(
        rows_kernel,
        grid=(2 * steps,),
        in_specs=[
            pl.BlockSpec((main, rows), lambda i: (jnp.minimum(i, steps - 1), index)),
            pl.BlockSpec((STEP * ch, rows), lambda i: ((jnp.minimum(i, steps - 1) + 1) * STEPS, index)),
            pl.BlockSpec((parts.shape[0], rows), lambda i: (0, index)),
            pl.BlockSpec(weights.shape, lambda i: (0, 0, 0)),
            pl.BlockSpec((each, count, width), lambda i: (jnp.maximum(i - steps, 0), 0, 0)),
        ],
        out_specs=pl.BlockSpec((each, count + 16, 2 * rows), lambda i: (jnp.maximum(i - steps, 0), 0, 0)),
        out_shape=jax.ShapeDtypeStruct((ch, count + 16, 2 * rows), jnp.int16),
        scratch_shapes=[pltpu.VMEM((ch, width, 2 * rows), jnp.bfloat16)],
        compiler_params=pltpu.CompilerParams(vmem_limit_bytes=40 << 20),
        cost_estimate=pl.CostEstimate(
            flops=8 * width * ch * SPAN * ch * rows + 4 * ch * width * rows * count,
            bytes_accessed=2 * words.size + 2 * own.size + 4 * ch * rows * count,
            transcendentals=0,
        ),
        name="row_products",
    )(words, words, parts, weights, own)


def finish_kernel(scale, slot_ref, coded_ref, *refs):
    out_ref, products, tile, mixed = refs[-4:]
    sources, lines, width = coded_ref.shape
    count = lines - 16
    pieces = width // LANES
    feeds = sources * count
    columns = 2 * (feeds // LANES)
    for source in range(sources):
        power = coded_ref[source, count : count + 16, :][:1].astype(jnp.float32)
        values = coded_ref[source, :count, :].astype(jnp.float32) * (jnp.exp2(power - RANGE) * scale)
        for piece in range(pieces):
            products[pl.ds(source * count * pieces + piece, count, stride=pieces), :] = values[
                :, piece * LANES : (piece + 1) * LANES
            ]

    together = 8 // pieces

    @pl.loop(0, feeds // LANES // together)
    def _(j):
        for part in range(together):
            for i in range(LANES):
                slot = slot_ref[(j * together + part) * LANES + i]
                tile[i * pieces : (i + 1) * pieces, :] = products[
                    pl.ds(pl.multiple_of(slot * pieces, pieces), pieces), :
                ]
            for piece in range(pieces):
                turned = tile[pl.ds(piece, LANES, stride=pieces), :].T
                mixed[pl.ds(part * pieces + piece, LANES, stride=8), :] = turned
        for row in range(LANES):
            out_ref[pl.ds(pl.multiple_of(row * columns + j * 8, 8), 8), :] = mixed[row * 8 : (row + 1) * 8, :]


def finish(coded, feed_slot, index, pieces, scale, before):
    sources, lines, width = coded.shape
    rows = width // 2
    feeds = sources * (lines - 16)
    columns = 2 * (feeds // LANES)
    earlier = [] if before is None else [before]
    return pl.pallas_call(
        functools.partial(finish_kernel, scale),
        grid=(1,),
        in_specs=[
            pl.BlockSpec(memory_space=pltpu.SMEM),
            pl.BlockSpec(coded.shape, lambda i: (0, 0, 0)),
        ]
        + [pl.BlockSpec(memory_space=pl.ANY)] * len(earlier),
        out_specs=pl.BlockSpec((rows * columns, LANES), lambda i: (index, 0)),
        out_shape=jax.ShapeDtypeStruct((pieces * rows * columns, LANES), jnp.float32),
        scratch_shapes=[
            pltpu.VMEM((feeds * width // LANES, LANES), jnp.float32),
            pltpu.VMEM((width, LANES), jnp.float32),
            pltpu.VMEM((8 * LANES, LANES), jnp.float32),
        ],
        input_output_aliases={2: 0} if earlier else {},
        compiler_params=pltpu.CompilerParams(vmem_limit_bytes=40 << 20),
        name="finish",
    )(feed_slot, coded, *earlier)


def through_rows(samples, gains, feed_slot):
    count, ch, frames = samples.shape
    spectra = frames - TAPS + 1
    pieces = ROWS // LANES
    lines = frames * ch
    unit = 16 * STEPS * 2
    total = pl.cdiv(lines + 4 * ch, unit) * unit
    words = jnp.transpose(samples, (2, 1, 0)).reshape(lines, count)
    scales = gains.reshape(2 * ch, count)
    weights = jnp.asarray(filter_weights(ch))
    slots = (feed_slot[:ROWS] - lax.axis_index("feed") * count).reshape(1, ROWS)
    picked = select_rows(words, scales, slots, total)
    own = own_spectra(words, scales.astype(jnp.float32), weights, ch, spectra)
    rows = sum_over_feed(picked)
    parts = rows[lines : lines + 4 * ch]
    out = None
    for index in range(pieces):
        coded = row_products(rows, parts, own, weights, index)
        moved = lax.all_to_all(coded, "feed", split_axis=0, concat_axis=0, tiled=True)
        out = finish(moved, feed_slot, index, pieces, 1.0 / spectra, out)
    feeds = feed_slot.shape[0]
    out = out.reshape(ROWS, feeds // LANES, 2, LANES)
    return jnp.transpose(out, (0, 2, 1, 3)).reshape(ROWS, 2, feeds)


def body(samples, gains, feed_slot):
    count, ch, frames = samples.shape
    spectra = frames - TAPS + 1
    even = count % LANES == 0 and spectra % (STEPS * STEP) == 0 and ch % STEPS == 0
    if lax.axis_size("feed") == ch == 16 and even:
        return through_rows(samples, gains, feed_slot)
    return through_spectra(samples, gains, feed_slot)


def solution(mesh):
    return jax.shard_map(
        body,
        mesh=mesh,
        in_specs=(P(("band", "feed"), None, None), P(None, "band", "feed"), P()),
        out_specs=P(("band", "feed"), None, None),
        check_vma=False,
    )
```

```python
import functools
import math

import jax
import jax.numpy as jnp
import numpy as np
from jax import lax
from jax.experimental import pallas as pl
from jax.experimental.pallas import tpu as pltpu
from jax.sharding import PartitionSpec as P

TAPS = 8
ROWS = 256
LANES = 128


def filter_taps(ch):
    length = TAPS * ch
    place = np.arange(length, dtype=np.float64)
    window = 0.5 - 0.5 * np.cos(2.0 * math.pi * place / (length - 1))
    return (np.sinc((place - 0.5 * (length - 1)) / ch) * window).reshape(TAPS, ch)


def twiddle(value, turn):
    real, imag = value
    if turn == 0:
        return value
    if turn == 0.25:
        return imag, -real
    half = math.sqrt(0.5)
    if turn == 0.125:
        return half * (real + imag), half * (imag - real)
    if turn == 0.375:
        return half * (imag - real), -half * (real + imag)
    c, s = math.cos(2.0 * math.pi * turn), math.sin(2.0 * math.pi * turn)
    return c * real + s * imag, c * imag - s * real


def fft(values):
    count = len(values)
    if count == 1:
        return values
    even, odd = fft(values[0::2]), fft(values[1::2])
    low, high = [], []
    for index in range(count // 2):
        real, imag = twiddle(odd[index], index / count)
        low.append((even[index][0] + real, even[index][1] + imag))
        high.append((even[index][0] - real, even[index][1] - imag))
    return low + high


def channel_kernel(taps, *refs):
    *samples_refs, gains_ref, out_ref, filtered = refs
    ch, block, width = out_ref.shape
    spectra = width // 2
    padded = len(samples_refs) * LANES
    for k in range(ch):
        words = jnp.concatenate(
            [ref[pl.ds(k, block, stride=ch), :] for ref in samples_refs], axis=1
        )
        levels = ((words >> 4) - 8, (words & 15) - 8)
        for part in range(2):
            value = levels[part].astype(jnp.float32)
            shifted = [value] + [pltpu.roll(value, padded - t, 1) for t in range(1, TAPS // 2)]
            near = float(taps[0, k]) * shifted[0]
            far = float(taps[TAPS // 2, k]) * shifted[0]
            for t in range(1, TAPS // 2):
                near = near + float(taps[t, k]) * shifted[t]
                far = far + float(taps[t + TAPS // 2, k]) * shifted[t]
            total = near + pltpu.roll(far, padded - TAPS // 2, 1)
            filtered[2 * k + part] = total[:, :spectra]
    for row in range(0, block, 8):
        gains = gains_ref[row : row + 8, :]
        for lane in range(0, spectra, LANES):
            spot = (slice(row, row + 8), slice(lane, lane + LANES))
            values = [(filtered[2 * k][spot], filtered[2 * k + 1][spot]) for k in range(ch)]
            for c, (real, imag) in enumerate(fft(values)):
                gain_real = gains[:, c : c + 1]
                gain_imag = gains[:, ch + c : ch + c + 1]
                out_ref[c, row : row + 8, lane : lane + LANES] = (
                    gain_real * real - gain_imag * imag
                ).astype(out_ref.dtype)
                out_ref[c, row : row + 8, spectra + lane : spectra + lane + LANES] = (
                    gain_real * imag + gain_imag * real
                ).astype(out_ref.dtype)


def channelize(samples, gains):
    count, ch, frames = samples.shape
    spectra = frames - TAPS + 1
    block = 16
    pieces = pl.cdiv(frames, LANES)
    scale = 0.125 / math.sqrt(ch) / 2048.0
    taps = (filter_taps(ch) * scale).astype(np.float32)
    return pl.pallas_call(
        functools.partial(channel_kernel, taps),
        grid=(count // block,),
        in_specs=[
            pl.BlockSpec((block * ch, LANES), functools.partial(lambda piece, i: (i, piece), piece))
            for piece in range(pieces)
        ]
        + [pl.BlockSpec((block, 2 * ch), lambda i: (i, 0))],
        out_specs=pl.BlockSpec((ch, block, 2 * spectra), lambda i: (0, i, 0)),
        out_shape=jax.ShapeDtypeStruct((ch, count, 2 * spectra), jnp.bfloat16),
        scratch_shapes=[pltpu.VMEM((2 * ch, block, spectra), jnp.float32)],
        compiler_params=pltpu.CompilerParams(vmem_limit_bytes=32 << 20),
        name="channelize",
    )(*[samples.reshape(count * ch, frames)] * pieces, gains)


def correlate_kernel(scale, slot_ref, row_ref, data_ref, out_ref, products, tile):
    feeds, width = data_ref.shape
    spectra = width // 2
    rows = row_ref.shape[0]
    pieces = 2 * rows // LANES
    step = 256
    picked = jnp.zeros((rows, width), jnp.float32)
    for first in range(0, feeds, 512):
        place = lax.broadcasted_iota(jnp.int32, (rows, 512), 1) + first
        choice = jnp.where(row_ref[...] == place, 1.0, 0.0).astype(jnp.bfloat16)
        picked = picked + jnp.dot(
            choice, data_ref[first : first + 512, :], preferred_element_type=jnp.float32
        )
    left = jnp.concatenate(
        [
            picked,
            jnp.concatenate([picked[:, spectra:], -picked[:, :spectra]], axis=1),
        ],
        axis=0,
    ).astype(jnp.bfloat16)

    @pl.loop(0, feeds // step)
    def _(i):
        first = pl.multiple_of(i * step, step)
        result = lax.dot_general(
            data_ref[pl.ds(first, step), :],
            left,
            (((1,), (1,)), ((), ())),
            preferred_element_type=jnp.float32,
        )
        for piece in range(pieces):
            products[pl.ds(first * pieces + piece, step, stride=pieces), :] = (
                result[:, piece * LANES : (piece + 1) * LANES] * scale
            )

    lines = 2 * (feeds // LANES)

    @pl.loop(0, feeds // LANES)
    def _(j):
        @pl.loop(0, LANES, unroll=16)
        def _(i):
            slot = slot_ref[j * LANES + i]
            tile[pl.ds(pl.multiple_of(i * pieces, pieces), pieces), :] = products[
                pl.ds(pl.multiple_of(slot * pieces, pieces), pieces), :
            ]

        for piece in range(pieces):
            part, first = divmod(piece * LANES, rows)
            turned = tile[pl.ds(piece, LANES, stride=pieces), :].T
            out_ref[pl.ds(first * lines + 2 * j + part, LANES, stride=lines), :] = turned


def correlate(data, feed_slot, first, rows):
    feeds, width = data.shape
    row_slots = lax.dynamic_slice_in_dim(feed_slot, first, rows, 0).reshape(rows, 1)
    lines = 2 * (feeds // LANES)
    out = pl.pallas_call(
        functools.partial(correlate_kernel, 2.0 / width),
        in_specs=[
            pl.BlockSpec(memory_space=pltpu.SMEM),
            pl.BlockSpec(memory_space=pltpu.VMEM),
            pl.BlockSpec(memory_space=pltpu.VMEM),
        ],
        out_specs=pl.BlockSpec(memory_space=pltpu.VMEM),
        out_shape=jax.ShapeDtypeStruct((rows * lines, LANES), jnp.float32),
        scratch_shapes=[
            pltpu.VMEM((feeds * 2 * rows // LANES, LANES), jnp.float32),
            pltpu.VMEM((LANES * 2 * rows // LANES, LANES), jnp.float32),
        ],
        compiler_params=pltpu.CompilerParams(vmem_limit_bytes=48 << 20),
        name="correlate",
    )(feed_slot, row_slots, data)
    out = out.reshape(rows, feeds // LANES, 2, LANES)
    return jnp.transpose(out, (0, 2, 1, 3)).reshape(rows, 2, feeds)


def through_spectra(samples, gains, feed_slot):
    count, ch, _ = samples.shape
    groups = lax.axis_size("feed") // ch
    first = lax.axis_index("feed") % groups * ROWS
    scales = jnp.transpose(gains, (2, 0, 1)).reshape(count, 2 * ch).astype(jnp.float32)
    spectra = channelize(samples, scales)
    width = spectra.shape[2]
    outgoing = jnp.broadcast_to(spectra[:, None], (ch, groups, count, width))
    outgoing = outgoing.reshape(ch * groups, count, width)
    moved = lax.all_to_all(outgoing, "feed", split_axis=0, concat_axis=0, tiled=True)
    return correlate(moved.reshape(-1, width), feed_slot, first, ROWS)


STEP = 8
SPAN = 16
STEPS = 8
RANGE = 14


def filter_weights(ch):
    taps = filter_taps(ch) * (0.125 / math.sqrt(ch) / 2048.0)
    half = ch // 2
    weights = np.zeros((ch, STEP, SPAN, ch))
    angle = 2.0 * math.pi * (np.arange(half + 1)[:, None] * np.arange(ch)[None, :] % ch) / ch
    sums = np.concatenate([np.cos(angle), np.sin(angle[1:half])], axis=0)
    for spectrum in range(STEP):
        for t in range(TAPS):
            weights[:, spectrum, spectrum + t] = taps[t] * sums
    weights = weights.reshape(ch * STEP, SPAN * ch)
    high = weights.astype(jnp.bfloat16)
    low = (weights - high.astype(np.float64)).astype(jnp.bfloat16)
    return np.concatenate([high, low])


def spectra_of(weights_ref, levels, gains, ch, store):
    count = levels[0].shape[1]
    half, size = ch // 2, ch * STEP
    beside = max(1, 256 // count)
    for first in range(0, STEPS, beside):
        totals = []
        for level in levels:
            slabs = [level[b * size : b * size + SPAN * ch] for b in range(first, first + beside)]
            slab = jnp.concatenate(slabs, axis=1) if beside > 1 else slabs[0]
            both = jnp.dot(weights_ref[...], slab, preferred_element_type=jnp.float32)
            totals.append(both[:size] + both[size:])
        for index in range(beside):
            lanes = slice(index * count, (index + 1) * count)
            parts = [
                [total[d * STEP : (d + 1) * STEP, lanes] for d in range(ch)] for total in totals
            ]
            for c in range(ch):
                place = min(c, ch - c)
                real, imag = parts[0][place], parts[1][place]
                if c % half:
                    sine_real, sine_imag = parts[0][half + place], parts[1][half + place]
                    if c < half:
                        real, imag = real + sine_imag, imag - sine_real
                    else:
                        real, imag = real - sine_imag, imag + sine_real
                gain_real, gain_imag = gains[c : c + 1], gains[ch + c : ch + c + 1]
                store(
                    first + index,
                    c,
                    gain_real * real - gain_imag * imag,
                    gain_real * imag + gain_imag * real,
                )


def levels_of(words):
    return [
        ((words >> 4) - 8).astype(jnp.float32).astype(jnp.bfloat16),
        ((words & 15) - 8).astype(jnp.float32).astype(jnp.bfloat16),
    ]


def own_kernel(main_ref, next_ref, gains_ref, weights_ref, out_ref, zero_ref, held):
    ch = out_ref.shape[0]
    zero_ref[...] = jnp.zeros_like(zero_ref)
    words = jnp.concatenate([main_ref[...], next_ref[...]], axis=0)

    def store(b, c, real, imag):
        held[c, b * 2 * STEP : (b + 1) * 2 * STEP, :] = jnp.concatenate([real, imag], axis=0).astype(held.dtype)

    spectra_of(weights_ref, levels_of(words), gains_ref[...], ch, store)
    for c in range(ch):
        out_ref[c] = held[c].T


def own_spectra(words, gains, weights, ch, spectra):
    count = words.shape[1]
    main = STEPS * STEP * ch
    return pl.pallas_call(
        own_kernel,
        grid=(spectra // (STEPS * STEP),),
        in_specs=[
            pl.BlockSpec((main, count), lambda i: (i, 0)),
            pl.BlockSpec((STEP * ch, count), lambda i: ((i + 1) * STEPS, 0)),
            pl.BlockSpec(gains.shape, lambda i: (0, 0)),
            pl.BlockSpec(weights.shape, lambda i: (0, 0)),
        ],
        out_specs=[
            pl.BlockSpec((ch, count, 2 * STEPS * STEP), lambda i: (0, 0, i)),
            pl.BlockSpec((16, LANES), lambda i: (0, 0)),
        ],
        out_shape=[
            jax.ShapeDtypeStruct((ch, count, 2 * spectra), jnp.bfloat16),
            jax.ShapeDtypeStruct((16, LANES), jnp.bfloat16),
        ],
        scratch_shapes=[pltpu.VMEM((ch, 2 * STEPS * STEP, count), jnp.bfloat16)],
        compiler_params=pltpu.CompilerParams(vmem_limit_bytes=58 << 20),
        cost_estimate=pl.CostEstimate(
            flops=4 * spectra * ch * 2 * SPAN * ch * count,
            bytes_accessed=4 * words.size + 4 * ch * spectra * count,
            transcendentals=0,
        ),
        name="own_spectra",
    )(words, words, gains, weights)


def select_kernel(last_rows, slots_ref, words_ref, parts_ref, out_ref):
    step = pl.program_id(0)
    count, rows = words_ref.shape[1], out_ref.shape[1]
    words = words_ref[...].astype(jnp.float32).astype(jnp.bfloat16)
    place = lax.broadcasted_iota(jnp.int32, (count, rows), 0)
    choice = jnp.where(slots_ref[...] == place, 1.0, 0.0).astype(jnp.bfloat16)
    out_ref[...] = jnp.dot(words, choice, preferred_element_type=jnp.float32).astype(out_ref.dtype)

    @pl.when(step == pl.num_programs(0) - 1)
    def _():
        extra = parts_ref.shape[0]
        out_ref[last_rows : last_rows + extra, :] = jnp.dot(
            parts_ref[...], choice, preferred_element_type=jnp.float32
        ).astype(out_ref.dtype)
        left = out_ref.shape[0] - last_rows - extra
        out_ref[last_rows + extra :, :] = jnp.zeros((left, rows), out_ref.dtype)


def select_rows(words, gains, slots, total):
    lines, count = words.shape
    rows = slots.shape[1]
    block = total // STEPS
    parts = jnp.concatenate([gains >> 4, gains & 15], axis=0).astype(jnp.bfloat16)
    return pl.pallas_call(
        functools.partial(select_kernel, lines - (STEPS - 1) * block),
        grid=(STEPS,),
        in_specs=[
            pl.BlockSpec((1, rows), lambda i: (0, 0)),
            pl.BlockSpec((block, count), lambda i: (i, 0)),
            pl.BlockSpec(parts.shape, lambda i: (0, 0)),
        ],
        out_specs=pl.BlockSpec((block, rows), lambda i: (i, 0)),
        out_shape=jax.ShapeDtypeStruct((total, rows), jnp.bfloat16),
        compiler_params=pltpu.CompilerParams(vmem_limit_bytes=24 << 20),
        name="select_rows",
    )(slots, words, parts)


def swap(value, bit):
    pairs = [(index, index ^ bit) for index in range(lax.axis_size("feed"))]
    return lax.ppermute(value, "feed", pairs)


def side(bit):
    return lax.axis_index("feed") // bit % 2


def reduce_half(value, bit):
    size = value.shape[0] // 2
    keep = lax.dynamic_slice_in_dim(value, side(bit) * size, size, 0)
    send = lax.dynamic_slice_in_dim(value, (1 - side(bit)) * size, size, 0)
    return keep + swap(send, bit)


def gather_half(value, bit, buffer):
    size = value.shape[0]
    other = swap(value, bit)
    buffer = lax.dynamic_update_slice_in_dim(buffer, value, side(bit) * size, 0)
    return lax.dynamic_update_slice_in_dim(buffer, other, (1 - side(bit)) * size, 0)


def sum_over_feed(value, zero):
    half = reduce_half(value, 1)
    size = half.shape[0] // 2
    left, right = half[:size], half[size:]
    left_1, right_1 = reduce_half(left, 2) + zero, reduce_half(right, 4)
    left_2, right_2 = reduce_half(left_1, 4), reduce_half(right_1, 2)
    left_3, right_3 = left_2 + swap(left_2, 8), right_2 + swap(right_2, 8)
    left_1, right_1 = gather_half(left_3, 4, left_1), gather_half(right_3, 2, right_1)
    left, right = gather_half(left_1, 2, left), gather_half(right_1, 4, right)
    return gather_half(jnp.concatenate([left, right], axis=0), 1, value)


def rows_kernel(main_ref, next_ref, parts_ref, weights_ref, own_ref, out_ref, left):
    step = pl.program_id(0)
    steps = pl.num_programs(0) // 2
    ch = left.shape[0]
    rows = main_ref.shape[1]

    @pl.when(step < steps)
    def _():
        words = jnp.concatenate([main_ref[...], next_ref[...]], axis=0).astype(jnp.float32).astype(jnp.int32)
        parts = parts_ref[...].astype(jnp.float32)
        gains = parts[: 2 * ch] * 16.0 + parts[2 * ch :]

        def store(b, c, real, imag):
            spot = pl.ds(pl.multiple_of(step * (2 * STEPS * STEP), 2 * STEPS * STEP) + b * 2 * STEP, 2 * STEP)
            left[c, spot, :rows] = jnp.concatenate([real, imag], axis=0).astype(left.dtype)
            left[c, spot, rows:] = jnp.concatenate([imag, -real], axis=0).astype(left.dtype)

        spectra_of(weights_ref, levels_of(words), gains, ch, store)

    @pl.when(step >= steps)
    def _():
        each = own_ref.shape[0]
        for index in range(each):
            products = jnp.dot(
                own_ref[index], left[(step - steps) * each + index], preferred_element_type=jnp.float32
            )
            count = products.shape[0]
            largest = jnp.maximum(jnp.max(jnp.abs(products), axis=0, keepdims=True), 2.0**-60)
            power = jnp.floor(jnp.log2(largest))
            coded = jnp.clip(jnp.round(products * jnp.exp2(RANGE - power)), -32767.0, 32767.0)
            out_ref[index, :count, :] = coded.astype(jnp.int32).astype(jnp.int16)
            line = jnp.broadcast_to(power, (out_ref.shape[1] - count, power.shape[1]))
            out_ref[index, count:, :] = line.astype(jnp.int32).astype(jnp.int16)


def row_products(words, parts, own, weights, index):
    ch, count, width = own.shape
    rows = LANES
    main = STEPS * STEP * ch
    steps = width // (2 * STEPS * STEP)
    each = ch // steps
    return pl.pallas_call(
        rows_kernel,
        grid=(2 * steps,),
        in_specs=[
            pl.BlockSpec((main, rows), lambda i: (jnp.minimum(i, steps - 1), index)),
            pl.BlockSpec((STEP * ch, rows), lambda i: ((jnp.minimum(i, steps - 1) + 1) * STEPS, index)),
            pl.BlockSpec((parts.shape[0], rows), lambda i: (0, index)),
            pl.BlockSpec(weights.shape, lambda i: (0, 0)),
            pl.BlockSpec((each, count, width), lambda i: (jnp.maximum(i - steps, 0), 0, 0)),
        ],
        out_specs=pl.BlockSpec((each, count + 16, 2 * rows), lambda i: (jnp.maximum(i - steps, 0), 0, 0)),
        out_shape=jax.ShapeDtypeStruct((ch, count + 16, 2 * rows), jnp.int16),
        scratch_shapes=[pltpu.VMEM((ch, width, 2 * rows), jnp.bfloat16)],
        compiler_params=pltpu.CompilerParams(vmem_limit_bytes=58 << 20),
        cost_estimate=pl.CostEstimate(
            flops=4 * width * ch * SPAN * ch * rows + 4 * ch * width * rows * count,
            bytes_accessed=2 * words.size + 2 * own.size + 4 * ch * rows * count,
            transcendentals=0,
        ),
        name="row_products",
    )(words, words, parts, weights, own)


def finish_kernel(scale, slot_ref, coded_ref, *refs):
    out_ref, products, tile, mixed = refs[-4:]
    sources, lines, width = coded_ref.shape
    count = lines - 16
    pieces = width // LANES
    feeds = sources * count
    columns = 2 * (feeds // LANES)
    for source in range(sources):
        power = coded_ref[source, count : count + 16, :][:1].astype(jnp.float32)
        values = coded_ref[source, :count, :].astype(jnp.float32) * (jnp.exp2(power - RANGE) * scale)
        for piece in range(pieces):
            products[pl.ds(source * count * pieces + piece, count, stride=pieces), :] = values[
                :, piece * LANES : (piece + 1) * LANES
            ]

    together = 8 // pieces

    @pl.loop(0, feeds // LANES // together)
    def _(j):
        for part in range(together):
            for i in range(LANES):
                slot = slot_ref[(j * together + part) * LANES + i]
                tile[i * pieces : (i + 1) * pieces, :] = products[
                    pl.ds(pl.multiple_of(slot * pieces, pieces), pieces), :
                ]
            for piece in range(pieces):
                turned = tile[pl.ds(piece, LANES, stride=pieces), :].T
                mixed[pl.ds(part * pieces + piece, LANES, stride=8), :] = turned
        for row in range(LANES):
            out_ref[pl.ds(pl.multiple_of(row * columns + j * 8, 8), 8), :] = mixed[row * 8 : (row + 1) * 8, :]


def finish(coded, feed_slot, index, pieces, scale, before):
    sources, lines, width = coded.shape
    rows = width // 2
    feeds = sources * (lines - 16)
    columns = 2 * (feeds // LANES)
    earlier = [] if before is None else [before]
    return pl.pallas_call(
        functools.partial(finish_kernel, scale),
        grid=(1,),
        in_specs=[
            pl.BlockSpec(memory_space=pltpu.SMEM),
            pl.BlockSpec(coded.shape, lambda i: (0, 0, 0)),
        ]
        + [pl.BlockSpec(memory_space=pl.ANY)] * len(earlier),
        out_specs=pl.BlockSpec((rows * columns, LANES), lambda i: (index, 0)),
        out_shape=jax.ShapeDtypeStruct((pieces * rows * columns, LANES), jnp.float32),
        scratch_shapes=[
            pltpu.VMEM((feeds * width // LANES, LANES), jnp.float32),
            pltpu.VMEM((width, LANES), jnp.float32),
            pltpu.VMEM((8 * LANES, LANES), jnp.float32),
        ],
        input_output_aliases={2: 0} if earlier else {},
        compiler_params=pltpu.CompilerParams(vmem_limit_bytes=58 << 20),
        name="finish",
    )(feed_slot, coded, *earlier)


def through_rows(samples, gains, feed_slot):
    count, ch, frames = samples.shape
    spectra = frames - TAPS + 1
    pieces = ROWS // LANES
    lines = frames * ch
    unit = 16 * STEPS * 2
    total = pl.cdiv(lines + 4 * ch, unit) * unit
    words = jnp.transpose(samples, (2, 1, 0)).reshape(lines, count)
    scales = gains.reshape(2 * ch, count)
    weights = jnp.asarray(filter_weights(ch))
    slots = (feed_slot[:ROWS] - lax.axis_index("feed") * count).reshape(1, ROWS)
    picked = select_rows(words, scales, slots, total)
    own, zero = own_spectra(words, scales.astype(jnp.float32), weights, ch, spectra)
    rows = sum_over_feed(picked, zero[0, 0])
    parts = rows[lines : lines + 4 * ch]
    out = None
    for index in range(pieces):
        coded = row_products(rows, parts, own, weights, index)
        moved = lax.all_to_all(coded, "feed", split_axis=0, concat_axis=0, tiled=True)
        out = finish(moved, feed_slot, index, pieces, 1.0 / spectra, out)
    feeds = feed_slot.shape[0]
    out = out.reshape(ROWS, feeds // LANES, 2, LANES)
    return jnp.transpose(out, (0, 2, 1, 3)).reshape(ROWS, 2, feeds)


def body(samples, gains, feed_slot):
    count, ch, frames = samples.shape
    spectra = frames - TAPS + 1
    even = count % LANES == 0 and spectra % (STEPS * STEP) == 0 and ch % STEPS == 0
    if lax.axis_size("feed") == ch == 16 and even:
        return through_rows(samples, gains, feed_slot)
    return through_spectra(samples, gains, feed_slot)


def solution(mesh):
    return jax.shard_map(
        body,
        mesh=mesh,
        in_specs=(P(("band", "feed"), None, None), P(None, "band", "feed"), P()),
        out_specs=P(("band", "feed"), None, None),
        check_vma=False,
    )
```

```python
import functools
import math

import jax
import jax.numpy as jnp
import numpy as np
from jax import lax
from jax.experimental import pallas as pl
from jax.experimental.pallas import tpu as pltpu
from jax.sharding import PartitionSpec as P

TAPS = 8
ROWS = 256
LANES = 128


def filter_taps(ch):
    length = TAPS * ch
    place = np.arange(length, dtype=np.float64)
    window = 0.5 - 0.5 * np.cos(2.0 * math.pi * place / (length - 1))
    return (np.sinc((place - 0.5 * (length - 1)) / ch) * window).reshape(TAPS, ch)


def twiddle(value, turn):
    real, imag = value
    if turn == 0:
        return value
    if turn == 0.25:
        return imag, -real
    half = math.sqrt(0.5)
    if turn == 0.125:
        return half * (real + imag), half * (imag - real)
    if turn == 0.375:
        return half * (imag - real), -half * (real + imag)
    c, s = math.cos(2.0 * math.pi * turn), math.sin(2.0 * math.pi * turn)
    return c * real + s * imag, c * imag - s * real


def fft(values):
    count = len(values)
    if count == 1:
        return values
    even, odd = fft(values[0::2]), fft(values[1::2])
    low, high = [], []
    for index in range(count // 2):
        real, imag = twiddle(odd[index], index / count)
        low.append((even[index][0] + real, even[index][1] + imag))
        high.append((even[index][0] - real, even[index][1] - imag))
    return low + high


def channel_kernel(taps, *refs):
    *samples_refs, gains_ref, out_ref, filtered = refs
    ch, block, width = out_ref.shape
    spectra = width // 2
    padded = len(samples_refs) * LANES
    for k in range(ch):
        words = jnp.concatenate(
            [ref[pl.ds(k, block, stride=ch), :] for ref in samples_refs], axis=1
        )
        levels = ((words >> 4) - 8, (words & 15) - 8)
        for part in range(2):
            value = levels[part].astype(jnp.float32)
            shifted = [value] + [pltpu.roll(value, padded - t, 1) for t in range(1, TAPS // 2)]
            near = float(taps[0, k]) * shifted[0]
            far = float(taps[TAPS // 2, k]) * shifted[0]
            for t in range(1, TAPS // 2):
                near = near + float(taps[t, k]) * shifted[t]
                far = far + float(taps[t + TAPS // 2, k]) * shifted[t]
            total = near + pltpu.roll(far, padded - TAPS // 2, 1)
            filtered[2 * k + part] = total[:, :spectra]
    for row in range(0, block, 8):
        gains = gains_ref[row : row + 8, :]
        for lane in range(0, spectra, LANES):
            spot = (slice(row, row + 8), slice(lane, lane + LANES))
            values = [(filtered[2 * k][spot], filtered[2 * k + 1][spot]) for k in range(ch)]
            for c, (real, imag) in enumerate(fft(values)):
                gain_real = gains[:, c : c + 1]
                gain_imag = gains[:, ch + c : ch + c + 1]
                out_ref[c, row : row + 8, lane : lane + LANES] = (
                    gain_real * real - gain_imag * imag
                ).astype(out_ref.dtype)
                out_ref[c, row : row + 8, spectra + lane : spectra + lane + LANES] = (
                    gain_real * imag + gain_imag * real
                ).astype(out_ref.dtype)


def channelize(samples, gains):
    count, ch, frames = samples.shape
    spectra = frames - TAPS + 1
    block = 16
    pieces = pl.cdiv(frames, LANES)
    scale = 0.125 / math.sqrt(ch) / 2048.0
    taps = (filter_taps(ch) * scale).astype(np.float32)
    return pl.pallas_call(
        functools.partial(channel_kernel, taps),
        grid=(count // block,),
        in_specs=[
            pl.BlockSpec((block * ch, LANES), functools.partial(lambda piece, i: (i, piece), piece))
            for piece in range(pieces)
        ]
        + [pl.BlockSpec((block, 2 * ch), lambda i: (i, 0))],
        out_specs=pl.BlockSpec((ch, block, 2 * spectra), lambda i: (0, i, 0)),
        out_shape=jax.ShapeDtypeStruct((ch, count, 2 * spectra), jnp.bfloat16),
        scratch_shapes=[pltpu.VMEM((2 * ch, block, spectra), jnp.float32)],
        compiler_params=pltpu.CompilerParams(vmem_limit_bytes=32 << 20),
        name="channelize",
    )(*[samples.reshape(count * ch, frames)] * pieces, gains)


def correlate_kernel(scale, slot_ref, row_ref, data_ref, out_ref, products, tile):
    feeds, width = data_ref.shape
    spectra = width // 2
    rows = row_ref.shape[0]
    pieces = 2 * rows // LANES
    step = 256
    picked = jnp.zeros((rows, width), jnp.float32)
    for first in range(0, feeds, 512):
        place = lax.broadcasted_iota(jnp.int32, (rows, 512), 1) + first
        choice = jnp.where(row_ref[...] == place, 1.0, 0.0).astype(jnp.bfloat16)
        picked = picked + jnp.dot(
            choice, data_ref[first : first + 512, :], preferred_element_type=jnp.float32
        )
    left = jnp.concatenate(
        [
            picked,
            jnp.concatenate([picked[:, spectra:], -picked[:, :spectra]], axis=1),
        ],
        axis=0,
    ).astype(jnp.bfloat16)

    @pl.loop(0, feeds // step)
    def _(i):
        first = pl.multiple_of(i * step, step)
        result = lax.dot_general(
            data_ref[pl.ds(first, step), :],
            left,
            (((1,), (1,)), ((), ())),
            preferred_element_type=jnp.float32,
        )
        for piece in range(pieces):
            products[pl.ds(first * pieces + piece, step, stride=pieces), :] = (
                result[:, piece * LANES : (piece + 1) * LANES] * scale
            )

    lines = 2 * (feeds // LANES)

    @pl.loop(0, feeds // LANES)
    def _(j):
        @pl.loop(0, LANES, unroll=16)
        def _(i):
            slot = slot_ref[j * LANES + i]
            tile[pl.ds(pl.multiple_of(i * pieces, pieces), pieces), :] = products[
                pl.ds(pl.multiple_of(slot * pieces, pieces), pieces), :
            ]

        for piece in range(pieces):
            part, first = divmod(piece * LANES, rows)
            turned = tile[pl.ds(piece, LANES, stride=pieces), :].T
            out_ref[pl.ds(first * lines + 2 * j + part, LANES, stride=lines), :] = turned


def correlate(data, feed_slot, first, rows):
    feeds, width = data.shape
    row_slots = lax.dynamic_slice_in_dim(feed_slot, first, rows, 0).reshape(rows, 1)
    lines = 2 * (feeds // LANES)
    out = pl.pallas_call(
        functools.partial(correlate_kernel, 2.0 / width),
        in_specs=[
            pl.BlockSpec(memory_space=pltpu.SMEM),
            pl.BlockSpec(memory_space=pltpu.VMEM),
            pl.BlockSpec(memory_space=pltpu.VMEM),
        ],
        out_specs=pl.BlockSpec(memory_space=pltpu.VMEM),
        out_shape=jax.ShapeDtypeStruct((rows * lines, LANES), jnp.float32),
        scratch_shapes=[
            pltpu.VMEM((feeds * 2 * rows // LANES, LANES), jnp.float32),
            pltpu.VMEM((LANES * 2 * rows // LANES, LANES), jnp.float32),
        ],
        compiler_params=pltpu.CompilerParams(vmem_limit_bytes=48 << 20),
        name="correlate",
    )(feed_slot, row_slots, data)
    out = out.reshape(rows, feeds // LANES, 2, LANES)
    return jnp.transpose(out, (0, 2, 1, 3)).reshape(rows, 2, feeds)


def through_spectra(samples, gains, feed_slot):
    count, ch, _ = samples.shape
    groups = lax.axis_size("feed") // ch
    first = lax.axis_index("feed") % groups * ROWS
    scales = jnp.transpose(gains, (2, 0, 1)).reshape(count, 2 * ch).astype(jnp.float32)
    spectra = channelize(samples, scales)
    width = spectra.shape[2]
    outgoing = jnp.broadcast_to(spectra[:, None], (ch, groups, count, width))
    outgoing = outgoing.reshape(ch * groups, count, width)
    moved = lax.all_to_all(outgoing, "feed", split_axis=0, concat_axis=0, tiled=True)
    return correlate(moved.reshape(-1, width), feed_slot, first, ROWS)


STEP = 8
SPAN = 16
STEPS = 8
RANGE = 14


def filter_weights(ch):
    taps = filter_taps(ch) * (0.125 / math.sqrt(ch) / 2048.0)
    half = ch // 2
    weights = np.zeros((ch, STEP, SPAN, ch))
    angle = 2.0 * math.pi * (np.arange(half + 1)[:, None] * np.arange(ch)[None, :] % ch) / ch
    sums = np.concatenate([np.cos(angle), np.sin(angle[1:half])], axis=0)
    for spectrum in range(STEP):
        for t in range(TAPS):
            weights[:, spectrum, spectrum + t] = taps[t] * sums
    weights = weights.reshape(ch * STEP, SPAN * ch)
    high = weights.astype(jnp.bfloat16)
    low = (weights - high.astype(np.float64)).astype(jnp.bfloat16)
    return np.concatenate([high, low])


def spectra_of(weights_ref, levels, gains, ch, store):
    count = levels[0].shape[1]
    half, size = ch // 2, ch * STEP
    beside = max(1, 256 // count)
    for first in range(0, STEPS, beside):
        totals = []
        for level in levels:
            slabs = [level[b * size : b * size + SPAN * ch] for b in range(first, first + beside)]
            slab = jnp.concatenate(slabs, axis=1) if beside > 1 else slabs[0]
            both = jnp.dot(weights_ref[...], slab, preferred_element_type=jnp.float32)
            totals.append(both[:size] + both[size:])
        for index in range(beside):
            lanes = slice(index * count, (index + 1) * count)
            parts = [
                [total[d * STEP : (d + 1) * STEP, lanes] for d in range(ch)] for total in totals
            ]
            for c in range(ch):
                place = min(c, ch - c)
                real, imag = parts[0][place], parts[1][place]
                if c % half:
                    sine_real, sine_imag = parts[0][half + place], parts[1][half + place]
                    if c < half:
                        real, imag = real + sine_imag, imag - sine_real
                    else:
                        real, imag = real - sine_imag, imag + sine_real
                gain_real, gain_imag = gains[c : c + 1], gains[ch + c : ch + c + 1]
                store(
                    first + index,
                    c,
                    gain_real * real - gain_imag * imag,
                    gain_real * imag + gain_imag * real,
                )


def levels_of(words):
    return [
        ((words >> 4) - 8).astype(jnp.float32).astype(jnp.bfloat16),
        ((words & 15) - 8).astype(jnp.float32).astype(jnp.bfloat16),
    ]


def own_kernel(main_ref, next_ref, gains_ref, weights_ref, out_ref, zero_ref, held):
    ch = out_ref.shape[0]
    zero_ref[...] = jnp.zeros_like(zero_ref)
    words = jnp.concatenate([main_ref[...], next_ref[...]], axis=0)

    def store(b, c, real, imag):
        held[c, b * 2 * STEP : (b + 1) * 2 * STEP, :] = jnp.concatenate([real, imag], axis=0).astype(held.dtype)

    spectra_of(weights_ref, levels_of(words), gains_ref[...], ch, store)
    for c in range(ch):
        out_ref[c] = held[c].T


def own_spectra(words, gains, weights, ch, spectra):
    count = words.shape[1]
    main = STEPS * STEP * ch
    return pl.pallas_call(
        own_kernel,
        grid=(spectra // (STEPS * STEP),),
        in_specs=[
            pl.BlockSpec((main, count), lambda i: (i, 0)),
            pl.BlockSpec((STEP * ch, count), lambda i: ((i + 1) * STEPS, 0)),
            pl.BlockSpec(gains.shape, lambda i: (0, 0)),
            pl.BlockSpec(weights.shape, lambda i: (0, 0)),
        ],
        out_specs=[
            pl.BlockSpec((ch, count, 2 * STEPS * STEP), lambda i: (0, 0, i)),
            pl.BlockSpec((16, LANES), lambda i: (0, 0)),
        ],
        out_shape=[
            jax.ShapeDtypeStruct((ch, count, 2 * spectra), jnp.bfloat16),
            jax.ShapeDtypeStruct((16, LANES), jnp.bfloat16),
        ],
        scratch_shapes=[pltpu.VMEM((ch, 2 * STEPS * STEP, count), jnp.bfloat16)],
        compiler_params=pltpu.CompilerParams(vmem_limit_bytes=12 << 20),
        cost_estimate=pl.CostEstimate(
            flops=4 * spectra * ch * 2 * SPAN * ch * count,
            bytes_accessed=4 * words.size + 4 * ch * spectra * count,
            transcendentals=0,
        ),
        name="own_spectra",
    )(words, words, gains, weights)


def select_kernel(last_rows, slots_ref, words_ref, parts_ref, out_ref):
    step = pl.program_id(0)
    count, rows = words_ref.shape[1], out_ref.shape[1]
    words = words_ref[...].astype(jnp.float32).astype(jnp.bfloat16)
    place = lax.broadcasted_iota(jnp.int32, (count, rows), 0)
    choice = jnp.where(slots_ref[...] == place, 1.0, 0.0).astype(jnp.bfloat16)
    out_ref[...] = jnp.dot(words, choice, preferred_element_type=jnp.float32).astype(out_ref.dtype)

    @pl.when(step == pl.num_programs(0) - 1)
    def _():
        extra = parts_ref.shape[0]
        out_ref[last_rows : last_rows + extra, :] = jnp.dot(
            parts_ref[...], choice, preferred_element_type=jnp.float32
        ).astype(out_ref.dtype)
        left = out_ref.shape[0] - last_rows - extra
        out_ref[last_rows + extra :, :] = jnp.zeros((left, rows), out_ref.dtype)


def select_rows(words, gains, slots, total):
    lines, count = words.shape
    rows = slots.shape[1]
    block = total // STEPS
    parts = jnp.concatenate([gains >> 4, gains & 15], axis=0).astype(jnp.bfloat16)
    return pl.pallas_call(
        functools.partial(select_kernel, lines - (STEPS - 1) * block),
        grid=(STEPS,),
        in_specs=[
            pl.BlockSpec((1, rows), lambda i: (0, 0)),
            pl.BlockSpec((block, count), lambda i: (i, 0)),
            pl.BlockSpec(parts.shape, lambda i: (0, 0)),
        ],
        out_specs=pl.BlockSpec((block, rows), lambda i: (i, 0)),
        out_shape=jax.ShapeDtypeStruct((total, rows), jnp.bfloat16),
        compiler_params=pltpu.CompilerParams(vmem_limit_bytes=8 << 20),
        name="select_rows",
    )(slots, words, parts)


def swap(value, bit):
    pairs = [(index, index ^ bit) for index in range(lax.axis_size("feed"))]
    return lax.ppermute(value, "feed", pairs)


def side(bit):
    return lax.axis_index("feed") // bit % 2


def reduce_half(value, bit):
    size = value.shape[0] // 2
    keep = lax.dynamic_slice_in_dim(value, side(bit) * size, size, 0)
    send = lax.dynamic_slice_in_dim(value, (1 - side(bit)) * size, size, 0)
    return keep + swap(send, bit)


def gather_half(value, bit, buffer):
    size = value.shape[0]
    other = swap(value, bit)
    buffer = lax.dynamic_update_slice_in_dim(buffer, value, side(bit) * size, 0)
    return lax.dynamic_update_slice_in_dim(buffer, other, (1 - side(bit)) * size, 0)


def sum_over_feed(value, zero):
    half = reduce_half(value, 1)
    size = half.shape[0] // 2
    left, right = half[:size], half[size:]
    left_1, right_1 = reduce_half(left, 2) + zero, reduce_half(right, 4)
    left_2, right_2 = reduce_half(left_1, 4), reduce_half(right_1, 2)
    left_3, right_3 = left_2 + swap(left_2, 8), right_2 + swap(right_2, 8)
    left_1, right_1 = gather_half(left_3, 4, left_1), gather_half(right_3, 2, right_1)
    left, right = gather_half(left_1, 2, left), gather_half(right_1, 4, right)
    return gather_half(jnp.concatenate([left, right], axis=0), 1, value)


def rows_kernel(main_ref, next_ref, parts_ref, weights_ref, own_ref, out_ref, left):
    step = pl.program_id(0)
    steps = pl.num_programs(0) // 2
    ch = left.shape[0]
    rows = main_ref.shape[1]

    @pl.when(step < steps)
    def _():
        words = jnp.concatenate([main_ref[...], next_ref[...]], axis=0).astype(jnp.float32).astype(jnp.int32)
        parts = parts_ref[...].astype(jnp.float32)
        gains = parts[: 2 * ch] * 16.0 + parts[2 * ch :]

        def store(b, c, real, imag):
            spot = pl.ds(pl.multiple_of(step * (2 * STEPS * STEP), 2 * STEPS * STEP) + b * 2 * STEP, 2 * STEP)
            left[c, spot, :rows] = jnp.concatenate([real, imag], axis=0).astype(left.dtype)
            left[c, spot, rows:] = jnp.concatenate([imag, -real], axis=0).astype(left.dtype)

        spectra_of(weights_ref, levels_of(words), gains, ch, store)

    @pl.when(step >= steps)
    def _():
        each = own_ref.shape[0]
        for index in range(each):
            products = jnp.dot(
                own_ref[index], left[(step - steps) * each + index], preferred_element_type=jnp.float32
            )
            count = products.shape[0]
            largest = jnp.maximum(jnp.max(jnp.abs(products), axis=0, keepdims=True), 2.0**-60)
            power = jnp.floor(jnp.log2(largest))
            coded = jnp.clip(jnp.round(products * jnp.exp2(RANGE - power)), -32767.0, 32767.0)
            out_ref[index, :count, :] = coded.astype(jnp.int32).astype(jnp.int16)
            line = jnp.broadcast_to(power, (out_ref.shape[1] - count, power.shape[1]))
            out_ref[index, count:, :] = line.astype(jnp.int32).astype(jnp.int16)


def row_products(words, parts, own, weights, index):
    ch, count, width = own.shape
    rows = LANES
    main = STEPS * STEP * ch
    steps = width // (2 * STEPS * STEP)
    each = ch // steps
    return pl.pallas_call(
        rows_kernel,
        grid=(2 * steps,),
        in_specs=[
            pl.BlockSpec((main, rows), lambda i: (jnp.minimum(i, steps - 1), index)),
            pl.BlockSpec((STEP * ch, rows), lambda i: ((jnp.minimum(i, steps - 1) + 1) * STEPS, index)),
            pl.BlockSpec((parts.shape[0], rows), lambda i: (0, index)),
            pl.BlockSpec(weights.shape, lambda i: (0, 0)),
            pl.BlockSpec((each, count, width), lambda i: (jnp.maximum(i - steps, 0), 0, 0)),
        ],
        out_specs=pl.BlockSpec((each, count + 16, 2 * rows), lambda i: (jnp.maximum(i - steps, 0), 0, 0)),
        out_shape=jax.ShapeDtypeStruct((ch, count + 16, 2 * rows), jnp.int16),
        scratch_shapes=[pltpu.VMEM((ch, width, 2 * rows), jnp.bfloat16)],
        compiler_params=pltpu.CompilerParams(vmem_limit_bytes=18 << 20),
        cost_estimate=pl.CostEstimate(
            flops=4 * width * ch * SPAN * ch * rows + 4 * ch * width * rows * count,
            bytes_accessed=2 * words.size + 2 * own.size + 4 * ch * rows * count,
            transcendentals=0,
        ),
        name="row_products",
    )(words, words, parts, weights, own)


def finish_kernel(scale, slot_ref, coded_ref, *refs):
    out_ref, products, tile, mixed = refs[-4:]
    sources, lines, width = coded_ref.shape
    count = lines - 16
    pieces = width // LANES
    feeds = sources * count
    columns = 2 * (feeds // LANES)
    for source in range(sources):
        power = coded_ref[source, count : count + 16, :][:1].astype(jnp.float32)
        values = coded_ref[source, :count, :].astype(jnp.float32) * (jnp.exp2(power - RANGE) * scale)
        for piece in range(pieces):
            products[pl.ds(source * count * pieces + piece, count, stride=pieces), :] = values[
                :, piece * LANES : (piece + 1) * LANES
            ]

    together = 8 // pieces

    @pl.loop(0, feeds // LANES // together)
    def _(j):
        for part in range(together):
            for i in range(LANES):
                slot = slot_ref[(j * together + part) * LANES + i]
                tile[i * pieces : (i + 1) * pieces, :] = products[
                    pl.ds(pl.multiple_of(slot * pieces, pieces), pieces), :
                ]
            for piece in range(pieces):
                turned = tile[pl.ds(piece, LANES, stride=pieces), :].T
                mixed[pl.ds(part * pieces + piece, LANES, stride=8), :] = turned
        for row in range(LANES):
            out_ref[pl.ds(pl.multiple_of(row * columns + j * 8, 8), 8), :] = mixed[row * 8 : (row + 1) * 8, :]


def finish(coded, feed_slot, index, pieces, scale, before):
    sources, lines, width = coded.shape
    rows = width // 2
    feeds = sources * (lines - 16)
    columns = 2 * (feeds // LANES)
    earlier = [] if before is None else [before]
    return pl.pallas_call(
        functools.partial(finish_kernel, scale),
        grid=(1,),
        in_specs=[
            pl.BlockSpec(memory_space=pltpu.SMEM),
            pl.BlockSpec(coded.shape, lambda i: (0, 0, 0)),
        ]
        + [pl.BlockSpec(memory_space=pl.ANY)] * len(earlier),
        out_specs=pl.BlockSpec((rows * columns, LANES), lambda i: (index, 0)),
        out_shape=jax.ShapeDtypeStruct((pieces * rows * columns, LANES), jnp.float32),
        scratch_shapes=[
            pltpu.VMEM((feeds * width // LANES, LANES), jnp.float32),
            pltpu.VMEM((width, LANES), jnp.float32),
            pltpu.VMEM((8 * LANES, LANES), jnp.float32),
        ],
        input_output_aliases={2: 0} if earlier else {},
        compiler_params=pltpu.CompilerParams(vmem_limit_bytes=22 << 20),
        name="finish",
    )(feed_slot, coded, *earlier)


def through_rows(samples, gains, feed_slot):
    count, ch, frames = samples.shape
    spectra = frames - TAPS + 1
    pieces = ROWS // LANES
    lines = frames * ch
    unit = 16 * STEPS * 2
    total = pl.cdiv(lines + 4 * ch, unit) * unit
    words = jnp.transpose(samples, (2, 1, 0)).reshape(lines, count)
    scales = gains.reshape(2 * ch, count)
    weights = jnp.asarray(filter_weights(ch))
    slots = (feed_slot[:ROWS] - lax.axis_index("feed") * count).reshape(1, ROWS)
    picked = select_rows(words, scales, slots, total)
    own, zero = own_spectra(words, scales.astype(jnp.float32), weights, ch, spectra)
    rows = sum_over_feed(picked, zero[0, 0])
    parts = rows[lines : lines + 4 * ch]
    out = None
    for index in range(pieces):
        coded = row_products(rows, parts, own, weights, index)
        moved = lax.all_to_all(coded, "feed", split_axis=0, concat_axis=0, tiled=True)
        out = finish(moved, feed_slot, index, pieces, 1.0 / spectra, out)
    feeds = feed_slot.shape[0]
    out = out.reshape(ROWS, feeds // LANES, 2, LANES)
    return jnp.transpose(out, (0, 2, 1, 3)).reshape(ROWS, 2, feeds)


def body(samples, gains, feed_slot):
    count, ch, frames = samples.shape
    spectra = frames - TAPS + 1
    even = count % LANES == 0 and spectra % (STEPS * STEP) == 0 and ch % STEPS == 0
    if lax.axis_size("feed") == ch == 16 and even:
        return through_rows(samples, gains, feed_slot)
    return through_spectra(samples, gains, feed_slot)


def solution(mesh):
    return jax.shard_map(
        body,
        mesh=mesh,
        in_specs=(P(("band", "feed"), None, None), P(None, "band", "feed"), P()),
        out_specs=P(("band", "feed"), None, None),
        check_vma=False,
    )
```

```python
import functools
import math

import jax
import jax.numpy as jnp
import numpy as np
from jax import lax
from jax.experimental import pallas as pl
from jax.experimental.pallas import tpu as pltpu
from jax.sharding import PartitionSpec as P

TAPS = 8
ROWS = 256
LANES = 128


def filter_taps(ch):
    length = TAPS * ch
    place = np.arange(length, dtype=np.float64)
    window = 0.5 - 0.5 * np.cos(2.0 * math.pi * place / (length - 1))
    return (np.sinc((place - 0.5 * (length - 1)) / ch) * window).reshape(TAPS, ch)


def twiddle(value, turn):
    real, imag = value
    if turn == 0:
        return value
    if turn == 0.25:
        return imag, -real
    half = math.sqrt(0.5)
    if turn == 0.125:
        return half * (real + imag), half * (imag - real)
    if turn == 0.375:
        return half * (imag - real), -half * (real + imag)
    c, s = math.cos(2.0 * math.pi * turn), math.sin(2.0 * math.pi * turn)
    return c * real + s * imag, c * imag - s * real


def fft(values):
    count = len(values)
    if count == 1:
        return values
    even, odd = fft(values[0::2]), fft(values[1::2])
    low, high = [], []
    for index in range(count // 2):
        real, imag = twiddle(odd[index], index / count)
        low.append((even[index][0] + real, even[index][1] + imag))
        high.append((even[index][0] - real, even[index][1] - imag))
    return low + high


def channel_kernel(taps, *refs):
    *samples_refs, gains_ref, out_ref, filtered = refs
    ch, block, width = out_ref.shape
    spectra = width // 2
    padded = len(samples_refs) * LANES
    for k in range(ch):
        words = jnp.concatenate(
            [ref[pl.ds(k, block, stride=ch), :] for ref in samples_refs], axis=1
        )
        levels = ((words >> 4) - 8, (words & 15) - 8)
        for part in range(2):
            value = levels[part].astype(jnp.float32)
            shifted = [value] + [pltpu.roll(value, padded - t, 1) for t in range(1, TAPS // 2)]
            near = float(taps[0, k]) * shifted[0]
            far = float(taps[TAPS // 2, k]) * shifted[0]
            for t in range(1, TAPS // 2):
                near = near + float(taps[t, k]) * shifted[t]
                far = far + float(taps[t + TAPS // 2, k]) * shifted[t]
            total = near + pltpu.roll(far, padded - TAPS // 2, 1)
            filtered[2 * k + part] = total[:, :spectra]
    for row in range(0, block, 8):
        gains = gains_ref[row : row + 8, :]
        for lane in range(0, spectra, LANES):
            spot = (slice(row, row + 8), slice(lane, lane + LANES))
            values = [(filtered[2 * k][spot], filtered[2 * k + 1][spot]) for k in range(ch)]
            for c, (real, imag) in enumerate(fft(values)):
                gain_real = gains[:, c : c + 1]
                gain_imag = gains[:, ch + c : ch + c + 1]
                out_ref[c, row : row + 8, lane : lane + LANES] = (
                    gain_real * real - gain_imag * imag
                ).astype(out_ref.dtype)
                out_ref[c, row : row + 8, spectra + lane : spectra + lane + LANES] = (
                    gain_real * imag + gain_imag * real
                ).astype(out_ref.dtype)


def channelize(samples, gains):
    count, ch, frames = samples.shape
    spectra = frames - TAPS + 1
    block = 16
    pieces = pl.cdiv(frames, LANES)
    scale = 0.125 / math.sqrt(ch) / 2048.0
    taps = (filter_taps(ch) * scale).astype(np.float32)
    return pl.pallas_call(
        functools.partial(channel_kernel, taps),
        grid=(count // block,),
        in_specs=[
            pl.BlockSpec((block * ch, LANES), functools.partial(lambda piece, i: (i, piece), piece))
            for piece in range(pieces)
        ]
        + [pl.BlockSpec((block, 2 * ch), lambda i: (i, 0))],
        out_specs=pl.BlockSpec((ch, block, 2 * spectra), lambda i: (0, i, 0)),
        out_shape=jax.ShapeDtypeStruct((ch, count, 2 * spectra), jnp.bfloat16),
        scratch_shapes=[pltpu.VMEM((2 * ch, block, spectra), jnp.float32)],
        compiler_params=pltpu.CompilerParams(vmem_limit_bytes=32 << 20),
        name="channelize",
    )(*[samples.reshape(count * ch, frames)] * pieces, gains)


def correlate_kernel(scale, slot_ref, row_ref, data_ref, out_ref, products, tile):
    feeds, width = data_ref.shape
    spectra = width // 2
    rows = row_ref.shape[0]
    pieces = 2 * rows // LANES
    step = 256
    picked = jnp.zeros((rows, width), jnp.float32)
    for first in range(0, feeds, 512):
        place = lax.broadcasted_iota(jnp.int32, (rows, 512), 1) + first
        choice = jnp.where(row_ref[...] == place, 1.0, 0.0).astype(jnp.bfloat16)
        picked = picked + jnp.dot(
            choice, data_ref[first : first + 512, :], preferred_element_type=jnp.float32
        )
    left = jnp.concatenate(
        [
            picked,
            jnp.concatenate([picked[:, spectra:], -picked[:, :spectra]], axis=1),
        ],
        axis=0,
    ).astype(jnp.bfloat16)

    @pl.loop(0, feeds // step)
    def _(i):
        first = pl.multiple_of(i * step, step)
        result = lax.dot_general(
            data_ref[pl.ds(first, step), :],
            left,
            (((1,), (1,)), ((), ())),
            preferred_element_type=jnp.float32,
        )
        for piece in range(pieces):
            products[pl.ds(first * pieces + piece, step, stride=pieces), :] = (
                result[:, piece * LANES : (piece + 1) * LANES] * scale
            )

    lines = 2 * (feeds // LANES)

    @pl.loop(0, feeds // LANES)
    def _(j):
        @pl.loop(0, LANES, unroll=16)
        def _(i):
            slot = slot_ref[j * LANES + i]
            tile[pl.ds(pl.multiple_of(i * pieces, pieces), pieces), :] = products[
                pl.ds(pl.multiple_of(slot * pieces, pieces), pieces), :
            ]

        for piece in range(pieces):
            part, first = divmod(piece * LANES, rows)
            turned = tile[pl.ds(piece, LANES, stride=pieces), :].T
            out_ref[pl.ds(first * lines + 2 * j + part, LANES, stride=lines), :] = turned


def correlate(data, feed_slot, first, rows):
    feeds, width = data.shape
    row_slots = lax.dynamic_slice_in_dim(feed_slot, first, rows, 0).reshape(rows, 1)
    lines = 2 * (feeds // LANES)
    out = pl.pallas_call(
        functools.partial(correlate_kernel, 2.0 / width),
        in_specs=[
            pl.BlockSpec(memory_space=pltpu.SMEM),
            pl.BlockSpec(memory_space=pltpu.VMEM),
            pl.BlockSpec(memory_space=pltpu.VMEM),
        ],
        out_specs=pl.BlockSpec(memory_space=pltpu.VMEM),
        out_shape=jax.ShapeDtypeStruct((rows * lines, LANES), jnp.float32),
        scratch_shapes=[
            pltpu.VMEM((feeds * 2 * rows // LANES, LANES), jnp.float32),
            pltpu.VMEM((LANES * 2 * rows // LANES, LANES), jnp.float32),
        ],
        compiler_params=pltpu.CompilerParams(vmem_limit_bytes=48 << 20),
        name="correlate",
    )(feed_slot, row_slots, data)
    out = out.reshape(rows, feeds // LANES, 2, LANES)
    return jnp.transpose(out, (0, 2, 1, 3)).reshape(rows, 2, feeds)


def through_spectra(samples, gains, feed_slot):
    count, ch, _ = samples.shape
    groups = lax.axis_size("feed") // ch
    first = lax.axis_index("feed") % groups * ROWS
    scales = jnp.transpose(gains, (2, 0, 1)).reshape(count, 2 * ch).astype(jnp.float32)
    spectra = channelize(samples, scales)
    width = spectra.shape[2]
    outgoing = jnp.broadcast_to(spectra[:, None], (ch, groups, count, width))
    outgoing = outgoing.reshape(ch * groups, count, width)
    moved = lax.all_to_all(outgoing, "feed", split_axis=0, concat_axis=0, tiled=True)
    return correlate(moved.reshape(-1, width), feed_slot, first, ROWS)


STEP = 8
SPAN = 16
STEPS = 8
RANGE = 14


def filter_weights(ch):
    taps = filter_taps(ch) * (0.125 / math.sqrt(ch) / 2048.0)
    half = ch // 2
    weights = np.zeros((ch, STEP, SPAN, ch))
    angle = 2.0 * math.pi * (np.arange(half + 1)[:, None] * np.arange(ch)[None, :] % ch) / ch
    sums = np.concatenate([np.cos(angle), np.sin(angle[1:half])], axis=0)
    for spectrum in range(STEP):
        for t in range(TAPS):
            weights[:, spectrum, spectrum + t] = taps[t] * sums
    weights = weights.reshape(ch * STEP, SPAN * ch)
    high = weights.astype(jnp.bfloat16)
    low = (weights - high.astype(np.float64)).astype(jnp.bfloat16)
    return np.concatenate([high, low])


def spectra_of(weights_ref, levels, gains, ch, store):
    count = levels[0].shape[1]
    half, size = ch // 2, ch * STEP
    beside = max(1, 256 // count)
    for first in range(0, STEPS, beside):
        totals = []
        for level in levels:
            slabs = [level[b * size : b * size + SPAN * ch] for b in range(first, first + beside)]
            slab = jnp.concatenate(slabs, axis=1) if beside > 1 else slabs[0]
            both = jnp.dot(weights_ref[...], slab, preferred_element_type=jnp.float32)
            totals.append(both[:size] + both[size:])
        for index in range(beside):
            lanes = slice(index * count, (index + 1) * count)
            parts = [
                [total[d * STEP : (d + 1) * STEP, lanes] for d in range(ch)] for total in totals
            ]
            for c in range(ch):
                place = min(c, ch - c)
                real, imag = parts[0][place], parts[1][place]
                if c % half:
                    sine_real, sine_imag = parts[0][half + place], parts[1][half + place]
                    if c < half:
                        real, imag = real + sine_imag, imag - sine_real
                    else:
                        real, imag = real - sine_imag, imag + sine_real
                gain_real, gain_imag = gains[c : c + 1], gains[ch + c : ch + c + 1]
                store(
                    first + index,
                    c,
                    gain_real * real - gain_imag * imag,
                    gain_real * imag + gain_imag * real,
                )


def levels_of(words):
    return [
        ((words >> 4) - 8).astype(jnp.float32).astype(jnp.bfloat16),
        ((words & 15) - 8).astype(jnp.float32).astype(jnp.bfloat16),
    ]


def own_kernel(main_ref, next_ref, gains_ref, weights_ref, after_ref, out_ref, zero_ref, held, turned, sems):
    step = pl.program_id(0)
    slot = step % 2
    ch = out_ref.shape[0]
    zero_ref[...] = jnp.zeros_like(zero_ref)
    words = jnp.concatenate([main_ref[...], next_ref[...]], axis=0)

    def copy(index):
        return pltpu.make_async_copy(turned.at[index % 2], out_ref.at[:, index], sems.at[index % 2])

    def store(b, c, real, imag):
        held[c, b * 2 * STEP : (b + 1) * 2 * STEP, :] = jnp.concatenate([real, imag], axis=0).astype(held.dtype)

    spectra_of(weights_ref, levels_of(words), gains_ref[...], ch, store)

    @pl.when(step >= 2)
    def _():
        copy(step - 2).wait()

    for c in range(ch):
        turned[slot, c] = held[c].T
    copy(step).start()

    @pl.when(step == pl.num_programs(0) - 1)
    def _():
        copy(step - 1).wait()
        copy(step).wait()


def own_spectra(words, gains, weights, ch, spectra, after):
    count = words.shape[1]
    main = STEPS * STEP * ch
    steps = spectra // (STEPS * STEP)
    return pl.pallas_call(
        own_kernel,
        grid=(steps,),
        in_specs=[
            pl.BlockSpec((main, count), lambda i: (i, 0)),
            pl.BlockSpec((STEP * ch, count), lambda i: ((i + 1) * STEPS, 0)),
            pl.BlockSpec(gains.shape, lambda i: (0, 0)),
            pl.BlockSpec(weights.shape, lambda i: (0, 0)),
            pl.BlockSpec(memory_space=pl.ANY),
        ],
        out_specs=[
            pl.BlockSpec(memory_space=pltpu.HBM),
            pl.BlockSpec((16, LANES), lambda i: (0, 0)),
        ],
        out_shape=[
            jax.ShapeDtypeStruct((ch, steps, count, 2 * STEPS * STEP), jnp.bfloat16),
            jax.ShapeDtypeStruct((16, LANES), jnp.bfloat16),
        ],
        scratch_shapes=[
            pltpu.VMEM((ch, 2 * STEPS * STEP, count), jnp.bfloat16),
            pltpu.VMEM((2, ch, count, 2 * STEPS * STEP), jnp.bfloat16),
            pltpu.SemaphoreType.DMA((2,)),
        ],
        compiler_params=pltpu.CompilerParams(vmem_limit_bytes=12 << 20),
        cost_estimate=pl.CostEstimate(
            flops=4 * spectra * ch * 2 * SPAN * ch * count,
            bytes_accessed=4 * words.size + 4 * ch * spectra * count,
            transcendentals=0,
        ),
        name="own_spectra",
    )(words, words, gains, weights, after)


def select_kernel(last_rows, slots_ref, words_ref, parts_ref, *outs):
    step = pl.program_id(0)
    count, rows = words_ref.shape[1], slots_ref.shape[1]
    words = words_ref[...].astype(jnp.float32).astype(jnp.bfloat16)
    place = lax.broadcasted_iota(jnp.int32, (count, rows), 0)
    choice = jnp.where(slots_ref[...] == place, 1.0, 0.0).astype(jnp.bfloat16)
    taken = jnp.dot(words, choice, preferred_element_type=jnp.float32).astype(outs[0].dtype)
    for index, out_ref in enumerate(outs):
        out_ref[...] = taken[:, index * LANES : (index + 1) * LANES]

    @pl.when(step == pl.num_programs(0) - 1)
    def _():
        extra = parts_ref.shape[0]
        gains = jnp.dot(parts_ref[...], choice, preferred_element_type=jnp.float32).astype(outs[0].dtype)
        for index, out_ref in enumerate(outs):
            out_ref[last_rows : last_rows + extra, :] = gains[:, index * LANES : (index + 1) * LANES]
            left = out_ref.shape[0] - last_rows - extra
            out_ref[last_rows + extra :, :] = jnp.zeros((left, LANES), out_ref.dtype)


def select_rows(words, gains, slots, total):
    lines, count = words.shape
    rows = slots.shape[1]
    block = total // STEPS
    parts = jnp.concatenate([gains >> 4, gains & 15], axis=0).astype(jnp.bfloat16)
    return pl.pallas_call(
        functools.partial(select_kernel, lines - (STEPS - 1) * block),
        grid=(STEPS,),
        in_specs=[
            pl.BlockSpec((1, rows), lambda i: (0, 0)),
            pl.BlockSpec((block, count), lambda i: (i, 0)),
            pl.BlockSpec(parts.shape, lambda i: (0, 0)),
        ],
        out_specs=[pl.BlockSpec((block, LANES), lambda i: (i, 0))] * (rows // LANES),
        out_shape=[jax.ShapeDtypeStruct((total, LANES), jnp.bfloat16)] * (rows // LANES),
        compiler_params=pltpu.CompilerParams(vmem_limit_bytes=8 << 20),
        name="select_rows",
    )(slots, words, parts)


def swap(value, bit):
    pairs = [(index, index ^ bit) for index in range(lax.axis_size("feed"))]
    return lax.ppermute(value, "feed", pairs)


def side(bit):
    return lax.axis_index("feed") // bit % 2


def reduce_half(value, bit):
    size = value.shape[0] // 2
    keep = lax.dynamic_slice_in_dim(value, side(bit) * size, size, 0)
    send = lax.dynamic_slice_in_dim(value, (1 - side(bit)) * size, size, 0)
    return keep + swap(send, bit)


def gather_half(value, bit, buffer):
    size = value.shape[0]
    other = swap(value, bit)
    buffer = lax.dynamic_update_slice_in_dim(buffer, value, side(bit) * size, 0)
    return lax.dynamic_update_slice_in_dim(buffer, other, (1 - side(bit)) * size, 0)


def sum_over_feed(value, work=None):
    half = reduce_half(value, 1)
    size = half.shape[0] // 2
    left, right = half[:size], half[size:]
    left_1, right_1 = reduce_half(left, 2), reduce_half(right, 4)
    left_2, right_2 = reduce_half(left_1, 4), reduce_half(right_1, 2)
    left_3, right_3 = left_2 + swap(left_2, 8), right_2 + swap(right_2, 8)
    if work is not None:
        left_3 = left_3 + work(left_2)
    left_1, right_1 = gather_half(left_3, 4, left_1), gather_half(right_3, 2, right_1)
    left, right = gather_half(left_1, 2, left), gather_half(right_1, 4, right)
    half = jnp.concatenate([left, right], axis=0)
    return half, lambda: gather_half(half, 1, value)


def rows_kernel(main_ref, next_ref, parts_ref, weights_ref, own_ref, after_ref, out_ref, left, own, sems):
    step = pl.program_id(0)
    steps = pl.num_programs(0) // 2
    ch = left.shape[0]
    rows = main_ref.shape[1]

    def copy(c):
        return pltpu.make_async_copy(own_ref.at[c], own.at[c], sems.at[c])

    @pl.when(step == 0)
    def _():
        for c in range(ch):
            copy(c).start()

    @pl.when(step < steps)
    def _():
        words = jnp.concatenate([main_ref[...], next_ref[...]], axis=0).astype(jnp.float32).astype(jnp.int32)
        parts = parts_ref[...].astype(jnp.float32)
        gains = parts[: 2 * ch] * 16.0 + parts[2 * ch :]

        def store(b, c, real, imag):
            spot = pl.ds(pl.multiple_of(step * (2 * STEPS * STEP), 2 * STEPS * STEP) + b * 2 * STEP, 2 * STEP)
            left[c, spot, :rows] = jnp.concatenate([real, imag], axis=0).astype(left.dtype)
            left[c, spot, rows:] = jnp.concatenate([imag, -real], axis=0).astype(left.dtype)

        spectra_of(weights_ref, levels_of(words), gains, ch, store)

    @pl.when(step >= steps)
    def _():
        each = out_ref.shape[0]
        for index in range(each):
            c = (step - steps) * each + index
            copy(c).wait()
            spectra = jnp.concatenate([own[c, part] for part in range(own.shape[1])], axis=1)
            products = jnp.dot(spectra, left[c], preferred_element_type=jnp.float32)
            count = products.shape[0]
            largest = jnp.maximum(jnp.max(jnp.abs(products), axis=0, keepdims=True), 2.0**-60)
            power = jnp.floor(jnp.log2(largest))
            coded = jnp.clip(jnp.round(products * jnp.exp2(RANGE - power)), -32767.0, 32767.0)
            out_ref[index, :count, :] = coded.astype(jnp.int32).astype(jnp.int16)
            line = jnp.broadcast_to(power, (out_ref.shape[1] - count, power.shape[1]))
            out_ref[index, count:, :] = line.astype(jnp.int32).astype(jnp.int16)


def row_products(words, parts, own, weights, after):
    ch, steps, count, width = own.shape
    rows = words.shape[1]
    main = STEPS * STEP * ch
    each = ch // steps
    return pl.pallas_call(
        rows_kernel,
        grid=(2 * steps,),
        in_specs=[
            pl.BlockSpec((main, rows), lambda i: (jnp.minimum(i, steps - 1), 0)),
            pl.BlockSpec((STEP * ch, rows), lambda i: ((jnp.minimum(i, steps - 1) + 1) * STEPS, 0)),
            pl.BlockSpec(parts.shape, lambda i: (0, 0)),
            pl.BlockSpec(weights.shape, lambda i: (0, 0)),
            pl.BlockSpec(memory_space=pltpu.HBM),
            pl.BlockSpec(memory_space=pl.ANY),
        ],
        out_specs=pl.BlockSpec((each, count + 16, 2 * rows), lambda i: (jnp.maximum(i - steps, 0), 0, 0)),
        out_shape=jax.ShapeDtypeStruct((ch, count + 16, 2 * rows), jnp.int16),
        scratch_shapes=[
            pltpu.VMEM((ch, steps * width, 2 * rows), jnp.bfloat16),
            pltpu.VMEM(own.shape, jnp.bfloat16),
            pltpu.SemaphoreType.DMA((ch,)),
        ],
        compiler_params=pltpu.CompilerParams(vmem_limit_bytes=24 << 20),
        cost_estimate=pl.CostEstimate(
            flops=4 * steps * width * ch * SPAN * ch * rows + 4 * ch * steps * width * rows * count,
            bytes_accessed=2 * words.size + 2 * own.size + 4 * ch * rows * count,
            transcendentals=0,
        ),
        name="row_products",
    )(words, words, parts, weights, own, after)


def finish_kernel(scale, slot_ref, coded_ref, *refs):
    out_ref, products, tile, mixed = refs[-4:]
    sources, lines, width = coded_ref.shape
    count = lines - 16
    pieces = width // LANES
    feeds = sources * count
    columns = 2 * (feeds // LANES)
    for source in range(sources):
        power = coded_ref[source, count : count + 16, :][:1].astype(jnp.float32)
        values = coded_ref[source, :count, :].astype(jnp.float32) * (jnp.exp2(power - RANGE) * scale)
        for piece in range(pieces):
            products[pl.ds(source * count * pieces + piece, count, stride=pieces), :] = values[
                :, piece * LANES : (piece + 1) * LANES
            ]

    together = 8 // pieces

    @pl.loop(0, feeds // LANES // together)
    def _(j):
        for part in range(together):
            for i in range(LANES):
                slot = slot_ref[(j * together + part) * LANES + i]
                tile[i * pieces : (i + 1) * pieces, :] = products[
                    pl.ds(pl.multiple_of(slot * pieces, pieces), pieces), :
                ]
            for piece in range(pieces):
                turned = tile[pl.ds(piece, LANES, stride=pieces), :].T
                mixed[pl.ds(part * pieces + piece, LANES, stride=8), :] = turned
        for row in range(LANES):
            out_ref[pl.ds(pl.multiple_of(row * columns + j * 8, 8), 8), :] = mixed[row * 8 : (row + 1) * 8, :]


def finish(coded, feed_slot, index, pieces, scale, before):
    sources, lines, width = coded.shape
    rows = width // 2
    feeds = sources * (lines - 16)
    columns = 2 * (feeds // LANES)
    earlier = [] if before is None else [before]
    return pl.pallas_call(
        functools.partial(finish_kernel, scale),
        grid=(1,),
        in_specs=[
            pl.BlockSpec(memory_space=pltpu.SMEM),
            pl.BlockSpec(coded.shape, lambda i: (0, 0, 0)),
        ]
        + [pl.BlockSpec(memory_space=pl.ANY)] * len(earlier),
        out_specs=pl.BlockSpec((rows * columns, LANES), lambda i: (index, 0)),
        out_shape=jax.ShapeDtypeStruct((pieces * rows * columns, LANES), jnp.float32),
        scratch_shapes=[
            pltpu.VMEM((feeds * width // LANES, LANES), jnp.float32),
            pltpu.VMEM((width, LANES), jnp.float32),
            pltpu.VMEM((8 * LANES, LANES), jnp.float32),
        ],
        input_output_aliases={2: 0} if earlier else {},
        compiler_params=pltpu.CompilerParams(vmem_limit_bytes=22 << 20),
        name="finish",
    )(feed_slot, coded, *earlier)


def through_rows(samples, gains, feed_slot):
    count, ch, frames = samples.shape
    spectra = frames - TAPS + 1
    pieces = ROWS // LANES
    lines = frames * ch
    unit = 16 * STEPS * 2
    total = pl.cdiv(lines + 4 * ch, unit) * unit
    words = jnp.transpose(samples, (2, 1, 0)).reshape(lines, count)
    scales = gains.reshape(2 * ch, count)
    weights = jnp.asarray(filter_weights(ch))
    slots = (feed_slot[:ROWS] - lax.axis_index("feed") * count).reshape(1, ROWS)
    picked = select_rows(words, scales, slots, total)
    held = []

    def work(after):
        own, zero = own_spectra(words, scales.astype(jnp.float32), weights, ch, spectra, after)
        held.append(own)
        return zero[0, 0]

    sums = [sum_over_feed(value, None if index else work) for index, value in enumerate(picked)]
    own = held[0]
    out = None
    for index in range(pieces):
        rows = sums[index][1]()
        parts = rows[lines : lines + 4 * ch]
        coded = row_products(rows, parts, own, weights, sums[-1][0])
        moved = lax.all_to_all(coded, "feed", split_axis=0, concat_axis=0, tiled=True)
        out = finish(moved, feed_slot, index, pieces, 1.0 / spectra, out)
    feeds = feed_slot.shape[0]
    out = out.reshape(ROWS, feeds // LANES, 2, LANES)
    return jnp.transpose(out, (0, 2, 1, 3)).reshape(ROWS, 2, feeds)


def body(samples, gains, feed_slot):
    count, ch, frames = samples.shape
    spectra = frames - TAPS + 1
    even = count % LANES == 0 and spectra % (STEPS * STEP) == 0 and ch % STEPS == 0
    if lax.axis_size("feed") == ch == 16 and even:
        return through_rows(samples, gains, feed_slot)
    return through_spectra(samples, gains, feed_slot)


def solution(mesh):
    return jax.shard_map(
        body,
        mesh=mesh,
        in_specs=(P(("band", "feed"), None, None), P(None, "band", "feed"), P()),
        out_specs=P(("band", "feed"), None, None),
        check_vma=False,
    )
```

```python
import functools
import math

import jax
import jax.numpy as jnp
import numpy as np
from jax import lax
from jax.experimental import pallas as pl
from jax.experimental.pallas import tpu as pltpu
from jax.sharding import PartitionSpec as P

TAPS = 8
ROWS = 256
LANES = 128


def filter_taps(ch):
    length = TAPS * ch
    place = np.arange(length, dtype=np.float64)
    window = 0.5 - 0.5 * np.cos(2.0 * math.pi * place / (length - 1))
    return (np.sinc((place - 0.5 * (length - 1)) / ch) * window).reshape(TAPS, ch)


def twiddle(value, turn):
    real, imag = value
    if turn == 0:
        return value
    if turn == 0.25:
        return imag, -real
    half = math.sqrt(0.5)
    if turn == 0.125:
        return half * (real + imag), half * (imag - real)
    if turn == 0.375:
        return half * (imag - real), -half * (real + imag)
    c, s = math.cos(2.0 * math.pi * turn), math.sin(2.0 * math.pi * turn)
    return c * real + s * imag, c * imag - s * real


def fft(values):
    count = len(values)
    if count == 1:
        return values
    even, odd = fft(values[0::2]), fft(values[1::2])
    low, high = [], []
    for index in range(count // 2):
        real, imag = twiddle(odd[index], index / count)
        low.append((even[index][0] + real, even[index][1] + imag))
        high.append((even[index][0] - real, even[index][1] - imag))
    return low + high


def channel_kernel(taps, *refs):
    *samples_refs, gains_ref, out_ref, filtered = refs
    ch, block, width = out_ref.shape
    spectra = width // 2
    padded = len(samples_refs) * LANES
    for k in range(ch):
        words = jnp.concatenate(
            [ref[pl.ds(k, block, stride=ch), :] for ref in samples_refs], axis=1
        )
        levels = ((words >> 4) - 8, (words & 15) - 8)
        for part in range(2):
            value = levels[part].astype(jnp.float32)
            shifted = [value] + [pltpu.roll(value, padded - t, 1) for t in range(1, TAPS // 2)]
            near = float(taps[0, k]) * shifted[0]
            far = float(taps[TAPS // 2, k]) * shifted[0]
            for t in range(1, TAPS // 2):
                near = near + float(taps[t, k]) * shifted[t]
                far = far + float(taps[t + TAPS // 2, k]) * shifted[t]
            total = near + pltpu.roll(far, padded - TAPS // 2, 1)
            filtered[2 * k + part] = total[:, :spectra]
    for row in range(0, block, 8):
        gains = gains_ref[row : row + 8, :]
        for lane in range(0, spectra, LANES):
            spot = (slice(row, row + 8), slice(lane, lane + LANES))
            values = [(filtered[2 * k][spot], filtered[2 * k + 1][spot]) for k in range(ch)]
            for c, (real, imag) in enumerate(fft(values)):
                gain_real = gains[:, c : c + 1]
                gain_imag = gains[:, ch + c : ch + c + 1]
                out_ref[c, row : row + 8, lane : lane + LANES] = (
                    gain_real * real - gain_imag * imag
                ).astype(out_ref.dtype)
                out_ref[c, row : row + 8, spectra + lane : spectra + lane + LANES] = (
                    gain_real * imag + gain_imag * real
                ).astype(out_ref.dtype)


def channelize(samples, gains):
    count, ch, frames = samples.shape
    spectra = frames - TAPS + 1
    block = 16
    pieces = pl.cdiv(frames, LANES)
    scale = 0.125 / math.sqrt(ch) / 2048.0
    taps = (filter_taps(ch) * scale).astype(np.float32)
    return pl.pallas_call(
        functools.partial(channel_kernel, taps),
        grid=(count // block,),
        in_specs=[
            pl.BlockSpec((block * ch, LANES), functools.partial(lambda piece, i: (i, piece), piece))
            for piece in range(pieces)
        ]
        + [pl.BlockSpec((block, 2 * ch), lambda i: (i, 0))],
        out_specs=pl.BlockSpec((ch, block, 2 * spectra), lambda i: (0, i, 0)),
        out_shape=jax.ShapeDtypeStruct((ch, count, 2 * spectra), jnp.bfloat16),
        scratch_shapes=[pltpu.VMEM((2 * ch, block, spectra), jnp.float32)],
        compiler_params=pltpu.CompilerParams(vmem_limit_bytes=32 << 20),
        name="channelize",
    )(*[samples.reshape(count * ch, frames)] * pieces, gains)


def correlate_kernel(scale, slot_ref, row_ref, data_ref, out_ref, products, tile):
    feeds, width = data_ref.shape
    spectra = width // 2
    rows = row_ref.shape[0]
    pieces = 2 * rows // LANES
    step = 256
    picked = jnp.zeros((rows, width), jnp.float32)
    for first in range(0, feeds, 512):
        place = lax.broadcasted_iota(jnp.int32, (rows, 512), 1) + first
        choice = jnp.where(row_ref[...] == place, 1.0, 0.0).astype(jnp.bfloat16)
        picked = picked + jnp.dot(
            choice, data_ref[first : first + 512, :], preferred_element_type=jnp.float32
        )
    left = jnp.concatenate(
        [
            picked,
            jnp.concatenate([picked[:, spectra:], -picked[:, :spectra]], axis=1),
        ],
        axis=0,
    ).astype(jnp.bfloat16)

    @pl.loop(0, feeds // step)
    def _(i):
        first = pl.multiple_of(i * step, step)
        result = lax.dot_general(
            data_ref[pl.ds(first, step), :],
            left,
            (((1,), (1,)), ((), ())),
            preferred_element_type=jnp.float32,
        )
        for piece in range(pieces):
            products[pl.ds(first * pieces + piece, step, stride=pieces), :] = (
                result[:, piece * LANES : (piece + 1) * LANES] * scale
            )

    lines = 2 * (feeds // LANES)

    @pl.loop(0, feeds // LANES)
    def _(j):
        @pl.loop(0, LANES, unroll=16)
        def _(i):
            slot = slot_ref[j * LANES + i]
            tile[pl.ds(pl.multiple_of(i * pieces, pieces), pieces), :] = products[
                pl.ds(pl.multiple_of(slot * pieces, pieces), pieces), :
            ]

        for piece in range(pieces):
            part, first = divmod(piece * LANES, rows)
            turned = tile[pl.ds(piece, LANES, stride=pieces), :].T
            out_ref[pl.ds(first * lines + 2 * j + part, LANES, stride=lines), :] = turned


def correlate(data, feed_slot, first, rows):
    feeds, width = data.shape
    row_slots = lax.dynamic_slice_in_dim(feed_slot, first, rows, 0).reshape(rows, 1)
    lines = 2 * (feeds // LANES)
    out = pl.pallas_call(
        functools.partial(correlate_kernel, 2.0 / width),
        in_specs=[
            pl.BlockSpec(memory_space=pltpu.SMEM),
            pl.BlockSpec(memory_space=pltpu.VMEM),
            pl.BlockSpec(memory_space=pltpu.VMEM),
        ],
        out_specs=pl.BlockSpec(memory_space=pltpu.VMEM),
        out_shape=jax.ShapeDtypeStruct((rows * lines, LANES), jnp.float32),
        scratch_shapes=[
            pltpu.VMEM((feeds * 2 * rows // LANES, LANES), jnp.float32),
            pltpu.VMEM((LANES * 2 * rows // LANES, LANES), jnp.float32),
        ],
        compiler_params=pltpu.CompilerParams(vmem_limit_bytes=48 << 20),
        name="correlate",
    )(feed_slot, row_slots, data)
    out = out.reshape(rows, feeds // LANES, 2, LANES)
    return jnp.transpose(out, (0, 2, 1, 3)).reshape(rows, 2, feeds)


def through_spectra(samples, gains, feed_slot):
    count, ch, _ = samples.shape
    groups = lax.axis_size("feed") // ch
    first = lax.axis_index("feed") % groups * ROWS
    scales = jnp.transpose(gains, (2, 0, 1)).reshape(count, 2 * ch).astype(jnp.float32)
    spectra = channelize(samples, scales)
    width = spectra.shape[2]
    outgoing = jnp.broadcast_to(spectra[:, None], (ch, groups, count, width))
    outgoing = outgoing.reshape(ch * groups, count, width)
    moved = lax.all_to_all(outgoing, "feed", split_axis=0, concat_axis=0, tiled=True)
    return correlate(moved.reshape(-1, width), feed_slot, first, ROWS)


STEP = 8
SPAN = 16
STEPS = 8
RANGE = 14


def filter_weights(ch):
    taps = filter_taps(ch) * (0.125 / math.sqrt(ch) / 2048.0)
    half = ch // 2
    weights = np.zeros((ch, STEP, SPAN, ch))
    angle = 2.0 * math.pi * (np.arange(half + 1)[:, None] * np.arange(ch)[None, :] % ch) / ch
    sums = np.concatenate([np.cos(angle), np.sin(angle[1:half])], axis=0)
    for spectrum in range(STEP):
        for t in range(TAPS):
            weights[:, spectrum, spectrum + t] = taps[t] * sums
    weights = weights.reshape(ch * STEP, SPAN * ch)
    high = weights.astype(jnp.bfloat16)
    low = (weights - high.astype(np.float64)).astype(jnp.bfloat16)
    return np.concatenate([high, low])


def spectra_of(weights_ref, levels, gains, ch, store):
    count = levels[0].shape[1]
    half, size = ch // 2, ch * STEP
    beside = max(1, 256 // count)
    for first in range(0, STEPS, beside):
        totals = []
        for level in levels:
            slabs = [level[b * size : b * size + SPAN * ch] for b in range(first, first + beside)]
            slab = jnp.concatenate(slabs, axis=1) if beside > 1 else slabs[0]
            both = jnp.dot(weights_ref[...], slab, preferred_element_type=jnp.float32)
            totals.append(both[:size] + both[size:])
        for index in range(beside):
            lanes = slice(index * count, (index + 1) * count)
            parts = [
                [total[d * STEP : (d + 1) * STEP, lanes] for d in range(ch)] for total in totals
            ]
            for c in range(ch):
                place = min(c, ch - c)
                real, imag = parts[0][place], parts[1][place]
                if c % half:
                    sine_real, sine_imag = parts[0][half + place], parts[1][half + place]
                    if c < half:
                        real, imag = real + sine_imag, imag - sine_real
                    else:
                        real, imag = real - sine_imag, imag + sine_real
                gain_real, gain_imag = gains[c : c + 1], gains[ch + c : ch + c + 1]
                store(
                    first + index,
                    c,
                    gain_real * real - gain_imag * imag,
                    gain_real * imag + gain_imag * real,
                )


def levels_of(words):
    return [
        ((words >> 4) - 8).astype(jnp.float32).astype(jnp.bfloat16),
        ((words & 15) - 8).astype(jnp.float32).astype(jnp.bfloat16),
    ]


def own_kernel(place_ref, main_ref, next_ref, gains_ref, weights_ref, after_ref, out_ref, zero_ref, held, turned, sems):
    step = pl.program_id(0)
    slot = step % 2
    ch = out_ref.shape[0]
    zero_ref[...] = jnp.zeros_like(zero_ref)
    words = jnp.concatenate([main_ref[...], next_ref[...]], axis=0)

    def copy(index):
        return pltpu.make_async_copy(turned.at[index % 2], out_ref.at[:, index], sems.at[index % 2])

    def store(b, c, real, imag):
        held[c, b * 2 * STEP : (b + 1) * 2 * STEP, :] = jnp.concatenate([real, imag], axis=0).astype(held.dtype)

    spectra_of(weights_ref, levels_of(words), gains_ref[...], ch, store)

    @pl.when(step >= 2)
    def _():
        copy(step - 2).wait()

    for c in range(ch):
        turned[slot, c ^ place_ref[0]] = held[c].T
    copy(step).start()

    @pl.when(step == pl.num_programs(0) - 1)
    def _():
        copy(step - 1).wait()
        copy(step).wait()


def own_spectra(place, words, gains, weights, ch, spectra, after):
    count = words.shape[1]
    main = STEPS * STEP * ch
    steps = spectra // (STEPS * STEP)
    return pl.pallas_call(
        own_kernel,
        grid=(steps,),
        in_specs=[
            pl.BlockSpec(memory_space=pltpu.SMEM),
            pl.BlockSpec((main, count), lambda i: (i, 0)),
            pl.BlockSpec((STEP * ch, count), lambda i: ((i + 1) * STEPS, 0)),
            pl.BlockSpec(gains.shape, lambda i: (0, 0)),
            pl.BlockSpec(weights.shape, lambda i: (0, 0)),
            pl.BlockSpec(memory_space=pl.ANY),
        ],
        out_specs=[
            pl.BlockSpec(memory_space=pltpu.HBM),
            pl.BlockSpec((16, LANES), lambda i: (0, 0)),
        ],
        out_shape=[
            jax.ShapeDtypeStruct((ch, steps, count, 2 * STEPS * STEP), jnp.bfloat16),
            jax.ShapeDtypeStruct((16, LANES), jnp.bfloat16),
        ],
        scratch_shapes=[
            pltpu.VMEM((ch, 2 * STEPS * STEP, count), jnp.bfloat16),
            pltpu.VMEM((2, ch, count, 2 * STEPS * STEP), jnp.bfloat16),
            pltpu.SemaphoreType.DMA((2,)),
        ],
        compiler_params=pltpu.CompilerParams(vmem_limit_bytes=12 << 20),
        cost_estimate=pl.CostEstimate(
            flops=4 * spectra * ch * 2 * SPAN * ch * count,
            bytes_accessed=4 * words.size + 4 * ch * spectra * count,
            transcendentals=0,
        ),
        name="own_spectra",
    )(place, words, words, gains, weights, after)


def select_kernel(last_rows, slots_ref, words_ref, parts_ref, *outs):
    step = pl.program_id(0)
    count, rows = words_ref.shape[1], slots_ref.shape[1]
    words = words_ref[...].astype(jnp.float32).astype(jnp.bfloat16)
    place = lax.broadcasted_iota(jnp.int32, (count, rows), 0)
    choice = jnp.where(slots_ref[...] == place, 1.0, 0.0).astype(jnp.bfloat16)
    taken = jnp.dot(words, choice, preferred_element_type=jnp.float32).astype(outs[0].dtype)
    for index, out_ref in enumerate(outs):
        out_ref[...] = taken[:, index * LANES : (index + 1) * LANES]

    @pl.when(step == pl.num_programs(0) - 1)
    def _():
        extra = parts_ref.shape[0]
        gains = jnp.dot(parts_ref[...], choice, preferred_element_type=jnp.float32).astype(outs[0].dtype)
        for index, out_ref in enumerate(outs):
            out_ref[last_rows : last_rows + extra, :] = gains[:, index * LANES : (index + 1) * LANES]
            left = out_ref.shape[0] - last_rows - extra
            out_ref[last_rows + extra :, :] = jnp.zeros((left, LANES), out_ref.dtype)


def select_rows(words, gains, slots, total):
    lines, count = words.shape
    rows = slots.shape[1]
    block = total // STEPS
    parts = jnp.concatenate([gains >> 4, gains & 15], axis=0).astype(jnp.bfloat16)
    return pl.pallas_call(
        functools.partial(select_kernel, lines - (STEPS - 1) * block),
        grid=(STEPS,),
        in_specs=[
            pl.BlockSpec((1, rows), lambda i: (0, 0)),
            pl.BlockSpec((block, count), lambda i: (i, 0)),
            pl.BlockSpec(parts.shape, lambda i: (0, 0)),
        ],
        out_specs=[pl.BlockSpec((block, LANES), lambda i: (i, 0))] * (rows // LANES),
        out_shape=[jax.ShapeDtypeStruct((total, LANES), jnp.bfloat16)] * (rows // LANES),
        compiler_params=pltpu.CompilerParams(vmem_limit_bytes=8 << 20),
        name="select_rows",
    )(slots, words, parts)


def swap(value, bit):
    pairs = [(index, index ^ bit) for index in range(lax.axis_size("feed"))]
    return lax.ppermute(value, "feed", pairs)


def side(bit):
    return lax.axis_index("feed") // bit % 2


def reduce_half(value, bit):
    size = value.shape[0] // 2
    keep = lax.dynamic_slice_in_dim(value, side(bit) * size, size, 0)
    send = lax.dynamic_slice_in_dim(value, (1 - side(bit)) * size, size, 0)
    return keep + swap(send, bit)


def gather_half(value, bit, buffer):
    size = value.shape[0]
    other = swap(value, bit)
    buffer = lax.dynamic_update_slice_in_dim(buffer, value, side(bit) * size, 0)
    return lax.dynamic_update_slice_in_dim(buffer, other, (1 - side(bit)) * size, 0)


def sum_over_feed(value, work=None):
    half = reduce_half(value, 1)
    size = half.shape[0] // 2
    left, right = half[:size], half[size:]
    left_1, right_1 = reduce_half(left, 2), reduce_half(right, 4)
    left_2, right_2 = reduce_half(left_1, 4), reduce_half(right_1, 2)
    left_3, right_3 = left_2 + swap(left_2, 8), right_2 + swap(right_2, 8)
    if work is not None:
        left_3 = left_3 + work(left_2)
    left_1, right_1 = gather_half(left_3, 4, left_1), gather_half(right_3, 2, right_1)
    left, right = gather_half(left_1, 2, left), gather_half(right_1, 4, right)
    half = jnp.concatenate([left, right], axis=0)
    return half, lambda: gather_half(half, 1, value)


def code(products, out_ref, index):
    largest = jnp.maximum(jnp.max(jnp.abs(products), axis=0, keepdims=True), 2.0**-60)
    power = jnp.floor(jnp.log2(largest))
    coded = jnp.clip(jnp.round(products * jnp.exp2(RANGE - power)), -32767.0, 32767.0)
    count = products.shape[0]
    out_ref[index, :count, :] = coded.astype(jnp.int32).astype(jnp.int16)
    line = jnp.broadcast_to(power, (out_ref.shape[1] - count, power.shape[1]))
    out_ref[index, count:, :] = line.astype(jnp.int32).astype(jnp.int16)


def rows_kernel(
    place_ref, main_ref, next_ref, parts_ref, weights_ref, own_ref, *refs
):
    out_ref, mine_ref, left, own, sems = refs[-5:]
    step = pl.program_id(0)
    steps = pl.num_programs(0) // 2
    ch = left.shape[0]
    rows = main_ref.shape[1]

    def copy(k):
        return pltpu.make_async_copy(own_ref.at[k], own.at[k], sems.at[k])

    @pl.when(step == 0)
    def _():
        for k in range(ch):
            copy(k).start()

    @pl.when(step < steps)
    def _():
        words = jnp.concatenate([main_ref[...], next_ref[...]], axis=0).astype(jnp.float32).astype(jnp.int32)
        parts = parts_ref[...].astype(jnp.float32)
        gains = parts[: 2 * ch] * 16.0 + parts[2 * ch :]

        def store(b, c, real, imag):
            spot = pl.ds(pl.multiple_of(step * (2 * STEPS * STEP), 2 * STEPS * STEP) + b * 2 * STEP, 2 * STEP)
            left[c, spot, :rows] = jnp.concatenate([real, imag], axis=0).astype(left.dtype)
            left[c, spot, rows:] = jnp.concatenate([imag, -real], axis=0).astype(left.dtype)

        spectra_of(weights_ref, levels_of(words), gains, ch, store)

    @pl.when(step >= steps)
    def _():
        each = out_ref.shape[0]
        for index in range(each):
            k = (step - steps) * each + index
            copy(k).wait()
            spectra = jnp.concatenate([own[k, part] for part in range(own.shape[1])], axis=1)
            code(jnp.dot(spectra, left[k ^ place_ref[0]], preferred_element_type=jnp.float32), out_ref, index)

    @pl.when(step == 2 * steps - 1)
    def _():
        mine_ref[...] = left[place_ref[0]]


def row_products(place, words, parts, own, weights, after):
    ch, steps, count, width = own.shape
    rows = words.shape[1]
    main = STEPS * STEP * ch
    each = ch // steps
    return pl.pallas_call(
        rows_kernel,
        grid=(2 * steps,),
        in_specs=[
            pl.BlockSpec(memory_space=pltpu.SMEM),
            pl.BlockSpec((main, rows), lambda i: (jnp.minimum(i, steps - 1), 0)),
            pl.BlockSpec((STEP * ch, rows), lambda i: ((jnp.minimum(i, steps - 1) + 1) * STEPS, 0)),
            pl.BlockSpec(parts.shape, lambda i: (0, 0)),
            pl.BlockSpec(weights.shape, lambda i: (0, 0)),
            pl.BlockSpec(memory_space=pltpu.HBM),
        ]
        + [pl.BlockSpec(memory_space=pl.ANY)] * len(after),
        out_specs=[
            pl.BlockSpec((each, count + 16, 2 * rows), lambda i: (jnp.maximum(i - steps, 0), 0, 0)),
            pl.BlockSpec((steps * width, 2 * rows), lambda i: (0, 0)),
        ],
        out_shape=[
            jax.ShapeDtypeStruct((ch, count + 16, 2 * rows), jnp.int16),
            jax.ShapeDtypeStruct((steps * width, 2 * rows), jnp.bfloat16),
        ],
        scratch_shapes=[
            pltpu.VMEM((ch, steps * width, 2 * rows), jnp.bfloat16),
            pltpu.VMEM(own.shape, jnp.bfloat16),
            pltpu.SemaphoreType.DMA((ch,)),
        ],
        compiler_params=pltpu.CompilerParams(vmem_limit_bytes=24 << 20),
        cost_estimate=pl.CostEstimate(
            flops=4 * steps * width * ch * SPAN * ch * rows + 4 * ch * steps * width * rows * count,
            bytes_accessed=2 * words.size + 2 * own.size + 4 * ch * rows * count,
            transcendentals=0,
        ),
        name="row_products",
    )(place, words, words, parts, weights, own, *after)


def near_kernel(mine_ref, *refs):
    *spectra_refs, out_ref = refs
    for index, ref in enumerate(spectra_refs):
        spectra = jnp.concatenate([ref[part] for part in range(ref.shape[0])], axis=1)
        code(jnp.dot(spectra, mine_ref[...], preferred_element_type=jnp.float32), out_ref, index)


def near_products(spectra, mine):
    count = spectra[0].shape[1]
    return pl.pallas_call(
        near_kernel,
        out_shape=jax.ShapeDtypeStruct((len(spectra), count + 16, mine.shape[1]), jnp.int16),
        compiler_params=pltpu.CompilerParams(vmem_limit_bytes=12 << 20),
        cost_estimate=pl.CostEstimate(
            flops=2 * len(spectra) * count * mine.size, bytes_accessed=4 * spectra[0].size * len(spectra), transcendentals=0
        ),
        name="near_products",
    )(mine, *spectra)


def finish_kernel(scale, sources, slot_ref, *refs):
    coded_refs, (out_ref, products, tile, mixed) = refs[:sources], refs[-4:]
    lines, width = coded_refs[0].shape
    count = lines - 16
    pieces = width // LANES
    feeds = sources * count
    columns = 2 * (feeds // LANES)
    for source in range(sources):
        coded_ref = coded_refs[source]
        power = coded_ref[count : count + 16, :][:1].astype(jnp.float32)
        values = coded_ref[:count, :].astype(jnp.float32) * (jnp.exp2(power - RANGE) * scale)
        for piece in range(pieces):
            products[pl.ds(source * count * pieces + piece, count, stride=pieces), :] = values[
                :, piece * LANES : (piece + 1) * LANES
            ]

    together = 8 // pieces

    @pl.loop(0, feeds // LANES // together)
    def _(j):
        for part in range(together):
            for i in range(LANES):
                slot = slot_ref[(j * together + part) * LANES + i]
                tile[i * pieces : (i + 1) * pieces, :] = products[
                    pl.ds(pl.multiple_of(slot * pieces, pieces), pieces), :
                ]
            for piece in range(pieces):
                turned = tile[pl.ds(piece, LANES, stride=pieces), :].T
                mixed[pl.ds(part * pieces + piece, LANES, stride=8), :] = turned
        for row in range(LANES):
            out_ref[pl.ds(pl.multiple_of(row * columns + j * 8, 8), 8), :] = mixed[row * 8 : (row + 1) * 8, :]


def finish(coded, slots, index, pieces, scale, before):
    sources = len(coded)
    lines, width = coded[0].shape
    rows = width // 2
    feeds = sources * (lines - 16)
    columns = 2 * (feeds // LANES)
    earlier = [] if before is None else [before]
    return pl.pallas_call(
        functools.partial(finish_kernel, scale, sources),
        grid=(1,),
        in_specs=[pl.BlockSpec(memory_space=pltpu.SMEM)]
        + [pl.BlockSpec((lines, width), lambda i: (0, 0))] * sources
        + [pl.BlockSpec(memory_space=pl.ANY)] * len(earlier),
        out_specs=pl.BlockSpec((rows * columns, LANES), lambda i: (index, 0)),
        out_shape=jax.ShapeDtypeStruct((pieces * rows * columns, LANES), jnp.float32),
        scratch_shapes=[
            pltpu.VMEM((feeds * width // LANES, LANES), jnp.float32),
            pltpu.VMEM((width, LANES), jnp.float32),
            pltpu.VMEM((8 * LANES, LANES), jnp.float32),
        ],
        input_output_aliases={1 + sources: 0} if earlier else {},
        compiler_params=pltpu.CompilerParams(vmem_limit_bytes=22 << 20),
        name="finish",
    )(slots, *coded, *earlier)


def across(value, k, where):
    pairs = [(index, index ^ k) for index in range(lax.axis_size("feed")) if index // 4 in where]
    return lax.ppermute(value, "feed", pairs)


def through_rows(samples, gains, feed_slot):
    count, ch, frames = samples.shape
    spectra = frames - TAPS + 1
    pieces = ROWS // LANES
    lines = frames * ch
    unit = 16 * STEPS * 2
    total = pl.cdiv(lines + 4 * ch, unit) * unit
    words = jnp.transpose(samples, (2, 1, 0)).reshape(lines, count)
    scales = gains.reshape(2 * ch, count)
    weights = jnp.asarray(filter_weights(ch))
    me = lax.axis_index("feed")
    place = me.reshape(1)
    slots = (feed_slot[:ROWS] - me * count).reshape(1, ROWS)
    picked = select_rows(words, scales, slots, total)
    held = []

    def work(after):
        own, zero = own_spectra(place, words, scales.astype(jnp.float32), weights, ch, spectra, after)
        held.append(own)
        return zero[0, 0]

    sums = [sum_over_feed(value, None if index else work) for index, value in enumerate(picked)]
    own = held[0]
    middle, devices = (1, 2), lax.axis_size("feed")
    met = range(12, devices)
    in_middle = (me // 4 == middle[0]) | (me // 4 == middle[1])
    spectra_met = [across(own[k], k, middle) for k in met]
    places = (feed_slot // count ^ me) * count + feed_slot % count
    out = None
    for index in range(pieces):
        rows = sums[index][1]()
        parts = rows[lines : lines + 4 * ch]
        after = [sums[-1][0]] + spectra_met[:2]
        coded, mine = row_products(place, rows, parts, own, weights, after)
        near = near_products(spectra_met, mine)
        moved = [coded[0]]
        for k in range(1, devices):
            if k in met:
                other = across(coded[k], k, (0, 3))
                moved.append(jnp.where(in_middle, near[k - met[0]], other))
            else:
                moved.append(across(coded[k], k, range(devices // 4)))
        out = finish(moved, places, index, pieces, 1.0 / spectra, out)
    feeds = feed_slot.shape[0]
    out = out.reshape(ROWS, feeds // LANES, 2, LANES)
    return jnp.transpose(out, (0, 2, 1, 3)).reshape(ROWS, 2, feeds)


def body(samples, gains, feed_slot):
    count, ch, frames = samples.shape
    spectra = frames - TAPS + 1
    even = count % LANES == 0 and spectra % (STEPS * STEP) == 0 and ch % STEPS == 0
    if lax.axis_size("feed") == ch == 16 and even:
        return through_rows(samples, gains, feed_slot)
    return through_spectra(samples, gains, feed_slot)


def solution(mesh):
    return jax.shard_map(
        body,
        mesh=mesh,
        in_specs=(P(("band", "feed"), None, None), P(None, "band", "feed"), P()),
        out_specs=P(("band", "feed"), None, None),
        check_vma=False,
    )
```

```python
import functools
import math

import jax
import jax.numpy as jnp
import numpy as np
from jax import lax
from jax.experimental import pallas as pl
from jax.experimental.pallas import tpu as pltpu
from jax.sharding import PartitionSpec as P

TAPS = 8
ROWS = 256
LANES = 128


def filter_taps(ch):
    length = TAPS * ch
    place = np.arange(length, dtype=np.float64)
    window = 0.5 - 0.5 * np.cos(2.0 * math.pi * place / (length - 1))
    return (np.sinc((place - 0.5 * (length - 1)) / ch) * window).reshape(TAPS, ch)


def twiddle(value, turn):
    real, imag = value
    if turn == 0:
        return value
    if turn == 0.25:
        return imag, -real
    half = math.sqrt(0.5)
    if turn == 0.125:
        return half * (real + imag), half * (imag - real)
    if turn == 0.375:
        return half * (imag - real), -half * (real + imag)
    c, s = math.cos(2.0 * math.pi * turn), math.sin(2.0 * math.pi * turn)
    return c * real + s * imag, c * imag - s * real


def fft(values):
    count = len(values)
    if count == 1:
        return values
    even, odd = fft(values[0::2]), fft(values[1::2])
    low, high = [], []
    for index in range(count // 2):
        real, imag = twiddle(odd[index], index / count)
        low.append((even[index][0] + real, even[index][1] + imag))
        high.append((even[index][0] - real, even[index][1] - imag))
    return low + high


def channel_kernel(taps, *refs):
    *samples_refs, gains_ref, out_ref, filtered = refs
    ch, block, width = out_ref.shape
    spectra = width // 2
    padded = len(samples_refs) * LANES
    for k in range(ch):
        words = jnp.concatenate(
            [ref[pl.ds(k, block, stride=ch), :] for ref in samples_refs], axis=1
        )
        levels = ((words >> 4) - 8, (words & 15) - 8)
        for part in range(2):
            value = levels[part].astype(jnp.float32)
            shifted = [value] + [pltpu.roll(value, padded - t, 1) for t in range(1, TAPS // 2)]
            near = float(taps[0, k]) * shifted[0]
            far = float(taps[TAPS // 2, k]) * shifted[0]
            for t in range(1, TAPS // 2):
                near = near + float(taps[t, k]) * shifted[t]
                far = far + float(taps[t + TAPS // 2, k]) * shifted[t]
            total = near + pltpu.roll(far, padded - TAPS // 2, 1)
            filtered[2 * k + part] = total[:, :spectra]
    for row in range(0, block, 8):
        gains = gains_ref[row : row + 8, :]
        for lane in range(0, spectra, LANES):
            spot = (slice(row, row + 8), slice(lane, lane + LANES))
            values = [(filtered[2 * k][spot], filtered[2 * k + 1][spot]) for k in range(ch)]
            for c, (real, imag) in enumerate(fft(values)):
                gain_real = gains[:, c : c + 1]
                gain_imag = gains[:, ch + c : ch + c + 1]
                out_ref[c, row : row + 8, lane : lane + LANES] = (
                    gain_real * real - gain_imag * imag
                ).astype(out_ref.dtype)
                out_ref[c, row : row + 8, spectra + lane : spectra + lane + LANES] = (
                    gain_real * imag + gain_imag * real
                ).astype(out_ref.dtype)


def channelize(samples, gains):
    count, ch, frames = samples.shape
    spectra = frames - TAPS + 1
    block = 16
    pieces = pl.cdiv(frames, LANES)
    scale = 0.125 / math.sqrt(ch) / 2048.0
    taps = (filter_taps(ch) * scale).astype(np.float32)
    return pl.pallas_call(
        functools.partial(channel_kernel, taps),
        grid=(count // block,),
        in_specs=[
            pl.BlockSpec((block * ch, LANES), functools.partial(lambda piece, i: (i, piece), piece))
            for piece in range(pieces)
        ]
        + [pl.BlockSpec((block, 2 * ch), lambda i: (i, 0))],
        out_specs=pl.BlockSpec((ch, block, 2 * spectra), lambda i: (0, i, 0)),
        out_shape=jax.ShapeDtypeStruct((ch, count, 2 * spectra), jnp.bfloat16),
        scratch_shapes=[pltpu.VMEM((2 * ch, block, spectra), jnp.float32)],
        compiler_params=pltpu.CompilerParams(vmem_limit_bytes=32 << 20),
        name="channelize",
    )(*[samples.reshape(count * ch, frames)] * pieces, gains)


def correlate_kernel(scale, slot_ref, row_ref, data_ref, out_ref, products, tile):
    feeds, width = data_ref.shape
    spectra = width // 2
    rows = row_ref.shape[0]
    pieces = 2 * rows // LANES
    step = 256
    picked = jnp.zeros((rows, width), jnp.float32)
    for first in range(0, feeds, 512):
        place = lax.broadcasted_iota(jnp.int32, (rows, 512), 1) + first
        choice = jnp.where(row_ref[...] == place, 1.0, 0.0).astype(jnp.bfloat16)
        picked = picked + jnp.dot(
            choice, data_ref[first : first + 512, :], preferred_element_type=jnp.float32
        )
    left = jnp.concatenate(
        [
            picked,
            jnp.concatenate([picked[:, spectra:], -picked[:, :spectra]], axis=1),
        ],
        axis=0,
    ).astype(jnp.bfloat16)

    @pl.loop(0, feeds // step)
    def _(i):
        first = pl.multiple_of(i * step, step)
        result = lax.dot_general(
            data_ref[pl.ds(first, step), :],
            left,
            (((1,), (1,)), ((), ())),
            preferred_element_type=jnp.float32,
        )
        for piece in range(pieces):
            products[pl.ds(first * pieces + piece, step, stride=pieces), :] = (
                result[:, piece * LANES : (piece + 1) * LANES] * scale
            )

    lines = 2 * (feeds // LANES)

    @pl.loop(0, feeds // LANES)
    def _(j):
        @pl.loop(0, LANES, unroll=16)
        def _(i):
            slot = slot_ref[j * LANES + i]
            tile[pl.ds(pl.multiple_of(i * pieces, pieces), pieces), :] = products[
                pl.ds(pl.multiple_of(slot * pieces, pieces), pieces), :
            ]

        for piece in range(pieces):
            part, first = divmod(piece * LANES, rows)
            turned = tile[pl.ds(piece, LANES, stride=pieces), :].T
            out_ref[pl.ds(first * lines + 2 * j + part, LANES, stride=lines), :] = turned


def correlate(data, feed_slot, first, rows):
    feeds, width = data.shape
    row_slots = lax.dynamic_slice_in_dim(feed_slot, first, rows, 0).reshape(rows, 1)
    lines = 2 * (feeds // LANES)
    out = pl.pallas_call(
        functools.partial(correlate_kernel, 2.0 / width),
        in_specs=[
            pl.BlockSpec(memory_space=pltpu.SMEM),
            pl.BlockSpec(memory_space=pltpu.VMEM),
            pl.BlockSpec(memory_space=pltpu.VMEM),
        ],
        out_specs=pl.BlockSpec(memory_space=pltpu.VMEM),
        out_shape=jax.ShapeDtypeStruct((rows * lines, LANES), jnp.float32),
        scratch_shapes=[
            pltpu.VMEM((feeds * 2 * rows // LANES, LANES), jnp.float32),
            pltpu.VMEM((LANES * 2 * rows // LANES, LANES), jnp.float32),
        ],
        compiler_params=pltpu.CompilerParams(vmem_limit_bytes=48 << 20),
        name="correlate",
    )(feed_slot, row_slots, data)
    out = out.reshape(rows, feeds // LANES, 2, LANES)
    return jnp.transpose(out, (0, 2, 1, 3)).reshape(rows, 2, feeds)


def through_spectra(samples, gains, feed_slot):
    count, ch, _ = samples.shape
    groups = lax.axis_size("feed") // ch
    first = lax.axis_index("feed") % groups * ROWS
    scales = jnp.transpose(gains, (2, 0, 1)).reshape(count, 2 * ch).astype(jnp.float32)
    spectra = channelize(samples, scales)
    width = spectra.shape[2]
    outgoing = jnp.broadcast_to(spectra[:, None], (ch, groups, count, width))
    outgoing = outgoing.reshape(ch * groups, count, width)
    moved = lax.all_to_all(outgoing, "feed", split_axis=0, concat_axis=0, tiled=True)
    return correlate(moved.reshape(-1, width), feed_slot, first, ROWS)


STEP = 8
SPAN = 16
STEPS = 8
RANGE = 14


def filter_weights(ch):
    taps = filter_taps(ch) * (0.125 / math.sqrt(ch) / 2048.0)
    half = ch // 2
    weights = np.zeros((ch, STEP, SPAN, ch))
    angle = 2.0 * math.pi * (np.arange(half + 1)[:, None] * np.arange(ch)[None, :] % ch) / ch
    sums = np.concatenate([np.cos(angle), np.sin(angle[1:half])], axis=0)
    for spectrum in range(STEP):
        for t in range(TAPS):
            weights[:, spectrum, spectrum + t] = taps[t] * sums
    weights = weights.reshape(ch * STEP, SPAN * ch)
    high = weights.astype(jnp.bfloat16)
    low = (weights - high.astype(np.float64)).astype(jnp.bfloat16)
    return np.concatenate([high, low])


def spectra_of(weights_ref, levels, gains, ch, store):
    count = levels[0].shape[1]
    half, size = ch // 2, ch * STEP
    beside = max(1, 256 // count)
    for first in range(0, STEPS, beside):
        totals = []
        for level in levels:
            slabs = [level[b * size : b * size + SPAN * ch] for b in range(first, first + beside)]
            slab = jnp.concatenate(slabs, axis=1) if beside > 1 else slabs[0]
            both = jnp.dot(weights_ref[...], slab, preferred_element_type=jnp.float32)
            totals.append(both[:size] + both[size:])
        for index in range(beside):
            lanes = slice(index * count, (index + 1) * count)
            parts = [
                [total[d * STEP : (d + 1) * STEP, lanes] for d in range(ch)] for total in totals
            ]
            for c in range(ch):
                place = min(c, ch - c)
                real, imag = parts[0][place], parts[1][place]
                if c % half:
                    sine_real, sine_imag = parts[0][half + place], parts[1][half + place]
                    if c < half:
                        real, imag = real + sine_imag, imag - sine_real
                    else:
                        real, imag = real - sine_imag, imag + sine_real
                gain_real, gain_imag = gains[c : c + 1], gains[ch + c : ch + c + 1]
                store(
                    first + index,
                    c,
                    gain_real * real - gain_imag * imag,
                    gain_real * imag + gain_imag * real,
                )


def levels_of(words):
    return [
        ((words >> 4) - 8).astype(jnp.float32).astype(jnp.bfloat16),
        ((words & 15) - 8).astype(jnp.float32).astype(jnp.bfloat16),
    ]


def own_kernel(place_ref, main_ref, next_ref, gains_ref, weights_ref, after_ref, out_ref, zero_ref, held, turned, sems):
    step = pl.program_id(0)
    slot = step % 2
    ch = out_ref.shape[0]
    zero_ref[...] = jnp.zeros_like(zero_ref)
    words = jnp.concatenate([main_ref[...], next_ref[...]], axis=0)

    def copy(index):
        return pltpu.make_async_copy(turned.at[index % 2], out_ref.at[:, index], sems.at[index % 2])

    def store(b, c, real, imag):
        held[c, b * 2 * STEP : (b + 1) * 2 * STEP, :] = jnp.concatenate([real, imag], axis=0).astype(held.dtype)

    spectra_of(weights_ref, levels_of(words), gains_ref[...], ch, store)

    @pl.when(step >= 2)
    def _():
        copy(step - 2).wait()

    for c in range(ch):
        turned[slot, c ^ place_ref[0]] = held[c].T
    copy(step).start()

    @pl.when(step == pl.num_programs(0) - 1)
    def _():
        copy(step - 1).wait()
        copy(step).wait()


def own_spectra(place, words, gains, weights, ch, spectra, after):
    count = words.shape[1]
    main = STEPS * STEP * ch
    steps = spectra // (STEPS * STEP)
    return pl.pallas_call(
        own_kernel,
        grid=(steps,),
        in_specs=[
            pl.BlockSpec(memory_space=pltpu.SMEM),
            pl.BlockSpec((main, count), lambda i: (i, 0)),
            pl.BlockSpec((STEP * ch, count), lambda i: ((i + 1) * STEPS, 0)),
            pl.BlockSpec(gains.shape, lambda i: (0, 0)),
            pl.BlockSpec(weights.shape, lambda i: (0, 0)),
            pl.BlockSpec(memory_space=pl.ANY),
        ],
        out_specs=[
            pl.BlockSpec(memory_space=pltpu.HBM),
            pl.BlockSpec((16, LANES), lambda i: (0, 0)),
        ],
        out_shape=[
            jax.ShapeDtypeStruct((ch, steps, count, 2 * STEPS * STEP), jnp.bfloat16),
            jax.ShapeDtypeStruct((16, LANES), jnp.bfloat16),
        ],
        scratch_shapes=[
            pltpu.VMEM((ch, 2 * STEPS * STEP, count), jnp.bfloat16),
            pltpu.VMEM((2, ch, count, 2 * STEPS * STEP), jnp.bfloat16),
            pltpu.SemaphoreType.DMA((2,)),
        ],
        compiler_params=pltpu.CompilerParams(vmem_limit_bytes=12 << 20),
        cost_estimate=pl.CostEstimate(
            flops=4 * spectra * ch * 2 * SPAN * ch * count,
            bytes_accessed=4 * words.size + 4 * ch * spectra * count,
            transcendentals=0,
        ),
        name="own_spectra",
    )(place, words, words, gains, weights, after)


def select_kernel(last_rows, slots_ref, words_ref, parts_ref, *outs):
    step = pl.program_id(0)
    count, rows = words_ref.shape[1], slots_ref.shape[1]
    words = words_ref[...].astype(jnp.float32).astype(jnp.bfloat16)
    place = lax.broadcasted_iota(jnp.int32, (count, rows), 0)
    choice = jnp.where(slots_ref[...] == place, 1.0, 0.0).astype(jnp.bfloat16)
    taken = jnp.dot(words, choice, preferred_element_type=jnp.float32).astype(outs[0].dtype)
    for index, out_ref in enumerate(outs):
        out_ref[...] = taken[:, index * LANES : (index + 1) * LANES]

    @pl.when(step == pl.num_programs(0) - 1)
    def _():
        extra = parts_ref.shape[0]
        gains = jnp.dot(parts_ref[...], choice, preferred_element_type=jnp.float32).astype(outs[0].dtype)
        for index, out_ref in enumerate(outs):
            out_ref[last_rows : last_rows + extra, :] = gains[:, index * LANES : (index + 1) * LANES]
            left = out_ref.shape[0] - last_rows - extra
            out_ref[last_rows + extra :, :] = jnp.zeros((left, LANES), out_ref.dtype)


def select_rows(words, gains, slots, total):
    lines, count = words.shape
    rows = slots.shape[1]
    block = total // STEPS
    parts = jnp.concatenate([gains >> 4, gains & 15], axis=0).astype(jnp.bfloat16)
    return pl.pallas_call(
        functools.partial(select_kernel, lines - (STEPS - 1) * block),
        grid=(STEPS,),
        in_specs=[
            pl.BlockSpec((1, rows), lambda i: (0, 0)),
            pl.BlockSpec((block, count), lambda i: (i, 0)),
            pl.BlockSpec(parts.shape, lambda i: (0, 0)),
        ],
        out_specs=[pl.BlockSpec((block, LANES), lambda i: (i, 0))] * (rows // LANES),
        out_shape=[jax.ShapeDtypeStruct((total, LANES), jnp.bfloat16)] * (rows // LANES),
        compiler_params=pltpu.CompilerParams(vmem_limit_bytes=8 << 20),
        name="select_rows",
    )(slots, words, parts)


def swap(value, bit):
    pairs = [(index, index ^ bit) for index in range(lax.axis_size("feed"))]
    return lax.ppermute(value, "feed", pairs)


def side(bit):
    return lax.axis_index("feed") // bit % 2


def reduce_half(value, bit):
    size = value.shape[0] // 2
    keep = lax.dynamic_slice_in_dim(value, side(bit) * size, size, 0)
    send = lax.dynamic_slice_in_dim(value, (1 - side(bit)) * size, size, 0)
    return keep + swap(send, bit)


def gather_half(value, bit, buffer):
    size = value.shape[0]
    other = swap(value, bit)
    buffer = lax.dynamic_update_slice_in_dim(buffer, value, side(bit) * size, 0)
    return lax.dynamic_update_slice_in_dim(buffer, other, (1 - side(bit)) * size, 0)


def sum_over_feed(value, work=None):
    half = reduce_half(value, 1)
    size = half.shape[0] // 2
    left, right = half[:size], half[size:]
    left_1, right_1 = reduce_half(left, 2), reduce_half(right, 4)
    left_2, right_2 = reduce_half(left_1, 4), reduce_half(right_1, 2)
    left_3, right_3 = left_2 + swap(left_2, 8), right_2 + swap(right_2, 8)
    if work is not None:
        left_3 = left_3 + work(left_2)
    left_1, right_1 = gather_half(left_3, 4, left_1), gather_half(right_3, 2, right_1)
    left, right = gather_half(left_1, 2, left), gather_half(right_1, 4, right)
    half = jnp.concatenate([left, right], axis=0)
    return half, lambda: gather_half(half, 1, value)


def code(products, out_ref, index):
    largest = jnp.maximum(jnp.max(jnp.abs(products), axis=0, keepdims=True), 2.0**-60)
    power = jnp.floor(jnp.log2(largest))
    coded = jnp.clip(jnp.round(products * jnp.exp2(RANGE - power)), -32767.0, 32767.0)
    count = products.shape[0]
    out_ref[index, :count, :] = coded.astype(jnp.int32).astype(jnp.int16)
    line = jnp.broadcast_to(power, (out_ref.shape[1] - count, power.shape[1]))
    out_ref[index, count:, :] = line.astype(jnp.int32).astype(jnp.int16)


def rows_kernel(
    place_ref, main_ref, next_ref, parts_ref, weights_ref, own_ref, *refs
):
    out_ref, mine_ref, left, own, sems = refs[-5:]
    step = pl.program_id(0)
    steps = pl.num_programs(0) // 2
    ch = left.shape[0]
    rows = main_ref.shape[1]

    def copy(k):
        return pltpu.make_async_copy(own_ref.at[k], own.at[k], sems.at[k])

    @pl.when(step == 0)
    def _():
        for k in range(ch):
            copy(k).start()

    @pl.when(step < steps)
    def _():
        words = jnp.concatenate([main_ref[...], next_ref[...]], axis=0).astype(jnp.float32).astype(jnp.int32)
        parts = parts_ref[...].astype(jnp.float32)
        gains = parts[: 2 * ch] * 16.0 + parts[2 * ch :]

        def store(b, c, real, imag):
            spot = pl.ds(pl.multiple_of(step * (2 * STEPS * STEP), 2 * STEPS * STEP) + b * 2 * STEP, 2 * STEP)
            left[c, spot, :rows] = jnp.concatenate([real, imag], axis=0).astype(left.dtype)
            left[c, spot, rows:] = jnp.concatenate([imag, -real], axis=0).astype(left.dtype)

        spectra_of(weights_ref, levels_of(words), gains, ch, store)

    @pl.when(step >= steps)
    def _():
        each = out_ref.shape[0]
        for index in range(each):
            k = (step - steps) * each + index
            copy(k).wait()
            spectra = jnp.concatenate([own[k, part] for part in range(own.shape[1])], axis=1)
            code(jnp.dot(spectra, left[k ^ place_ref[0]], preferred_element_type=jnp.float32), out_ref, index)

    @pl.when(step == 2 * steps - 1)
    def _():
        mine_ref[...] = left[place_ref[0]]


def row_products(place, words, parts, own, weights, after):
    ch, steps, count, width = own.shape
    rows = words.shape[1]
    main = STEPS * STEP * ch
    each = ch // steps
    return pl.pallas_call(
        rows_kernel,
        grid=(2 * steps,),
        in_specs=[
            pl.BlockSpec(memory_space=pltpu.SMEM),
            pl.BlockSpec((main, rows), lambda i: (jnp.minimum(i, steps - 1), 0)),
            pl.BlockSpec((STEP * ch, rows), lambda i: ((jnp.minimum(i, steps - 1) + 1) * STEPS, 0)),
            pl.BlockSpec(parts.shape, lambda i: (0, 0)),
            pl.BlockSpec(weights.shape, lambda i: (0, 0)),
            pl.BlockSpec(memory_space=pltpu.HBM),
        ]
        + [pl.BlockSpec(memory_space=pl.ANY)] * len(after),
        out_specs=[
            pl.BlockSpec((each, count + 16, 2 * rows), lambda i: (jnp.maximum(i - steps, 0), 0, 0)),
            pl.BlockSpec((steps * width, 2 * rows), lambda i: (0, 0)),
        ],
        out_shape=[
            jax.ShapeDtypeStruct((ch, count + 16, 2 * rows), jnp.int16),
            jax.ShapeDtypeStruct((steps * width, 2 * rows), jnp.bfloat16),
        ],
        scratch_shapes=[
            pltpu.VMEM((ch, steps * width, 2 * rows), jnp.bfloat16),
            pltpu.VMEM(own.shape, jnp.bfloat16),
            pltpu.SemaphoreType.DMA((ch,)),
        ],
        compiler_params=pltpu.CompilerParams(vmem_limit_bytes=24 << 20),
        cost_estimate=pl.CostEstimate(
            flops=4 * steps * width * ch * SPAN * ch * rows + 4 * ch * steps * width * rows * count,
            bytes_accessed=2 * words.size + 2 * own.size + 4 * ch * rows * count,
            transcendentals=0,
        ),
        name="row_products",
    )(place, words, words, parts, weights, own, *after)


def near_kernel(mine_ref, *refs):
    *spectra_refs, out_ref = refs
    for index, ref in enumerate(spectra_refs):
        spectra = jnp.concatenate([ref[part] for part in range(ref.shape[0])], axis=1)
        code(jnp.dot(spectra, mine_ref[...], preferred_element_type=jnp.float32), out_ref, index)


def near_products(spectra, mine):
    count = spectra[0].shape[1]
    return pl.pallas_call(
        near_kernel,
        out_shape=jax.ShapeDtypeStruct((len(spectra), count + 16, mine.shape[1]), jnp.int16),
        compiler_params=pltpu.CompilerParams(vmem_limit_bytes=12 << 20),
        cost_estimate=pl.CostEstimate(
            flops=2 * len(spectra) * count * mine.size, bytes_accessed=4 * spectra[0].size * len(spectra), transcendentals=0
        ),
        name="near_products",
    )(mine, *spectra)


def finish_kernel(scale, sources, slot_ref, *refs):
    coded_refs, (out_ref, products, tile, mixed) = refs[:sources], refs[-4:]
    lines, width = coded_refs[0].shape
    count = lines - 16
    pieces = width // LANES
    feeds = sources * count
    columns = 2 * (feeds // LANES)
    for source in range(sources):
        coded_ref = coded_refs[source]
        power = coded_ref[count : count + 16, :][:1].astype(jnp.float32)
        values = coded_ref[:count, :].astype(jnp.float32) * (jnp.exp2(power - RANGE) * scale)
        for piece in range(pieces):
            products[pl.ds(source * count * pieces + piece, count, stride=pieces), :] = values[
                :, piece * LANES : (piece + 1) * LANES
            ]

    together = 8 // pieces

    @pl.loop(0, feeds // LANES // together)
    def _(j):
        for part in range(together):
            for i in range(LANES):
                slot = slot_ref[(j * together + part) * LANES + i]
                tile[i * pieces : (i + 1) * pieces, :] = products[
                    pl.ds(pl.multiple_of(slot * pieces, pieces), pieces), :
                ]
            for piece in range(pieces):
                turned = tile[pl.ds(piece, LANES, stride=pieces), :].T
                mixed[pl.ds(part * pieces + piece, LANES, stride=8), :] = turned
        for row in range(LANES):
            out_ref[pl.ds(pl.multiple_of(row * columns + j * 8, 8), 8), :] = mixed[row * 8 : (row + 1) * 8, :]


def finish(coded, slots, index, pieces, scale, before):
    sources = len(coded)
    lines, width = coded[0].shape
    rows = width // 2
    feeds = sources * (lines - 16)
    columns = 2 * (feeds // LANES)
    earlier = [] if before is None else [before]
    return pl.pallas_call(
        functools.partial(finish_kernel, scale, sources),
        grid=(1,),
        in_specs=[pl.BlockSpec(memory_space=pltpu.SMEM)]
        + [pl.BlockSpec((lines, width), lambda i: (0, 0))] * sources
        + [pl.BlockSpec(memory_space=pl.ANY)] * len(earlier),
        out_specs=pl.BlockSpec((rows * columns, LANES), lambda i: (index, 0)),
        out_shape=jax.ShapeDtypeStruct((pieces * rows * columns, LANES), jnp.float32),
        scratch_shapes=[
            pltpu.VMEM((feeds * width // LANES, LANES), jnp.float32),
            pltpu.VMEM((width, LANES), jnp.float32),
            pltpu.VMEM((8 * LANES, LANES), jnp.float32),
        ],
        input_output_aliases={1 + sources: 0} if earlier else {},
        compiler_params=pltpu.CompilerParams(vmem_limit_bytes=22 << 20),
        name="finish",
    )(slots, *coded, *earlier)


def across(value, k, where):
    pairs = [(index, index ^ k) for index in range(lax.axis_size("feed")) if index // 4 in where]
    return lax.ppermute(value, "feed", pairs)


def through_rows(samples, gains, feed_slot):
    count, ch, frames = samples.shape
    spectra = frames - TAPS + 1
    pieces = ROWS // LANES
    lines = frames * ch
    unit = 16 * STEPS * 2
    total = pl.cdiv(lines + 4 * ch, unit) * unit
    words = jnp.transpose(samples, (2, 1, 0)).reshape(lines, count)
    scales = gains.reshape(2 * ch, count)
    weights = jnp.asarray(filter_weights(ch))
    me = lax.axis_index("feed")
    place = me.reshape(1)
    slots = (feed_slot[:ROWS] - me * count).reshape(1, ROWS)
    picked = select_rows(words, scales, slots, total)
    held = []

    def work(after):
        own, zero = own_spectra(place, words, scales.astype(jnp.float32), weights, ch, spectra, after)
        held.append(own)
        return zero[0, 0]

    sums = [sum_over_feed(value, None if index else work) for index, value in enumerate(picked)]
    own = held[0]
    middle, devices = (1, 2), lax.axis_size("feed")
    met = range(devices, devices)
    in_middle = (me // 4 == middle[0]) | (me // 4 == middle[1])
    spectra_met = [across(own[k], k, middle) for k in met]
    places = (feed_slot // count ^ me) * count + feed_slot % count
    out = None
    for index in range(pieces):
        rows = sums[index][1]()
        parts = rows[lines : lines + 4 * ch]
        after = [sums[-1][0]] + spectra_met[:2]
        coded, mine = row_products(place, rows, parts, own, weights, after)
        near = near_products(spectra_met, mine) if spectra_met else None
        moved = [coded[0]]
        for k in range(1, devices):
            if k in met:
                other = across(coded[k], k, (0, 3))
                moved.append(jnp.where(in_middle, near[k - met[0]], other))
            else:
                moved.append(across(coded[k], k, range(devices // 4)))
        out = finish(moved, places, index, pieces, 1.0 / spectra, out)
    feeds = feed_slot.shape[0]
    out = out.reshape(ROWS, feeds // LANES, 2, LANES)
    return jnp.transpose(out, (0, 2, 1, 3)).reshape(ROWS, 2, feeds)


def body(samples, gains, feed_slot):
    count, ch, frames = samples.shape
    spectra = frames - TAPS + 1
    even = count % LANES == 0 and spectra % (STEPS * STEP) == 0 and ch % STEPS == 0
    if lax.axis_size("feed") == ch == 16 and even:
        return through_rows(samples, gains, feed_slot)
    return through_spectra(samples, gains, feed_slot)


def solution(mesh):
    return jax.shard_map(
        body,
        mesh=mesh,
        in_specs=(P(("band", "feed"), None, None), P(None, "band", "feed"), P()),
        out_specs=P(("band", "feed"), None, None),
        check_vma=False,
    )
```

```python
import functools
import math

import jax
import jax.numpy as jnp
import numpy as np
from jax import lax
from jax.experimental import pallas as pl
from jax.experimental.pallas import tpu as pltpu
from jax.sharding import PartitionSpec as P

TAPS = 8
ROWS = 256
LANES = 128


def filter_taps(ch):
    length = TAPS * ch
    place = np.arange(length, dtype=np.float64)
    window = 0.5 - 0.5 * np.cos(2.0 * math.pi * place / (length - 1))
    return (np.sinc((place - 0.5 * (length - 1)) / ch) * window).reshape(TAPS, ch)


def twiddle(value, turn):
    real, imag = value
    if turn == 0:
        return value
    if turn == 0.25:
        return imag, -real
    half = math.sqrt(0.5)
    if turn == 0.125:
        return half * (real + imag), half * (imag - real)
    if turn == 0.375:
        return half * (imag - real), -half * (real + imag)
    c, s = math.cos(2.0 * math.pi * turn), math.sin(2.0 * math.pi * turn)
    return c * real + s * imag, c * imag - s * real


def fft(values):
    count = len(values)
    if count == 1:
        return values
    even, odd = fft(values[0::2]), fft(values[1::2])
    low, high = [], []
    for index in range(count // 2):
        real, imag = twiddle(odd[index], index / count)
        low.append((even[index][0] + real, even[index][1] + imag))
        high.append((even[index][0] - real, even[index][1] - imag))
    return low + high


def channel_kernel(taps, *refs):
    *samples_refs, gains_ref, out_ref, filtered = refs
    ch, block, width = out_ref.shape
    spectra = width // 2
    padded = len(samples_refs) * LANES
    for k in range(ch):
        words = jnp.concatenate(
            [ref[pl.ds(k, block, stride=ch), :] for ref in samples_refs], axis=1
        )
        levels = ((words >> 4) - 8, (words & 15) - 8)
        for part in range(2):
            value = levels[part].astype(jnp.float32)
            shifted = [value] + [pltpu.roll(value, padded - t, 1) for t in range(1, TAPS // 2)]
            near = float(taps[0, k]) * shifted[0]
            far = float(taps[TAPS // 2, k]) * shifted[0]
            for t in range(1, TAPS // 2):
                near = near + float(taps[t, k]) * shifted[t]
                far = far + float(taps[t + TAPS // 2, k]) * shifted[t]
            total = near + pltpu.roll(far, padded - TAPS // 2, 1)
            filtered[2 * k + part] = total[:, :spectra]
    for row in range(0, block, 8):
        gains = gains_ref[row : row + 8, :]
        for lane in range(0, spectra, LANES):
            spot = (slice(row, row + 8), slice(lane, lane + LANES))
            values = [(filtered[2 * k][spot], filtered[2 * k + 1][spot]) for k in range(ch)]
            for c, (real, imag) in enumerate(fft(values)):
                gain_real = gains[:, c : c + 1]
                gain_imag = gains[:, ch + c : ch + c + 1]
                out_ref[c, row : row + 8, lane : lane + LANES] = (
                    gain_real * real - gain_imag * imag
                ).astype(out_ref.dtype)
                out_ref[c, row : row + 8, spectra + lane : spectra + lane + LANES] = (
                    gain_real * imag + gain_imag * real
                ).astype(out_ref.dtype)


def channelize(samples, gains):
    count, ch, frames = samples.shape
    spectra = frames - TAPS + 1
    block = 16
    pieces = pl.cdiv(frames, LANES)
    scale = 0.125 / math.sqrt(ch) / 2048.0
    taps = (filter_taps(ch) * scale).astype(np.float32)
    return pl.pallas_call(
        functools.partial(channel_kernel, taps),
        grid=(count // block,),
        in_specs=[
            pl.BlockSpec((block * ch, LANES), functools.partial(lambda piece, i: (i, piece), piece))
            for piece in range(pieces)
        ]
        + [pl.BlockSpec((block, 2 * ch), lambda i: (i, 0))],
        out_specs=pl.BlockSpec((ch, block, 2 * spectra), lambda i: (0, i, 0)),
        out_shape=jax.ShapeDtypeStruct((ch, count, 2 * spectra), jnp.bfloat16),
        scratch_shapes=[pltpu.VMEM((2 * ch, block, spectra), jnp.float32)],
        compiler_params=pltpu.CompilerParams(vmem_limit_bytes=32 << 20),
        name="channelize",
    )(*[samples.reshape(count * ch, frames)] * pieces, gains)


def correlate_kernel(scale, slot_ref, row_ref, data_ref, out_ref, products, tile):
    feeds, width = data_ref.shape
    spectra = width // 2
    rows = row_ref.shape[0]
    pieces = 2 * rows // LANES
    step = 256
    picked = jnp.zeros((rows, width), jnp.float32)
    for first in range(0, feeds, 512):
        place = lax.broadcasted_iota(jnp.int32, (rows, 512), 1) + first
        choice = jnp.where(row_ref[...] == place, 1.0, 0.0).astype(jnp.bfloat16)
        picked = picked + jnp.dot(
            choice, data_ref[first : first + 512, :], preferred_element_type=jnp.float32
        )
    left = jnp.concatenate(
        [
            picked,
            jnp.concatenate([picked[:, spectra:], -picked[:, :spectra]], axis=1),
        ],
        axis=0,
    ).astype(jnp.bfloat16)

    @pl.loop(0, feeds // step)
    def _(i):
        first = pl.multiple_of(i * step, step)
        result = lax.dot_general(
            data_ref[pl.ds(first, step), :],
            left,
            (((1,), (1,)), ((), ())),
            preferred_element_type=jnp.float32,
        )
        for piece in range(pieces):
            products[pl.ds(first * pieces + piece, step, stride=pieces), :] = (
                result[:, piece * LANES : (piece + 1) * LANES] * scale
            )

    lines = 2 * (feeds // LANES)

    @pl.loop(0, feeds // LANES)
    def _(j):
        @pl.loop(0, LANES, unroll=16)
        def _(i):
            slot = slot_ref[j * LANES + i]
            tile[pl.ds(pl.multiple_of(i * pieces, pieces), pieces), :] = products[
                pl.ds(pl.multiple_of(slot * pieces, pieces), pieces), :
            ]

        for piece in range(pieces):
            part, first = divmod(piece * LANES, rows)
            turned = tile[pl.ds(piece, LANES, stride=pieces), :].T
            out_ref[pl.ds(first * lines + 2 * j + part, LANES, stride=lines), :] = turned


def correlate(data, feed_slot, first, rows):
    feeds, width = data.shape
    row_slots = lax.dynamic_slice_in_dim(feed_slot, first, rows, 0).reshape(rows, 1)
    lines = 2 * (feeds // LANES)
    out = pl.pallas_call(
        functools.partial(correlate_kernel, 2.0 / width),
        in_specs=[
            pl.BlockSpec(memory_space=pltpu.SMEM),
            pl.BlockSpec(memory_space=pltpu.VMEM),
            pl.BlockSpec(memory_space=pltpu.VMEM),
        ],
        out_specs=pl.BlockSpec(memory_space=pltpu.VMEM),
        out_shape=jax.ShapeDtypeStruct((rows * lines, LANES), jnp.float32),
        scratch_shapes=[
            pltpu.VMEM((feeds * 2 * rows // LANES, LANES), jnp.float32),
            pltpu.VMEM((LANES * 2 * rows // LANES, LANES), jnp.float32),
        ],
        compiler_params=pltpu.CompilerParams(vmem_limit_bytes=48 << 20),
        name="correlate",
    )(feed_slot, row_slots, data)
    out = out.reshape(rows, feeds // LANES, 2, LANES)
    return jnp.transpose(out, (0, 2, 1, 3)).reshape(rows, 2, feeds)


def through_spectra(samples, gains, feed_slot):
    count, ch, _ = samples.shape
    groups = lax.axis_size("feed") // ch
    first = lax.axis_index("feed") % groups * ROWS
    scales = jnp.transpose(gains, (2, 0, 1)).reshape(count, 2 * ch).astype(jnp.float32)
    spectra = channelize(samples, scales)
    width = spectra.shape[2]
    outgoing = jnp.broadcast_to(spectra[:, None], (ch, groups, count, width))
    outgoing = outgoing.reshape(ch * groups, count, width)
    moved = lax.all_to_all(outgoing, "feed", split_axis=0, concat_axis=0, tiled=True)
    return correlate(moved.reshape(-1, width), feed_slot, first, ROWS)


STEP = 8
SPAN = 16
STEPS = 8
RANGE = 14


def filter_weights(ch):
    taps = filter_taps(ch) * (0.125 / math.sqrt(ch) / 2048.0)
    half = ch // 2
    weights = np.zeros((ch, STEP, SPAN, ch))
    angle = 2.0 * math.pi * (np.arange(half + 1)[:, None] * np.arange(ch)[None, :] % ch) / ch
    sums = np.concatenate([np.cos(angle), np.sin(angle[1:half])], axis=0)
    for spectrum in range(STEP):
        for t in range(TAPS):
            weights[:, spectrum, spectrum + t] = taps[t] * sums
    weights = weights.reshape(ch * STEP, SPAN * ch)
    high = weights.astype(jnp.bfloat16)
    low = (weights - high.astype(np.float64)).astype(jnp.bfloat16)
    return np.concatenate([high, low])


def spectra_of(weights_ref, levels, gains, ch, store):
    count = levels[0].shape[1]
    half, size = ch // 2, ch * STEP
    beside = max(1, 256 // count)
    for first in range(0, STEPS, beside):
        totals = []
        for level in levels:
            slabs = [level[b * size : b * size + SPAN * ch] for b in range(first, first + beside)]
            slab = jnp.concatenate(slabs, axis=1) if beside > 1 else slabs[0]
            both = jnp.dot(weights_ref[...], slab, preferred_element_type=jnp.float32)
            totals.append(both[:size] + both[size:])
        for index in range(beside):
            lanes = slice(index * count, (index + 1) * count)
            parts = [
                [total[d * STEP : (d + 1) * STEP, lanes] for d in range(ch)] for total in totals
            ]
            for c in range(ch):
                place = min(c, ch - c)
                real, imag = parts[0][place], parts[1][place]
                if c % half:
                    sine_real, sine_imag = parts[0][half + place], parts[1][half + place]
                    if c < half:
                        real, imag = real + sine_imag, imag - sine_real
                    else:
                        real, imag = real - sine_imag, imag + sine_real
                gain_real, gain_imag = gains[c : c + 1], gains[ch + c : ch + c + 1]
                store(
                    first + index,
                    c,
                    gain_real * real - gain_imag * imag,
                    gain_real * imag + gain_imag * real,
                )


def levels_of(words):
    return [
        ((words >> 4) - 8).astype(jnp.float32).astype(jnp.bfloat16),
        ((words & 15) - 8).astype(jnp.float32).astype(jnp.bfloat16),
    ]


def own_kernel(main_ref, next_ref, gains_ref, weights_ref, after_ref, out_ref, zero_ref, held, turned, sems):
    step = pl.program_id(0)
    slot = step % 2
    ch = out_ref.shape[0]
    zero_ref[...] = jnp.zeros_like(zero_ref)
    words = jnp.concatenate([main_ref[...], next_ref[...]], axis=0)

    def copy(index):
        return pltpu.make_async_copy(turned.at[index % 2], out_ref.at[:, index], sems.at[index % 2])

    def store(b, c, real, imag):
        held[c, b * 2 * STEP : (b + 1) * 2 * STEP, :] = jnp.concatenate([real, imag], axis=0).astype(held.dtype)

    spectra_of(weights_ref, levels_of(words), gains_ref[...], ch, store)

    @pl.when(step >= 2)
    def _():
        copy(step - 2).wait()

    for c in range(ch):
        turned[slot, c] = held[c].T
    copy(step).start()

    @pl.when(step == pl.num_programs(0) - 1)
    def _():
        copy(step - 1).wait()
        copy(step).wait()


def own_spectra(words, gains, weights, ch, spectra, after):
    count = words.shape[1]
    main = STEPS * STEP * ch
    steps = spectra // (STEPS * STEP)
    return pl.pallas_call(
        own_kernel,
        grid=(steps,),
        in_specs=[
            pl.BlockSpec((main, count), lambda i: (i, 0)),
            pl.BlockSpec((STEP * ch, count), lambda i: ((i + 1) * STEPS, 0)),
            pl.BlockSpec(gains.shape, lambda i: (0, 0)),
            pl.BlockSpec(weights.shape, lambda i: (0, 0)),
            pl.BlockSpec(memory_space=pl.ANY),
        ],
        out_specs=[
            pl.BlockSpec(memory_space=pltpu.HBM),
            pl.BlockSpec((16, LANES), lambda i: (0, 0)),
        ],
        out_shape=[
            pltpu.HBM((ch, steps, count, 2 * STEPS * STEP), jnp.bfloat16),
            jax.ShapeDtypeStruct((16, LANES), jnp.bfloat16),
        ],
        scratch_shapes=[
            pltpu.VMEM((ch, 2 * STEPS * STEP, count), jnp.bfloat16),
            pltpu.VMEM((2, ch, count, 2 * STEPS * STEP), jnp.bfloat16),
            pltpu.SemaphoreType.DMA((2,)),
        ],
        compiler_params=pltpu.CompilerParams(vmem_limit_bytes=12 << 20),
        cost_estimate=pl.CostEstimate(
            flops=4 * spectra * ch * 2 * SPAN * ch * count,
            bytes_accessed=4 * words.size + 4 * ch * spectra * count,
            transcendentals=0,
        ),
        name="own_spectra",
    )(words, words, gains, weights, after)


def select_kernel(last_rows, slots_ref, words_ref, parts_ref, *outs):
    step = pl.program_id(0)
    count, rows = words_ref.shape[1], slots_ref.shape[1]
    words = words_ref[...].astype(jnp.float32).astype(jnp.bfloat16)
    place = lax.broadcasted_iota(jnp.int32, (count, rows), 0)
    choice = jnp.where(slots_ref[...] == place, 1.0, 0.0).astype(jnp.bfloat16)
    taken = jnp.dot(words, choice, preferred_element_type=jnp.float32).astype(outs[0].dtype)
    for index, out_ref in enumerate(outs):
        out_ref[...] = taken[:, index * LANES : (index + 1) * LANES]

    @pl.when(step == pl.num_programs(0) - 1)
    def _():
        extra = parts_ref.shape[0]
        gains = jnp.dot(parts_ref[...], choice, preferred_element_type=jnp.float32).astype(outs[0].dtype)
        for index, out_ref in enumerate(outs):
            out_ref[last_rows : last_rows + extra, :] = gains[:, index * LANES : (index + 1) * LANES]
            left = out_ref.shape[0] - last_rows - extra
            out_ref[last_rows + extra :, :] = jnp.zeros((left, LANES), out_ref.dtype)


def select_rows(words, gains, slots, total):
    lines, count = words.shape
    rows = slots.shape[1]
    block = total // STEPS
    parts = jnp.concatenate([gains >> 4, gains & 15], axis=0).astype(jnp.bfloat16)
    return pl.pallas_call(
        functools.partial(select_kernel, lines - (STEPS - 1) * block),
        grid=(STEPS,),
        in_specs=[
            pl.BlockSpec((1, rows), lambda i: (0, 0)),
            pl.BlockSpec((block, count), lambda i: (i, 0)),
            pl.BlockSpec(parts.shape, lambda i: (0, 0)),
        ],
        out_specs=[pl.BlockSpec((block, LANES), lambda i: (i, 0))] * (rows // LANES),
        out_shape=[jax.ShapeDtypeStruct((total, LANES), jnp.bfloat16)] * (rows // LANES),
        compiler_params=pltpu.CompilerParams(vmem_limit_bytes=8 << 20),
        name="select_rows",
    )(slots, words, parts)


def swap(value, bit):
    pairs = [(index, index ^ bit) for index in range(lax.axis_size("feed"))]
    return lax.ppermute(value, "feed", pairs)


def side(bit):
    return lax.axis_index("feed") // bit % 2


def reduce_half(value, bit):
    size = value.shape[0] // 2
    keep = lax.dynamic_slice_in_dim(value, side(bit) * size, size, 0)
    send = lax.dynamic_slice_in_dim(value, (1 - side(bit)) * size, size, 0)
    return keep + swap(send, bit)


def gather_half(value, bit, buffer):
    size = value.shape[0]
    other = swap(value, bit)
    buffer = lax.dynamic_update_slice_in_dim(buffer, value, side(bit) * size, 0)
    return lax.dynamic_update_slice_in_dim(buffer, other, (1 - side(bit)) * size, 0)


def sum_over_feed(value, work=None):
    half = reduce_half(value, 1)
    size = half.shape[0] // 2
    left, right = half[:size], half[size:]
    left_1, right_1 = reduce_half(left, 2), reduce_half(right, 4)
    left_2, right_2 = reduce_half(left_1, 4), reduce_half(right_1, 2)
    left_3, right_3 = left_2 + swap(left_2, 8), right_2 + swap(right_2, 8)
    if work is not None:
        left_3 = left_3 + work(left_2)
    left_1, right_1 = gather_half(left_3, 4, left_1), gather_half(right_3, 2, right_1)
    left, right = gather_half(left_1, 2, left), gather_half(right_1, 4, right)
    half = jnp.concatenate([left, right], axis=0)
    return (left_1, right_1), lambda: gather_half(half, 1, value)


def rows_kernel(main_ref, next_ref, parts_ref, weights_ref, own_ref, *refs):
    out_ref, left, own, sems = refs[-4:]
    step = pl.program_id(0)
    ch, steps = own.shape[:2]
    rows = main_ref.shape[1]

    def copy(c):
        return pltpu.make_async_copy(own_ref.at[c], own.at[c], sems.at[c])

    @pl.when(step < steps)
    def _():
        for index in range(ch // steps):
            copy(step * (ch // steps) + index).start()
        words = jnp.concatenate([main_ref[...], next_ref[...]], axis=0).astype(jnp.float32).astype(jnp.int32)
        parts = parts_ref[...].astype(jnp.float32)
        gains = parts[: 2 * ch] * 16.0 + parts[2 * ch :]

        def store(b, c, real, imag):
            spot = pl.ds(pl.multiple_of(step * (2 * STEPS * STEP), 2 * STEPS * STEP) + b * 2 * STEP, 2 * STEP)
            left[c, spot, :rows] = jnp.concatenate([real, imag], axis=0).astype(left.dtype)
            left[c, spot, rows:] = jnp.concatenate([imag, -real], axis=0).astype(left.dtype)

        spectra_of(weights_ref, levels_of(words), gains, ch, store)

    @pl.when(step >= steps)
    def _():
        each = out_ref.shape[0]
        for index in range(each):
            c = (step - steps) * each + index
            copy(c).wait()
            spectra = jnp.concatenate([own[c, part] for part in range(own.shape[1])], axis=1)
            products = jnp.dot(spectra, left[c], preferred_element_type=jnp.float32)
            count = products.shape[0]
            largest = jnp.maximum(jnp.max(jnp.abs(products), axis=0, keepdims=True), 2.0**-60)
            power = jnp.floor(jnp.log2(largest))
            coded = jnp.clip(jnp.round(products * jnp.exp2(RANGE - power)), -32767.0, 32767.0)
            out_ref[index, :count, :] = coded.astype(jnp.int32).astype(jnp.int16)
            line = jnp.broadcast_to(power, (out_ref.shape[1] - count, power.shape[1]))
            out_ref[index, count:, :] = line.astype(jnp.int32).astype(jnp.int16)


def row_products(words, parts, own, weights, after):
    ch, steps, count, width = own.shape
    rows = words.shape[1]
    main = STEPS * STEP * ch
    each = 4
    return pl.pallas_call(
        rows_kernel,
        grid=(steps + ch // each,),
        in_specs=[
            pl.BlockSpec((main, rows), lambda i: (jnp.minimum(i, steps - 1), 0)),
            pl.BlockSpec((STEP * ch, rows), lambda i: ((jnp.minimum(i, steps - 1) + 1) * STEPS, 0)),
            pl.BlockSpec(parts.shape, lambda i: (0, 0)),
            pl.BlockSpec(weights.shape, lambda i: (0, 0)),
            pl.BlockSpec(memory_space=pltpu.HBM),
        ]
        + [pl.BlockSpec(memory_space=pl.ANY)] * len(after),
        out_specs=pl.BlockSpec((each, count + 16, 2 * rows), lambda i: (jnp.maximum(i - steps, 0), 0, 0)),
        out_shape=pltpu.HBM((ch, count + 16, 2 * rows), jnp.int16),
        scratch_shapes=[
            pltpu.VMEM((ch, steps * width, 2 * rows), jnp.bfloat16),
            pltpu.VMEM(own.shape, jnp.bfloat16),
            pltpu.SemaphoreType.DMA((ch,)),
        ],
        compiler_params=pltpu.CompilerParams(vmem_limit_bytes=24 << 20),
        cost_estimate=pl.CostEstimate(
            flops=4 * steps * width * ch * SPAN * ch * rows + 4 * ch * steps * width * rows * count,
            bytes_accessed=2 * words.size + 2 * own.size + 4 * ch * rows * count,
            transcendentals=0,
        ),
        name="row_products",
    )(words, words, parts, weights, own, *after)


def finish_kernel(scale, slot_ref, coded_ref, *refs):
    out_ref, products, tile, mixed = refs[-4:]
    sources, lines, width = coded_ref.shape
    count = lines - 16
    pieces = width // LANES
    feeds = sources * count
    columns = 2 * (feeds // LANES)
    for source in range(sources):
        power = coded_ref[source, count : count + 16, :][:1].astype(jnp.float32)
        values = coded_ref[source, :count, :].astype(jnp.float32) * (jnp.exp2(power - RANGE) * scale)
        for piece in range(pieces):
            products[pl.ds(source * count * pieces + piece, count, stride=pieces), :] = values[
                :, piece * LANES : (piece + 1) * LANES
            ]

    together = 8 // pieces

    @pl.loop(0, feeds // LANES // together)
    def _(j):
        for part in range(together):
            for i in range(LANES):
                slot = slot_ref[(j * together + part) * LANES + i]
                tile[i * pieces : (i + 1) * pieces, :] = products[
                    pl.ds(pl.multiple_of(slot * pieces, pieces), pieces), :
                ]
            for piece in range(pieces):
                turned = tile[pl.ds(piece, LANES, stride=pieces), :].T
                mixed[pl.ds(part * pieces + piece, LANES, stride=8), :] = turned
        for row in range(LANES):
            out_ref[pl.ds(pl.multiple_of(row * columns + j * 8, 8), 8), :] = mixed[row * 8 : (row + 1) * 8, :]


def finish(coded, feed_slot, index, pieces, scale, before):
    sources, lines, width = coded.shape
    rows = width // 2
    feeds = sources * (lines - 16)
    columns = 2 * (feeds // LANES)
    earlier = [] if before is None else [before]
    return pl.pallas_call(
        functools.partial(finish_kernel, scale),
        grid=(1,),
        in_specs=[
            pl.BlockSpec(memory_space=pltpu.SMEM),
            pl.BlockSpec(coded.shape, lambda i: (0, 0, 0)),
        ]
        + [pl.BlockSpec(memory_space=pl.ANY)] * len(earlier),
        out_specs=pl.BlockSpec((rows * columns, LANES), lambda i: (index, 0)),
        out_shape=jax.ShapeDtypeStruct((pieces * rows * columns, LANES), jnp.float32),
        scratch_shapes=[
            pltpu.VMEM((feeds * width // LANES, LANES), jnp.float32),
            pltpu.VMEM((width, LANES), jnp.float32),
            pltpu.VMEM((8 * LANES, LANES), jnp.float32),
        ],
        input_output_aliases={2: 0} if earlier else {},
        compiler_params=pltpu.CompilerParams(vmem_limit_bytes=22 << 20),
        name="finish",
    )(feed_slot, coded, *earlier)


def through_rows(samples, gains, feed_slot):
    count, ch, frames = samples.shape
    spectra = frames - TAPS + 1
    pieces = ROWS // LANES
    lines = frames * ch
    unit = 16 * STEPS * 2
    total = pl.cdiv(lines + 4 * ch, unit) * unit
    words = jnp.transpose(samples, (2, 1, 0)).reshape(lines, count)
    scales = gains.reshape(2 * ch, count)
    weights = jnp.asarray(filter_weights(ch))
    slots = (feed_slot[:ROWS] - lax.axis_index("feed") * count).reshape(1, ROWS)
    picked = select_rows(words, scales, slots, total)
    held = []

    def work(after):
        own, zero = own_spectra(words, scales.astype(jnp.float32), weights, ch, spectra, after)
        held.append(own)
        return zero[0, 0]

    sums = [sum_over_feed(value, None if index else work) for index, value in enumerate(picked)]
    own = held[0]
    out, after = None, sums[-1][0]
    for index in range(pieces):
        rows = sums[index][1]()
        parts = rows[lines : lines + 4 * ch]
        coded = row_products(rows, parts, own, weights, after)
        after = [coded]
        moved = lax.all_to_all(coded, "feed", split_axis=0, concat_axis=0, tiled=True)
        out = finish(moved, feed_slot, index, pieces, 1.0 / spectra, out)
    feeds = feed_slot.shape[0]
    out = out.reshape(ROWS, feeds // LANES, 2, LANES)
    return jnp.transpose(out, (0, 2, 1, 3)).reshape(ROWS, 2, feeds)


def body(samples, gains, feed_slot):
    count, ch, frames = samples.shape
    spectra = frames - TAPS + 1
    even = count % LANES == 0 and spectra % (STEPS * STEP) == 0 and ch % STEPS == 0
    if lax.axis_size("feed") == ch == 16 and even:
        return through_rows(samples, gains, feed_slot)
    return through_spectra(samples, gains, feed_slot)


def solution(mesh):
    return jax.shard_map(
        body,
        mesh=mesh,
        in_specs=(P(("band", "feed"), None, None), P(None, "band", "feed"), P()),
        out_specs=P(("band", "feed"), None, None),
        check_vma=False,
    )
```

```python
import functools
import math

import jax
import jax.numpy as jnp
import numpy as np
from jax import lax
from jax.experimental import pallas as pl
from jax.experimental.pallas import tpu as pltpu
from jax.sharding import PartitionSpec as P

TAPS = 8
ROWS = 256
LANES = 128


def filter_taps(ch):
    length = TAPS * ch
    place = np.arange(length, dtype=np.float64)
    window = 0.5 - 0.5 * np.cos(2.0 * math.pi * place / (length - 1))
    return (np.sinc((place - 0.5 * (length - 1)) / ch) * window).reshape(TAPS, ch)


def twiddle(value, turn):
    real, imag = value
    if turn == 0:
        return value
    if turn == 0.25:
        return imag, -real
    half = math.sqrt(0.5)
    if turn == 0.125:
        return half * (real + imag), half * (imag - real)
    if turn == 0.375:
        return half * (imag - real), -half * (real + imag)
    c, s = math.cos(2.0 * math.pi * turn), math.sin(2.0 * math.pi * turn)
    return c * real + s * imag, c * imag - s * real


def fft(values):
    count = len(values)
    if count == 1:
        return values
    even, odd = fft(values[0::2]), fft(values[1::2])
    low, high = [], []
    for index in range(count // 2):
        real, imag = twiddle(odd[index], index / count)
        low.append((even[index][0] + real, even[index][1] + imag))
        high.append((even[index][0] - real, even[index][1] - imag))
    return low + high


def channel_kernel(taps, *refs):
    *samples_refs, gains_ref, out_ref, filtered = refs
    ch, block, width = out_ref.shape
    spectra = width // 2
    padded = len(samples_refs) * LANES
    for k in range(ch):
        words = jnp.concatenate(
            [ref[pl.ds(k, block, stride=ch), :] for ref in samples_refs], axis=1
        )
        levels = ((words >> 4) - 8, (words & 15) - 8)
        for part in range(2):
            value = levels[part].astype(jnp.float32)
            shifted = [value] + [pltpu.roll(value, padded - t, 1) for t in range(1, TAPS // 2)]
            near = float(taps[0, k]) * shifted[0]
            far = float(taps[TAPS // 2, k]) * shifted[0]
            for t in range(1, TAPS // 2):
                near = near + float(taps[t, k]) * shifted[t]
                far = far + float(taps[t + TAPS // 2, k]) * shifted[t]
            total = near + pltpu.roll(far, padded - TAPS // 2, 1)
            filtered[2 * k + part] = total[:, :spectra]
    for row in range(0, block, 8):
        gains = gains_ref[row : row + 8, :]
        for lane in range(0, spectra, LANES):
            spot = (slice(row, row + 8), slice(lane, lane + LANES))
            values = [(filtered[2 * k][spot], filtered[2 * k + 1][spot]) for k in range(ch)]
            for c, (real, imag) in enumerate(fft(values)):
                gain_real = gains[:, c : c + 1]
                gain_imag = gains[:, ch + c : ch + c + 1]
                out_ref[c, row : row + 8, lane : lane + LANES] = (
                    gain_real * real - gain_imag * imag
                ).astype(out_ref.dtype)
                out_ref[c, row : row + 8, spectra + lane : spectra + lane + LANES] = (
                    gain_real * imag + gain_imag * real
                ).astype(out_ref.dtype)


def channelize(samples, gains):
    count, ch, frames = samples.shape
    spectra = frames - TAPS + 1
    block = 16
    pieces = pl.cdiv(frames, LANES)
    scale = 0.125 / math.sqrt(ch) / 2048.0
    taps = (filter_taps(ch) * scale).astype(np.float32)
    return pl.pallas_call(
        functools.partial(channel_kernel, taps),
        grid=(count // block,),
        in_specs=[
            pl.BlockSpec((block * ch, LANES), functools.partial(lambda piece, i: (i, piece), piece))
            for piece in range(pieces)
        ]
        + [pl.BlockSpec((block, 2 * ch), lambda i: (i, 0))],
        out_specs=pl.BlockSpec((ch, block, 2 * spectra), lambda i: (0, i, 0)),
        out_shape=jax.ShapeDtypeStruct((ch, count, 2 * spectra), jnp.bfloat16),
        scratch_shapes=[pltpu.VMEM((2 * ch, block, spectra), jnp.float32)],
        compiler_params=pltpu.CompilerParams(vmem_limit_bytes=32 << 20),
        name="channelize",
    )(*[samples.reshape(count * ch, frames)] * pieces, gains)


def correlate_kernel(scale, slot_ref, row_ref, data_ref, out_ref, products, tile):
    feeds, width = data_ref.shape
    spectra = width // 2
    rows = row_ref.shape[0]
    pieces = 2 * rows // LANES
    step = 256
    picked = jnp.zeros((rows, width), jnp.float32)
    for first in range(0, feeds, 512):
        place = lax.broadcasted_iota(jnp.int32, (rows, 512), 1) + first
        choice = jnp.where(row_ref[...] == place, 1.0, 0.0).astype(jnp.bfloat16)
        picked = picked + jnp.dot(
            choice, data_ref[first : first + 512, :], preferred_element_type=jnp.float32
        )
    left = jnp.concatenate(
        [
            picked,
            jnp.concatenate([picked[:, spectra:], -picked[:, :spectra]], axis=1),
        ],
        axis=0,
    ).astype(jnp.bfloat16)

    @pl.loop(0, feeds // step)
    def _(i):
        first = pl.multiple_of(i * step, step)
        result = lax.dot_general(
            data_ref[pl.ds(first, step), :],
            left,
            (((1,), (1,)), ((), ())),
            preferred_element_type=jnp.float32,
        )
        for piece in range(pieces):
            products[pl.ds(first * pieces + piece, step, stride=pieces), :] = (
                result[:, piece * LANES : (piece + 1) * LANES] * scale
            )

    lines = 2 * (feeds // LANES)

    @pl.loop(0, feeds // LANES)
    def _(j):
        @pl.loop(0, LANES, unroll=16)
        def _(i):
            slot = slot_ref[j * LANES + i]
            tile[pl.ds(pl.multiple_of(i * pieces, pieces), pieces), :] = products[
                pl.ds(pl.multiple_of(slot * pieces, pieces), pieces), :
            ]

        for piece in range(pieces):
            part, first = divmod(piece * LANES, rows)
            turned = tile[pl.ds(piece, LANES, stride=pieces), :].T
            out_ref[pl.ds(first * lines + 2 * j + part, LANES, stride=lines), :] = turned


def correlate(data, feed_slot, first, rows):
    feeds, width = data.shape
    row_slots = lax.dynamic_slice_in_dim(feed_slot, first, rows, 0).reshape(rows, 1)
    lines = 2 * (feeds // LANES)
    out = pl.pallas_call(
        functools.partial(correlate_kernel, 2.0 / width),
        in_specs=[
            pl.BlockSpec(memory_space=pltpu.SMEM),
            pl.BlockSpec(memory_space=pltpu.VMEM),
            pl.BlockSpec(memory_space=pltpu.VMEM),
        ],
        out_specs=pl.BlockSpec(memory_space=pltpu.VMEM),
        out_shape=jax.ShapeDtypeStruct((rows * lines, LANES), jnp.float32),
        scratch_shapes=[
            pltpu.VMEM((feeds * 2 * rows // LANES, LANES), jnp.float32),
            pltpu.VMEM((LANES * 2 * rows // LANES, LANES), jnp.float32),
        ],
        compiler_params=pltpu.CompilerParams(vmem_limit_bytes=48 << 20),
        name="correlate",
    )(feed_slot, row_slots, data)
    out = out.reshape(rows, feeds // LANES, 2, LANES)
    return jnp.transpose(out, (0, 2, 1, 3)).reshape(rows, 2, feeds)


def through_spectra(samples, gains, feed_slot):
    count, ch, _ = samples.shape
    groups = lax.axis_size("feed") // ch
    first = lax.axis_index("feed") % groups * ROWS
    scales = jnp.transpose(gains, (2, 0, 1)).reshape(count, 2 * ch).astype(jnp.float32)
    spectra = channelize(samples, scales)
    width = spectra.shape[2]
    outgoing = jnp.broadcast_to(spectra[:, None], (ch, groups, count, width))
    outgoing = outgoing.reshape(ch * groups, count, width)
    moved = lax.all_to_all(outgoing, "feed", split_axis=0, concat_axis=0, tiled=True)
    return correlate(moved.reshape(-1, width), feed_slot, first, ROWS)


STEP = 8
SPAN = 16
STEPS = 8
RANGE = 14


def filter_weights(ch):
    taps = filter_taps(ch) * (0.125 / math.sqrt(ch) / 2048.0)
    half = ch // 2
    weights = np.zeros((ch, STEP, SPAN, ch))
    angle = 2.0 * math.pi * (np.arange(half + 1)[:, None] * np.arange(ch)[None, :] % ch) / ch
    sums = np.concatenate([np.cos(angle), np.sin(angle[1:half])], axis=0)
    for spectrum in range(STEP):
        for t in range(TAPS):
            weights[:, spectrum, spectrum + t] = taps[t] * sums
    weights = weights.reshape(ch * STEP, SPAN * ch)
    high = weights.astype(jnp.bfloat16)
    low = (weights - high.astype(np.float64)).astype(jnp.bfloat16)
    return np.concatenate([high, low])


def spectra_of(weights_ref, levels, gains, ch, store):
    count = levels[0].shape[1]
    half, size = ch // 2, ch * STEP
    beside = max(1, 256 // count)
    for first in range(0, STEPS, beside):
        totals = []
        for level in levels:
            slabs = [level[b * size : b * size + SPAN * ch] for b in range(first, first + beside)]
            slab = jnp.concatenate(slabs, axis=1) if beside > 1 else slabs[0]
            both = jnp.dot(weights_ref[...], slab, preferred_element_type=jnp.float32)
            totals.append(both[:size] + both[size:])
        for index in range(beside):
            lanes = slice(index * count, (index + 1) * count)
            parts = [
                [total[d * STEP : (d + 1) * STEP, lanes] for d in range(ch)] for total in totals
            ]
            for c in range(ch):
                place = min(c, ch - c)
                real, imag = parts[0][place], parts[1][place]
                if c % half:
                    sine_real, sine_imag = parts[0][half + place], parts[1][half + place]
                    if c < half:
                        real, imag = real + sine_imag, imag - sine_real
                    else:
                        real, imag = real - sine_imag, imag + sine_real
                gain_real, gain_imag = gains[c : c + 1], gains[ch + c : ch + c + 1]
                store(
                    first + index,
                    c,
                    gain_real * real - gain_imag * imag,
                    gain_real * imag + gain_imag * real,
                )


def levels_of(words):
    return [
        ((words >> 4) - 8).astype(jnp.float32).astype(jnp.bfloat16),
        ((words & 15) - 8).astype(jnp.float32).astype(jnp.bfloat16),
    ]


def own_kernel(main_ref, next_ref, gains_ref, weights_ref, after_ref, out_ref, zero_ref, held):
    step = pl.program_id(0)
    ch = out_ref.shape[0]
    zero_ref[...] = jnp.zeros_like(zero_ref)
    words = jnp.concatenate([main_ref[...], next_ref[...]], axis=0)

    def store(b, c, real, imag):
        held[c, b * 2 * STEP : (b + 1) * 2 * STEP, :] = jnp.concatenate([real, imag], axis=0).astype(held.dtype)

    spectra_of(weights_ref, levels_of(words), gains_ref[...], ch, store)
    for c in range(ch):
        out_ref[c, step] = held[c].T


def own_spectra(words, gains, weights, ch, spectra, after):
    count = words.shape[1]
    main = STEPS * STEP * ch
    steps = spectra // (STEPS * STEP)
    return pl.pallas_call(
        own_kernel,
        grid=(steps,),
        in_specs=[
            pl.BlockSpec((main, count), lambda i: (i, 0)),
            pl.BlockSpec((STEP * ch, count), lambda i: ((i + 1) * STEPS, 0)),
            pl.BlockSpec(gains.shape, lambda i: (0, 0)),
            pl.BlockSpec(weights.shape, lambda i: (0, 0)),
            pl.BlockSpec(memory_space=pl.ANY),
        ],
        out_specs=[
            pl.BlockSpec(memory_space=pltpu.VMEM),
            pl.BlockSpec((16, LANES), lambda i: (0, 0)),
        ],
        out_shape=[
            jax.ShapeDtypeStruct((ch, steps, count, 2 * STEPS * STEP), jnp.bfloat16),
            jax.ShapeDtypeStruct((16, LANES), jnp.bfloat16),
        ],
        scratch_shapes=[
            pltpu.VMEM((ch, 2 * STEPS * STEP, count), jnp.bfloat16),
        ],
        compiler_params=pltpu.CompilerParams(vmem_limit_bytes=12 << 20),
        cost_estimate=pl.CostEstimate(
            flops=4 * spectra * ch * 2 * SPAN * ch * count,
            bytes_accessed=4 * words.size + 4 * ch * spectra * count,
            transcendentals=0,
        ),
        name="own_spectra",
    )(words, words, gains, weights, after)


def select_kernel(last_rows, slots_ref, words_ref, parts_ref, *outs):
    step = pl.program_id(0)
    count, rows = words_ref.shape[1], slots_ref.shape[1]
    words = words_ref[...].astype(jnp.float32).astype(jnp.bfloat16)
    place = lax.broadcasted_iota(jnp.int32, (count, rows), 0)
    choice = jnp.where(slots_ref[...] == place, 1.0, 0.0).astype(jnp.bfloat16)
    taken = jnp.dot(words, choice, preferred_element_type=jnp.float32).astype(outs[0].dtype)
    for index, out_ref in enumerate(outs):
        out_ref[...] = taken[:, index * LANES : (index + 1) * LANES]

    @pl.when(step == pl.num_programs(0) - 1)
    def _():
        extra = parts_ref.shape[0]
        gains = jnp.dot(parts_ref[...], choice, preferred_element_type=jnp.float32).astype(outs[0].dtype)
        for index, out_ref in enumerate(outs):
            out_ref[last_rows : last_rows + extra, :] = gains[:, index * LANES : (index + 1) * LANES]
            left = out_ref.shape[0] - last_rows - extra
            out_ref[last_rows + extra :, :] = jnp.zeros((left, LANES), out_ref.dtype)


def select_rows(words, gains, slots, total):
    lines, count = words.shape
    rows = slots.shape[1]
    block = total // STEPS
    parts = jnp.concatenate([gains >> 4, gains & 15], axis=0).astype(jnp.bfloat16)
    return pl.pallas_call(
        functools.partial(select_kernel, lines - (STEPS - 1) * block),
        grid=(STEPS,),
        in_specs=[
            pl.BlockSpec((1, rows), lambda i: (0, 0)),
            pl.BlockSpec((block, count), lambda i: (i, 0)),
            pl.BlockSpec(parts.shape, lambda i: (0, 0)),
        ],
        out_specs=[pl.BlockSpec((block, LANES), lambda i: (i, 0))] * (rows // LANES),
        out_shape=[jax.ShapeDtypeStruct((total, LANES), jnp.bfloat16)] * (rows // LANES),
        compiler_params=pltpu.CompilerParams(vmem_limit_bytes=8 << 20),
        name="select_rows",
    )(slots, words, parts)


def swap(value, bit):
    pairs = [(index, index ^ bit) for index in range(lax.axis_size("feed"))]
    return lax.ppermute(value, "feed", pairs)


def side(bit):
    return lax.axis_index("feed") // bit % 2


def reduce_half(value, bit):
    size = value.shape[0] // 2
    keep = lax.dynamic_slice_in_dim(value, side(bit) * size, size, 0)
    send = lax.dynamic_slice_in_dim(value, (1 - side(bit)) * size, size, 0)
    return keep + swap(send, bit)


def gather_half(value, bit, buffer):
    size = value.shape[0]
    other = swap(value, bit)
    buffer = lax.dynamic_update_slice_in_dim(buffer, value, side(bit) * size, 0)
    return lax.dynamic_update_slice_in_dim(buffer, other, (1 - side(bit)) * size, 0)


def sum_over_feed(value, work=None):
    half = reduce_half(value, 1)
    size = half.shape[0] // 2
    left, right = half[:size], half[size:]
    left_1, right_1 = reduce_half(left, 2), reduce_half(right, 4)
    left_2, right_2 = reduce_half(left_1, 4), reduce_half(right_1, 2)
    left_3, right_3 = left_2 + swap(left_2, 8), right_2 + swap(right_2, 8)
    if work is not None:
        left_3 = left_3 + work(left_2)
    left_1, right_1 = gather_half(left_3, 4, left_1), gather_half(right_3, 2, right_1)
    left, right = gather_half(left_1, 2, left), gather_half(right_1, 4, right)
    half = jnp.concatenate([left, right], axis=0)
    return half, lambda: gather_half(half, 1, value)


def rows_kernel(main_ref, next_ref, parts_ref, weights_ref, own_ref, *refs):
    out_ref, done_ref, left = refs[-3:]
    step = pl.program_id(0)
    done_ref[...] = jnp.zeros_like(done_ref)
    ch, steps = own_ref.shape[:2]
    rows = main_ref.shape[1]

    @pl.when(step < steps)
    def _():
        words = jnp.concatenate([main_ref[...], next_ref[...]], axis=0).astype(jnp.float32).astype(jnp.int32)
        parts = parts_ref[...].astype(jnp.float32)
        gains = parts[: 2 * ch] * 16.0 + parts[2 * ch :]

        def store(b, c, real, imag):
            spot = pl.ds(pl.multiple_of(step * (2 * STEPS * STEP), 2 * STEPS * STEP) + b * 2 * STEP, 2 * STEP)
            left[c, spot, :rows] = jnp.concatenate([real, imag], axis=0).astype(left.dtype)
            left[c, spot, rows:] = jnp.concatenate([imag, -real], axis=0).astype(left.dtype)

        spectra_of(weights_ref, levels_of(words), gains, ch, store)

    @pl.when(step >= steps)
    def _():
        each = out_ref.shape[0]
        for index in range(each):
            c = (step - steps) * each + index
            spectra = jnp.concatenate([own_ref[c, part] for part in range(steps)], axis=1)
            products = jnp.dot(spectra, left[c], preferred_element_type=jnp.float32)
            count = products.shape[0]
            largest = jnp.maximum(jnp.max(jnp.abs(products), axis=0, keepdims=True), 2.0**-60)
            power = jnp.floor(jnp.log2(largest))
            coded = jnp.clip(jnp.round(products * jnp.exp2(RANGE - power)), -32767.0, 32767.0)
            out_ref[index, :count, :] = coded.astype(jnp.int32).astype(jnp.int16)
            line = jnp.broadcast_to(power, (out_ref.shape[1] - count, power.shape[1]))
            out_ref[index, count:, :] = line.astype(jnp.int32).astype(jnp.int16)


def row_products(words, parts, own, weights, after):
    ch, steps, count, width = own.shape
    rows = words.shape[1]
    main = STEPS * STEP * ch
    each = 4
    return pl.pallas_call(
        rows_kernel,
        grid=(steps + ch // each,),
        in_specs=[
            pl.BlockSpec((main, rows), lambda i: (jnp.minimum(i, steps - 1), 0)),
            pl.BlockSpec((STEP * ch, rows), lambda i: ((jnp.minimum(i, steps - 1) + 1) * STEPS, 0)),
            pl.BlockSpec(parts.shape, lambda i: (0, 0)),
            pl.BlockSpec(weights.shape, lambda i: (0, 0)),
            pl.BlockSpec(memory_space=pltpu.VMEM),
        ]
        + [pl.BlockSpec(memory_space=pl.ANY)] * len(after),
        out_specs=[
            pl.BlockSpec((each, count + 16, 2 * rows), lambda i: (jnp.maximum(i - steps, 0), 0, 0)),
            pl.BlockSpec((16, LANES), lambda i: (0, 0)),
        ],
        out_shape=[
            pltpu.HBM((ch, count + 16, 2 * rows), jnp.int16),
            jax.ShapeDtypeStruct((16, LANES), jnp.bfloat16),
        ],
        scratch_shapes=[
            pltpu.VMEM((ch, steps * width, 2 * rows), jnp.bfloat16),
        ],
        compiler_params=pltpu.CompilerParams(vmem_limit_bytes=18 << 20),
        cost_estimate=pl.CostEstimate(
            flops=4 * steps * width * ch * SPAN * ch * rows + 4 * ch * steps * width * rows * count,
            bytes_accessed=2 * words.size + 2 * own.size + 4 * ch * rows * count,
            transcendentals=0,
        ),
        name="row_products",
    )(words, words, parts, weights, own, *after)


def finish_kernel(scale, slot_ref, coded_ref, *refs):
    out_ref, products, tile, mixed = refs[-4:]
    sources, lines, width = coded_ref.shape
    count = lines - 16
    pieces = width // LANES
    feeds = sources * count
    columns = 2 * (feeds // LANES)
    for source in range(sources):
        power = coded_ref[source, count : count + 16, :][:1].astype(jnp.float32)
        values = coded_ref[source, :count, :].astype(jnp.float32) * (jnp.exp2(power - RANGE) * scale)
        for piece in range(pieces):
            products[pl.ds(source * count * pieces + piece, count, stride=pieces), :] = values[
                :, piece * LANES : (piece + 1) * LANES
            ]

    together = 8 // pieces

    @pl.loop(0, feeds // LANES // together)
    def _(j):
        for part in range(together):
            for i in range(LANES):
                slot = slot_ref[(j * together + part) * LANES + i]
                tile[i * pieces : (i + 1) * pieces, :] = products[
                    pl.ds(pl.multiple_of(slot * pieces, pieces), pieces), :
                ]
            for piece in range(pieces):
                turned = tile[pl.ds(piece, LANES, stride=pieces), :].T
                mixed[pl.ds(part * pieces + piece, LANES, stride=8), :] = turned
        for row in range(LANES):
            out_ref[pl.ds(pl.multiple_of(row * columns + j * 8, 8), 8), :] = mixed[row * 8 : (row + 1) * 8, :]


def finish(coded, feed_slot, index, pieces, scale, before):
    sources, lines, width = coded.shape
    rows = width // 2
    feeds = sources * (lines - 16)
    columns = 2 * (feeds // LANES)
    earlier = [] if before is None else [before]
    return pl.pallas_call(
        functools.partial(finish_kernel, scale),
        grid=(1,),
        in_specs=[
            pl.BlockSpec(memory_space=pltpu.SMEM),
            pl.BlockSpec(coded.shape, lambda i: (0, 0, 0)),
        ]
        + [pl.BlockSpec(memory_space=pl.ANY)] * len(earlier),
        out_specs=pl.BlockSpec((rows * columns, LANES), lambda i: (index, 0)),
        out_shape=jax.ShapeDtypeStruct((pieces * rows * columns, LANES), jnp.float32),
        scratch_shapes=[
            pltpu.VMEM((feeds * width // LANES, LANES), jnp.float32),
            pltpu.VMEM((width, LANES), jnp.float32),
            pltpu.VMEM((8 * LANES, LANES), jnp.float32),
        ],
        input_output_aliases={2: 0} if earlier else {},
        compiler_params=pltpu.CompilerParams(vmem_limit_bytes=22 << 20),
        name="finish",
    )(feed_slot, coded, *earlier)


def through_rows(samples, gains, feed_slot):
    count, ch, frames = samples.shape
    spectra = frames - TAPS + 1
    pieces = ROWS // LANES
    lines = frames * ch
    unit = 16 * STEPS * 2
    total = pl.cdiv(lines + 4 * ch, unit) * unit
    words = jnp.transpose(samples, (2, 1, 0)).reshape(lines, count)
    scales = gains.reshape(2 * ch, count)
    weights = jnp.asarray(filter_weights(ch))
    slots = (feed_slot[:ROWS] - lax.axis_index("feed") * count).reshape(1, ROWS)
    picked = select_rows(words, scales, slots, total)
    held = []

    def work(after):
        own, zero = own_spectra(words, scales.astype(jnp.float32), weights, ch, spectra, after)
        held.append(own)
        return zero[0, 0]

    sums = [sum_over_feed(value, None if index else work) for index, value in enumerate(picked)]
    own = held[0]
    out, after = None, [sums[-1][0]]
    for index in range(pieces):
        rows = sums[index][1]()
        parts = rows[lines : lines + 4 * ch]
        coded, done = row_products(rows, parts, own, weights, after)
        after = [done]
        moved = lax.all_to_all(coded, "feed", split_axis=0, concat_axis=0, tiled=True)
        out = finish(moved, feed_slot, index, pieces, 1.0 / spectra, out)
    feeds = feed_slot.shape[0]
    out = out.reshape(ROWS, feeds // LANES, 2, LANES)
    return jnp.transpose(out, (0, 2, 1, 3)).reshape(ROWS, 2, feeds)


def body(samples, gains, feed_slot):
    count, ch, frames = samples.shape
    spectra = frames - TAPS + 1
    even = count % LANES == 0 and spectra % (STEPS * STEP) == 0 and ch % STEPS == 0
    if lax.axis_size("feed") == ch == 16 and even:
        return through_rows(samples, gains, feed_slot)
    return through_spectra(samples, gains, feed_slot)


def solution(mesh):
    return jax.shard_map(
        body,
        mesh=mesh,
        in_specs=(P(("band", "feed"), None, None), P(None, "band", "feed"), P()),
        out_specs=P(("band", "feed"), None, None),
        check_vma=False,
    )
```

```python
import functools
import math

import jax
import jax.numpy as jnp
import numpy as np
from jax import lax
from jax.experimental import pallas as pl
from jax.experimental.pallas import tpu as pltpu
from jax.sharding import PartitionSpec as P

TAPS = 8
ROWS = 256
LANES = 128


def filter_taps(ch):
    length = TAPS * ch
    place = np.arange(length, dtype=np.float64)
    window = 0.5 - 0.5 * np.cos(2.0 * math.pi * place / (length - 1))
    return (np.sinc((place - 0.5 * (length - 1)) / ch) * window).reshape(TAPS, ch)


def twiddle(value, turn):
    real, imag = value
    if turn == 0:
        return value
    if turn == 0.25:
        return imag, -real
    half = math.sqrt(0.5)
    if turn == 0.125:
        return half * (real + imag), half * (imag - real)
    if turn == 0.375:
        return half * (imag - real), -half * (real + imag)
    c, s = math.cos(2.0 * math.pi * turn), math.sin(2.0 * math.pi * turn)
    return c * real + s * imag, c * imag - s * real


def fft(values):
    count = len(values)
    if count == 1:
        return values
    even, odd = fft(values[0::2]), fft(values[1::2])
    low, high = [], []
    for index in range(count // 2):
        real, imag = twiddle(odd[index], index / count)
        low.append((even[index][0] + real, even[index][1] + imag))
        high.append((even[index][0] - real, even[index][1] - imag))
    return low + high


def channel_kernel(taps, *refs):
    *samples_refs, gains_ref, out_ref, filtered = refs
    ch, block, width = out_ref.shape
    spectra = width // 2
    padded = len(samples_refs) * LANES
    for k in range(ch):
        words = jnp.concatenate(
            [ref[pl.ds(k, block, stride=ch), :] for ref in samples_refs], axis=1
        )
        levels = ((words >> 4) - 8, (words & 15) - 8)
        for part in range(2):
            value = levels[part].astype(jnp.float32)
            shifted = [value] + [pltpu.roll(value, padded - t, 1) for t in range(1, TAPS // 2)]
            near = float(taps[0, k]) * shifted[0]
            far = float(taps[TAPS // 2, k]) * shifted[0]
            for t in range(1, TAPS // 2):
                near = near + float(taps[t, k]) * shifted[t]
                far = far + float(taps[t + TAPS // 2, k]) * shifted[t]
            total = near + pltpu.roll(far, padded - TAPS // 2, 1)
            filtered[2 * k + part] = total[:, :spectra]
    for row in range(0, block, 8):
        gains = gains_ref[row : row + 8, :]
        for lane in range(0, spectra, LANES):
            spot = (slice(row, row + 8), slice(lane, lane + LANES))
            values = [(filtered[2 * k][spot], filtered[2 * k + 1][spot]) for k in range(ch)]
            for c, (real, imag) in enumerate(fft(values)):
                gain_real = gains[:, c : c + 1]
                gain_imag = gains[:, ch + c : ch + c + 1]
                out_ref[c, row : row + 8, lane : lane + LANES] = (
                    gain_real * real - gain_imag * imag
                ).astype(out_ref.dtype)
                out_ref[c, row : row + 8, spectra + lane : spectra + lane + LANES] = (
                    gain_real * imag + gain_imag * real
                ).astype(out_ref.dtype)


def channelize(samples, gains):
    count, ch, frames = samples.shape
    spectra = frames - TAPS + 1
    block = 16
    pieces = pl.cdiv(frames, LANES)
    scale = 0.125 / math.sqrt(ch) / 2048.0
    taps = (filter_taps(ch) * scale).astype(np.float32)
    return pl.pallas_call(
        functools.partial(channel_kernel, taps),
        grid=(count // block,),
        in_specs=[
            pl.BlockSpec((block * ch, LANES), functools.partial(lambda piece, i: (i, piece), piece))
            for piece in range(pieces)
        ]
        + [pl.BlockSpec((block, 2 * ch), lambda i: (i, 0))],
        out_specs=pl.BlockSpec((ch, block, 2 * spectra), lambda i: (0, i, 0)),
        out_shape=jax.ShapeDtypeStruct((ch, count, 2 * spectra), jnp.bfloat16),
        scratch_shapes=[pltpu.VMEM((2 * ch, block, spectra), jnp.float32)],
        compiler_params=pltpu.CompilerParams(vmem_limit_bytes=32 << 20),
        name="channelize",
    )(*[samples.reshape(count * ch, frames)] * pieces, gains)


def correlate_kernel(scale, slot_ref, row_ref, data_ref, out_ref, products, tile):
    feeds, width = data_ref.shape
    spectra = width // 2
    rows = row_ref.shape[0]
    pieces = 2 * rows // LANES
    step = 256
    picked = jnp.zeros((rows, width), jnp.float32)
    for first in range(0, feeds, 512):
        place = lax.broadcasted_iota(jnp.int32, (rows, 512), 1) + first
        choice = jnp.where(row_ref[...] == place, 1.0, 0.0).astype(jnp.bfloat16)
        picked = picked + jnp.dot(
            choice, data_ref[first : first + 512, :], preferred_element_type=jnp.float32
        )
    left = jnp.concatenate(
        [
            picked,
            jnp.concatenate([picked[:, spectra:], -picked[:, :spectra]], axis=1),
        ],
        axis=0,
    ).astype(jnp.bfloat16)

    @pl.loop(0, feeds // step)
    def _(i):
        first = pl.multiple_of(i * step, step)
        result = lax.dot_general(
            data_ref[pl.ds(first, step), :],
            left,
            (((1,), (1,)), ((), ())),
            preferred_element_type=jnp.float32,
        )
        for piece in range(pieces):
            products[pl.ds(first * pieces + piece, step, stride=pieces), :] = (
                result[:, piece * LANES : (piece + 1) * LANES] * scale
            )

    lines = 2 * (feeds // LANES)

    @pl.loop(0, feeds // LANES)
    def _(j):
        @pl.loop(0, LANES, unroll=16)
        def _(i):
            slot = slot_ref[j * LANES + i]
            tile[pl.ds(pl.multiple_of(i * pieces, pieces), pieces), :] = products[
                pl.ds(pl.multiple_of(slot * pieces, pieces), pieces), :
            ]

        for piece in range(pieces):
            part, first = divmod(piece * LANES, rows)
            turned = tile[pl.ds(piece, LANES, stride=pieces), :].T
            out_ref[pl.ds(first * lines + 2 * j + part, LANES, stride=lines), :] = turned


def correlate(data, feed_slot, first, rows):
    feeds, width = data.shape
    row_slots = lax.dynamic_slice_in_dim(feed_slot, first, rows, 0).reshape(rows, 1)
    lines = 2 * (feeds // LANES)
    out = pl.pallas_call(
        functools.partial(correlate_kernel, 2.0 / width),
        in_specs=[
            pl.BlockSpec(memory_space=pltpu.SMEM),
            pl.BlockSpec(memory_space=pltpu.VMEM),
            pl.BlockSpec(memory_space=pltpu.VMEM),
        ],
        out_specs=pl.BlockSpec(memory_space=pltpu.VMEM),
        out_shape=jax.ShapeDtypeStruct((rows * lines, LANES), jnp.float32),
        scratch_shapes=[
            pltpu.VMEM((feeds * 2 * rows // LANES, LANES), jnp.float32),
            pltpu.VMEM((LANES * 2 * rows // LANES, LANES), jnp.float32),
        ],
        compiler_params=pltpu.CompilerParams(vmem_limit_bytes=48 << 20),
        name="correlate",
    )(feed_slot, row_slots, data)
    out = out.reshape(rows, feeds // LANES, 2, LANES)
    return jnp.transpose(out, (0, 2, 1, 3)).reshape(rows, 2, feeds)


def through_spectra(samples, gains, feed_slot):
    count, ch, _ = samples.shape
    groups = lax.axis_size("feed") // ch
    first = lax.axis_index("feed") % groups * ROWS
    scales = jnp.transpose(gains, (2, 0, 1)).reshape(count, 2 * ch).astype(jnp.float32)
    spectra = channelize(samples, scales)
    width = spectra.shape[2]
    outgoing = jnp.broadcast_to(spectra[:, None], (ch, groups, count, width))
    outgoing = outgoing.reshape(ch * groups, count, width)
    moved = lax.all_to_all(outgoing, "feed", split_axis=0, concat_axis=0, tiled=True)
    return correlate(moved.reshape(-1, width), feed_slot, first, ROWS)


STEP = 8
SPAN = 16
STEPS = 8
RANGE = 14


def filter_weights(ch):
    taps = filter_taps(ch) * (0.125 / math.sqrt(ch) / 2048.0)
    half = ch // 2
    weights = np.zeros((ch, STEP, SPAN, ch))
    angle = 2.0 * math.pi * (np.arange(half + 1)[:, None] * np.arange(ch)[None, :] % ch) / ch
    sums = np.concatenate([np.cos(angle), np.sin(angle[1:half])], axis=0)
    for spectrum in range(STEP):
        for t in range(TAPS):
            weights[:, spectrum, spectrum + t] = taps[t] * sums
    weights = weights.reshape(ch * STEP, SPAN * ch)
    high = weights.astype(jnp.bfloat16)
    low = (weights - high.astype(np.float64)).astype(jnp.bfloat16)
    return np.concatenate([high, low])


def spectra_of(weights_ref, levels, gains, ch, store):
    count = levels[0].shape[1]
    half, size = ch // 2, ch * STEP
    beside = max(1, 256 // count)
    for first in range(0, STEPS, beside):
        totals = []
        for level in levels:
            slabs = [level[b * size : b * size + SPAN * ch] for b in range(first, first + beside)]
            slab = jnp.concatenate(slabs, axis=1) if beside > 1 else slabs[0]
            both = jnp.dot(weights_ref[...], slab, preferred_element_type=jnp.float32)
            totals.append(both[:size] + both[size:])
        for index in range(beside):
            lanes = slice(index * count, (index + 1) * count)
            parts = [
                [total[d * STEP : (d + 1) * STEP, lanes] for d in range(ch)] for total in totals
            ]
            for c in range(ch):
                place = min(c, ch - c)
                real, imag = parts[0][place], parts[1][place]
                if c % half:
                    sine_real, sine_imag = parts[0][half + place], parts[1][half + place]
                    if c < half:
                        real, imag = real + sine_imag, imag - sine_real
                    else:
                        real, imag = real - sine_imag, imag + sine_real
                gain_real, gain_imag = gains[c : c + 1], gains[ch + c : ch + c + 1]
                store(
                    first + index,
                    c,
                    gain_real * real - gain_imag * imag,
                    gain_real * imag + gain_imag * real,
                )


def levels_of(words):
    return [
        ((words >> 4) - 8).astype(jnp.float32).astype(jnp.bfloat16),
        ((words & 15) - 8).astype(jnp.float32).astype(jnp.bfloat16),
    ]


def own_kernel(main_ref, next_ref, gains_ref, weights_ref, after_ref, out_ref, zero_ref, held):
    step = pl.program_id(0)
    ch = out_ref.shape[0]
    zero_ref[...] = jnp.zeros_like(zero_ref)
    words = jnp.concatenate([main_ref[...], next_ref[...]], axis=0)

    def store(b, c, real, imag):
        held[c, b * 2 * STEP : (b + 1) * 2 * STEP, :] = jnp.concatenate([real, imag], axis=0).astype(held.dtype)

    spectra_of(weights_ref, levels_of(words), gains_ref[...], ch, store)
    for c in range(ch):
        out_ref[c, step] = held[c].T


def own_spectra(words, gains, weights, ch, spectra, after):
    count = words.shape[1]
    main = STEPS * STEP * ch
    steps = spectra // (STEPS * STEP)
    return pl.pallas_call(
        own_kernel,
        grid=(steps,),
        in_specs=[
            pl.BlockSpec((main, count), lambda i: (i, 0)),
            pl.BlockSpec((STEP * ch, count), lambda i: ((i + 1) * STEPS, 0)),
            pl.BlockSpec(gains.shape, lambda i: (0, 0)),
            pl.BlockSpec(weights.shape, lambda i: (0, 0)),
            pl.BlockSpec(memory_space=pl.ANY),
        ],
        out_specs=[
            pl.BlockSpec(memory_space=pltpu.VMEM),
            pl.BlockSpec((16, LANES), lambda i: (0, 0)),
        ],
        out_shape=[
            jax.ShapeDtypeStruct((ch, steps, count, 2 * STEPS * STEP), jnp.bfloat16),
            jax.ShapeDtypeStruct((16, LANES), jnp.bfloat16),
        ],
        scratch_shapes=[
            pltpu.VMEM((ch, 2 * STEPS * STEP, count), jnp.bfloat16),
        ],
        compiler_params=pltpu.CompilerParams(vmem_limit_bytes=12 << 20),
        cost_estimate=pl.CostEstimate(
            flops=4 * spectra * ch * 2 * SPAN * ch * count,
            bytes_accessed=4 * words.size + 4 * ch * spectra * count,
            transcendentals=0,
        ),
        name="own_spectra",
    )(words, words, gains, weights, after)


def select_kernel(last_rows, slots_ref, words_ref, parts_ref, *outs):
    step = pl.program_id(0)
    count, rows = words_ref.shape[1], slots_ref.shape[1]
    words = words_ref[...].astype(jnp.float32).astype(jnp.bfloat16)
    place = lax.broadcasted_iota(jnp.int32, (count, rows), 0)
    choice = jnp.where(slots_ref[...] == place, 1.0, 0.0).astype(jnp.bfloat16)
    taken = jnp.dot(words, choice, preferred_element_type=jnp.float32).astype(outs[0].dtype)
    for index, out_ref in enumerate(outs):
        out_ref[...] = taken[:, index * LANES : (index + 1) * LANES]

    @pl.when(step == pl.num_programs(0) - 1)
    def _():
        extra = parts_ref.shape[0]
        gains = jnp.dot(parts_ref[...], choice, preferred_element_type=jnp.float32).astype(outs[0].dtype)
        for index, out_ref in enumerate(outs):
            out_ref[last_rows : last_rows + extra, :] = gains[:, index * LANES : (index + 1) * LANES]
            left = out_ref.shape[0] - last_rows - extra
            out_ref[last_rows + extra :, :] = jnp.zeros((left, LANES), out_ref.dtype)


def select_rows(words, gains, slots, total):
    lines, count = words.shape
    rows = slots.shape[1]
    block = total // STEPS
    parts = jnp.concatenate([gains >> 4, gains & 15], axis=0).astype(jnp.bfloat16)
    return pl.pallas_call(
        functools.partial(select_kernel, lines - (STEPS - 1) * block),
        grid=(STEPS,),
        in_specs=[
            pl.BlockSpec((1, rows), lambda i: (0, 0)),
            pl.BlockSpec((block, count), lambda i: (i, 0)),
            pl.BlockSpec(parts.shape, lambda i: (0, 0)),
        ],
        out_specs=[pl.BlockSpec((block, LANES), lambda i: (i, 0))] * (rows // LANES),
        out_shape=[jax.ShapeDtypeStruct((total, LANES), jnp.bfloat16)] * (rows // LANES),
        compiler_params=pltpu.CompilerParams(vmem_limit_bytes=8 << 20),
        name="select_rows",
    )(slots, words, parts)


def swap(value, bit):
    pairs = [(index, index ^ bit) for index in range(lax.axis_size("feed"))]
    return lax.ppermute(value, "feed", pairs)


def side(bit):
    return lax.axis_index("feed") // bit % 2


def reduce_half(value, bit):
    size = value.shape[0] // 2
    keep = lax.dynamic_slice_in_dim(value, side(bit) * size, size, 0)
    send = lax.dynamic_slice_in_dim(value, (1 - side(bit)) * size, size, 0)
    return keep + swap(send, bit)


def gather_half(value, bit, buffer):
    size = value.shape[0]
    other = swap(value, bit)
    buffer = lax.dynamic_update_slice_in_dim(buffer, value, side(bit) * size, 0)
    return lax.dynamic_update_slice_in_dim(buffer, other, (1 - side(bit)) * size, 0)


def sum_over_feed(value, behind=None, work=None):
    half = reduce_half(value, 1)
    size = half.shape[0] // 2
    left, right = half[:size], half[size:]
    left_1, right_1 = reduce_half(left, 2), reduce_half(right, 4)
    left_2, right_2 = reduce_half(left_1, 4), reduce_half(right_1, 2)
    if behind is not None:
        left_2, right_2 = left_2 + behind, right_2 + behind
    left_3, right_3 = left_2 + swap(left_2, 8), right_2 + swap(right_2, 8)
    if work is not None:
        left_3 = left_3 + work(left_2)
    crossed = (left_3[0, 0] + right_3[0, 0]) * 0
    left_1, right_1 = gather_half(left_3, 4, left_1), gather_half(right_3, 2, right_1)
    left, right = gather_half(left_1, 2, left), gather_half(right_1, 4, right)
    half = jnp.concatenate([left, right], axis=0)
    return half, lambda: gather_half(half, 1, value), crossed


def rows_kernel(main_ref, next_ref, parts_ref, weights_ref, out_ref):
    step = pl.program_id(0)
    ch, rows = out_ref.shape[0], main_ref.shape[1]
    words = jnp.concatenate([main_ref[...], next_ref[...]], axis=0).astype(jnp.float32).astype(jnp.int32)
    parts = parts_ref[...].astype(jnp.float32)
    gains = parts[: 2 * ch] * 16.0 + parts[2 * ch :]

    def store(b, c, real, imag):
        spot = pl.ds(pl.multiple_of(step * (2 * STEPS * STEP), 2 * STEPS * STEP) + b * 2 * STEP, 2 * STEP)
        out_ref[c, spot, :rows] = jnp.concatenate([real, imag], axis=0).astype(out_ref.dtype)
        out_ref[c, spot, rows:] = jnp.concatenate([imag, -real], axis=0).astype(out_ref.dtype)

    spectra_of(weights_ref, levels_of(words), gains, ch, store)


def row_spectra(words, parts, weights, ch, spectra):
    rows = words.shape[1]
    main = STEPS * STEP * ch
    return pl.pallas_call(
        rows_kernel,
        grid=(spectra // (STEPS * STEP),),
        in_specs=[
            pl.BlockSpec((main, rows), lambda i: (i, 0)),
            pl.BlockSpec((STEP * ch, rows), lambda i: ((i + 1) * STEPS, 0)),
            pl.BlockSpec(parts.shape, lambda i: (0, 0)),
            pl.BlockSpec(weights.shape, lambda i: (0, 0)),
        ],
        out_specs=pl.BlockSpec(memory_space=pltpu.VMEM),
        out_shape=jax.ShapeDtypeStruct((ch, 2 * spectra, 2 * rows), jnp.bfloat16),
        compiler_params=pltpu.CompilerParams(vmem_limit_bytes=8 << 20),
        cost_estimate=pl.CostEstimate(
            flops=8 * spectra * ch * SPAN * ch * rows,
            bytes_accessed=2 * words.size + 8 * ch * spectra * rows,
            transcendentals=0,
        ),
        name="row_spectra",
    )(words, words, parts, weights)


def products_kernel(own_ref, left_ref, *refs):
    out_ref, done_ref = refs[-2:]
    done_ref[...] = jnp.zeros_like(done_ref)
    each, steps = out_ref.shape[0], own_ref.shape[1]
    for index in range(each):
        c = pl.program_id(0) * each + index
        spectra = jnp.concatenate([own_ref[c, part] for part in range(steps)], axis=1)
        products = jnp.dot(spectra, left_ref[c], preferred_element_type=jnp.float32)
        count = products.shape[0]
        largest = jnp.maximum(jnp.max(jnp.abs(products), axis=0, keepdims=True), 2.0**-60)
        power = jnp.floor(jnp.log2(largest))
        coded = jnp.clip(jnp.round(products * jnp.exp2(RANGE - power)), -32767.0, 32767.0)
        out_ref[index, :count, :] = coded.astype(jnp.int32).astype(jnp.int16)
        line = jnp.broadcast_to(power, (out_ref.shape[1] - count, power.shape[1]))
        out_ref[index, count:, :] = line.astype(jnp.int32).astype(jnp.int16)


def row_products(own, left, after):
    ch, steps, count, width = own.shape
    columns = left.shape[2]
    each = 4
    return pl.pallas_call(
        products_kernel,
        grid=(ch // each,),
        in_specs=[pl.BlockSpec(memory_space=pltpu.VMEM)] * 2 + [pl.BlockSpec(memory_space=pl.ANY)] * len(after),
        out_specs=[
            pl.BlockSpec((each, count + 16, columns), lambda i: (i, 0, 0)),
            pl.BlockSpec((16, LANES), lambda i: (0, 0)),
        ],
        out_shape=[
            pltpu.HBM((ch, count + 16, columns), jnp.int16),
            jax.ShapeDtypeStruct((16, LANES), jnp.bfloat16),
        ],
        compiler_params=pltpu.CompilerParams(vmem_limit_bytes=10 << 20),
        cost_estimate=pl.CostEstimate(
            flops=2 * left.size * count, bytes_accessed=2 * left.size + 2 * own.size, transcendentals=0
        ),
        name="row_products",
    )(own, left, *after)


def finish_kernel(scale, slot_ref, coded_ref, *refs):
    out_ref, products, tile, mixed = refs[-4:]
    step = pl.program_id(0)
    sources, lines, width = coded_ref.shape
    count = lines - 16
    pieces = width // LANES
    together = 8 // pieces

    @pl.when(step == 0)
    def _():
        for source in range(sources):
            power = coded_ref[source, count : count + 16, :][:1].astype(jnp.float32)
            values = coded_ref[source, :count, :].astype(jnp.float32) * (jnp.exp2(power - RANGE) * scale)
            for piece in range(pieces):
                products[pl.ds(source * count * pieces + piece, count, stride=pieces), :] = values[
                    :, piece * LANES : (piece + 1) * LANES
                ]

    for part in range(together):
        for i in range(LANES):
            slot = slot_ref[(step * together + part) * LANES + i]
            tile[i * pieces : (i + 1) * pieces, :] = products[
                pl.ds(pl.multiple_of(slot * pieces, pieces), pieces), :
            ]
        for piece in range(pieces):
            turned = tile[pl.ds(piece, LANES, stride=pieces), :].T
            mixed[pl.ds(part * pieces + piece, LANES, stride=8), :] = turned
    out_ref[...] = mixed[...].reshape(out_ref.shape)


def finish(coded, feed_slot, index, pieces, scale, before):
    sources, lines, width = coded.shape
    rows = width // 2
    feeds = sources * (lines - 16)
    columns = 2 * (feeds // LANES)
    earlier = [] if before is None else [before]
    return pl.pallas_call(
        functools.partial(finish_kernel, scale),
        grid=(columns // 8,),
        in_specs=[
            pl.BlockSpec(memory_space=pltpu.SMEM),
            pl.BlockSpec(memory_space=pltpu.VMEM),
        ]
        + [pl.BlockSpec(memory_space=pl.ANY)] * len(earlier),
        out_specs=pl.BlockSpec((rows, 8, LANES), lambda i: (index, i, 0)),
        out_shape=jax.ShapeDtypeStruct((pieces * rows, columns, LANES), jnp.float32),
        scratch_shapes=[
            pltpu.VMEM((feeds * width // LANES, LANES), jnp.float32),
            pltpu.VMEM((width, LANES), jnp.float32),
            pltpu.VMEM((8 * LANES, LANES), jnp.float32),
        ],
        input_output_aliases={2: 0} if earlier else {},
        compiler_params=pltpu.CompilerParams(vmem_limit_bytes=14 << 20),
        name="finish",
    )(feed_slot, coded, *earlier)


def through_rows(samples, gains, feed_slot):
    count, ch, frames = samples.shape
    spectra = frames - TAPS + 1
    pieces = ROWS // LANES
    lines = frames * ch
    unit = 16 * STEPS * 2
    total = pl.cdiv(lines + 4 * ch, unit) * unit
    words = jnp.transpose(samples, (2, 1, 0)).reshape(lines, count)
    scales = gains.reshape(2 * ch, count)
    weights = jnp.asarray(filter_weights(ch))
    slots = (feed_slot[:ROWS] - lax.axis_index("feed") * count).reshape(1, ROWS)
    picked = select_rows(pltpu.with_memory_space_constraint(words, pltpu.HBM), scales, slots, total)
    held = []

    def work(after):
        own, zero = own_spectra(words, scales.astype(jnp.float32), weights, ch, spectra, after)
        held.append(own)
        return zero[0, 0]

    sums, behind = [], None
    for index, value in enumerate(picked):
        sums.append(sum_over_feed(value, behind, None if index else work))
        behind = sums[-1][2]
    own = held[0]
    out, after = None, [sums[-1][0]]
    for index in range(pieces):
        rows = sums[index][1]()
        parts = rows[lines : lines + 4 * ch]
        left = row_spectra(rows, parts, weights, ch, spectra)
        coded, done = row_products(own, left, after)
        after = [done]
        moved = lax.all_to_all(coded, "feed", split_axis=0, concat_axis=0, tiled=True)
        out = finish(moved, feed_slot, index, pieces, 1.0 / spectra, out)
    feeds = feed_slot.shape[0]
    out = out.reshape(ROWS, feeds // LANES, 2, LANES)
    return jnp.transpose(out, (0, 2, 1, 3)).reshape(ROWS, 2, feeds)


def body(samples, gains, feed_slot):
    count, ch, frames = samples.shape
    spectra = frames - TAPS + 1
    even = count % LANES == 0 and spectra % (STEPS * STEP) == 0 and ch % STEPS == 0
    if lax.axis_size("feed") == ch == 16 and even:
        return through_rows(samples, gains, feed_slot)
    return through_spectra(samples, gains, feed_slot)


def solution(mesh):
    return jax.shard_map(
        body,
        mesh=mesh,
        in_specs=(P(("band", "feed"), None, None), P(None, "band", "feed"), P()),
        out_specs=P(("band", "feed"), None, None),
        check_vma=False,
    )
```

```python
import functools
import math

import jax
import jax.numpy as jnp
import numpy as np
from jax import lax
from jax.experimental import pallas as pl
from jax.experimental.pallas import tpu as pltpu
from jax.sharding import PartitionSpec as P

TAPS = 8
ROWS = 256
LANES = 128


def filter_taps(ch):
    length = TAPS * ch
    place = np.arange(length, dtype=np.float64)
    window = 0.5 - 0.5 * np.cos(2.0 * math.pi * place / (length - 1))
    return (np.sinc((place - 0.5 * (length - 1)) / ch) * window).reshape(TAPS, ch)


def twiddle(value, turn):
    real, imag = value
    if turn == 0:
        return value
    if turn == 0.25:
        return imag, -real
    half = math.sqrt(0.5)
    if turn == 0.125:
        return half * (real + imag), half * (imag - real)
    if turn == 0.375:
        return half * (imag - real), -half * (real + imag)
    c, s = math.cos(2.0 * math.pi * turn), math.sin(2.0 * math.pi * turn)
    return c * real + s * imag, c * imag - s * real


def fft(values):
    count = len(values)
    if count == 1:
        return values
    even, odd = fft(values[0::2]), fft(values[1::2])
    low, high = [], []
    for index in range(count // 2):
        real, imag = twiddle(odd[index], index / count)
        low.append((even[index][0] + real, even[index][1] + imag))
        high.append((even[index][0] - real, even[index][1] - imag))
    return low + high


def channel_kernel(taps, *refs):
    *samples_refs, gains_ref, out_ref, filtered = refs
    ch, block, width = out_ref.shape
    spectra = width // 2
    padded = len(samples_refs) * LANES
    for k in range(ch):
        words = jnp.concatenate(
            [ref[pl.ds(k, block, stride=ch), :] for ref in samples_refs], axis=1
        )
        levels = ((words >> 4) - 8, (words & 15) - 8)
        for part in range(2):
            value = levels[part].astype(jnp.float32)
            shifted = [value] + [pltpu.roll(value, padded - t, 1) for t in range(1, TAPS // 2)]
            near = float(taps[0, k]) * shifted[0]
            far = float(taps[TAPS // 2, k]) * shifted[0]
            for t in range(1, TAPS // 2):
                near = near + float(taps[t, k]) * shifted[t]
                far = far + float(taps[t + TAPS // 2, k]) * shifted[t]
            total = near + pltpu.roll(far, padded - TAPS // 2, 1)
            filtered[2 * k + part] = total[:, :spectra]
    for row in range(0, block, 8):
        gains = gains_ref[row : row + 8, :]
        for lane in range(0, spectra, LANES):
            spot = (slice(row, row + 8), slice(lane, lane + LANES))
            values = [(filtered[2 * k][spot], filtered[2 * k + 1][spot]) for k in range(ch)]
            for c, (real, imag) in enumerate(fft(values)):
                gain_real = gains[:, c : c + 1]
                gain_imag = gains[:, ch + c : ch + c + 1]
                out_ref[c, row : row + 8, lane : lane + LANES] = (
                    gain_real * real - gain_imag * imag
                ).astype(out_ref.dtype)
                out_ref[c, row : row + 8, spectra + lane : spectra + lane + LANES] = (
                    gain_real * imag + gain_imag * real
                ).astype(out_ref.dtype)


def channelize(samples, gains):
    count, ch, frames = samples.shape
    spectra = frames - TAPS + 1
    block = 16
    pieces = pl.cdiv(frames, LANES)
    scale = 0.125 / math.sqrt(ch) / 2048.0
    taps = (filter_taps(ch) * scale).astype(np.float32)
    return pl.pallas_call(
        functools.partial(channel_kernel, taps),
        grid=(count // block,),
        in_specs=[
            pl.BlockSpec((block * ch, LANES), functools.partial(lambda piece, i: (i, piece), piece))
            for piece in range(pieces)
        ]
        + [pl.BlockSpec((block, 2 * ch), lambda i: (i, 0))],
        out_specs=pl.BlockSpec((ch, block, 2 * spectra), lambda i: (0, i, 0)),
        out_shape=jax.ShapeDtypeStruct((ch, count, 2 * spectra), jnp.bfloat16),
        scratch_shapes=[pltpu.VMEM((2 * ch, block, spectra), jnp.float32)],
        compiler_params=pltpu.CompilerParams(vmem_limit_bytes=32 << 20),
        name="channelize",
    )(*[samples.reshape(count * ch, frames)] * pieces, gains)


def correlate_kernel(scale, slot_ref, row_ref, data_ref, out_ref, products, tile):
    feeds, width = data_ref.shape
    spectra = width // 2
    rows = row_ref.shape[0]
    pieces = 2 * rows // LANES
    step = 256
    picked = jnp.zeros((rows, width), jnp.float32)
    for first in range(0, feeds, 512):
        place = lax.broadcasted_iota(jnp.int32, (rows, 512), 1) + first
        choice = jnp.where(row_ref[...] == place, 1.0, 0.0).astype(jnp.bfloat16)
        picked = picked + jnp.dot(
            choice, data_ref[first : first + 512, :], preferred_element_type=jnp.float32
        )
    left = jnp.concatenate(
        [
            picked,
            jnp.concatenate([picked[:, spectra:], -picked[:, :spectra]], axis=1),
        ],
        axis=0,
    ).astype(jnp.bfloat16)

    @pl.loop(0, feeds // step)
    def _(i):
        first = pl.multiple_of(i * step, step)
        result = lax.dot_general(
            data_ref[pl.ds(first, step), :],
            left,
            (((1,), (1,)), ((), ())),
            preferred_element_type=jnp.float32,
        )
        for piece in range(pieces):
            products[pl.ds(first * pieces + piece, step, stride=pieces), :] = (
                result[:, piece * LANES : (piece + 1) * LANES] * scale
            )

    lines = 2 * (feeds // LANES)

    @pl.loop(0, feeds // LANES)
    def _(j):
        @pl.loop(0, LANES, unroll=16)
        def _(i):
            slot = slot_ref[j * LANES + i]
            tile[pl.ds(pl.multiple_of(i * pieces, pieces), pieces), :] = products[
                pl.ds(pl.multiple_of(slot * pieces, pieces), pieces), :
            ]

        for piece in range(pieces):
            part, first = divmod(piece * LANES, rows)
            turned = tile[pl.ds(piece, LANES, stride=pieces), :].T
            out_ref[pl.ds(first * lines + 2 * j + part, LANES, stride=lines), :] = turned


def correlate(data, feed_slot, first, rows):
    feeds, width = data.shape
    row_slots = lax.dynamic_slice_in_dim(feed_slot, first, rows, 0).reshape(rows, 1)
    lines = 2 * (feeds // LANES)
    out = pl.pallas_call(
        functools.partial(correlate_kernel, 2.0 / width),
        in_specs=[
            pl.BlockSpec(memory_space=pltpu.SMEM),
            pl.BlockSpec(memory_space=pltpu.VMEM),
            pl.BlockSpec(memory_space=pltpu.VMEM),
        ],
        out_specs=pl.BlockSpec(memory_space=pltpu.VMEM),
        out_shape=jax.ShapeDtypeStruct((rows * lines, LANES), jnp.float32),
        scratch_shapes=[
            pltpu.VMEM((feeds * 2 * rows // LANES, LANES), jnp.float32),
            pltpu.VMEM((LANES * 2 * rows // LANES, LANES), jnp.float32),
        ],
        compiler_params=pltpu.CompilerParams(vmem_limit_bytes=48 << 20),
        name="correlate",
    )(feed_slot, row_slots, data)
    out = out.reshape(rows, feeds // LANES, 2, LANES)
    return jnp.transpose(out, (0, 2, 1, 3)).reshape(rows, 2, feeds)


def through_spectra(samples, gains, feed_slot):
    count, ch, _ = samples.shape
    groups = lax.axis_size("feed") // ch
    first = lax.axis_index("feed") % groups * ROWS
    scales = jnp.transpose(gains, (2, 0, 1)).reshape(count, 2 * ch).astype(jnp.float32)
    spectra = channelize(samples, scales)
    width = spectra.shape[2]
    outgoing = jnp.broadcast_to(spectra[:, None], (ch, groups, count, width))
    outgoing = outgoing.reshape(ch * groups, count, width)
    moved = lax.all_to_all(outgoing, "feed", split_axis=0, concat_axis=0, tiled=True)
    return correlate(moved.reshape(-1, width), feed_slot, first, ROWS)


STEP = 8
SPAN = 16
STEPS = 8
RANGE = 14
EXTRA = 8


def filter_weights(ch):
    taps = filter_taps(ch) * (0.125 / math.sqrt(ch) / 2048.0)
    half = ch // 2
    weights = np.zeros((ch, STEP, SPAN, ch))
    angle = 2.0 * math.pi * (np.arange(half + 1)[:, None] * np.arange(ch)[None, :] % ch) / ch
    sums = np.concatenate([np.cos(angle), np.sin(angle[1:half])], axis=0)
    for spectrum in range(STEP):
        for t in range(TAPS):
            weights[:, spectrum, spectrum + t] = taps[t] * sums
    weights = weights.reshape(ch * STEP, SPAN * ch)
    high = weights.astype(jnp.bfloat16)
    low = (weights - high.astype(np.float64)).astype(jnp.bfloat16)
    return np.concatenate([high, low])


def spectra_of(weights_ref, levels, gains, ch, store):
    count = levels[0].shape[1]
    half, size = ch // 2, ch * STEP
    beside = max(1, 256 // count)
    for first in range(0, STEPS, beside):
        totals = []
        for level in levels:
            slabs = [level[b * size : b * size + SPAN * ch] for b in range(first, first + beside)]
            slab = jnp.concatenate(slabs, axis=1) if beside > 1 else slabs[0]
            both = jnp.dot(weights_ref[...], slab, preferred_element_type=jnp.float32)
            totals.append(both[:size] + both[size:])
        for index in range(beside):
            lanes = slice(index * count, (index + 1) * count)
            parts = [
                [total[d * STEP : (d + 1) * STEP, lanes] for d in range(ch)] for total in totals
            ]
            for c in range(ch):
                place = min(c, ch - c)
                real, imag = parts[0][place], parts[1][place]
                if c % half:
                    sine_real, sine_imag = parts[0][half + place], parts[1][half + place]
                    if c < half:
                        real, imag = real + sine_imag, imag - sine_real
                    else:
                        real, imag = real - sine_imag, imag + sine_real
                gain_real, gain_imag = gains[c : c + 1], gains[ch + c : ch + c + 1]
                store(
                    first + index,
                    c,
                    gain_real * real - gain_imag * imag,
                    gain_real * imag + gain_imag * real,
                )


def levels_of(words):
    return [
        ((words >> 4) - 8).astype(jnp.float32).astype(jnp.bfloat16),
        ((words & 15) - 8).astype(jnp.float32).astype(jnp.bfloat16),
    ]


def own_kernel(main_ref, next_ref, gains_ref, weights_ref, after_ref, out_ref, zero_ref, held):
    step = pl.program_id(0)
    ch = out_ref.shape[0]
    zero_ref[...] = jnp.zeros_like(zero_ref)
    words = jnp.concatenate([main_ref[...], next_ref[...]], axis=0)

    def store(b, c, real, imag):
        held[c, b * 2 * STEP : (b + 1) * 2 * STEP, :] = jnp.concatenate([real, imag], axis=0).astype(held.dtype)

    spectra_of(weights_ref, levels_of(words), gains_ref[...], ch, store)
    for c in range(ch):
        out_ref[c, step] = held[c].T


def own_spectra(words, gains, weights, ch, spectra, after):
    count = words.shape[1]
    main = STEPS * STEP * ch
    steps = spectra // (STEPS * STEP)
    return pl.pallas_call(
        own_kernel,
        grid=(steps,),
        in_specs=[
            pl.BlockSpec((main, count), lambda i: (i, 0)),
            pl.BlockSpec((STEP * ch, count), lambda i: ((i + 1) * STEPS, 0)),
            pl.BlockSpec(gains.shape, lambda i: (0, 0)),
            pl.BlockSpec(weights.shape, lambda i: (0, 0)),
            pl.BlockSpec(memory_space=pl.ANY),
        ],
        out_specs=[
            pl.BlockSpec(memory_space=pltpu.VMEM),
            pl.BlockSpec((16, LANES), lambda i: (0, 0)),
        ],
        out_shape=[
            jax.ShapeDtypeStruct((ch, steps, count, 2 * STEPS * STEP), jnp.bfloat16),
            jax.ShapeDtypeStruct((16, LANES), jnp.bfloat16),
        ],
        scratch_shapes=[
            pltpu.VMEM((ch, 2 * STEPS * STEP, count), jnp.bfloat16),
        ],
        compiler_params=pltpu.CompilerParams(vmem_limit_bytes=12 << 20),
        cost_estimate=pl.CostEstimate(
            flops=4 * spectra * ch * 2 * SPAN * ch * count,
            bytes_accessed=4 * words.size + 4 * ch * spectra * count,
            transcendentals=0,
        ),
        name="own_spectra",
    )(words, words, gains, weights, after)


def select_kernel(last_rows, place_ref, slots_ref, words_ref, gains_ref, *outs):
    step = pl.program_id(0)
    count, rows = words_ref.shape[1], len(outs) * LANES
    words = words_ref[...].astype(jnp.float32).astype(jnp.bfloat16)
    place = lax.broadcasted_iota(jnp.int32, (count, rows), 0) + place_ref[0] * count
    slots = jnp.concatenate([slots_ref[index : index + 1, :] for index in range(len(outs))], axis=1)
    choice = jnp.where(slots == place, 1.0, 0.0).astype(jnp.bfloat16)
    taken = jnp.dot(words, choice, preferred_element_type=jnp.float32).astype(outs[0].dtype)
    for index, out_ref in enumerate(outs):
        out_ref[...] = taken[:, index * LANES : (index + 1) * LANES]

    @pl.when(step == pl.num_programs(0) - 1)
    def _():
        gains = gains_ref[...]
        parts = jnp.concatenate([gains >> 4, gains & 15], axis=0).astype(jnp.float32).astype(jnp.bfloat16)
        extra = parts.shape[0]
        gains = jnp.dot(parts, choice, preferred_element_type=jnp.float32).astype(outs[0].dtype)
        for index, out_ref in enumerate(outs):
            out_ref[last_rows : last_rows + extra, :] = gains[:, index * LANES : (index + 1) * LANES]
            left = out_ref.shape[0] - last_rows - extra
            out_ref[last_rows + extra :, :] = jnp.zeros((left, LANES), out_ref.dtype)


def select_rows(place, words, gains, slots, rows, total):
    lines, count = words.shape
    block = total // STEPS
    return pl.pallas_call(
        functools.partial(select_kernel, lines - (STEPS - 1) * block),
        grid=(STEPS,),
        in_specs=[
            pl.BlockSpec(memory_space=pltpu.SMEM),
            pl.BlockSpec((8, LANES), lambda i: (0, 0)),
            pl.BlockSpec((block, count), lambda i: (i, 0)),
            pl.BlockSpec(gains.shape, lambda i: (0, 0)),
        ],
        out_specs=[pl.BlockSpec((block, LANES), lambda i: (i, 0))] * (rows // LANES),
        out_shape=[jax.ShapeDtypeStruct((total, LANES), jnp.bfloat16)] * (rows // LANES),
        compiler_params=pltpu.CompilerParams(vmem_limit_bytes=8 << 20),
        name="select_rows",
    )(place, slots, words, gains)


def swap(value, bit):
    pairs = [(index, index ^ bit) for index in range(lax.axis_size("feed"))]
    return lax.ppermute(value, "feed", pairs)


def side(bit):
    return lax.axis_index("feed") // bit % 2


def reduce_half(value, bit):
    size = value.shape[0] // 2
    keep = lax.dynamic_slice_in_dim(value, side(bit) * size, size, 0)
    send = lax.dynamic_slice_in_dim(value, (1 - side(bit)) * size, size, 0)
    return keep + swap(send, bit)


def gather_half(value, bit, buffer):
    size = value.shape[0]
    other = swap(value, bit)
    buffer = lax.dynamic_update_slice_in_dim(buffer, value, side(bit) * size, 0)
    return lax.dynamic_update_slice_in_dim(buffer, other, (1 - side(bit)) * size, 0)


def sum_over_feed(value, work=None):
    half = reduce_half(value, 1)
    size = half.shape[0] // 2
    left, right = half[:size], half[size:]
    left_1, right_1 = reduce_half(left, 2), reduce_half(right, 4)
    left_2, right_2 = reduce_half(left_1, 4), reduce_half(right_1, 2)
    left_3, right_3 = left_2 + swap(left_2, 8), right_2 + swap(right_2, 8)
    if work is not None:
        left_3 = left_3 + work(left_2)
    left_1, right_1 = gather_half(left_3, 4, left_1), gather_half(right_3, 2, right_1)
    left, right = gather_half(left_1, 2, left), gather_half(right_1, 4, right)
    half = jnp.concatenate([left, right], axis=0)
    return half, lambda: gather_half(half, 1, value)


def rows_kernel(main_ref, next_ref, parts_ref, weights_ref, out_ref):
    step = pl.program_id(0)
    ch, rows = out_ref.shape[0], main_ref.shape[1]
    words = jnp.concatenate([main_ref[...], next_ref[...]], axis=0).astype(jnp.float32).astype(jnp.int32)
    parts = parts_ref[...].astype(jnp.float32)
    gains = parts[: 2 * ch] * 16.0 + parts[2 * ch :]

    def store(b, c, real, imag):
        spot = pl.ds(pl.multiple_of(step * (2 * STEPS * STEP), 2 * STEPS * STEP) + b * 2 * STEP, 2 * STEP)
        out_ref[c, spot, :rows] = jnp.concatenate([real, imag], axis=0).astype(out_ref.dtype)
        out_ref[c, spot, rows:] = jnp.concatenate([imag, -real], axis=0).astype(out_ref.dtype)

    spectra_of(weights_ref, levels_of(words), gains, ch, store)


def row_spectra(words, parts, weights, ch, spectra):
    rows = words.shape[1]
    main = STEPS * STEP * ch
    return pl.pallas_call(
        rows_kernel,
        grid=(spectra // (STEPS * STEP),),
        in_specs=[
            pl.BlockSpec((main, rows), lambda i: (i, 0)),
            pl.BlockSpec((STEP * ch, rows), lambda i: ((i + 1) * STEPS, 0)),
            pl.BlockSpec(parts.shape, lambda i: (0, 0)),
            pl.BlockSpec(weights.shape, lambda i: (0, 0)),
        ],
        out_specs=pl.BlockSpec(memory_space=pltpu.VMEM),
        out_shape=jax.ShapeDtypeStruct((ch, 2 * spectra, 2 * rows), jnp.bfloat16),
        compiler_params=pltpu.CompilerParams(vmem_limit_bytes=8 << 20),
        cost_estimate=pl.CostEstimate(
            flops=8 * spectra * ch * SPAN * ch * rows,
            bytes_accessed=2 * words.size + 8 * ch * spectra * rows,
            transcendentals=0,
        ),
        name="row_spectra",
    )(words, words, parts, weights)


def products_kernel(own_ref, left_ref, *refs):
    out_ref, done_ref = refs[-2:]
    done_ref[...] = jnp.zeros_like(done_ref)
    each, steps = out_ref.shape[0], own_ref.shape[1]
    for index in range(each):
        c = pl.program_id(0) * each + index
        spectra = jnp.concatenate([own_ref[c, part] for part in range(steps)], axis=1)
        products = jnp.dot(spectra, left_ref[c], preferred_element_type=jnp.float32)
        count = products.shape[0]
        largest = jnp.maximum(jnp.max(jnp.abs(products), axis=0, keepdims=True), 2.0**-60)
        power = jnp.floor(jnp.log2(largest))
        coded = jnp.clip(jnp.round(products * jnp.exp2(RANGE - power)), -32767.0, 32767.0)
        out_ref[index, :count, :] = coded.astype(jnp.int32).astype(jnp.int16)
        line = jnp.broadcast_to(power, (out_ref.shape[1] - count, power.shape[1]))
        out_ref[index, count:, :] = line.astype(jnp.int32).astype(jnp.int16)


def row_products(own, left, after):
    ch, steps, count, width = own.shape
    columns = left.shape[2]
    each = 4
    return pl.pallas_call(
        products_kernel,
        grid=(ch // each,),
        in_specs=[pl.BlockSpec(memory_space=pltpu.VMEM)] * 2 + [pl.BlockSpec(memory_space=pl.ANY)] * len(after),
        out_specs=[
            pl.BlockSpec((each, count + EXTRA, columns), lambda i: (i, 0, 0)),
            pl.BlockSpec((16, LANES), lambda i: (0, 0)),
        ],
        out_shape=[
            pltpu.HBM((ch, count + EXTRA, columns), jnp.int16),
            jax.ShapeDtypeStruct((16, LANES), jnp.bfloat16),
        ],
        compiler_params=pltpu.CompilerParams(vmem_limit_bytes=10 << 20),
        cost_estimate=pl.CostEstimate(
            flops=2 * left.size * count, bytes_accessed=2 * left.size + 2 * own.size, transcendentals=0
        ),
        name="row_products",
    )(own, left, *after)


def finish_kernel(scale, slot_ref, coded_ref, *refs):
    out_ref, products, tile, mixed = refs[-4:]
    step = pl.program_id(0)
    sources, lines, width = coded_ref.shape
    count = lines - EXTRA
    pieces = width // LANES
    together = 8 // pieces

    @pl.when(step == 0)
    def _():
        for source in range(sources):
            power = coded_ref[source, count:, :][:1].astype(jnp.float32)
            values = coded_ref[source, :count, :].astype(jnp.float32) * (jnp.exp2(power - RANGE) * scale)
            for piece in range(pieces):
                products[pl.ds(source * count * pieces + piece, count, stride=pieces), :] = values[
                    :, piece * LANES : (piece + 1) * LANES
                ]

    for part in range(together):
        for i in range(LANES):
            line = slot_ref[(step * together + part) * LANES + i]
            tile[i * pieces : (i + 1) * pieces, :] = products[pl.ds(pl.multiple_of(line, pieces), pieces), :]
        for piece in range(pieces):
            turned = tile[pl.ds(piece, LANES, stride=pieces), :].T
            mixed[pl.ds(part * pieces + piece, LANES, stride=8), :] = turned
    out_ref[...] = mixed[...].reshape(out_ref.shape)


def finish(coded, places, index, pieces, scale, before):
    sources, lines, width = coded.shape
    rows = width // 2
    feeds = sources * (lines - EXTRA)
    columns = 2 * (feeds // LANES)
    earlier = [] if before is None else [before]
    return pl.pallas_call(
        functools.partial(finish_kernel, scale),
        grid=(columns // 8,),
        in_specs=[
            pl.BlockSpec(memory_space=pltpu.SMEM),
            pl.BlockSpec(memory_space=pltpu.VMEM),
        ]
        + [pl.BlockSpec(memory_space=pl.ANY)] * len(earlier),
        out_specs=pl.BlockSpec((rows, 8, LANES), lambda i: (index, i, 0)),
        out_shape=jax.ShapeDtypeStruct((pieces * rows, columns, LANES), jnp.float32),
        scratch_shapes=[
            pltpu.VMEM((feeds * width // LANES, LANES), jnp.float32),
            pltpu.VMEM((width, LANES), jnp.float32),
            pltpu.VMEM((8 * LANES, LANES), jnp.float32),
        ],
        input_output_aliases={2: 0} if earlier else {},
        compiler_params=pltpu.CompilerParams(vmem_limit_bytes=14 << 20),
        name="finish",
    )(places, coded, *earlier)


def through_rows(samples, gains, feed_slot):
    count, ch, frames = samples.shape
    spectra = frames - TAPS + 1
    pieces = ROWS // LANES
    lines = frames * ch
    unit = 16 * STEPS * 2
    total = pl.cdiv(lines + 4 * ch, unit) * unit
    words = jnp.transpose(samples, (2, 1, 0)).reshape(lines, count)
    scales = gains.reshape(2 * ch, count)
    weights = jnp.asarray(filter_weights(ch))
    place = lax.axis_index("feed").reshape(1)
    picked = select_rows(place, words, scales, feed_slot.reshape(-1, LANES), ROWS, total)
    held = []

    def work(after):
        own, zero = own_spectra(words, scales.astype(jnp.float32), weights, ch, spectra, after)
        held.append(own)
        return zero[0, 0]

    sums = [sum_over_feed(value, None if index else work) for index, value in enumerate(picked)]
    own = held[0]
    out, after = None, [sums[-1][0]]
    for index in range(pieces):
        rows = sums[index][1]()
        parts = rows[lines : lines + 4 * ch]
        left = row_spectra(rows, parts, weights, ch, spectra)
        coded, done = row_products(own, left, after)
        after = [done]
        moved = lax.all_to_all(coded, "feed", split_axis=0, concat_axis=0, tiled=True)
        out = finish(moved, feed_slot * 2, index, pieces, 1.0 / spectra, out)
    feeds = feed_slot.shape[0]
    out = out.reshape(ROWS, feeds // LANES, 2, LANES)
    return jnp.transpose(out, (0, 2, 1, 3)).reshape(ROWS, 2, feeds)


def body(samples, gains, feed_slot):
    count, ch, frames = samples.shape
    spectra = frames - TAPS + 1
    even = count % LANES == 0 and spectra % (STEPS * STEP) == 0 and ch % STEPS == 0
    if lax.axis_size("feed") == ch == 16 and even:
        return through_rows(samples, gains, feed_slot)
    return through_spectra(samples, gains, feed_slot)


def solution(mesh):
    return jax.shard_map(
        body,
        mesh=mesh,
        in_specs=(P(("band", "feed"), None, None), P(None, "band", "feed"), P()),
        out_specs=P(("band", "feed"), None, None),
        check_vma=False,
    )
```

```python
import functools
import math

import jax
import jax.numpy as jnp
import numpy as np
from jax import lax
from jax.experimental import pallas as pl
from jax.experimental.pallas import tpu as pltpu
from jax.sharding import PartitionSpec as P

TAPS = 8
ROWS = 256
LANES = 128


def filter_taps(ch):
    length = TAPS * ch
    place = np.arange(length, dtype=np.float64)
    window = 0.5 - 0.5 * np.cos(2.0 * math.pi * place / (length - 1))
    return (np.sinc((place - 0.5 * (length - 1)) / ch) * window).reshape(TAPS, ch)


def twiddle(value, turn):
    real, imag = value
    if turn == 0:
        return value
    if turn == 0.25:
        return imag, -real
    half = math.sqrt(0.5)
    if turn == 0.125:
        return half * (real + imag), half * (imag - real)
    if turn == 0.375:
        return half * (imag - real), -half * (real + imag)
    c, s = math.cos(2.0 * math.pi * turn), math.sin(2.0 * math.pi * turn)
    return c * real + s * imag, c * imag - s * real


def fft(values):
    count = len(values)
    if count == 1:
        return values
    even, odd = fft(values[0::2]), fft(values[1::2])
    low, high = [], []
    for index in range(count // 2):
        real, imag = twiddle(odd[index], index / count)
        low.append((even[index][0] + real, even[index][1] + imag))
        high.append((even[index][0] - real, even[index][1] - imag))
    return low + high


def channel_kernel(taps, *refs):
    *samples_refs, gains_ref, out_ref, filtered = refs
    ch, block, width = out_ref.shape
    spectra = width // 2
    padded = len(samples_refs) * LANES
    for k in range(ch):
        words = jnp.concatenate(
            [ref[pl.ds(k, block, stride=ch), :] for ref in samples_refs], axis=1
        )
        levels = ((words >> 4) - 8, (words & 15) - 8)
        for part in range(2):
            value = levels[part].astype(jnp.float32)
            shifted = [value] + [pltpu.roll(value, padded - t, 1) for t in range(1, TAPS // 2)]
            near = float(taps[0, k]) * shifted[0]
            far = float(taps[TAPS // 2, k]) * shifted[0]
            for t in range(1, TAPS // 2):
                near = near + float(taps[t, k]) * shifted[t]
                far = far + float(taps[t + TAPS // 2, k]) * shifted[t]
            total = near + pltpu.roll(far, padded - TAPS // 2, 1)
            filtered[2 * k + part] = total[:, :spectra]
    for row in range(0, block, 8):
        gains = gains_ref[row : row + 8, :]
        for lane in range(0, spectra, LANES):
            spot = (slice(row, row + 8), slice(lane, lane + LANES))
            values = [(filtered[2 * k][spot], filtered[2 * k + 1][spot]) for k in range(ch)]
            for c, (real, imag) in enumerate(fft(values)):
                gain_real = gains[:, c : c + 1]
                gain_imag = gains[:, ch + c : ch + c + 1]
                out_ref[c, row : row + 8, lane : lane + LANES] = (
                    gain_real * real - gain_imag * imag
                ).astype(out_ref.dtype)
                out_ref[c, row : row + 8, spectra + lane : spectra + lane + LANES] = (
                    gain_real * imag + gain_imag * real
                ).astype(out_ref.dtype)


def channelize(samples, gains):
    count, ch, frames = samples.shape
    spectra = frames - TAPS + 1
    block = 16
    pieces = pl.cdiv(frames, LANES)
    scale = 0.125 / math.sqrt(ch) / 2048.0
    taps = (filter_taps(ch) * scale).astype(np.float32)
    return pl.pallas_call(
        functools.partial(channel_kernel, taps),
        grid=(count // block,),
        in_specs=[
            pl.BlockSpec((block * ch, LANES), functools.partial(lambda piece, i: (i, piece), piece))
            for piece in range(pieces)
        ]
        + [pl.BlockSpec((block, 2 * ch), lambda i: (i, 0))],
        out_specs=pl.BlockSpec((ch, block, 2 * spectra), lambda i: (0, i, 0)),
        out_shape=jax.ShapeDtypeStruct((ch, count, 2 * spectra), jnp.bfloat16),
        scratch_shapes=[pltpu.VMEM((2 * ch, block, spectra), jnp.float32)],
        compiler_params=pltpu.CompilerParams(vmem_limit_bytes=32 << 20),
        name="channelize",
    )(*[samples.reshape(count * ch, frames)] * pieces, gains)


def correlate_kernel(scale, slot_ref, row_ref, data_ref, out_ref, products, tile):
    feeds, width = data_ref.shape
    spectra = width // 2
    rows = row_ref.shape[0]
    pieces = 2 * rows // LANES
    step = 256
    picked = jnp.zeros((rows, width), jnp.float32)
    for first in range(0, feeds, 512):
        place = lax.broadcasted_iota(jnp.int32, (rows, 512), 1) + first
        choice = jnp.where(row_ref[...] == place, 1.0, 0.0).astype(jnp.bfloat16)
        picked = picked + jnp.dot(
            choice, data_ref[first : first + 512, :], preferred_element_type=jnp.float32
        )
    left = jnp.concatenate(
        [
            picked,
            jnp.concatenate([picked[:, spectra:], -picked[:, :spectra]], axis=1),
        ],
        axis=0,
    ).astype(jnp.bfloat16)

    @pl.loop(0, feeds // step)
    def _(i):
        first = pl.multiple_of(i * step, step)
        result = lax.dot_general(
            data_ref[pl.ds(first, step), :],
            left,
            (((1,), (1,)), ((), ())),
            preferred_element_type=jnp.float32,
        )
        for piece in range(pieces):
            products[pl.ds(first * pieces + piece, step, stride=pieces), :] = (
                result[:, piece * LANES : (piece + 1) * LANES] * scale
            )

    lines = 2 * (feeds // LANES)

    @pl.loop(0, feeds // LANES)
    def _(j):
        @pl.loop(0, LANES, unroll=16)
        def _(i):
            slot = slot_ref[j * LANES + i]
            tile[pl.ds(pl.multiple_of(i * pieces, pieces), pieces), :] = products[
                pl.ds(pl.multiple_of(slot * pieces, pieces), pieces), :
            ]

        for piece in range(pieces):
            part, first = divmod(piece * LANES, rows)
            turned = tile[pl.ds(piece, LANES, stride=pieces), :].T
            out_ref[pl.ds(first * lines + 2 * j + part, LANES, stride=lines), :] = turned


def correlate(data, feed_slot, first, rows):
    feeds, width = data.shape
    row_slots = lax.dynamic_slice_in_dim(feed_slot, first, rows, 0).reshape(rows, 1)
    lines = 2 * (feeds // LANES)
    out = pl.pallas_call(
        functools.partial(correlate_kernel, 2.0 / width),
        in_specs=[
            pl.BlockSpec(memory_space=pltpu.SMEM),
            pl.BlockSpec(memory_space=pltpu.VMEM),
            pl.BlockSpec(memory_space=pltpu.VMEM),
        ],
        out_specs=pl.BlockSpec(memory_space=pltpu.VMEM),
        out_shape=jax.ShapeDtypeStruct((rows * lines, LANES), jnp.float32),
        scratch_shapes=[
            pltpu.VMEM((feeds * 2 * rows // LANES, LANES), jnp.float32),
            pltpu.VMEM((LANES * 2 * rows // LANES, LANES), jnp.float32),
        ],
        compiler_params=pltpu.CompilerParams(vmem_limit_bytes=48 << 20),
        name="correlate",
    )(feed_slot, row_slots, data)
    out = out.reshape(rows, feeds // LANES, 2, LANES)
    return jnp.transpose(out, (0, 2, 1, 3)).reshape(rows, 2, feeds)


def through_spectra(samples, gains, feed_slot):
    count, ch, _ = samples.shape
    groups = lax.axis_size("feed") // ch
    first = lax.axis_index("feed") % groups * ROWS
    scales = jnp.transpose(gains, (2, 0, 1)).reshape(count, 2 * ch).astype(jnp.float32)
    spectra = channelize(samples, scales)
    width = spectra.shape[2]
    outgoing = jnp.broadcast_to(spectra[:, None], (ch, groups, count, width))
    outgoing = outgoing.reshape(ch * groups, count, width)
    moved = lax.all_to_all(outgoing, "feed", split_axis=0, concat_axis=0, tiled=True)
    return correlate(moved.reshape(-1, width), feed_slot, first, ROWS)


STEP = 8
SPAN = 16
STEPS = 8
RANGE = 14
EXTRA = 8


def filter_weights(ch):
    taps = filter_taps(ch) * (0.125 / math.sqrt(ch) / 2048.0)
    half = ch // 2
    weights = np.zeros((ch, STEP, SPAN, ch))
    angle = 2.0 * math.pi * (np.arange(half + 1)[:, None] * np.arange(ch)[None, :] % ch) / ch
    sums = np.concatenate([np.cos(angle), np.sin(angle[1:half])], axis=0)
    for spectrum in range(STEP):
        for t in range(TAPS):
            weights[:, spectrum, spectrum + t] = taps[t] * sums
    weights = weights.reshape(ch * STEP, SPAN * ch)
    high = weights.astype(jnp.bfloat16)
    low = (weights - high.astype(np.float64)).astype(jnp.bfloat16)
    return np.concatenate([high, low])


def spectra_of(weights_ref, levels, gains, ch, store):
    count = levels[0].shape[1]
    half, size = ch // 2, ch * STEP
    beside = max(1, 256 // count)
    for first in range(0, STEPS, beside):
        totals = []
        for level in levels:
            slabs = [level[b * size : b * size + SPAN * ch] for b in range(first, first + beside)]
            slab = jnp.concatenate(slabs, axis=1) if beside > 1 else slabs[0]
            both = jnp.dot(weights_ref[...], slab, preferred_element_type=jnp.float32)
            totals.append(both[:size] + both[size:])
        for index in range(beside):
            lanes = slice(index * count, (index + 1) * count)
            parts = [
                [total[d * STEP : (d + 1) * STEP, lanes] for d in range(ch)] for total in totals
            ]
            for c in range(ch):
                place = min(c, ch - c)
                real, imag = parts[0][place], parts[1][place]
                if c % half:
                    sine_real, sine_imag = parts[0][half + place], parts[1][half + place]
                    if c < half:
                        real, imag = real + sine_imag, imag - sine_real
                    else:
                        real, imag = real - sine_imag, imag + sine_real
                gain_real, gain_imag = gains[c : c + 1], gains[ch + c : ch + c + 1]
                store(
                    first + index,
                    c,
                    gain_real * real - gain_imag * imag,
                    gain_real * imag + gain_imag * real,
                )


def levels_of(words):
    return [
        ((words >> 4) - 8).astype(jnp.float32).astype(jnp.bfloat16),
        ((words & 15) - 8).astype(jnp.float32).astype(jnp.bfloat16),
    ]


def own_kernel(main_ref, next_ref, gains_ref, weights_ref, *refs):
    out_ref, zero_ref, held = refs[-3:]
    step = pl.program_id(0)
    ch = out_ref.shape[0]
    zero_ref[...] = jnp.zeros_like(zero_ref)
    words = jnp.concatenate([main_ref[...], next_ref[...]], axis=0)

    def store(b, c, real, imag):
        held[c, b * 2 * STEP : (b + 1) * 2 * STEP, :] = jnp.concatenate([real, imag], axis=0).astype(held.dtype)

    spectra_of(weights_ref, levels_of(words), gains_ref[...], ch, store)
    for c in range(ch):
        out_ref[c, step] = held[c].T


def own_spectra(words, gains, weights, ch, spectra, after):
    count = words.shape[1]
    main = STEPS * STEP * ch
    steps = spectra // (STEPS * STEP)
    return pl.pallas_call(
        own_kernel,
        grid=(steps,),
        in_specs=[
            pl.BlockSpec((main, count), lambda i: (i, 0)),
            pl.BlockSpec((STEP * ch, count), lambda i: ((i + 1) * STEPS, 0)),
            pl.BlockSpec(gains.shape, lambda i: (0, 0)),
            pl.BlockSpec(weights.shape, lambda i: (0, 0)),
        ]
        + [pl.BlockSpec(memory_space=pl.ANY)] * len(after),
        out_specs=[
            pl.BlockSpec(memory_space=pltpu.VMEM),
            pl.BlockSpec((16, LANES), lambda i: (0, 0)),
        ],
        out_shape=[
            jax.ShapeDtypeStruct((ch, steps, count, 2 * STEPS * STEP), jnp.bfloat16),
            jax.ShapeDtypeStruct((16, LANES), jnp.bfloat16),
        ],
        scratch_shapes=[
            pltpu.VMEM((ch, 2 * STEPS * STEP, count), jnp.bfloat16),
        ],
        compiler_params=pltpu.CompilerParams(vmem_limit_bytes=12 << 20),
        cost_estimate=pl.CostEstimate(
            flops=4 * spectra * ch * 2 * SPAN * ch * count,
            bytes_accessed=4 * words.size + 4 * ch * spectra * count,
            transcendentals=0,
        ),
        name="own_spectra",
    )(words, words, gains, weights, *after)


def select_kernel(last_rows, place_ref, slots_ref, words_ref, gains_ref, *outs):
    step = pl.program_id(0)
    count, rows = words_ref.shape[1], len(outs) * LANES
    words = words_ref[...].astype(jnp.float32).astype(jnp.bfloat16)
    place = lax.broadcasted_iota(jnp.int32, (count, rows), 0) + place_ref[0] * count
    slots = jnp.concatenate([slots_ref[index : index + 1, :] for index in range(len(outs))], axis=1)
    choice = jnp.where(slots == place, 1.0, 0.0).astype(jnp.bfloat16)
    taken = jnp.dot(words, choice, preferred_element_type=jnp.float32).astype(outs[0].dtype)
    for index, out_ref in enumerate(outs):
        out_ref[...] = taken[:, index * LANES : (index + 1) * LANES]

    @pl.when(step == pl.num_programs(0) - 1)
    def _():
        gains = gains_ref[...]
        parts = jnp.concatenate([gains >> 4, gains & 15], axis=0).astype(jnp.float32).astype(jnp.bfloat16)
        extra = parts.shape[0]
        gains = jnp.dot(parts, choice, preferred_element_type=jnp.float32).astype(outs[0].dtype)
        for index, out_ref in enumerate(outs):
            out_ref[last_rows : last_rows + extra, :] = gains[:, index * LANES : (index + 1) * LANES]
            left = out_ref.shape[0] - last_rows - extra
            out_ref[last_rows + extra :, :] = jnp.zeros((left, LANES), out_ref.dtype)


def select_rows(place, words, gains, slots, rows, total):
    lines, count = words.shape
    block = total // STEPS
    return pl.pallas_call(
        functools.partial(select_kernel, lines - (STEPS - 1) * block),
        grid=(STEPS,),
        in_specs=[
            pl.BlockSpec(memory_space=pltpu.SMEM),
            pl.BlockSpec((8, LANES), lambda i: (0, 0)),
            pl.BlockSpec((block, count), lambda i: (i, 0)),
            pl.BlockSpec(gains.shape, lambda i: (0, 0)),
        ],
        out_specs=[pl.BlockSpec((block, LANES), lambda i: (i, 0))] * (rows // LANES),
        out_shape=[jax.ShapeDtypeStruct((total, LANES), jnp.bfloat16)] * (rows // LANES),
        compiler_params=pltpu.CompilerParams(vmem_limit_bytes=8 << 20),
        name="select_rows",
    )(place, slots, words, gains)


def swap(value, bit):
    pairs = [(index, index ^ bit) for index in range(lax.axis_size("feed"))]
    return lax.ppermute(value, "feed", pairs)


def side(bit):
    return lax.axis_index("feed") // bit % 2


def reduce_half(value, bit):
    size = value.shape[0] // 2
    keep = lax.dynamic_slice_in_dim(value, side(bit) * size, size, 0)
    send = lax.dynamic_slice_in_dim(value, (1 - side(bit)) * size, size, 0)
    return keep + swap(send, bit)


def gather_half(value, bit, buffer):
    size = value.shape[0]
    other = swap(value, bit)
    buffer = lax.dynamic_update_slice_in_dim(buffer, value, side(bit) * size, 0)
    return lax.dynamic_update_slice_in_dim(buffer, other, (1 - side(bit)) * size, 0)


def quarters(half, behind):
    size = half.shape[0] // 2
    half = half + behind
    left, right = half[:size], half[size:]
    left_1, right_1 = reduce_half(left, 2), reduce_half(right, 4)
    return (left, right), (left_1, right_1)


def eighths(first):
    return reduce_half(first[0], 4), reduce_half(first[1], 2)


def cross(second, behind):
    second = [value + behind for value in second]
    return [value + swap(value, 8) for value in second]


def gathered(half, first, third):
    left_1, right_1 = gather_half(third[0], 4, first[0]), gather_half(third[1], 2, first[1])
    left, right = gather_half(left_1, 2, half[0]), gather_half(right_1, 4, half[1])
    return jnp.concatenate([left, right], axis=0)


def zero_after(values):
    return sum(value[0, 0] for value in values) * 0


def rows_kernel(main_ref, next_ref, parts_ref, weights_ref, out_ref):
    step = pl.program_id(0)
    ch, rows = out_ref.shape[0], main_ref.shape[1]
    words = jnp.concatenate([main_ref[...], next_ref[...]], axis=0).astype(jnp.float32).astype(jnp.int32)
    parts = parts_ref[...].astype(jnp.float32)
    gains = parts[: 2 * ch] * 16.0 + parts[2 * ch :]

    def store(b, c, real, imag):
        spot = pl.ds(pl.multiple_of(step * (2 * STEPS * STEP), 2 * STEPS * STEP) + b * 2 * STEP, 2 * STEP)
        out_ref[c, spot, :rows] = jnp.concatenate([real, imag], axis=0).astype(out_ref.dtype)
        out_ref[c, spot, rows:] = jnp.concatenate([imag, -real], axis=0).astype(out_ref.dtype)

    spectra_of(weights_ref, levels_of(words), gains, ch, store)


def row_spectra(words, parts, weights, ch, spectra):
    rows = words.shape[1]
    main = STEPS * STEP * ch
    return pl.pallas_call(
        rows_kernel,
        grid=(spectra // (STEPS * STEP),),
        in_specs=[
            pl.BlockSpec((main, rows), lambda i: (i, 0)),
            pl.BlockSpec((STEP * ch, rows), lambda i: ((i + 1) * STEPS, 0)),
            pl.BlockSpec(parts.shape, lambda i: (0, 0)),
            pl.BlockSpec(weights.shape, lambda i: (0, 0)),
        ],
        out_specs=pl.BlockSpec(memory_space=pltpu.VMEM),
        out_shape=jax.ShapeDtypeStruct((ch, 2 * spectra, 2 * rows), jnp.bfloat16),
        compiler_params=pltpu.CompilerParams(vmem_limit_bytes=8 << 20),
        cost_estimate=pl.CostEstimate(
            flops=8 * spectra * ch * SPAN * ch * rows,
            bytes_accessed=2 * words.size + 8 * ch * spectra * rows,
            transcendentals=0,
        ),
        name="row_spectra",
    )(words, words, parts, weights)


def products_kernel(own_ref, left_ref, *refs):
    out_ref, done_ref = refs[-2:]
    done_ref[...] = jnp.zeros_like(done_ref)
    each, steps = out_ref.shape[0], own_ref.shape[1]
    for index in range(each):
        c = pl.program_id(0) * each + index
        spectra = jnp.concatenate([own_ref[c, part] for part in range(steps)], axis=1)
        products = jnp.dot(spectra, left_ref[c], preferred_element_type=jnp.float32)
        count = products.shape[0]
        largest = jnp.maximum(jnp.max(jnp.abs(products), axis=0, keepdims=True), 2.0**-60)
        power = jnp.floor(jnp.log2(largest))
        coded = jnp.clip(jnp.round(products * jnp.exp2(RANGE - power)), -32767.0, 32767.0)
        out_ref[index, :count, :] = coded.astype(jnp.int32).astype(jnp.int16)
        line = jnp.broadcast_to(power, (out_ref.shape[1] - count, power.shape[1]))
        out_ref[index, count:, :] = line.astype(jnp.int32).astype(jnp.int16)


def row_products(own, left, after):
    ch, steps, count, width = own.shape
    columns = left.shape[2]
    each = 4
    return pl.pallas_call(
        products_kernel,
        grid=(ch // each,),
        in_specs=[pl.BlockSpec(memory_space=pltpu.VMEM)] * 2 + [pl.BlockSpec(memory_space=pl.ANY)] * len(after),
        out_specs=[
            pl.BlockSpec((each, count + EXTRA, columns), lambda i: (i, 0, 0)),
            pl.BlockSpec((16, LANES), lambda i: (0, 0)),
        ],
        out_shape=[
            pltpu.HBM((ch, count + EXTRA, columns), jnp.int16),
            jax.ShapeDtypeStruct((16, LANES), jnp.bfloat16),
        ],
        compiler_params=pltpu.CompilerParams(vmem_limit_bytes=10 << 20),
        cost_estimate=pl.CostEstimate(
            flops=2 * left.size * count, bytes_accessed=2 * left.size + 2 * own.size, transcendentals=0
        ),
        name="row_products",
    )(own, left, *after)


def finish_kernel(scale, slot_ref, coded_ref, *refs):
    out_ref, products, tile, mixed = refs[-4:]
    step = pl.program_id(0)
    sources, lines, width = coded_ref.shape
    count = lines - EXTRA
    pieces = width // LANES
    together = 8 // pieces

    @pl.when(step == 0)
    def _():
        for source in range(sources):
            power = coded_ref[source, count:, :][:1].astype(jnp.float32)
            values = coded_ref[source, :count, :].astype(jnp.float32) * (jnp.exp2(power - RANGE) * scale)
            for piece in range(pieces):
                products[pl.ds(source * count * pieces + piece, count, stride=pieces), :] = values[
                    :, piece * LANES : (piece + 1) * LANES
                ]

    for part in range(together):
        for i in range(LANES):
            line = slot_ref[(step * together + part) * LANES + i]
            tile[i * pieces : (i + 1) * pieces, :] = products[pl.ds(pl.multiple_of(line, pieces), pieces), :]
        for piece in range(pieces):
            turned = tile[pl.ds(piece, LANES, stride=pieces), :].T
            mixed[pl.ds(part * pieces + piece, LANES, stride=8), :] = turned
    out_ref[...] = mixed[...].reshape(out_ref.shape)


def finish(coded, places, index, pieces, scale, before):
    sources, lines, width = coded.shape
    rows = width // 2
    feeds = sources * (lines - EXTRA)
    columns = 2 * (feeds // LANES)
    earlier = [] if before is None else [before]
    return pl.pallas_call(
        functools.partial(finish_kernel, scale),
        grid=(columns // 8,),
        in_specs=[
            pl.BlockSpec(memory_space=pltpu.SMEM),
            pl.BlockSpec(memory_space=pltpu.VMEM),
        ]
        + [pl.BlockSpec(memory_space=pl.ANY)] * len(earlier),
        out_specs=pl.BlockSpec((rows, 8, LANES), lambda i: (index, i, 0)),
        out_shape=jax.ShapeDtypeStruct((pieces * rows, columns, LANES), jnp.float32),
        scratch_shapes=[
            pltpu.VMEM((feeds * width // LANES, LANES), jnp.float32),
            pltpu.VMEM((width, LANES), jnp.float32),
            pltpu.VMEM((8 * LANES, LANES), jnp.float32),
        ],
        input_output_aliases={2: 0} if earlier else {},
        compiler_params=pltpu.CompilerParams(vmem_limit_bytes=14 << 20),
        name="finish",
    )(places, coded, *earlier)


def through_rows(samples, gains, feed_slot):
    count, ch, frames = samples.shape
    spectra = frames - TAPS + 1
    pieces = ROWS // LANES
    lines = frames * ch
    unit = 16 * STEPS * 2
    total = pl.cdiv(lines + 4 * ch, unit) * unit
    words = jnp.transpose(samples, (2, 1, 0)).reshape(lines, count)
    scales = gains.reshape(2 * ch, count)
    weights = jnp.asarray(filter_weights(ch))
    place = lax.axis_index("feed").reshape(1)
    picked = select_rows(place, words, scales, feed_slot.reshape(-1, LANES), ROWS, total)
    nothing = jnp.zeros((), jnp.bfloat16)
    halves, firsts, behind = [], [], nothing
    for value in picked:
        half, first = quarters(reduce_half(value, 1), behind)
        behind = zero_after(first)
        halves.append(half)
        firsts.append(first)
    seconds = [eighths(first) for first in firsts]
    own, zero = own_spectra(words, scales.astype(jnp.float32), weights, ch, spectra, sum(seconds, ()))
    thirds, behind = [], nothing
    for second in seconds:
        third = cross(second, behind)
        if not thirds:
            third[0] = third[0] + zero[0, 0]
        behind = zero_after(third)
        thirds.append(third)
    ends = [gathered(*parts) for parts in zip(halves, firsts, thirds)]
    out, lefts = None, []
    for index in range(pieces):
        end = ends[index] if not lefts else ends[index] + zero_after([lefts[-1][0]])
        rows = gather_half(end, 1, picked[index])
        parts = rows[lines : lines + 4 * ch]
        lefts.append(row_spectra(rows, parts, weights, ch, spectra))
    after = [end]
    for index in range(pieces):
        coded, done = row_products(own, lefts[index], after)
        after = [done]
        moved = lax.all_to_all(coded, "feed", split_axis=0, concat_axis=0, tiled=True)
        out = finish(moved, feed_slot * 2, index, pieces, 1.0 / spectra, out)
    feeds = feed_slot.shape[0]
    out = out.reshape(ROWS, feeds // LANES, 2, LANES)
    return jnp.transpose(out, (0, 2, 1, 3)).reshape(ROWS, 2, feeds)


def body(samples, gains, feed_slot):
    count, ch, frames = samples.shape
    spectra = frames - TAPS + 1
    even = count % LANES == 0 and spectra % (STEPS * STEP) == 0 and ch % STEPS == 0
    if lax.axis_size("feed") == ch == 16 and even:
        return through_rows(samples, gains, feed_slot)
    return through_spectra(samples, gains, feed_slot)


def solution(mesh):
    return jax.shard_map(
        body,
        mesh=mesh,
        in_specs=(P(("band", "feed"), None, None), P(None, "band", "feed"), P()),
        out_specs=P(("band", "feed"), None, None),
        check_vma=False,
    )
```

```python
import functools
import math

import jax
import jax.numpy as jnp
import numpy as np
from jax import lax
from jax.experimental import pallas as pl
from jax.experimental.pallas import tpu as pltpu
from jax.sharding import PartitionSpec as P

TAPS = 8
ROWS = 256
LANES = 128


def filter_taps(ch):
    length = TAPS * ch
    place = np.arange(length, dtype=np.float64)
    window = 0.5 - 0.5 * np.cos(2.0 * math.pi * place / (length - 1))
    return (np.sinc((place - 0.5 * (length - 1)) / ch) * window).reshape(TAPS, ch)


def twiddle(value, turn):
    real, imag = value
    if turn == 0:
        return value
    if turn == 0.25:
        return imag, -real
    half = math.sqrt(0.5)
    if turn == 0.125:
        return half * (real + imag), half * (imag - real)
    if turn == 0.375:
        return half * (imag - real), -half * (real + imag)
    c, s = math.cos(2.0 * math.pi * turn), math.sin(2.0 * math.pi * turn)
    return c * real + s * imag, c * imag - s * real


def fft(values):
    count = len(values)
    if count == 1:
        return values
    even, odd = fft(values[0::2]), fft(values[1::2])
    low, high = [], []
    for index in range(count // 2):
        real, imag = twiddle(odd[index], index / count)
        low.append((even[index][0] + real, even[index][1] + imag))
        high.append((even[index][0] - real, even[index][1] - imag))
    return low + high


def channel_kernel(taps, *refs):
    *samples_refs, gains_ref, out_ref, filtered = refs
    ch, block, width = out_ref.shape
    spectra = width // 2
    padded = len(samples_refs) * LANES
    for k in range(ch):
        words = jnp.concatenate(
            [ref[pl.ds(k, block, stride=ch), :] for ref in samples_refs], axis=1
        )
        levels = ((words >> 4) - 8, (words & 15) - 8)
        for part in range(2):
            value = levels[part].astype(jnp.float32)
            shifted = [value] + [pltpu.roll(value, padded - t, 1) for t in range(1, TAPS // 2)]
            near = float(taps[0, k]) * shifted[0]
            far = float(taps[TAPS // 2, k]) * shifted[0]
            for t in range(1, TAPS // 2):
                near = near + float(taps[t, k]) * shifted[t]
                far = far + float(taps[t + TAPS // 2, k]) * shifted[t]
            total = near + pltpu.roll(far, padded - TAPS // 2, 1)
            filtered[2 * k + part] = total[:, :spectra]
    for row in range(0, block, 8):
        gains = gains_ref[row : row + 8, :]
        for lane in range(0, spectra, LANES):
            spot = (slice(row, row + 8), slice(lane, lane + LANES))
            values = [(filtered[2 * k][spot], filtered[2 * k + 1][spot]) for k in range(ch)]
            for c, (real, imag) in enumerate(fft(values)):
                gain_real = gains[:, c : c + 1]
                gain_imag = gains[:, ch + c : ch + c + 1]
                out_ref[c, row : row + 8, lane : lane + LANES] = (
                    gain_real * real - gain_imag * imag
                ).astype(out_ref.dtype)
                out_ref[c, row : row + 8, spectra + lane : spectra + lane + LANES] = (
                    gain_real * imag + gain_imag * real
                ).astype(out_ref.dtype)


def channelize(samples, gains):
    count, ch, frames = samples.shape
    spectra = frames - TAPS + 1
    block = 16
    pieces = pl.cdiv(frames, LANES)
    scale = 0.125 / math.sqrt(ch) / 2048.0
    taps = (filter_taps(ch) * scale).astype(np.float32)
    return pl.pallas_call(
        functools.partial(channel_kernel, taps),
        grid=(count // block,),
        in_specs=[
            pl.BlockSpec((block * ch, LANES), functools.partial(lambda piece, i: (i, piece), piece))
            for piece in range(pieces)
        ]
        + [pl.BlockSpec((block, 2 * ch), lambda i: (i, 0))],
        out_specs=pl.BlockSpec((ch, block, 2 * spectra), lambda i: (0, i, 0)),
        out_shape=jax.ShapeDtypeStruct((ch, count, 2 * spectra), jnp.bfloat16),
        scratch_shapes=[pltpu.VMEM((2 * ch, block, spectra), jnp.float32)],
        compiler_params=pltpu.CompilerParams(vmem_limit_bytes=32 << 20),
        name="channelize",
    )(*[samples.reshape(count * ch, frames)] * pieces, gains)


def correlate_kernel(scale, slot_ref, row_ref, data_ref, out_ref, products, tile):
    feeds, width = data_ref.shape
    spectra = width // 2
    rows = row_ref.shape[0]
    pieces = 2 * rows // LANES
    step = 256
    picked = jnp.zeros((rows, width), jnp.float32)
    for first in range(0, feeds, 512):
        place = lax.broadcasted_iota(jnp.int32, (rows, 512), 1) + first
        choice = jnp.where(row_ref[...] == place, 1.0, 0.0).astype(jnp.bfloat16)
        picked = picked + jnp.dot(
            choice, data_ref[first : first + 512, :], preferred_element_type=jnp.float32
        )
    left = jnp.concatenate(
        [
            picked,
            jnp.concatenate([picked[:, spectra:], -picked[:, :spectra]], axis=1),
        ],
        axis=0,
    ).astype(jnp.bfloat16)

    @pl.loop(0, feeds // step)
    def _(i):
        first = pl.multiple_of(i * step, step)
        result = lax.dot_general(
            data_ref[pl.ds(first, step), :],
            left,
            (((1,), (1,)), ((), ())),
            preferred_element_type=jnp.float32,
        )
        for piece in range(pieces):
            products[pl.ds(first * pieces + piece, step, stride=pieces), :] = (
                result[:, piece * LANES : (piece + 1) * LANES] * scale
            )

    lines = 2 * (feeds // LANES)

    @pl.loop(0, feeds // LANES)
    def _(j):
        @pl.loop(0, LANES, unroll=16)
        def _(i):
            slot = slot_ref[j * LANES + i]
            tile[pl.ds(pl.multiple_of(i * pieces, pieces), pieces), :] = products[
                pl.ds(pl.multiple_of(slot * pieces, pieces), pieces), :
            ]

        for piece in range(pieces):
            part, first = divmod(piece * LANES, rows)
            turned = tile[pl.ds(piece, LANES, stride=pieces), :].T
            out_ref[pl.ds(first * lines + 2 * j + part, LANES, stride=lines), :] = turned


def correlate(data, feed_slot, first, rows):
    feeds, width = data.shape
    row_slots = lax.dynamic_slice_in_dim(feed_slot, first, rows, 0).reshape(rows, 1)
    lines = 2 * (feeds // LANES)
    out = pl.pallas_call(
        functools.partial(correlate_kernel, 2.0 / width),
        in_specs=[
            pl.BlockSpec(memory_space=pltpu.SMEM),
            pl.BlockSpec(memory_space=pltpu.VMEM),
            pl.BlockSpec(memory_space=pltpu.VMEM),
        ],
        out_specs=pl.BlockSpec(memory_space=pltpu.VMEM),
        out_shape=jax.ShapeDtypeStruct((rows * lines, LANES), jnp.float32),
        scratch_shapes=[
            pltpu.VMEM((feeds * 2 * rows // LANES, LANES), jnp.float32),
            pltpu.VMEM((LANES * 2 * rows // LANES, LANES), jnp.float32),
        ],
        compiler_params=pltpu.CompilerParams(vmem_limit_bytes=48 << 20),
        name="correlate",
    )(feed_slot, row_slots, data)
    out = out.reshape(rows, feeds // LANES, 2, LANES)
    return jnp.transpose(out, (0, 2, 1, 3)).reshape(rows, 2, feeds)


def through_spectra(samples, gains, feed_slot):
    count, ch, _ = samples.shape
    groups = lax.axis_size("feed") // ch
    first = lax.axis_index("feed") % groups * ROWS
    scales = jnp.transpose(gains, (2, 0, 1)).reshape(count, 2 * ch).astype(jnp.float32)
    spectra = channelize(samples, scales)
    width = spectra.shape[2]
    outgoing = jnp.broadcast_to(spectra[:, None], (ch, groups, count, width))
    outgoing = outgoing.reshape(ch * groups, count, width)
    moved = lax.all_to_all(outgoing, "feed", split_axis=0, concat_axis=0, tiled=True)
    return correlate(moved.reshape(-1, width), feed_slot, first, ROWS)


STEP = 8
SPAN = 16
STEPS = 8
RANGE = 14
EXTRA = 8


def filter_weights(ch):
    taps = filter_taps(ch) * (0.125 / math.sqrt(ch) / 2048.0)
    half = ch // 2
    weights = np.zeros((ch, STEP, SPAN, ch))
    angle = 2.0 * math.pi * (np.arange(half + 1)[:, None] * np.arange(ch)[None, :] % ch) / ch
    sums = np.concatenate([np.cos(angle), np.sin(angle[1:half])], axis=0)
    for spectrum in range(STEP):
        for t in range(TAPS):
            weights[:, spectrum, spectrum + t] = taps[t] * sums
    weights = weights.reshape(ch * STEP, SPAN * ch)
    high = weights.astype(jnp.bfloat16)
    low = (weights - high.astype(np.float64)).astype(jnp.bfloat16)
    return np.concatenate([high, low])


def spectra_of(weights_ref, levels, gains, ch, store):
    count = levels[0].shape[1]
    half, size = ch // 2, ch * STEP
    beside = max(1, 256 // count)
    for first in range(0, STEPS, beside):
        totals = []
        for level in levels:
            slabs = [level[b * size : b * size + SPAN * ch] for b in range(first, first + beside)]
            slab = jnp.concatenate(slabs, axis=1) if beside > 1 else slabs[0]
            both = jnp.dot(weights_ref[...], slab, preferred_element_type=jnp.float32)
            totals.append(both[:size] + both[size:])
        for index in range(beside):
            lanes = slice(index * count, (index + 1) * count)
            parts = [
                [total[d * STEP : (d + 1) * STEP, lanes] for d in range(ch)] for total in totals
            ]
            for c in range(ch):
                place = min(c, ch - c)
                real, imag = parts[0][place], parts[1][place]
                if c % half:
                    sine_real, sine_imag = parts[0][half + place], parts[1][half + place]
                    if c < half:
                        real, imag = real + sine_imag, imag - sine_real
                    else:
                        real, imag = real - sine_imag, imag + sine_real
                gain_real, gain_imag = gains[c : c + 1], gains[ch + c : ch + c + 1]
                store(
                    first + index,
                    c,
                    gain_real * real - gain_imag * imag,
                    gain_real * imag + gain_imag * real,
                )


def levels_of(words):
    return [
        ((words >> 4) - 8).astype(jnp.float32).astype(jnp.bfloat16),
        ((words & 15) - 8).astype(jnp.float32).astype(jnp.bfloat16),
    ]


def own_kernel(main_ref, next_ref, gains_ref, weights_ref, *refs):
    out_ref, zero_ref, held = refs[-3:]
    step = pl.program_id(0)
    ch = out_ref.shape[0]
    zero_ref[...] = jnp.zeros_like(zero_ref)
    words = jnp.concatenate([main_ref[...], next_ref[...]], axis=0)

    def store(b, c, real, imag):
        held[c, b * 2 * STEP : (b + 1) * 2 * STEP, :] = jnp.concatenate([real, imag], axis=0).astype(held.dtype)

    spectra_of(weights_ref, levels_of(words), gains_ref[...], ch, store)
    for c in range(ch):
        out_ref[c, step] = held[c].T


def own_spectra(words, gains, weights, ch, spectra, after):
    count = words.shape[1]
    main = STEPS * STEP * ch
    steps = spectra // (STEPS * STEP)
    return pl.pallas_call(
        own_kernel,
        grid=(steps,),
        in_specs=[
            pl.BlockSpec((main, count), lambda i: (i, 0)),
            pl.BlockSpec((STEP * ch, count), lambda i: ((i + 1) * STEPS, 0)),
            pl.BlockSpec(gains.shape, lambda i: (0, 0)),
            pl.BlockSpec(weights.shape, lambda i: (0, 0)),
        ]
        + [pl.BlockSpec(memory_space=pl.ANY)] * len(after),
        out_specs=[
            pl.BlockSpec(memory_space=pltpu.VMEM),
            pl.BlockSpec((16, LANES), lambda i: (0, 0)),
        ],
        out_shape=[
            jax.ShapeDtypeStruct((ch, steps, count, 2 * STEPS * STEP), jnp.bfloat16),
            jax.ShapeDtypeStruct((16, LANES), jnp.bfloat16),
        ],
        scratch_shapes=[
            pltpu.VMEM((ch, 2 * STEPS * STEP, count), jnp.bfloat16),
        ],
        compiler_params=pltpu.CompilerParams(vmem_limit_bytes=12 << 20),
        cost_estimate=pl.CostEstimate(
            flops=4 * spectra * ch * 2 * SPAN * ch * count,
            bytes_accessed=4 * words.size + 4 * ch * spectra * count,
            transcendentals=0,
        ),
        name="own_spectra",
    )(words, words, gains, weights, *after)


def select_kernel(last_rows, place_ref, slots_ref, words_ref, gains_ref, *outs):
    step = pl.program_id(0)
    count, rows = words_ref.shape[1], len(outs) * LANES
    words = words_ref[...].astype(jnp.float32).astype(jnp.bfloat16)
    place = lax.broadcasted_iota(jnp.int32, (count, rows), 0) + place_ref[0] * count
    slots = jnp.concatenate([slots_ref[index : index + 1, :] for index in range(len(outs))], axis=1)
    choice = jnp.where(slots == place, 1.0, 0.0).astype(jnp.bfloat16)
    taken = jnp.dot(words, choice, preferred_element_type=jnp.float32).astype(outs[0].dtype)
    for index, out_ref in enumerate(outs):
        out_ref[...] = taken[:, index * LANES : (index + 1) * LANES]

    @pl.when(step == pl.num_programs(0) - 1)
    def _():
        gains = gains_ref[...]
        parts = jnp.concatenate([gains >> 4, gains & 15], axis=0).astype(jnp.float32).astype(jnp.bfloat16)
        extra = parts.shape[0]
        gains = jnp.dot(parts, choice, preferred_element_type=jnp.float32).astype(outs[0].dtype)
        for index, out_ref in enumerate(outs):
            out_ref[last_rows : last_rows + extra, :] = gains[:, index * LANES : (index + 1) * LANES]
            left = out_ref.shape[0] - last_rows - extra
            out_ref[last_rows + extra :, :] = jnp.zeros((left, LANES), out_ref.dtype)


def at_hand(value):
    return pltpu.with_memory_space_constraint(value, pltpu.HBM)


def select_rows(place, words, gains, slots, rows, total):
    lines, count = words.shape
    block = total // STEPS
    return pl.pallas_call(
        functools.partial(select_kernel, lines - (STEPS - 1) * block),
        grid=(STEPS,),
        in_specs=[
            pl.BlockSpec(memory_space=pltpu.SMEM),
            pl.BlockSpec((8, LANES), lambda i: (0, 0)),
            pl.BlockSpec((block, count), lambda i: (i, 0)),
            pl.BlockSpec(gains.shape, lambda i: (0, 0)),
        ],
        out_specs=[pl.BlockSpec((block, LANES), lambda i: (i, 0))] * (rows // LANES),
        out_shape=[jax.ShapeDtypeStruct((total, LANES), jnp.bfloat16)] * (rows // LANES),
        compiler_params=pltpu.CompilerParams(vmem_limit_bytes=8 << 20),
        name="select_rows",
    )(place, at_hand(slots), words, at_hand(gains))


def swap(value, bit):
    pairs = [(index, index ^ bit) for index in range(lax.axis_size("feed"))]
    return lax.ppermute(value, "feed", pairs)


def side(bit):
    return lax.axis_index("feed") // bit % 2


def reduce_half(value, bit):
    size = value.shape[0] // 2
    keep = lax.dynamic_slice_in_dim(value, side(bit) * size, size, 0)
    send = lax.dynamic_slice_in_dim(value, (1 - side(bit)) * size, size, 0)
    return keep + swap(send, bit)


def gather_half(value, bit, buffer):
    size = value.shape[0]
    other = swap(value, bit)
    buffer = lax.dynamic_update_slice_in_dim(buffer, value, side(bit) * size, 0)
    return lax.dynamic_update_slice_in_dim(buffer, other, (1 - side(bit)) * size, 0)


def quarters(half):
    size = half.shape[0] // 2
    left, right = half[:size], half[size:]
    left_1, right_1 = reduce_half(left, 2), reduce_half(right, 4)
    return (left, right), (left_1, right_1)


def eighths(first):
    return reduce_half(first[0], 4), reduce_half(first[1], 2)


def cross(second):
    return [value + swap(value, 8) for value in second]


def gathered(half, first, third):
    left_1, right_1 = gather_half(third[0], 4, first[0]), gather_half(third[1], 2, first[1])
    left, right = gather_half(left_1, 2, half[0]), gather_half(right_1, 4, half[1])
    return jnp.concatenate([left, right], axis=0)


def rows_kernel(main_ref, next_ref, parts_ref, weights_ref, out_ref):
    step = pl.program_id(0)
    ch, rows = out_ref.shape[0], main_ref.shape[1]
    words = jnp.concatenate([main_ref[...], next_ref[...]], axis=0).astype(jnp.float32).astype(jnp.int32)
    parts = parts_ref[...].astype(jnp.float32)
    gains = parts[: 2 * ch] * 16.0 + parts[2 * ch :]

    def store(b, c, real, imag):
        spot = pl.ds(pl.multiple_of(step * (2 * STEPS * STEP), 2 * STEPS * STEP) + b * 2 * STEP, 2 * STEP)
        out_ref[c, spot, :rows] = jnp.concatenate([real, imag], axis=0).astype(out_ref.dtype)
        out_ref[c, spot, rows:] = jnp.concatenate([imag, -real], axis=0).astype(out_ref.dtype)

    spectra_of(weights_ref, levels_of(words), gains, ch, store)


def row_spectra(words, parts, weights, ch, spectra):
    rows = words.shape[1]
    main = STEPS * STEP * ch
    return pl.pallas_call(
        rows_kernel,
        grid=(spectra // (STEPS * STEP),),
        in_specs=[
            pl.BlockSpec((main, rows), lambda i: (i, 0)),
            pl.BlockSpec((STEP * ch, rows), lambda i: ((i + 1) * STEPS, 0)),
            pl.BlockSpec(parts.shape, lambda i: (0, 0)),
            pl.BlockSpec(weights.shape, lambda i: (0, 0)),
        ],
        out_specs=pl.BlockSpec(memory_space=pltpu.VMEM),
        out_shape=jax.ShapeDtypeStruct((ch, 2 * spectra, 2 * rows), jnp.bfloat16),
        compiler_params=pltpu.CompilerParams(vmem_limit_bytes=8 << 20),
        cost_estimate=pl.CostEstimate(
            flops=8 * spectra * ch * SPAN * ch * rows,
            bytes_accessed=2 * words.size + 8 * ch * spectra * rows,
            transcendentals=0,
        ),
        name="row_spectra",
    )(words, words, parts, weights)


def products_kernel(own_ref, left_ref, *refs):
    out_ref, done_ref = refs[-2:]
    done_ref[...] = jnp.zeros_like(done_ref)
    each, steps = out_ref.shape[0], own_ref.shape[1]
    for index in range(each):
        c = pl.program_id(0) * each + index
        spectra = jnp.concatenate([own_ref[c, part] for part in range(steps)], axis=1)
        products = jnp.dot(spectra, left_ref[c], preferred_element_type=jnp.float32)
        count = products.shape[0]
        largest = jnp.maximum(jnp.max(jnp.abs(products), axis=0, keepdims=True), 2.0**-60)
        power = jnp.floor(jnp.log2(largest))
        coded = jnp.clip(jnp.round(products * jnp.exp2(RANGE - power)), -32767.0, 32767.0)
        out_ref[index, :count, :] = coded.astype(jnp.int32).astype(jnp.int16)
        line = jnp.broadcast_to(power, (out_ref.shape[1] - count, power.shape[1]))
        out_ref[index, count:, :] = line.astype(jnp.int32).astype(jnp.int16)


def row_products(own, left, after):
    ch, steps, count, width = own.shape
    columns = left.shape[2]
    each = 4
    return pl.pallas_call(
        products_kernel,
        grid=(ch // each,),
        in_specs=[pl.BlockSpec(memory_space=pltpu.VMEM)] * 2 + [pl.BlockSpec(memory_space=pl.ANY)] * len(after),
        out_specs=[
            pl.BlockSpec((each, count + EXTRA, columns), lambda i: (i, 0, 0)),
            pl.BlockSpec((16, LANES), lambda i: (0, 0)),
        ],
        out_shape=[
            pltpu.HBM((ch, count + EXTRA, columns), jnp.int16),
            jax.ShapeDtypeStruct((16, LANES), jnp.bfloat16),
        ],
        compiler_params=pltpu.CompilerParams(vmem_limit_bytes=10 << 20),
        cost_estimate=pl.CostEstimate(
            flops=2 * left.size * count, bytes_accessed=2 * left.size + 2 * own.size, transcendentals=0
        ),
        name="row_products",
    )(own, left, *after)


def finish_kernel(scale, slot_ref, coded_ref, *refs):
    out_ref, products, tile, mixed = refs[-4:]
    step = pl.program_id(0)
    sources, lines, width = coded_ref.shape
    count = lines - EXTRA
    pieces = width // LANES
    together = 8 // pieces

    @pl.when(step == 0)
    def _():
        for source in range(sources):
            power = coded_ref[source, count:, :][:1].astype(jnp.float32)
            values = coded_ref[source, :count, :].astype(jnp.float32) * (jnp.exp2(power - RANGE) * scale)
            for piece in range(pieces):
                products[pl.ds(source * count * pieces + piece, count, stride=pieces), :] = values[
                    :, piece * LANES : (piece + 1) * LANES
                ]

    for part in range(together):
        for i in range(LANES):
            line = slot_ref[(step * together + part) * LANES + i]
            tile[i * pieces : (i + 1) * pieces, :] = products[pl.ds(pl.multiple_of(line, pieces), pieces), :]
        for piece in range(pieces):
            turned = tile[pl.ds(piece, LANES, stride=pieces), :].T
            mixed[pl.ds(part * pieces + piece, LANES, stride=8), :] = turned
    out_ref[...] = mixed[...].reshape(out_ref.shape)


def finish(coded, places, index, pieces, scale, before):
    sources, lines, width = coded.shape
    rows = width // 2
    feeds = sources * (lines - EXTRA)
    columns = 2 * (feeds // LANES)
    earlier = [] if before is None else [before]
    return pl.pallas_call(
        functools.partial(finish_kernel, scale),
        grid=(columns // 8,),
        in_specs=[
            pl.BlockSpec(memory_space=pltpu.SMEM),
            pl.BlockSpec(memory_space=pltpu.VMEM),
        ]
        + [pl.BlockSpec(memory_space=pl.ANY)] * len(earlier),
        out_specs=pl.BlockSpec((rows, 8, LANES), lambda i: (index, i, 0)),
        out_shape=jax.ShapeDtypeStruct((pieces * rows, columns, LANES), jnp.float32),
        scratch_shapes=[
            pltpu.VMEM((feeds * width // LANES, LANES), jnp.float32),
            pltpu.VMEM((width, LANES), jnp.float32),
            pltpu.VMEM((8 * LANES, LANES), jnp.float32),
        ],
        input_output_aliases={2: 0} if earlier else {},
        compiler_params=pltpu.CompilerParams(vmem_limit_bytes=14 << 20),
        name="finish",
    )(places, coded, *earlier)


def through_rows(samples, gains, feed_slot):
    count, ch, frames = samples.shape
    spectra = frames - TAPS + 1
    pieces = ROWS // LANES
    lines = frames * ch
    unit = 16 * STEPS * 2
    total = pl.cdiv(lines + 4 * ch, unit) * unit
    words = jnp.transpose(samples, (2, 1, 0)).reshape(lines, count)
    scales = gains.reshape(2 * ch, count)
    weights = jnp.asarray(filter_weights(ch))
    place = lax.axis_index("feed").reshape(1)
    picked = select_rows(place, words, scales, feed_slot.reshape(-1, LANES), ROWS, total)
    halves, firsts = zip(*[quarters(reduce_half(value, 1)) for value in picked])
    seconds = [eighths(first) for first in firsts]
    own, zero = own_spectra(words, scales.astype(jnp.float32), weights, ch, spectra, sum(seconds, ()))
    thirds = [cross(second) for second in seconds]
    thirds[0][0] = thirds[0][0] + zero[0, 0]
    ends = [gathered(*parts) for parts in zip(halves, firsts, thirds)]
    out, after = None, [ends[-1]]
    for index in range(pieces):
        rows = gather_half(ends[index], 1, picked[index])
        parts = rows[lines : lines + 4 * ch]
        left = row_spectra(rows, parts, weights, ch, spectra)
        coded, done = row_products(own, left, after)
        after = [done]
        moved = lax.all_to_all(coded, "feed", split_axis=0, concat_axis=0, tiled=True)
        out = finish(moved, feed_slot * 2, index, pieces, 1.0 / spectra, out)
    feeds = feed_slot.shape[0]
    out = out.reshape(ROWS, feeds // LANES, 2, LANES)
    return jnp.transpose(out, (0, 2, 1, 3)).reshape(ROWS, 2, feeds)


def body(samples, gains, feed_slot):
    count, ch, frames = samples.shape
    spectra = frames - TAPS + 1
    even = count % LANES == 0 and spectra % (STEPS * STEP) == 0 and ch % STEPS == 0
    if lax.axis_size("feed") == ch == 16 and even:
        return through_rows(samples, gains, feed_slot)
    return through_spectra(samples, gains, feed_slot)


def solution(mesh):
    return jax.shard_map(
        body,
        mesh=mesh,
        in_specs=(P(("band", "feed"), None, None), P(None, "band", "feed"), P()),
        out_specs=P(("band", "feed"), None, None),
        check_vma=False,
    )
```

```python
import functools
import math

import jax
import jax.numpy as jnp
import numpy as np
from jax import lax
from jax.experimental import pallas as pl
from jax.experimental.pallas import tpu as pltpu
from jax.sharding import PartitionSpec as P

TAPS = 8
ROWS = 256
LANES = 128


def filter_taps(ch):
    length = TAPS * ch
    place = np.arange(length, dtype=np.float64)
    window = 0.5 - 0.5 * np.cos(2.0 * math.pi * place / (length - 1))
    return (np.sinc((place - 0.5 * (length - 1)) / ch) * window).reshape(TAPS, ch)


def twiddle(value, turn):
    real, imag = value
    if turn == 0:
        return value
    if turn == 0.25:
        return imag, -real
    half = math.sqrt(0.5)
    if turn == 0.125:
        return half * (real + imag), half * (imag - real)
    if turn == 0.375:
        return half * (imag - real), -half * (real + imag)
    c, s = math.cos(2.0 * math.pi * turn), math.sin(2.0 * math.pi * turn)
    return c * real + s * imag, c * imag - s * real


def fft(values):
    count = len(values)
    if count == 1:
        return values
    even, odd = fft(values[0::2]), fft(values[1::2])
    low, high = [], []
    for index in range(count // 2):
        real, imag = twiddle(odd[index], index / count)
        low.append((even[index][0] + real, even[index][1] + imag))
        high.append((even[index][0] - real, even[index][1] - imag))
    return low + high


def channel_kernel(taps, *refs):
    *samples_refs, gains_ref, out_ref, filtered = refs
    ch, block, width = out_ref.shape
    spectra = width // 2
    padded = len(samples_refs) * LANES
    for k in range(ch):
        words = jnp.concatenate(
            [ref[pl.ds(k, block, stride=ch), :] for ref in samples_refs], axis=1
        )
        levels = ((words >> 4) - 8, (words & 15) - 8)
        for part in range(2):
            value = levels[part].astype(jnp.float32)
            shifted = [value] + [pltpu.roll(value, padded - t, 1) for t in range(1, TAPS // 2)]
            near = float(taps[0, k]) * shifted[0]
            far = float(taps[TAPS // 2, k]) * shifted[0]
            for t in range(1, TAPS // 2):
                near = near + float(taps[t, k]) * shifted[t]
                far = far + float(taps[t + TAPS // 2, k]) * shifted[t]
            total = near + pltpu.roll(far, padded - TAPS // 2, 1)
            filtered[2 * k + part] = total[:, :spectra]
    for row in range(0, block, 8):
        gains = gains_ref[row : row + 8, :]
        for lane in range(0, spectra, LANES):
            spot = (slice(row, row + 8), slice(lane, lane + LANES))
            values = [(filtered[2 * k][spot], filtered[2 * k + 1][spot]) for k in range(ch)]
            for c, (real, imag) in enumerate(fft(values)):
                gain_real = gains[:, c : c + 1]
                gain_imag = gains[:, ch + c : ch + c + 1]
                out_ref[c, row : row + 8, lane : lane + LANES] = (
                    gain_real * real - gain_imag * imag
                ).astype(out_ref.dtype)
                out_ref[c, row : row + 8, spectra + lane : spectra + lane + LANES] = (
                    gain_real * imag + gain_imag * real
                ).astype(out_ref.dtype)


def channelize(samples, gains):
    count, ch, frames = samples.shape
    spectra = frames - TAPS + 1
    block = 16
    pieces = pl.cdiv(frames, LANES)
    scale = 0.125 / math.sqrt(ch) / 2048.0
    taps = (filter_taps(ch) * scale).astype(np.float32)
    return pl.pallas_call(
        functools.partial(channel_kernel, taps),
        grid=(count // block,),
        in_specs=[
            pl.BlockSpec((block * ch, LANES), functools.partial(lambda piece, i: (i, piece), piece))
            for piece in range(pieces)
        ]
        + [pl.BlockSpec((block, 2 * ch), lambda i: (i, 0))],
        out_specs=pl.BlockSpec((ch, block, 2 * spectra), lambda i: (0, i, 0)),
        out_shape=jax.ShapeDtypeStruct((ch, count, 2 * spectra), jnp.bfloat16),
        scratch_shapes=[pltpu.VMEM((2 * ch, block, spectra), jnp.float32)],
        compiler_params=pltpu.CompilerParams(vmem_limit_bytes=32 << 20),
        name="channelize",
    )(*[samples.reshape(count * ch, frames)] * pieces, gains)


def correlate_kernel(scale, slot_ref, row_ref, data_ref, out_ref, products, tile):
    feeds, width = data_ref.shape
    spectra = width // 2
    rows = row_ref.shape[0]
    pieces = 2 * rows // LANES
    step = 256
    picked = jnp.zeros((rows, width), jnp.float32)
    for first in range(0, feeds, 512):
        place = lax.broadcasted_iota(jnp.int32, (rows, 512), 1) + first
        choice = jnp.where(row_ref[...] == place, 1.0, 0.0).astype(jnp.bfloat16)
        picked = picked + jnp.dot(
            choice, data_ref[first : first + 512, :], preferred_element_type=jnp.float32
        )
    left = jnp.concatenate(
        [
            picked,
            jnp.concatenate([picked[:, spectra:], -picked[:, :spectra]], axis=1),
        ],
        axis=0,
    ).astype(jnp.bfloat16)

    @pl.loop(0, feeds // step)
    def _(i):
        first = pl.multiple_of(i * step, step)
        result = lax.dot_general(
            data_ref[pl.ds(first, step), :],
            left,
            (((1,), (1,)), ((), ())),
            preferred_element_type=jnp.float32,
        )
        for piece in range(pieces):
            products[pl.ds(first * pieces + piece, step, stride=pieces), :] = (
                result[:, piece * LANES : (piece + 1) * LANES] * scale
            )

    lines = 2 * (feeds // LANES)

    @pl.loop(0, feeds // LANES)
    def _(j):
        @pl.loop(0, LANES, unroll=16)
        def _(i):
            slot = slot_ref[j * LANES + i]
            tile[pl.ds(pl.multiple_of(i * pieces, pieces), pieces), :] = products[
                pl.ds(pl.multiple_of(slot * pieces, pieces), pieces), :
            ]

        for piece in range(pieces):
            part, first = divmod(piece * LANES, rows)
            turned = tile[pl.ds(piece, LANES, stride=pieces), :].T
            out_ref[pl.ds(first * lines + 2 * j + part, LANES, stride=lines), :] = turned


def correlate(data, feed_slot, first, rows):
    feeds, width = data.shape
    row_slots = lax.dynamic_slice_in_dim(feed_slot, first, rows, 0).reshape(rows, 1)
    lines = 2 * (feeds // LANES)
    out = pl.pallas_call(
        functools.partial(correlate_kernel, 2.0 / width),
        in_specs=[
            pl.BlockSpec(memory_space=pltpu.SMEM),
            pl.BlockSpec(memory_space=pltpu.VMEM),
            pl.BlockSpec(memory_space=pltpu.VMEM),
        ],
        out_specs=pl.BlockSpec(memory_space=pltpu.VMEM),
        out_shape=jax.ShapeDtypeStruct((rows * lines, LANES), jnp.float32),
        scratch_shapes=[
            pltpu.VMEM((feeds * 2 * rows // LANES, LANES), jnp.float32),
            pltpu.VMEM((LANES * 2 * rows // LANES, LANES), jnp.float32),
        ],
        compiler_params=pltpu.CompilerParams(vmem_limit_bytes=48 << 20),
        name="correlate",
    )(feed_slot, row_slots, data)
    out = out.reshape(rows, feeds // LANES, 2, LANES)
    return jnp.transpose(out, (0, 2, 1, 3)).reshape(rows, 2, feeds)


def through_spectra(samples, gains, feed_slot):
    count, ch, _ = samples.shape
    groups = lax.axis_size("feed") // ch
    first = lax.axis_index("feed") % groups * ROWS
    scales = jnp.transpose(gains, (2, 0, 1)).reshape(count, 2 * ch).astype(jnp.float32)
    spectra = channelize(samples, scales)
    width = spectra.shape[2]
    outgoing = jnp.broadcast_to(spectra[:, None], (ch, groups, count, width))
    outgoing = outgoing.reshape(ch * groups, count, width)
    moved = lax.all_to_all(outgoing, "feed", split_axis=0, concat_axis=0, tiled=True)
    return correlate(moved.reshape(-1, width), feed_slot, first, ROWS)


STEP = 8
SPAN = 16
STEPS = 8
RANGE = 14
EXTRA = 8


def filter_weights(ch):
    taps = filter_taps(ch) * (0.125 / math.sqrt(ch) / 2048.0)
    half = ch // 2
    weights = np.zeros((ch, STEP, SPAN, ch))
    angle = 2.0 * math.pi * (np.arange(half + 1)[:, None] * np.arange(ch)[None, :] % ch) / ch
    sums = np.concatenate([np.cos(angle), np.sin(angle[1:half])], axis=0)
    for spectrum in range(STEP):
        for t in range(TAPS):
            weights[:, spectrum, spectrum + t] = taps[t] * sums
    weights = weights.reshape(ch * STEP, SPAN * ch)
    high = weights.astype(jnp.bfloat16)
    low = (weights - high.astype(np.float64)).astype(jnp.bfloat16)
    return np.concatenate([high, low])


def spectra_of(weights_ref, levels, gains, ch, store):
    count = levels[0].shape[1]
    half, size = ch // 2, ch * STEP
    beside = max(1, 256 // count)
    for first in range(0, STEPS, beside):
        totals = []
        for level in levels:
            slabs = [level[b * size : b * size + SPAN * ch] for b in range(first, first + beside)]
            slab = jnp.concatenate(slabs, axis=1) if beside > 1 else slabs[0]
            both = jnp.dot(weights_ref[...], slab, preferred_element_type=jnp.float32)
            totals.append(both[:size] + both[size:])
        for index in range(beside):
            lanes = slice(index * count, (index + 1) * count)
            parts = [
                [total[d * STEP : (d + 1) * STEP, lanes] for d in range(ch)] for total in totals
            ]
            for c in range(ch):
                place = min(c, ch - c)
                real, imag = parts[0][place], parts[1][place]
                if c % half:
                    sine_real, sine_imag = parts[0][half + place], parts[1][half + place]
                    if c < half:
                        real, imag = real + sine_imag, imag - sine_real
                    else:
                        real, imag = real - sine_imag, imag + sine_real
                gain_real, gain_imag = gains[c : c + 1], gains[ch + c : ch + c + 1]
                store(
                    first + index,
                    c,
                    gain_real * real - gain_imag * imag,
                    gain_real * imag + gain_imag * real,
                )


def levels_of(words):
    return [
        ((words >> 4) - 8).astype(jnp.float32).astype(jnp.bfloat16),
        ((words & 15) - 8).astype(jnp.float32).astype(jnp.bfloat16),
    ]


def own_kernel(main_ref, next_ref, gains_ref, weights_ref, *refs):
    out_ref, zero_ref, held = refs[-3:]
    step = pl.program_id(0)
    ch = out_ref.shape[0]
    zero_ref[...] = jnp.zeros_like(zero_ref)
    words = jnp.concatenate([main_ref[...], next_ref[...]], axis=0)

    def store(b, c, real, imag):
        held[c, b * 2 * STEP : (b + 1) * 2 * STEP, :] = jnp.concatenate([real, imag], axis=0).astype(held.dtype)

    spectra_of(weights_ref, levels_of(words), gains_ref[...], ch, store)
    for c in range(ch):
        out_ref[c, step] = held[c].T


def own_spectra(words, gains, weights, ch, spectra, after):
    count = words.shape[1]
    main = STEPS * STEP * ch
    steps = spectra // (STEPS * STEP)
    return pl.pallas_call(
        own_kernel,
        grid=(steps,),
        in_specs=[
            pl.BlockSpec((main, count), lambda i: (i, 0)),
            pl.BlockSpec((STEP * ch, count), lambda i: ((i + 1) * STEPS, 0)),
            pl.BlockSpec(gains.shape, lambda i: (0, 0)),
            pl.BlockSpec(weights.shape, lambda i: (0, 0)),
        ]
        + [pl.BlockSpec(memory_space=pl.ANY)] * len(after),
        out_specs=[
            pl.BlockSpec(memory_space=pltpu.VMEM),
            pl.BlockSpec((16, LANES), lambda i: (0, 0)),
        ],
        out_shape=[
            jax.ShapeDtypeStruct((ch, steps, count, 2 * STEPS * STEP), jnp.bfloat16),
            jax.ShapeDtypeStruct((16, LANES), jnp.bfloat16),
        ],
        scratch_shapes=[
            pltpu.VMEM((ch, 2 * STEPS * STEP, count), jnp.bfloat16),
        ],
        compiler_params=pltpu.CompilerParams(vmem_limit_bytes=12 << 20),
        cost_estimate=pl.CostEstimate(
            flops=4 * spectra * ch * 2 * SPAN * ch * count,
            bytes_accessed=4 * words.size + 4 * ch * spectra * count,
            transcendentals=0,
        ),
        name="own_spectra",
    )(words, words, gains, weights, *after)


def select_kernel(block, place_ref, slots_ref, words_ref, gains_ref, *outs):
    lines, count = words_ref.shape
    rows = len(outs) * LANES
    place = lax.broadcasted_iota(jnp.int32, (count, rows), 0) + place_ref[0] * count
    slots = jnp.concatenate([slots_ref[index : index + 1, :] for index in range(len(outs))], axis=1)
    choice = jnp.where(slots == place, 1.0, 0.0).astype(jnp.bfloat16)

    def put(first, values):
        size = values.shape[0]
        values = values.astype(jnp.float32).astype(jnp.bfloat16)
        taken = jnp.dot(values, choice, preferred_element_type=jnp.float32).astype(outs[0].dtype)
        for index, out_ref in enumerate(outs):
            out_ref[first : first + size, :] = taken[:, index * LANES : (index + 1) * LANES]

    for first in range(0, lines, block):
        put(first, words_ref[first : min(first + block, lines), :])
    gains = gains_ref[...]
    put(lines, jnp.concatenate([gains >> 4, gains & 15], axis=0))
    first = lines + 2 * gains.shape[0]
    for out_ref in outs:
        out_ref[first:, :] = jnp.zeros((out_ref.shape[0] - first, LANES), out_ref.dtype)


def at_hand(value):
    return pltpu.with_memory_space_constraint(value, pltpu.HBM)


def select_rows(place, words, gains, slots, rows, total):
    return pl.pallas_call(
        functools.partial(select_kernel, total // STEPS),
        grid=(1,),
        in_specs=[
            pl.BlockSpec(memory_space=pltpu.SMEM),
            pl.BlockSpec((8, LANES), lambda i: (0, 0)),
            pl.BlockSpec(memory_space=pltpu.VMEM),
            pl.BlockSpec(gains.shape, lambda i: (0, 0)),
        ],
        out_specs=[pl.BlockSpec(memory_space=pltpu.VMEM)] * (rows // LANES),
        out_shape=[jax.ShapeDtypeStruct((total, LANES), jnp.bfloat16)] * (rows // LANES),
        compiler_params=pltpu.CompilerParams(vmem_limit_bytes=12 << 20),
        name="select_rows",
    )(place, at_hand(slots), words, at_hand(gains))


def swap(value, bit):
    pairs = [(index, index ^ bit) for index in range(lax.axis_size("feed"))]
    return lax.ppermute(value, "feed", pairs)


def side(bit):
    return lax.axis_index("feed") // bit % 2


def reduce_half(value, bit):
    size = value.shape[0] // 2
    keep = lax.dynamic_slice_in_dim(value, side(bit) * size, size, 0)
    send = lax.dynamic_slice_in_dim(value, (1 - side(bit)) * size, size, 0)
    return keep + swap(send, bit)


def gather_half(value, bit, buffer):
    size = value.shape[0]
    other = swap(value, bit)
    buffer = lax.dynamic_update_slice_in_dim(buffer, value, side(bit) * size, 0)
    return lax.dynamic_update_slice_in_dim(buffer, other, (1 - side(bit)) * size, 0)


def quarters(half):
    size = half.shape[0] // 2
    left, right = half[:size], half[size:]
    left_1, right_1 = reduce_half(left, 2), reduce_half(right, 4)
    return (left, right), (left_1, right_1)


def eighths(first):
    return reduce_half(first[0], 4), reduce_half(first[1], 2)


def cross(second):
    return [value + swap(value, 8) for value in second]


def gathered(half, first, third):
    left_1, right_1 = gather_half(third[0], 4, first[0]), gather_half(third[1], 2, first[1])
    left, right = gather_half(left_1, 2, half[0]), gather_half(right_1, 4, half[1])
    return jnp.concatenate([left, right], axis=0)


def rows_kernel(words_ref, parts_ref, weights_ref, out_ref):
    ch, rows = out_ref.shape[0], words_ref.shape[1]
    width = 2 * STEPS * STEP
    main = STEPS * STEP * ch
    parts = parts_ref[...].astype(jnp.float32)
    gains = parts[: 2 * ch] * 16.0 + parts[2 * ch :]

    @pl.loop(0, out_ref.shape[1] // width)
    def _(step):
        words = words_ref[pl.ds(pl.multiple_of(step * main, main), main + STEP * ch), :]
        words = words.astype(jnp.float32).astype(jnp.int32)

        def store(b, c, real, imag):
            spot = pl.ds(pl.multiple_of(step * width, width) + b * 2 * STEP, 2 * STEP)
            out_ref[c, spot, :rows] = jnp.concatenate([real, imag], axis=0).astype(out_ref.dtype)
            out_ref[c, spot, rows:] = jnp.concatenate([imag, -real], axis=0).astype(out_ref.dtype)

        spectra_of(weights_ref, levels_of(words), gains, ch, store)


def row_spectra(words, parts, weights, ch, spectra):
    rows = words.shape[1]
    return pl.pallas_call(
        rows_kernel,
        grid=(1,),
        in_specs=[
            pl.BlockSpec(memory_space=pltpu.VMEM),
            pl.BlockSpec(parts.shape, lambda i: (0, 0)),
            pl.BlockSpec(weights.shape, lambda i: (0, 0)),
        ],
        out_specs=pl.BlockSpec(memory_space=pltpu.VMEM),
        out_shape=jax.ShapeDtypeStruct((ch, 2 * spectra, 2 * rows), jnp.bfloat16),
        compiler_params=pltpu.CompilerParams(vmem_limit_bytes=8 << 20),
        cost_estimate=pl.CostEstimate(
            flops=8 * spectra * ch * SPAN * ch * rows,
            bytes_accessed=2 * words.size + 8 * ch * spectra * rows,
            transcendentals=0,
        ),
        name="row_spectra",
    )(words, parts, weights)


def products_kernel(own_ref, left_ref, *refs):
    out_ref, done_ref = refs[-2:]
    done_ref[...] = jnp.zeros_like(done_ref)
    each, steps = out_ref.shape[0], own_ref.shape[1]
    for index in range(each):
        c = pl.program_id(0) * each + index
        spectra = jnp.concatenate([own_ref[c, part] for part in range(steps)], axis=1)
        products = jnp.dot(spectra, left_ref[c], preferred_element_type=jnp.float32)
        count = products.shape[0]
        largest = jnp.maximum(jnp.max(jnp.abs(products), axis=0, keepdims=True), 2.0**-60)
        power = jnp.floor(jnp.log2(largest))
        coded = jnp.clip(jnp.round(products * jnp.exp2(RANGE - power)), -32767.0, 32767.0)
        out_ref[index, :count, :] = coded.astype(jnp.int32).astype(jnp.int16)
        line = jnp.broadcast_to(power, (out_ref.shape[1] - count, power.shape[1]))
        out_ref[index, count:, :] = line.astype(jnp.int32).astype(jnp.int16)


def row_products(own, left, after):
    ch, steps, count, width = own.shape
    columns = left.shape[2]
    each = 4
    return pl.pallas_call(
        products_kernel,
        grid=(ch // each,),
        in_specs=[pl.BlockSpec(memory_space=pltpu.VMEM)] * 2 + [pl.BlockSpec(memory_space=pl.ANY)] * len(after),
        out_specs=[
            pl.BlockSpec((each, count + EXTRA, columns), lambda i: (i, 0, 0)),
            pl.BlockSpec((16, LANES), lambda i: (0, 0)),
        ],
        out_shape=[
            pltpu.HBM((ch, count + EXTRA, columns), jnp.int16),
            jax.ShapeDtypeStruct((16, LANES), jnp.bfloat16),
        ],
        compiler_params=pltpu.CompilerParams(vmem_limit_bytes=10 << 20),
        cost_estimate=pl.CostEstimate(
            flops=2 * left.size * count, bytes_accessed=2 * left.size + 2 * own.size, transcendentals=0
        ),
        name="row_products",
    )(own, left, *after)


def finish_kernel(scale, slot_ref, coded_ref, *refs):
    out_ref, products, tile, mixed = refs[-4:]
    step = pl.program_id(0)
    sources, lines, width = coded_ref.shape
    count = lines - EXTRA
    pieces = width // LANES
    together = 8 // pieces

    @pl.when(step == 0)
    def _():
        for source in range(sources):
            power = coded_ref[source, count:, :][:1].astype(jnp.float32)
            values = coded_ref[source, :count, :].astype(jnp.float32) * (jnp.exp2(power - RANGE) * scale)
            for piece in range(pieces):
                products[pl.ds(source * count * pieces + piece, count, stride=pieces), :] = values[
                    :, piece * LANES : (piece + 1) * LANES
                ]

    tiles = out_ref.shape[1] // 8

    @pl.loop(0, tiles)
    def _(j):
        for part in range(together):
            for i in range(LANES):
                line = slot_ref[((step * tiles + j) * together + part) * LANES + i]
                tile[i * pieces : (i + 1) * pieces, :] = products[pl.ds(pl.multiple_of(line, pieces), pieces), :]
            for piece in range(pieces):
                turned = tile[pl.ds(piece, LANES, stride=pieces), :].T
                mixed[pl.ds(part * pieces + piece, LANES, stride=8), :] = turned
        out_ref[:, pl.ds(pl.multiple_of(j * 8, 8), 8), :] = mixed[...].reshape(out_ref.shape[0], 8, LANES)


def finish(coded, places, index, pieces, scale, before):
    sources, lines, width = coded.shape
    rows = width // 2
    feeds = sources * (lines - EXTRA)
    columns = 2 * (feeds // LANES)
    earlier = [] if before is None else [before]
    return pl.pallas_call(
        functools.partial(finish_kernel, scale),
        grid=(columns // 16,),
        in_specs=[
            pl.BlockSpec(memory_space=pltpu.SMEM),
            pl.BlockSpec(memory_space=pltpu.VMEM),
        ]
        + [pl.BlockSpec(memory_space=pl.ANY)] * len(earlier),
        out_specs=pl.BlockSpec((rows, 16, LANES), lambda i: (index, i, 0)),
        out_shape=jax.ShapeDtypeStruct((pieces * rows, columns, LANES), jnp.float32),
        scratch_shapes=[
            pltpu.VMEM((feeds * width // LANES, LANES), jnp.float32),
            pltpu.VMEM((width, LANES), jnp.float32),
            pltpu.VMEM((8 * LANES, LANES), jnp.float32),
        ],
        input_output_aliases={2: 0} if earlier else {},
        compiler_params=pltpu.CompilerParams(vmem_limit_bytes=14 << 20),
        name="finish",
    )(places, coded, *earlier)


def through_rows(samples, gains, feed_slot):
    count, ch, frames = samples.shape
    spectra = frames - TAPS + 1
    pieces = ROWS // LANES
    lines = frames * ch
    unit = 16 * STEPS * 2
    total = pl.cdiv(lines + 4 * ch, unit) * unit
    words = jnp.transpose(samples, (2, 1, 0)).reshape(lines, count)
    scales = gains.reshape(2 * ch, count)
    weights = jnp.asarray(filter_weights(ch))
    place = lax.axis_index("feed").reshape(1)
    picked = select_rows(place, words, scales, feed_slot.reshape(-1, LANES), ROWS, total)
    halves, firsts = zip(*[quarters(reduce_half(value, 1)) for value in picked])
    seconds = [eighths(first) for first in firsts]
    own, zero = own_spectra(words, scales.astype(jnp.float32), weights, ch, spectra, sum(seconds, ()))
    thirds = [cross(second) for second in seconds]
    thirds[0][0] = thirds[0][0] + zero[0, 0]
    ends = [gathered(*parts) for parts in zip(halves, firsts, thirds)]
    out, after = None, [ends[-1]]
    for index in range(pieces):
        rows = gather_half(ends[index], 1, picked[index])
        parts = rows[lines : lines + 4 * ch]
        left = row_spectra(rows, parts, weights, ch, spectra)
        coded, done = row_products(own, left, after)
        after = [done]
        moved = lax.all_to_all(coded, "feed", split_axis=0, concat_axis=0, tiled=True)
        out = finish(moved, feed_slot * 2, index, pieces, 1.0 / spectra, out)
    feeds = feed_slot.shape[0]
    out = out.reshape(ROWS, feeds // LANES, 2, LANES)
    return jnp.transpose(out, (0, 2, 1, 3)).reshape(ROWS, 2, feeds)


def body(samples, gains, feed_slot):
    count, ch, frames = samples.shape
    spectra = frames - TAPS + 1
    even = count % LANES == 0 and spectra % (STEPS * STEP) == 0 and ch % STEPS == 0
    if lax.axis_size("feed") == ch == 16 and even:
        return through_rows(samples, gains, feed_slot)
    return through_spectra(samples, gains, feed_slot)


def solution(mesh):
    return jax.shard_map(
        body,
        mesh=mesh,
        in_specs=(P(("band", "feed"), None, None), P(None, "band", "feed"), P()),
        out_specs=P(("band", "feed"), None, None),
        check_vma=False,
    )
```

```python
import functools
import math

import jax
import jax.numpy as jnp
import numpy as np
from jax import lax
from jax.experimental import pallas as pl
from jax.experimental.pallas import tpu as pltpu
from jax.sharding import PartitionSpec as P

TAPS = 8
ROWS = 256
LANES = 128


def filter_taps(ch):
    length = TAPS * ch
    place = np.arange(length, dtype=np.float64)
    window = 0.5 - 0.5 * np.cos(2.0 * math.pi * place / (length - 1))
    return (np.sinc((place - 0.5 * (length - 1)) / ch) * window).reshape(TAPS, ch)


def twiddle(value, turn):
    real, imag = value
    if turn == 0:
        return value
    if turn == 0.25:
        return imag, -real
    half = math.sqrt(0.5)
    if turn == 0.125:
        return half * (real + imag), half * (imag - real)
    if turn == 0.375:
        return half * (imag - real), -half * (real + imag)
    c, s = math.cos(2.0 * math.pi * turn), math.sin(2.0 * math.pi * turn)
    return c * real + s * imag, c * imag - s * real


def fft(values):
    count = len(values)
    if count == 1:
        return values
    even, odd = fft(values[0::2]), fft(values[1::2])
    low, high = [], []
    for index in range(count // 2):
        real, imag = twiddle(odd[index], index / count)
        low.append((even[index][0] + real, even[index][1] + imag))
        high.append((even[index][0] - real, even[index][1] - imag))
    return low + high


def channel_kernel(taps, *refs):
    *samples_refs, gains_ref, out_ref, filtered = refs
    ch, block, width = out_ref.shape
    spectra = width // 2
    padded = len(samples_refs) * LANES
    for k in range(ch):
        words = jnp.concatenate(
            [ref[pl.ds(k, block, stride=ch), :] for ref in samples_refs], axis=1
        )
        levels = ((words >> 4) - 8, (words & 15) - 8)
        for part in range(2):
            value = levels[part].astype(jnp.float32)
            shifted = [value] + [pltpu.roll(value, padded - t, 1) for t in range(1, TAPS // 2)]
            near = float(taps[0, k]) * shifted[0]
            far = float(taps[TAPS // 2, k]) * shifted[0]
            for t in range(1, TAPS // 2):
                near = near + float(taps[t, k]) * shifted[t]
                far = far + float(taps[t + TAPS // 2, k]) * shifted[t]
            total = near + pltpu.roll(far, padded - TAPS // 2, 1)
            filtered[2 * k + part] = total[:, :spectra]
    for row in range(0, block, 8):
        gains = gains_ref[row : row + 8, :]
        for lane in range(0, spectra, LANES):
            spot = (slice(row, row + 8), slice(lane, lane + LANES))
            values = [(filtered[2 * k][spot], filtered[2 * k + 1][spot]) for k in range(ch)]
            for c, (real, imag) in enumerate(fft(values)):
                gain_real = gains[:, c : c + 1]
                gain_imag = gains[:, ch + c : ch + c + 1]
                out_ref[c, row : row + 8, lane : lane + LANES] = (
                    gain_real * real - gain_imag * imag
                ).astype(out_ref.dtype)
                out_ref[c, row : row + 8, spectra + lane : spectra + lane + LANES] = (
                    gain_real * imag + gain_imag * real
                ).astype(out_ref.dtype)


def channelize(samples, gains):
    count, ch, frames = samples.shape
    spectra = frames - TAPS + 1
    block = 16
    pieces = pl.cdiv(frames, LANES)
    scale = 0.125 / math.sqrt(ch) / 2048.0
    taps = (filter_taps(ch) * scale).astype(np.float32)
    return pl.pallas_call(
        functools.partial(channel_kernel, taps),
        grid=(count // block,),
        in_specs=[
            pl.BlockSpec((block * ch, LANES), functools.partial(lambda piece, i: (i, piece), piece))
            for piece in range(pieces)
        ]
        + [pl.BlockSpec((block, 2 * ch), lambda i: (i, 0))],
        out_specs=pl.BlockSpec((ch, block, 2 * spectra), lambda i: (0, i, 0)),
        out_shape=jax.ShapeDtypeStruct((ch, count, 2 * spectra), jnp.bfloat16),
        scratch_shapes=[pltpu.VMEM((2 * ch, block, spectra), jnp.float32)],
        compiler_params=pltpu.CompilerParams(vmem_limit_bytes=32 << 20),
        name="channelize",
    )(*[samples.reshape(count * ch, frames)] * pieces, gains)


def correlate_kernel(scale, slot_ref, row_ref, data_ref, out_ref, products, tile):
    feeds, width = data_ref.shape
    spectra = width // 2
    rows = row_ref.shape[0]
    pieces = 2 * rows // LANES
    step = 256
    picked = jnp.zeros((rows, width), jnp.float32)
    for first in range(0, feeds, 512):
        place = lax.broadcasted_iota(jnp.int32, (rows, 512), 1) + first
        choice = jnp.where(row_ref[...] == place, 1.0, 0.0).astype(jnp.bfloat16)
        picked = picked + jnp.dot(
            choice, data_ref[first : first + 512, :], preferred_element_type=jnp.float32
        )
    left = jnp.concatenate(
        [
            picked,
            jnp.concatenate([picked[:, spectra:], -picked[:, :spectra]], axis=1),
        ],
        axis=0,
    ).astype(jnp.bfloat16)

    @pl.loop(0, feeds // step)
    def _(i):
        first = pl.multiple_of(i * step, step)
        result = lax.dot_general(
            data_ref[pl.ds(first, step), :],
            left,
            (((1,), (1,)), ((), ())),
            preferred_element_type=jnp.float32,
        )
        for piece in range(pieces):
            products[pl.ds(first * pieces + piece, step, stride=pieces), :] = (
                result[:, piece * LANES : (piece + 1) * LANES] * scale
            )

    lines = 2 * (feeds // LANES)

    @pl.loop(0, feeds // LANES)
    def _(j):
        @pl.loop(0, LANES, unroll=16)
        def _(i):
            slot = slot_ref[j * LANES + i]
            tile[pl.ds(pl.multiple_of(i * pieces, pieces), pieces), :] = products[
                pl.ds(pl.multiple_of(slot * pieces, pieces), pieces), :
            ]

        for piece in range(pieces):
            part, first = divmod(piece * LANES, rows)
            turned = tile[pl.ds(piece, LANES, stride=pieces), :].T
            out_ref[pl.ds(first * lines + 2 * j + part, LANES, stride=lines), :] = turned


def correlate(data, feed_slot, first, rows):
    feeds, width = data.shape
    row_slots = lax.dynamic_slice_in_dim(feed_slot, first, rows, 0).reshape(rows, 1)
    lines = 2 * (feeds // LANES)
    out = pl.pallas_call(
        functools.partial(correlate_kernel, 2.0 / width),
        in_specs=[
            pl.BlockSpec(memory_space=pltpu.SMEM),
            pl.BlockSpec(memory_space=pltpu.VMEM),
            pl.BlockSpec(memory_space=pltpu.VMEM),
        ],
        out_specs=pl.BlockSpec(memory_space=pltpu.VMEM),
        out_shape=jax.ShapeDtypeStruct((rows * lines, LANES), jnp.float32),
        scratch_shapes=[
            pltpu.VMEM((feeds * 2 * rows // LANES, LANES), jnp.float32),
            pltpu.VMEM((LANES * 2 * rows // LANES, LANES), jnp.float32),
        ],
        compiler_params=pltpu.CompilerParams(vmem_limit_bytes=48 << 20),
        name="correlate",
    )(feed_slot, row_slots, data)
    out = out.reshape(rows, feeds // LANES, 2, LANES)
    return jnp.transpose(out, (0, 2, 1, 3)).reshape(rows, 2, feeds)


def through_spectra(samples, gains, feed_slot):
    count, ch, _ = samples.shape
    groups = lax.axis_size("feed") // ch
    first = lax.axis_index("feed") % groups * ROWS
    scales = jnp.transpose(gains, (2, 0, 1)).reshape(count, 2 * ch).astype(jnp.float32)
    spectra = channelize(samples, scales)
    width = spectra.shape[2]
    outgoing = jnp.broadcast_to(spectra[:, None], (ch, groups, count, width))
    outgoing = outgoing.reshape(ch * groups, count, width)
    moved = lax.all_to_all(outgoing, "feed", split_axis=0, concat_axis=0, tiled=True)
    return correlate(moved.reshape(-1, width), feed_slot, first, ROWS)


STEP = 8
SPAN = 16
STEPS = 8
RANGE = 14
FIT = 1.0 - 2.0**-15
EXTRA = 8


def filter_weights(ch):
    taps = filter_taps(ch) * (0.125 / math.sqrt(ch) / 2048.0)
    half = ch // 2
    weights = np.zeros((ch, STEP, SPAN, ch))
    angle = 2.0 * math.pi * (np.arange(half + 1)[:, None] * np.arange(ch)[None, :] % ch) / ch
    sums = np.concatenate([np.cos(angle), np.sin(angle[1:half])], axis=0)
    for spectrum in range(STEP):
        for t in range(TAPS):
            weights[:, spectrum, spectrum + t] = taps[t] * sums
    weights = weights.reshape(ch * STEP, SPAN * ch)
    high = weights.astype(jnp.bfloat16)
    low = (weights - high.astype(np.float64)).astype(jnp.bfloat16)
    return np.concatenate([high, low])


def spectra_of(weights_ref, levels, gains, ch, store):
    count = levels[0].shape[1]
    half, size = ch // 2, ch * STEP
    beside = max(1, 256 // count)
    for first in range(0, STEPS, beside):
        totals = []
        for level in levels:
            slabs = [level[b * size : b * size + SPAN * ch] for b in range(first, first + beside)]
            slab = jnp.concatenate(slabs, axis=1) if beside > 1 else slabs[0]
            both = jnp.dot(weights_ref[...], slab, preferred_element_type=jnp.float32)
            totals.append(both[:size] + both[size:])
        for index in range(beside):
            lanes = slice(index * count, (index + 1) * count)
            parts = [
                [total[d * STEP : (d + 1) * STEP, lanes] for d in range(ch)] for total in totals
            ]
            for c in range(ch):
                place = min(c, ch - c)
                real, imag = parts[0][place], parts[1][place]
                if c % half:
                    sine_real, sine_imag = parts[0][half + place], parts[1][half + place]
                    if c < half:
                        real, imag = real + sine_imag, imag - sine_real
                    else:
                        real, imag = real - sine_imag, imag + sine_real
                gain_real, gain_imag = gains[c : c + 1], gains[ch + c : ch + c + 1]
                store(
                    first + index,
                    c,
                    gain_real * real - gain_imag * imag,
                    gain_real * imag + gain_imag * real,
                )


def levels_of(words):
    return [
        ((words >> 4) - 8).astype(jnp.float32).astype(jnp.bfloat16),
        ((words & 15) - 8).astype(jnp.float32).astype(jnp.bfloat16),
    ]


def own_kernel(main_ref, next_ref, gains_ref, weights_ref, *refs):
    out_ref, zero_ref, held = refs[-3:]
    step = pl.program_id(0)
    ch = out_ref.shape[0]
    zero_ref[...] = jnp.zeros_like(zero_ref)
    words = jnp.concatenate([main_ref[...], next_ref[...]], axis=0)

    def store(b, c, real, imag):
        held[c, b * 2 * STEP : (b + 1) * 2 * STEP, :] = jnp.concatenate([real, imag], axis=0).astype(held.dtype)

    spectra_of(weights_ref, levels_of(words), gains_ref[...], ch, store)
    for c in range(ch):
        out_ref[c, step] = held[c].T


def own_spectra(words, gains, weights, ch, spectra, after):
    count = words.shape[1]
    main = STEPS * STEP * ch
    steps = spectra // (STEPS * STEP)
    return pl.pallas_call(
        own_kernel,
        grid=(steps,),
        in_specs=[
            pl.BlockSpec((main, count), lambda i: (i, 0)),
            pl.BlockSpec((STEP * ch, count), lambda i: ((i + 1) * STEPS, 0)),
            pl.BlockSpec(gains.shape, lambda i: (0, 0)),
            pl.BlockSpec(weights.shape, lambda i: (0, 0)),
        ]
        + [pl.BlockSpec(memory_space=pl.ANY)] * len(after),
        out_specs=[
            pl.BlockSpec(memory_space=pltpu.VMEM),
            pl.BlockSpec((16, LANES), lambda i: (0, 0)),
        ],
        out_shape=[
            jax.ShapeDtypeStruct((ch, steps, count, 2 * STEPS * STEP), jnp.bfloat16),
            jax.ShapeDtypeStruct((16, LANES), jnp.bfloat16),
        ],
        scratch_shapes=[
            pltpu.VMEM((ch, 2 * STEPS * STEP, count), jnp.bfloat16),
        ],
        compiler_params=pltpu.CompilerParams(vmem_limit_bytes=12 << 20),
        cost_estimate=pl.CostEstimate(
            flops=4 * spectra * ch * 2 * SPAN * ch * count,
            bytes_accessed=4 * words.size + 4 * ch * spectra * count,
            transcendentals=0,
        ),
        name="own_spectra",
    )(words, words, gains, weights, *after)


def select_kernel(blocks, place_ref, slots_ref, words_ref, gains_ref, *outs):
    lines, count = words_ref.shape
    pieces = len(outs) // 2
    rows = pieces * LANES
    size = outs[0].shape[0]
    place = lax.broadcasted_iota(jnp.int32, (count, rows), 0) + place_ref[0] * count
    slots = jnp.concatenate([slots_ref[index : index + 1, :] for index in range(pieces)], axis=1)
    choice = jnp.where(slots == place, 1.0, 0.0).astype(jnp.bfloat16)
    gains = gains_ref[...]
    parts = jnp.concatenate([gains >> 4, gains & 15], axis=0)

    def put(refs, first, values):
        values = values.astype(jnp.float32).astype(jnp.bfloat16)
        taken = jnp.dot(values, choice, preferred_element_type=jnp.float32).astype(outs[0].dtype)
        for index, out_ref in enumerate(refs):
            out_ref[first : first + values.shape[0], :] = taken[:, index * LANES : (index + 1) * LANES]

    for side in range(2):

        @pl.when(place_ref[0] % 2 == side)
        def _():
            for half in range(2):
                refs = outs[:pieces] if half == side else outs[pieces:]
                end = min((half + 1) * size, lines)
                for first in range(half * size, end, size // blocks):
                    last = min(first + size // blocks, end)
                    put(refs, first - half * size, words_ref[first:last, :])
            first = lines - size
            put(refs, first, parts)
            first += parts.shape[0]
            for out_ref in refs:
                out_ref[first:, :] = jnp.zeros((size - first, LANES), out_ref.dtype)


def at_hand(value):
    return pltpu.with_memory_space_constraint(value, pltpu.HBM)


def select_rows(place, words, gains, slots, rows, total):
    pieces = rows // LANES
    outs = pl.pallas_call(
        functools.partial(select_kernel, STEPS // 2),
        grid=(1,),
        in_specs=[
            pl.BlockSpec(memory_space=pltpu.SMEM),
            pl.BlockSpec((8, LANES), lambda i: (0, 0)),
            pl.BlockSpec(memory_space=pltpu.VMEM),
            pl.BlockSpec(gains.shape, lambda i: (0, 0)),
        ],
        out_specs=[pl.BlockSpec(memory_space=pltpu.VMEM)] * (2 * pieces),
        out_shape=[jax.ShapeDtypeStruct((total // 2, LANES), jnp.bfloat16)] * (2 * pieces),
        compiler_params=pltpu.CompilerParams(vmem_limit_bytes=12 << 20),
        name="select_rows",
    )(place, at_hand(slots), words, at_hand(gains))
    return outs[:pieces], outs[pieces:]


def swap(value, bit):
    pairs = [(index, index ^ bit) for index in range(lax.axis_size("feed"))]
    return lax.ppermute(value, "feed", pairs)


def side(bit):
    return lax.axis_index("feed") // bit % 2


def reduce_half(value, bit):
    size = value.shape[0] // 2
    keep = lax.dynamic_slice_in_dim(value, side(bit) * size, size, 0)
    send = lax.dynamic_slice_in_dim(value, (1 - side(bit)) * size, size, 0)
    return keep + swap(send, bit)


def gather_half(value, bit, buffer):
    size = value.shape[0]
    other = swap(value, bit)
    buffer = lax.dynamic_update_slice_in_dim(buffer, value, side(bit) * size, 0)
    return lax.dynamic_update_slice_in_dim(buffer, other, (1 - side(bit)) * size, 0)


def both_halves(half):
    other, first = swap(half, 1), side(1) == 0
    return jnp.concatenate([jnp.where(first, half, other), jnp.where(first, other, half)], axis=0)


def quarters(half):
    size = half.shape[0] // 2
    left, right = half[:size], half[size:]
    left_1, right_1 = reduce_half(left, 2), reduce_half(right, 4)
    return (left, right), (left_1, right_1)


def eighths(first):
    return reduce_half(first[0], 4), reduce_half(first[1], 2)


def cross(second):
    return [value + swap(value, 8) for value in second]


def gathered(half, first, third):
    left_1, right_1 = gather_half(third[0], 4, first[0]), gather_half(third[1], 2, first[1])
    left, right = gather_half(left_1, 2, half[0]), gather_half(right_1, 4, half[1])
    return jnp.concatenate([left, right], axis=0)


def rows_kernel(words_ref, parts_ref, weights_ref, out_ref):
    ch, rows = out_ref.shape[0], words_ref.shape[1]
    width = 2 * STEPS * STEP
    main = STEPS * STEP * ch
    parts = parts_ref[...].astype(jnp.float32)
    gains = parts[: 2 * ch] * 16.0 + parts[2 * ch :]

    @pl.loop(0, out_ref.shape[1] // width)
    def _(step):
        words = words_ref[pl.ds(pl.multiple_of(step * main, main), main + STEP * ch), :]
        words = words.astype(jnp.float32).astype(jnp.int32)

        def store(b, c, real, imag):
            spot = pl.ds(pl.multiple_of(step * width, width) + b * 2 * STEP, 2 * STEP)
            out_ref[c, spot, :rows] = jnp.concatenate([real, imag], axis=0).astype(out_ref.dtype)
            out_ref[c, spot, rows:] = jnp.concatenate([imag, -real], axis=0).astype(out_ref.dtype)

        spectra_of(weights_ref, levels_of(words), gains, ch, store)


def row_spectra(words, parts, weights, ch, spectra):
    rows = words.shape[1]
    return pl.pallas_call(
        rows_kernel,
        grid=(1,),
        in_specs=[
            pl.BlockSpec(memory_space=pltpu.VMEM),
            pl.BlockSpec(parts.shape, lambda i: (0, 0)),
            pl.BlockSpec(weights.shape, lambda i: (0, 0)),
        ],
        out_specs=pl.BlockSpec(memory_space=pltpu.VMEM),
        out_shape=jax.ShapeDtypeStruct((ch, 2 * spectra, 2 * rows), jnp.bfloat16),
        compiler_params=pltpu.CompilerParams(vmem_limit_bytes=8 << 20),
        cost_estimate=pl.CostEstimate(
            flops=8 * spectra * ch * SPAN * ch * rows,
            bytes_accessed=2 * words.size + 8 * ch * spectra * rows,
            transcendentals=0,
        ),
        name="row_spectra",
    )(words, parts, weights)


def products_kernel(own_ref, left_ref, *refs):
    out_ref, done_ref = refs[-2:]
    done_ref[...] = jnp.zeros_like(done_ref)
    each, steps = out_ref.shape[0], own_ref.shape[1]
    for index in range(each):
        c = pl.program_id(0) * each + index
        spectra = jnp.concatenate([own_ref[c, part] for part in range(steps)], axis=1)
        products = jnp.dot(spectra, left_ref[c], preferred_element_type=jnp.float32)
        count = products.shape[0]
        largest = jnp.maximum(jnp.max(jnp.abs(products), axis=0, keepdims=True), 2.0**-60)
        power = jnp.floor(jnp.log2(largest))
        coded = jnp.round(products * (jnp.exp2(RANGE - power) * FIT))
        out_ref[index, :count, :] = coded.astype(jnp.int32).astype(jnp.int16)
        line = jnp.broadcast_to(power, (out_ref.shape[1] - count, power.shape[1]))
        out_ref[index, count:, :] = line.astype(jnp.int32).astype(jnp.int16)


def row_products(own, left, after):
    ch, steps, count, width = own.shape
    columns = left.shape[2]
    each = 4
    return pl.pallas_call(
        products_kernel,
        grid=(ch // each,),
        in_specs=[pl.BlockSpec(memory_space=pltpu.VMEM)] * 2 + [pl.BlockSpec(memory_space=pl.ANY)] * len(after),
        out_specs=[
            pl.BlockSpec((each, count + EXTRA, columns), lambda i: (i, 0, 0)),
            pl.BlockSpec((16, LANES), lambda i: (0, 0)),
        ],
        out_shape=[
            pltpu.HBM((ch, count + EXTRA, columns), jnp.int16),
            jax.ShapeDtypeStruct((16, LANES), jnp.bfloat16),
        ],
        compiler_params=pltpu.CompilerParams(vmem_limit_bytes=10 << 20),
        cost_estimate=pl.CostEstimate(
            flops=2 * left.size * count, bytes_accessed=2 * left.size + 2 * own.size, transcendentals=0
        ),
        name="row_products",
    )(own, left, *after)


def finish_kernel(scale, slot_ref, coded_ref, *refs):
    out_ref, products, tile, mixed = refs[-4:]
    step = pl.program_id(0)
    sources, lines, width = coded_ref.shape
    count = lines - EXTRA
    pieces = width // LANES
    together = 8 // pieces

    @pl.when(step == 0)
    def _():
        for source in range(sources):
            power = coded_ref[source, count:, :][:1].astype(jnp.float32)
            values = coded_ref[source, :count, :].astype(jnp.float32) * (jnp.exp2(power - RANGE) * (scale / FIT))
            for piece in range(pieces):
                products[pl.ds(source * count * pieces + piece, count, stride=pieces), :] = values[
                    :, piece * LANES : (piece + 1) * LANES
                ]

    tiles = out_ref.shape[1] // 8

    @pl.loop(0, tiles)
    def _(j):
        for part in range(together):
            for i in range(LANES):
                line = slot_ref[((step * tiles + j) * together + part) * LANES + i]
                tile[i * pieces : (i + 1) * pieces, :] = products[pl.ds(pl.multiple_of(line, pieces), pieces), :]
            for piece in range(pieces):
                turned = tile[pl.ds(piece, LANES, stride=pieces), :].T
                mixed[pl.ds(part * pieces + piece, LANES, stride=8), :] = turned
        out_ref[:, pl.ds(pl.multiple_of(j * 8, 8), 8), :] = mixed[...].reshape(out_ref.shape[0], 8, LANES)


def finish(coded, places, index, pieces, scale, before):
    sources, lines, width = coded.shape
    rows = width // 2
    feeds = sources * (lines - EXTRA)
    columns = 2 * (feeds // LANES)
    earlier = [] if before is None else [before]
    return pl.pallas_call(
        functools.partial(finish_kernel, scale),
        grid=(columns // 16,),
        in_specs=[
            pl.BlockSpec(memory_space=pltpu.SMEM),
            pl.BlockSpec(memory_space=pltpu.VMEM),
        ]
        + [pl.BlockSpec(memory_space=pl.ANY)] * len(earlier),
        out_specs=pl.BlockSpec((rows, 16, LANES), lambda i: (index, i, 0)),
        out_shape=jax.ShapeDtypeStruct((pieces * rows, columns, LANES), jnp.float32),
        scratch_shapes=[
            pltpu.VMEM((feeds * width // LANES, LANES), jnp.float32),
            pltpu.VMEM((width, LANES), jnp.float32),
            pltpu.VMEM((8 * LANES, LANES), jnp.float32),
        ],
        input_output_aliases={2: 0} if earlier else {},
        compiler_params=pltpu.CompilerParams(vmem_limit_bytes=14 << 20),
        name="finish",
    )(places, coded, *earlier)


def through_rows(samples, gains, feed_slot):
    count, ch, frames = samples.shape
    spectra = frames - TAPS + 1
    pieces = ROWS // LANES
    lines = frames * ch
    unit = 16 * STEPS * 2
    total = pl.cdiv(lines + 4 * ch, unit) * unit
    words = jnp.transpose(samples, (2, 1, 0)).reshape(lines, count)
    scales = gains.reshape(2 * ch, count)
    weights = jnp.asarray(filter_weights(ch))
    place = lax.axis_index("feed").reshape(1)
    kept, sent = select_rows(place, words, scales, feed_slot.reshape(-1, LANES), ROWS, total)
    halves, firsts = zip(*[quarters(keep + swap(send, 1)) for keep, send in zip(kept, sent)])
    seconds = [eighths(first) for first in firsts]
    own, zero = own_spectra(words, scales.astype(jnp.float32), weights, ch, spectra, sum(seconds, ()))
    thirds = [cross(second) for second in seconds]
    thirds[0][0] = thirds[0][0] + zero[0, 0]
    ends = [gathered(*parts) for parts in zip(halves, firsts, thirds)]
    out, after = None, [ends[-1]]
    for index in range(pieces):
        rows = both_halves(ends[index])
        parts = rows[lines : lines + 4 * ch]
        left = row_spectra(rows, parts, weights, ch, spectra)
        coded, done = row_products(own, left, after)
        after = [done]
        moved = lax.all_to_all(coded, "feed", split_axis=0, concat_axis=0, tiled=True)
        out = finish(moved, feed_slot * 2, index, pieces, 1.0 / spectra, out)
    feeds = feed_slot.shape[0]
    out = out.reshape(ROWS, feeds // LANES, 2, LANES)
    return jnp.transpose(out, (0, 2, 1, 3)).reshape(ROWS, 2, feeds)


def body(samples, gains, feed_slot):
    count, ch, frames = samples.shape
    spectra = frames - TAPS + 1
    even = count % LANES == 0 and spectra % (STEPS * STEP) == 0 and ch % STEPS == 0
    if lax.axis_size("feed") == ch == 16 and even:
        return through_rows(samples, gains, feed_slot)
    return through_spectra(samples, gains, feed_slot)


def solution(mesh):
    return jax.shard_map(
        body,
        mesh=mesh,
        in_specs=(P(("band", "feed"), None, None), P(None, "band", "feed"), P()),
        out_specs=P(("band", "feed"), None, None),
        check_vma=False,
    )
```

```python
import functools
import math

import jax
import jax.numpy as jnp
import numpy as np
from jax import lax
from jax.experimental import pallas as pl
from jax.experimental.pallas import tpu as pltpu
from jax.sharding import PartitionSpec as P

TAPS = 8
ROWS = 256
LANES = 128


def filter_taps(ch):
    length = TAPS * ch
    place = np.arange(length, dtype=np.float64)
    window = 0.5 - 0.5 * np.cos(2.0 * math.pi * place / (length - 1))
    return (np.sinc((place - 0.5 * (length - 1)) / ch) * window).reshape(TAPS, ch)


def twiddle(value, turn):
    real, imag = value
    if turn == 0:
        return value
    if turn == 0.25:
        return imag, -real
    half = math.sqrt(0.5)
    if turn == 0.125:
        return half * (real + imag), half * (imag - real)
    if turn == 0.375:
        return half * (imag - real), -half * (real + imag)
    c, s = math.cos(2.0 * math.pi * turn), math.sin(2.0 * math.pi * turn)
    return c * real + s * imag, c * imag - s * real


def fft(values):
    count = len(values)
    if count == 1:
        return values
    even, odd = fft(values[0::2]), fft(values[1::2])
    low, high = [], []
    for index in range(count // 2):
        real, imag = twiddle(odd[index], index / count)
        low.append((even[index][0] + real, even[index][1] + imag))
        high.append((even[index][0] - real, even[index][1] - imag))
    return low + high


def channel_kernel(taps, *refs):
    *samples_refs, gains_ref, out_ref, filtered = refs
    ch, block, width = out_ref.shape
    spectra = width // 2
    padded = len(samples_refs) * LANES
    for k in range(ch):
        words = jnp.concatenate(
            [ref[pl.ds(k, block, stride=ch), :] for ref in samples_refs], axis=1
        )
        levels = ((words >> 4) - 8, (words & 15) - 8)
        for part in range(2):
            value = levels[part].astype(jnp.float32)
            shifted = [value] + [pltpu.roll(value, padded - t, 1) for t in range(1, TAPS // 2)]
            near = float(taps[0, k]) * shifted[0]
            far = float(taps[TAPS // 2, k]) * shifted[0]
            for t in range(1, TAPS // 2):
                near = near + float(taps[t, k]) * shifted[t]
                far = far + float(taps[t + TAPS // 2, k]) * shifted[t]
            total = near + pltpu.roll(far, padded - TAPS // 2, 1)
            filtered[2 * k + part] = total[:, :spectra]
    for row in range(0, block, 8):
        gains = gains_ref[row : row + 8, :]
        for lane in range(0, spectra, LANES):
            spot = (slice(row, row + 8), slice(lane, lane + LANES))
            values = [(filtered[2 * k][spot], filtered[2 * k + 1][spot]) for k in range(ch)]
            for c, (real, imag) in enumerate(fft(values)):
                gain_real = gains[:, c : c + 1]
                gain_imag = gains[:, ch + c : ch + c + 1]
                out_ref[c, row : row + 8, lane : lane + LANES] = (
                    gain_real * real - gain_imag * imag
                ).astype(out_ref.dtype)
                out_ref[c, row : row + 8, spectra + lane : spectra + lane + LANES] = (
                    gain_real * imag + gain_imag * real
                ).astype(out_ref.dtype)


def channelize(samples, gains):
    count, ch, frames = samples.shape
    spectra = frames - TAPS + 1
    block = 16
    pieces = pl.cdiv(frames, LANES)
    scale = 0.125 / math.sqrt(ch) / 2048.0
    taps = (filter_taps(ch) * scale).astype(np.float32)
    return pl.pallas_call(
        functools.partial(channel_kernel, taps),
        grid=(count // block,),
        in_specs=[
            pl.BlockSpec((block * ch, LANES), functools.partial(lambda piece, i: (i, piece), piece))
            for piece in range(pieces)
        ]
        + [pl.BlockSpec((block, 2 * ch), lambda i: (i, 0))],
        out_specs=pl.BlockSpec((ch, block, 2 * spectra), lambda i: (0, i, 0)),
        out_shape=jax.ShapeDtypeStruct((ch, count, 2 * spectra), jnp.bfloat16),
        scratch_shapes=[pltpu.VMEM((2 * ch, block, spectra), jnp.float32)],
        compiler_params=pltpu.CompilerParams(vmem_limit_bytes=32 << 20),
        name="channelize",
    )(*[samples.reshape(count * ch, frames)] * pieces, gains)


def correlate_kernel(scale, slot_ref, row_ref, data_ref, out_ref, products, tile):
    feeds, width = data_ref.shape
    spectra = width // 2
    rows = row_ref.shape[0]
    pieces = 2 * rows // LANES
    step = 256
    picked = jnp.zeros((rows, width), jnp.float32)
    for first in range(0, feeds, 512):
        place = lax.broadcasted_iota(jnp.int32, (rows, 512), 1) + first
        choice = jnp.where(row_ref[...] == place, 1.0, 0.0).astype(jnp.bfloat16)
        picked = picked + jnp.dot(
            choice, data_ref[first : first + 512, :], preferred_element_type=jnp.float32
        )
    left = jnp.concatenate(
        [
            picked,
            jnp.concatenate([picked[:, spectra:], -picked[:, :spectra]], axis=1),
        ],
        axis=0,
    ).astype(jnp.bfloat16)

    @pl.loop(0, feeds // step)
    def _(i):
        first = pl.multiple_of(i * step, step)
        result = lax.dot_general(
            data_ref[pl.ds(first, step), :],
            left,
            (((1,), (1,)), ((), ())),
            preferred_element_type=jnp.float32,
        )
        for piece in range(pieces):
            products[pl.ds(first * pieces + piece, step, stride=pieces), :] = (
                result[:, piece * LANES : (piece + 1) * LANES] * scale
            )

    lines = 2 * (feeds // LANES)

    @pl.loop(0, feeds // LANES)
    def _(j):
        @pl.loop(0, LANES, unroll=16)
        def _(i):
            slot = slot_ref[j * LANES + i]
            tile[pl.ds(pl.multiple_of(i * pieces, pieces), pieces), :] = products[
                pl.ds(pl.multiple_of(slot * pieces, pieces), pieces), :
            ]

        for piece in range(pieces):
            part, first = divmod(piece * LANES, rows)
            turned = tile[pl.ds(piece, LANES, stride=pieces), :].T
            out_ref[pl.ds(first * lines + 2 * j + part, LANES, stride=lines), :] = turned


def correlate(data, feed_slot, first, rows):
    feeds, width = data.shape
    row_slots = lax.dynamic_slice_in_dim(feed_slot, first, rows, 0).reshape(rows, 1)
    lines = 2 * (feeds // LANES)
    out = pl.pallas_call(
        functools.partial(correlate_kernel, 2.0 / width),
        in_specs=[
            pl.BlockSpec(memory_space=pltpu.SMEM),
            pl.BlockSpec(memory_space=pltpu.VMEM),
            pl.BlockSpec(memory_space=pltpu.VMEM),
        ],
        out_specs=pl.BlockSpec(memory_space=pltpu.VMEM),
        out_shape=jax.ShapeDtypeStruct((rows * lines, LANES), jnp.float32),
        scratch_shapes=[
            pltpu.VMEM((feeds * 2 * rows // LANES, LANES), jnp.float32),
            pltpu.VMEM((LANES * 2 * rows // LANES, LANES), jnp.float32),
        ],
        compiler_params=pltpu.CompilerParams(vmem_limit_bytes=48 << 20),
        name="correlate",
    )(feed_slot, row_slots, data)
    out = out.reshape(rows, feeds // LANES, 2, LANES)
    return jnp.transpose(out, (0, 2, 1, 3)).reshape(rows, 2, feeds)


def through_spectra(samples, gains, feed_slot):
    count, ch, _ = samples.shape
    groups = lax.axis_size("feed") // ch
    first = lax.axis_index("feed") % groups * ROWS
    scales = jnp.transpose(gains, (2, 0, 1)).reshape(count, 2 * ch).astype(jnp.float32)
    spectra = channelize(samples, scales)
    width = spectra.shape[2]
    outgoing = jnp.broadcast_to(spectra[:, None], (ch, groups, count, width))
    outgoing = outgoing.reshape(ch * groups, count, width)
    moved = lax.all_to_all(outgoing, "feed", split_axis=0, concat_axis=0, tiled=True)
    return correlate(moved.reshape(-1, width), feed_slot, first, ROWS)


STEP = 8
SPAN = 16
STEPS = 8
RANGE = 14
FIT = 1.0 - 2.0**-15
EXTRA = 8


def filter_weights(ch):
    taps = filter_taps(ch) * (0.125 / math.sqrt(ch) / 2048.0)
    half = ch // 2
    weights = np.zeros((ch, STEP, SPAN, ch))
    angle = 2.0 * math.pi * (np.arange(half + 1)[:, None] * np.arange(ch)[None, :] % ch) / ch
    sums = np.concatenate([np.cos(angle), np.sin(angle[1:half])], axis=0)
    for spectrum in range(STEP):
        for t in range(TAPS):
            weights[:, spectrum, spectrum + t] = taps[t] * sums
    weights = weights.reshape(ch * STEP, SPAN * ch)
    high = weights.astype(jnp.bfloat16)
    low = (weights - high.astype(np.float64)).astype(jnp.bfloat16)
    return np.concatenate([high, low])


def spectra_of(weights_ref, levels, gains, ch, store):
    count = levels[0].shape[1]
    half, size = ch // 2, ch * STEP
    beside = max(1, 256 // count)
    for first in range(0, STEPS, beside):
        totals = []
        for level in levels:
            slabs = [level[b * size : b * size + SPAN * ch] for b in range(first, first + beside)]
            slab = jnp.concatenate(slabs, axis=1) if beside > 1 else slabs[0]
            both = jnp.dot(weights_ref[...], slab, preferred_element_type=jnp.float32)
            totals.append(both[:size] + both[size:])
        for index in range(beside):
            lanes = slice(index * count, (index + 1) * count)
            parts = [
                [total[d * STEP : (d + 1) * STEP, lanes] for d in range(ch)] for total in totals
            ]
            for c in range(ch):
                place = min(c, ch - c)
                real, imag = parts[0][place], parts[1][place]
                if c % half:
                    sine_real, sine_imag = parts[0][half + place], parts[1][half + place]
                    if c < half:
                        real, imag = real + sine_imag, imag - sine_real
                    else:
                        real, imag = real - sine_imag, imag + sine_real
                gain_real, gain_imag = gains[c : c + 1], gains[ch + c : ch + c + 1]
                store(
                    first + index,
                    c,
                    gain_real * real - gain_imag * imag,
                    gain_real * imag + gain_imag * real,
                )


def levels_of(words):
    return [
        ((words >> 4) - 8).astype(jnp.float32).astype(jnp.bfloat16),
        ((words & 15) - 8).astype(jnp.float32).astype(jnp.bfloat16),
    ]


def own_kernel(main_ref, next_ref, gains_ref, weights_ref, *refs):
    out_ref, zero_ref, held = refs[-3:]
    step = pl.program_id(0)
    ch = out_ref.shape[0]
    zero_ref[...] = jnp.zeros_like(zero_ref)
    words = jnp.concatenate([main_ref[...], next_ref[...]], axis=0)

    def store(b, c, real, imag):
        held[c, b * 2 * STEP : (b + 1) * 2 * STEP, :] = jnp.concatenate([real, imag], axis=0).astype(held.dtype)

    spectra_of(weights_ref, levels_of(words), gains_ref[...], ch, store)
    for c in range(ch):
        out_ref[c, step] = held[c].T


def own_spectra(words, gains, weights, ch, spectra, after):
    count = words.shape[1]
    main = STEPS * STEP * ch
    steps = spectra // (STEPS * STEP)
    return pl.pallas_call(
        own_kernel,
        grid=(steps,),
        in_specs=[
            pl.BlockSpec((main, count), lambda i: (i, 0)),
            pl.BlockSpec((STEP * ch, count), lambda i: ((i + 1) * STEPS, 0)),
            pl.BlockSpec(gains.shape, lambda i: (0, 0)),
            pl.BlockSpec(weights.shape, lambda i: (0, 0)),
        ]
        + [pl.BlockSpec(memory_space=pl.ANY)] * len(after),
        out_specs=[
            pl.BlockSpec(memory_space=pltpu.VMEM),
            pl.BlockSpec((16, LANES), lambda i: (0, 0)),
        ],
        out_shape=[
            jax.ShapeDtypeStruct((ch, steps, count, 2 * STEPS * STEP), jnp.bfloat16),
            jax.ShapeDtypeStruct((16, LANES), jnp.bfloat16),
        ],
        scratch_shapes=[
            pltpu.VMEM((ch, 2 * STEPS * STEP, count), jnp.bfloat16),
        ],
        compiler_params=pltpu.CompilerParams(vmem_limit_bytes=12 << 20),
        cost_estimate=pl.CostEstimate(
            flops=4 * spectra * ch * 2 * SPAN * ch * count,
            bytes_accessed=4 * words.size + 4 * ch * spectra * count,
            transcendentals=0,
        ),
        name="own_spectra",
    )(words, words, gains, weights, *after)


def select_kernel(block, place_ref, slots_ref, words_ref, gains_ref, *outs):
    lines, count = words_ref.shape
    rows = len(outs) * LANES
    place = lax.broadcasted_iota(jnp.int32, (count, rows), 0) + place_ref[0] * count
    slots = jnp.concatenate([slots_ref[index : index + 1, :] for index in range(len(outs))], axis=1)
    choice = jnp.where(slots == place, 1.0, 0.0).astype(jnp.bfloat16)

    def put(first, values):
        size = values.shape[0]
        values = values.astype(jnp.float32).astype(jnp.bfloat16)
        taken = jnp.dot(values, choice, preferred_element_type=jnp.float32).astype(outs[0].dtype)
        for index, out_ref in enumerate(outs):
            out_ref[first : first + size, :] = taken[:, index * LANES : (index + 1) * LANES]

    for first in range(0, lines, block):
        put(first, words_ref[first : min(first + block, lines), :])
    gains = gains_ref[...]
    put(lines, jnp.concatenate([gains >> 4, gains & 15], axis=0))
    first = lines + 2 * gains.shape[0]
    for out_ref in outs:
        out_ref[first:, :] = jnp.zeros((out_ref.shape[0] - first, LANES), out_ref.dtype)


def at_hand(value):
    return pltpu.with_memory_space_constraint(value, pltpu.HBM)


def select_rows(place, words, gains, slots, rows, total):
    return pl.pallas_call(
        functools.partial(select_kernel, total // STEPS),
        grid=(1,),
        in_specs=[
            pl.BlockSpec(memory_space=pltpu.SMEM),
            pl.BlockSpec((8, LANES), lambda i: (0, 0)),
            pl.BlockSpec(memory_space=pltpu.VMEM),
            pl.BlockSpec(gains.shape, lambda i: (0, 0)),
        ],
        out_specs=[pl.BlockSpec(memory_space=pltpu.VMEM)] * (rows // LANES),
        out_shape=[jax.ShapeDtypeStruct((total, LANES), jnp.bfloat16)] * (rows // LANES),
        compiler_params=pltpu.CompilerParams(vmem_limit_bytes=12 << 20),
        name="select_rows",
    )(place, at_hand(slots), words, at_hand(gains))


def swap(value, bit):
    pairs = [(index, index ^ bit) for index in range(lax.axis_size("feed"))]
    return lax.ppermute(value, "feed", pairs)


def side(bit):
    return lax.axis_index("feed") // bit % 2


def reduce_half(value, bit):
    size = value.shape[0] // 2
    keep = lax.dynamic_slice_in_dim(value, side(bit) * size, size, 0)
    send = lax.dynamic_slice_in_dim(value, (1 - side(bit)) * size, size, 0)
    return keep + swap(send, bit)


def add_kernel(place_ref, value_ref, other_ref, out_ref):
    size = out_ref.shape[0]
    block = size // STEPS
    start = place_ref[0] % 2 * size

    @pl.loop(0, STEPS)
    def _(step):
        mine = value_ref[pl.ds(pl.multiple_of(start + step * block, 16), block), :]
        spot = pl.ds(pl.multiple_of(step * block, 16), block)
        out_ref[spot, :] = mine + other_ref[spot, :]


def reduce_core(place, value):
    size = value.shape[0] // 2
    send = lax.dynamic_slice_in_dim(value, (1 - side(1)) * size, size, 0)
    return pl.pallas_call(
        add_kernel,
        grid=(1,),
        in_specs=[pl.BlockSpec(memory_space=pltpu.SMEM)] + [pl.BlockSpec(memory_space=pltpu.VMEM)] * 2,
        out_specs=pl.BlockSpec(memory_space=pltpu.VMEM),
        out_shape=jax.ShapeDtypeStruct((size, value.shape[1]), value.dtype),
        compiler_params=pltpu.CompilerParams(vmem_limit_bytes=4 << 20),
        name="add_halves",
    )(place, value, swap(send, 1))


def gather_half(value, bit, buffer):
    size = value.shape[0]
    other = swap(value, bit)
    buffer = lax.dynamic_update_slice_in_dim(buffer, value, side(bit) * size, 0)
    return lax.dynamic_update_slice_in_dim(buffer, other, (1 - side(bit)) * size, 0)


def quarters(half):
    size = half.shape[0] // 2
    left, right = half[:size], half[size:]
    left_1, right_1 = reduce_half(left, 2), reduce_half(right, 4)
    return (left, right), (left_1, right_1)


def eighths(first):
    return reduce_half(first[0], 4), reduce_half(first[1], 2)


def cross(second):
    return [value + swap(value, 8) for value in second]


def gathered(half, first, third):
    left_1, right_1 = gather_half(third[0], 4, first[0]), gather_half(third[1], 2, first[1])
    left, right = gather_half(left_1, 2, half[0]), gather_half(right_1, 4, half[1])
    return jnp.concatenate([left, right], axis=0)


def rows_kernel(words_ref, parts_ref, weights_ref, out_ref):
    ch, rows = out_ref.shape[0], words_ref.shape[1]
    width = 2 * STEPS * STEP
    main = STEPS * STEP * ch
    parts = parts_ref[...].astype(jnp.float32)
    gains = parts[: 2 * ch] * 16.0 + parts[2 * ch :]

    @pl.loop(0, out_ref.shape[1] // width)
    def _(step):
        words = words_ref[pl.ds(pl.multiple_of(step * main, main), main + STEP * ch), :]
        words = words.astype(jnp.float32).astype(jnp.int32)

        def store(b, c, real, imag):
            spot = pl.ds(pl.multiple_of(step * width, width) + b * 2 * STEP, 2 * STEP)
            out_ref[c, spot, :rows] = jnp.concatenate([real, imag], axis=0).astype(out_ref.dtype)
            out_ref[c, spot, rows:] = jnp.concatenate([imag, -real], axis=0).astype(out_ref.dtype)

        spectra_of(weights_ref, levels_of(words), gains, ch, store)


def row_spectra(words, parts, weights, ch, spectra):
    rows = words.shape[1]
    return pl.pallas_call(
        rows_kernel,
        grid=(1,),
        in_specs=[
            pl.BlockSpec(memory_space=pltpu.VMEM),
            pl.BlockSpec(parts.shape, lambda i: (0, 0)),
            pl.BlockSpec(weights.shape, lambda i: (0, 0)),
        ],
        out_specs=pl.BlockSpec(memory_space=pltpu.VMEM),
        out_shape=jax.ShapeDtypeStruct((ch, 2 * spectra, 2 * rows), jnp.bfloat16),
        compiler_params=pltpu.CompilerParams(vmem_limit_bytes=8 << 20),
        cost_estimate=pl.CostEstimate(
            flops=8 * spectra * ch * SPAN * ch * rows,
            bytes_accessed=2 * words.size + 8 * ch * spectra * rows,
            transcendentals=0,
        ),
        name="row_spectra",
    )(words, parts, weights)


def products_kernel(own_ref, left_ref, *refs):
    out_ref, done_ref = refs[-2:]
    done_ref[...] = jnp.zeros_like(done_ref)
    each, steps = out_ref.shape[0], own_ref.shape[1]
    for index in range(each):
        c = pl.program_id(0) * each + index
        spectra = jnp.concatenate([own_ref[c, part] for part in range(steps)], axis=1)
        products = jnp.dot(spectra, left_ref[c], preferred_element_type=jnp.float32)
        count = products.shape[0]
        largest = jnp.maximum(jnp.max(jnp.abs(products), axis=0, keepdims=True), 2.0**-60)
        power = jnp.floor(jnp.log2(largest))
        coded = jnp.round(products * (jnp.exp2(RANGE - power) * FIT))
        out_ref[index, :count, :] = coded.astype(jnp.int32).astype(jnp.int16)
        line = jnp.broadcast_to(power, (out_ref.shape[1] - count, power.shape[1]))
        out_ref[index, count:, :] = line.astype(jnp.int32).astype(jnp.int16)


def row_products(own, left, after):
    ch, steps, count, width = own.shape
    columns = left.shape[2]
    each = 4
    return pl.pallas_call(
        products_kernel,
        grid=(ch // each,),
        in_specs=[pl.BlockSpec(memory_space=pltpu.VMEM)] * 2 + [pl.BlockSpec(memory_space=pl.ANY)] * len(after),
        out_specs=[
            pl.BlockSpec((each, count + EXTRA, columns), lambda i: (i, 0, 0)),
            pl.BlockSpec((16, LANES), lambda i: (0, 0)),
        ],
        out_shape=[
            pltpu.HBM((ch, count + EXTRA, columns), jnp.int16),
            jax.ShapeDtypeStruct((16, LANES), jnp.bfloat16),
        ],
        compiler_params=pltpu.CompilerParams(vmem_limit_bytes=10 << 20),
        cost_estimate=pl.CostEstimate(
            flops=2 * left.size * count, bytes_accessed=2 * left.size + 2 * own.size, transcendentals=0
        ),
        name="row_products",
    )(own, left, *after)


def finish_kernel(scale, slot_ref, coded_ref, *refs):
    out_ref, products, tile, mixed = refs[-4:]
    step = pl.program_id(0)
    sources, lines, width = coded_ref.shape
    count = lines - EXTRA
    pieces = width // LANES
    together = 8 // pieces

    @pl.when(step == 0)
    def _():
        for source in range(sources):
            power = coded_ref[source, count:, :][:1].astype(jnp.float32)
            values = coded_ref[source, :count, :].astype(jnp.float32) * (jnp.exp2(power - RANGE) * (scale / FIT))
            for piece in range(pieces):
                products[pl.ds(source * count * pieces + piece, count, stride=pieces), :] = values[
                    :, piece * LANES : (piece + 1) * LANES
                ]

    tiles = out_ref.shape[1] // 8

    @pl.loop(0, tiles)
    def _(j):
        for part in range(together):
            for i in range(LANES):
                line = slot_ref[((step * tiles + j) * together + part) * LANES + i]
                tile[i * pieces : (i + 1) * pieces, :] = products[pl.ds(pl.multiple_of(line, pieces), pieces), :]
            for piece in range(pieces):
                turned = tile[pl.ds(piece, LANES, stride=pieces), :].T
                mixed[pl.ds(part * pieces + piece, LANES, stride=8), :] = turned
        out_ref[:, pl.ds(pl.multiple_of(j * 8, 8), 8), :] = mixed[...].reshape(out_ref.shape[0], 8, LANES)


def finish(coded, places, index, pieces, scale, before):
    sources, lines, width = coded.shape
    rows = width // 2
    feeds = sources * (lines - EXTRA)
    columns = 2 * (feeds // LANES)
    earlier = [] if before is None else [before]
    return pl.pallas_call(
        functools.partial(finish_kernel, scale),
        grid=(columns // 16,),
        in_specs=[
            pl.BlockSpec(memory_space=pltpu.SMEM),
            pl.BlockSpec(memory_space=pltpu.VMEM),
        ]
        + [pl.BlockSpec(memory_space=pl.ANY)] * len(earlier),
        out_specs=pl.BlockSpec((rows, 16, LANES), lambda i: (index, i, 0)),
        out_shape=jax.ShapeDtypeStruct((pieces * rows, columns, LANES), jnp.float32),
        scratch_shapes=[
            pltpu.VMEM((feeds * width // LANES, LANES), jnp.float32),
            pltpu.VMEM((width, LANES), jnp.float32),
            pltpu.VMEM((8 * LANES, LANES), jnp.float32),
        ],
        input_output_aliases={2: 0} if earlier else {},
        compiler_params=pltpu.CompilerParams(vmem_limit_bytes=14 << 20),
        name="finish",
    )(places, coded, *earlier)


def through_rows(samples, gains, feed_slot):
    count, ch, frames = samples.shape
    spectra = frames - TAPS + 1
    pieces = ROWS // LANES
    lines = frames * ch
    unit = 16 * STEPS * 2
    total = pl.cdiv(lines + 4 * ch, unit) * unit
    words = jnp.transpose(samples, (2, 1, 0)).reshape(lines, count)
    scales = gains.reshape(2 * ch, count)
    weights = jnp.asarray(filter_weights(ch))
    place = lax.axis_index("feed").reshape(1)
    picked = select_rows(place, words, scales, feed_slot.reshape(-1, LANES), ROWS, total)
    halves, firsts = zip(*[quarters(reduce_core(place, value)) for value in picked])
    seconds = [eighths(first) for first in firsts]
    own, zero = own_spectra(words, scales.astype(jnp.float32), weights, ch, spectra, sum(seconds, ()))
    thirds = [cross(second) for second in seconds]
    thirds[0][0] = thirds[0][0] + zero[0, 0]
    ends = [gathered(*parts) for parts in zip(halves, firsts, thirds)]
    out, after = None, [ends[-1]]
    for index in range(pieces):
        rows = gather_half(ends[index], 1, picked[index])
        parts = rows[lines : lines + 4 * ch]
        left = row_spectra(rows, parts, weights, ch, spectra)
        coded, done = row_products(own, left, after)
        after = [done]
        moved = lax.all_to_all(coded, "feed", split_axis=0, concat_axis=0, tiled=True)
        out = finish(moved, feed_slot * 2, index, pieces, 1.0 / spectra, out)
    feeds = feed_slot.shape[0]
    out = out.reshape(ROWS, feeds // LANES, 2, LANES)
    return jnp.transpose(out, (0, 2, 1, 3)).reshape(ROWS, 2, feeds)


def body(samples, gains, feed_slot):
    count, ch, frames = samples.shape
    spectra = frames - TAPS + 1
    even = count % LANES == 0 and spectra % (STEPS * STEP) == 0 and ch % STEPS == 0
    if lax.axis_size("feed") == ch == 16 and even:
        return through_rows(samples, gains, feed_slot)
    return through_spectra(samples, gains, feed_slot)


def solution(mesh):
    return jax.shard_map(
        body,
        mesh=mesh,
        in_specs=(P(("band", "feed"), None, None), P(None, "band", "feed"), P()),
        out_specs=P(("band", "feed"), None, None),
        check_vma=False,
    )
```

```python
import functools
import math

import jax
import jax.numpy as jnp
import numpy as np
from jax import lax
from jax.experimental import pallas as pl
from jax.experimental.pallas import tpu as pltpu
from jax.sharding import PartitionSpec as P

TAPS = 8
ROWS = 256
LANES = 128


def filter_taps(ch):
    length = TAPS * ch
    place = np.arange(length, dtype=np.float64)
    window = 0.5 - 0.5 * np.cos(2.0 * math.pi * place / (length - 1))
    return (np.sinc((place - 0.5 * (length - 1)) / ch) * window).reshape(TAPS, ch)


def twiddle(value, turn):
    real, imag = value
    if turn == 0:
        return value
    if turn == 0.25:
        return imag, -real
    half = math.sqrt(0.5)
    if turn == 0.125:
        return half * (real + imag), half * (imag - real)
    if turn == 0.375:
        return half * (imag - real), -half * (real + imag)
    c, s = math.cos(2.0 * math.pi * turn), math.sin(2.0 * math.pi * turn)
    return c * real + s * imag, c * imag - s * real


def fft(values):
    count = len(values)
    if count == 1:
        return values
    even, odd = fft(values[0::2]), fft(values[1::2])
    low, high = [], []
    for index in range(count // 2):
        real, imag = twiddle(odd[index], index / count)
        low.append((even[index][0] + real, even[index][1] + imag))
        high.append((even[index][0] - real, even[index][1] - imag))
    return low + high


def channel_kernel(taps, *refs):
    *samples_refs, gains_ref, out_ref, filtered = refs
    ch, block, width = out_ref.shape
    spectra = width // 2
    padded = len(samples_refs) * LANES
    for k in range(ch):
        words = jnp.concatenate(
            [ref[pl.ds(k, block, stride=ch), :] for ref in samples_refs], axis=1
        )
        levels = ((words >> 4) - 8, (words & 15) - 8)
        for part in range(2):
            value = levels[part].astype(jnp.float32)
            shifted = [value] + [pltpu.roll(value, padded - t, 1) for t in range(1, TAPS // 2)]
            near = float(taps[0, k]) * shifted[0]
            far = float(taps[TAPS // 2, k]) * shifted[0]
            for t in range(1, TAPS // 2):
                near = near + float(taps[t, k]) * shifted[t]
                far = far + float(taps[t + TAPS // 2, k]) * shifted[t]
            total = near + pltpu.roll(far, padded - TAPS // 2, 1)
            filtered[2 * k + part] = total[:, :spectra]
    for row in range(0, block, 8):
        gains = gains_ref[row : row + 8, :]
        for lane in range(0, spectra, LANES):
            spot = (slice(row, row + 8), slice(lane, lane + LANES))
            values = [(filtered[2 * k][spot], filtered[2 * k + 1][spot]) for k in range(ch)]
            for c, (real, imag) in enumerate(fft(values)):
                gain_real = gains[:, c : c + 1]
                gain_imag = gains[:, ch + c : ch + c + 1]
                out_ref[c, row : row + 8, lane : lane + LANES] = (
                    gain_real * real - gain_imag * imag
                ).astype(out_ref.dtype)
                out_ref[c, row : row + 8, spectra + lane : spectra + lane + LANES] = (
                    gain_real * imag + gain_imag * real
                ).astype(out_ref.dtype)


def channelize(samples, gains):
    count, ch, frames = samples.shape
    spectra = frames - TAPS + 1
    block = 16
    pieces = pl.cdiv(frames, LANES)
    scale = 0.125 / math.sqrt(ch) / 2048.0
    taps = (filter_taps(ch) * scale).astype(np.float32)
    return pl.pallas_call(
        functools.partial(channel_kernel, taps),
        grid=(count // block,),
        in_specs=[
            pl.BlockSpec((block * ch, LANES), functools.partial(lambda piece, i: (i, piece), piece))
            for piece in range(pieces)
        ]
        + [pl.BlockSpec((block, 2 * ch), lambda i: (i, 0))],
        out_specs=pl.BlockSpec((ch, block, 2 * spectra), lambda i: (0, i, 0)),
        out_shape=jax.ShapeDtypeStruct((ch, count, 2 * spectra), jnp.bfloat16),
        scratch_shapes=[pltpu.VMEM((2 * ch, block, spectra), jnp.float32)],
        compiler_params=pltpu.CompilerParams(vmem_limit_bytes=32 << 20),
        name="channelize",
    )(*[samples.reshape(count * ch, frames)] * pieces, gains)


def correlate_kernel(scale, slot_ref, row_ref, data_ref, out_ref, products, tile):
    feeds, width = data_ref.shape
    spectra = width // 2
    rows = row_ref.shape[0]
    pieces = 2 * rows // LANES
    step = 256
    picked = jnp.zeros((rows, width), jnp.float32)
    for first in range(0, feeds, 512):
        place = lax.broadcasted_iota(jnp.int32, (rows, 512), 1) + first
        choice = jnp.where(row_ref[...] == place, 1.0, 0.0).astype(jnp.bfloat16)
        picked = picked + jnp.dot(
            choice, data_ref[first : first + 512, :], preferred_element_type=jnp.float32
        )
    left = jnp.concatenate(
        [
            picked,
            jnp.concatenate([picked[:, spectra:], -picked[:, :spectra]], axis=1),
        ],
        axis=0,
    ).astype(jnp.bfloat16)

    @pl.loop(0, feeds // step)
    def _(i):
        first = pl.multiple_of(i * step, step)
        result = lax.dot_general(
            data_ref[pl.ds(first, step), :],
            left,
            (((1,), (1,)), ((), ())),
            preferred_element_type=jnp.float32,
        )
        for piece in range(pieces):
            products[pl.ds(first * pieces + piece, step, stride=pieces), :] = (
                result[:, piece * LANES : (piece + 1) * LANES] * scale
            )

    lines = 2 * (feeds // LANES)

    @pl.loop(0, feeds // LANES)
    def _(j):
        @pl.loop(0, LANES, unroll=16)
        def _(i):
            slot = slot_ref[j * LANES + i]
            tile[pl.ds(pl.multiple_of(i * pieces, pieces), pieces), :] = products[
                pl.ds(pl.multiple_of(slot * pieces, pieces), pieces), :
            ]

        for piece in range(pieces):
            part, first = divmod(piece * LANES, rows)
            turned = tile[pl.ds(piece, LANES, stride=pieces), :].T
            out_ref[pl.ds(first * lines + 2 * j + part, LANES, stride=lines), :] = turned


def correlate(data, feed_slot, first, rows):
    feeds, width = data.shape
    row_slots = lax.dynamic_slice_in_dim(feed_slot, first, rows, 0).reshape(rows, 1)
    lines = 2 * (feeds // LANES)
    out = pl.pallas_call(
        functools.partial(correlate_kernel, 2.0 / width),
        in_specs=[
            pl.BlockSpec(memory_space=pltpu.SMEM),
            pl.BlockSpec(memory_space=pltpu.VMEM),
            pl.BlockSpec(memory_space=pltpu.VMEM),
        ],
        out_specs=pl.BlockSpec(memory_space=pltpu.VMEM),
        out_shape=jax.ShapeDtypeStruct((rows * lines, LANES), jnp.float32),
        scratch_shapes=[
            pltpu.VMEM((feeds * 2 * rows // LANES, LANES), jnp.float32),
            pltpu.VMEM((LANES * 2 * rows // LANES, LANES), jnp.float32),
        ],
        compiler_params=pltpu.CompilerParams(vmem_limit_bytes=48 << 20),
        name="correlate",
    )(feed_slot, row_slots, data)
    out = out.reshape(rows, feeds // LANES, 2, LANES)
    return jnp.transpose(out, (0, 2, 1, 3)).reshape(rows, 2, feeds)


def through_spectra(samples, gains, feed_slot):
    count, ch, _ = samples.shape
    groups = lax.axis_size("feed") // ch
    first = lax.axis_index("feed") % groups * ROWS
    scales = jnp.transpose(gains, (2, 0, 1)).reshape(count, 2 * ch).astype(jnp.float32)
    spectra = channelize(samples, scales)
    width = spectra.shape[2]
    outgoing = jnp.broadcast_to(spectra[:, None], (ch, groups, count, width))
    outgoing = outgoing.reshape(ch * groups, count, width)
    moved = lax.all_to_all(outgoing, "feed", split_axis=0, concat_axis=0, tiled=True)
    return correlate(moved.reshape(-1, width), feed_slot, first, ROWS)


STEP = 8
SPAN = 16
STEPS = 8
RANGE = 14
FIT = 1.0 - 2.0**-15
EXTRA = 8


def filter_weights(ch):
    taps = filter_taps(ch) * (0.125 / math.sqrt(ch) / 2048.0)
    half = ch // 2
    weights = np.zeros((ch, STEP, SPAN, ch))
    angle = 2.0 * math.pi * (np.arange(half + 1)[:, None] * np.arange(ch)[None, :] % ch) / ch
    sums = np.concatenate([np.cos(angle), np.sin(angle[1:half])], axis=0)
    for spectrum in range(STEP):
        for t in range(TAPS):
            weights[:, spectrum, spectrum + t] = taps[t] * sums
    weights = weights.reshape(ch * STEP, SPAN * ch)
    high = weights.astype(jnp.bfloat16)
    low = (weights - high.astype(np.float64)).astype(jnp.bfloat16)
    return np.concatenate([high, low])


def spectra_of(weights_ref, levels, gains, ch, store):
    count = levels[0].shape[1]
    half, size = ch // 2, ch * STEP
    beside = max(1, 256 // count)
    for first in range(0, STEPS, beside):
        totals = []
        for level in levels:
            slabs = [level[b * size : b * size + SPAN * ch] for b in range(first, first + beside)]
            slab = jnp.concatenate(slabs, axis=1) if beside > 1 else slabs[0]
            both = jnp.dot(weights_ref[...], slab, preferred_element_type=jnp.float32)
            totals.append(both[:size] + both[size:])
        for index in range(beside):
            lanes = slice(index * count, (index + 1) * count)
            parts = [
                [total[d * STEP : (d + 1) * STEP, lanes] for d in range(ch)] for total in totals
            ]
            for c in range(ch):
                place = min(c, ch - c)
                real, imag = parts[0][place], parts[1][place]
                if c % half:
                    sine_real, sine_imag = parts[0][half + place], parts[1][half + place]
                    if c < half:
                        real, imag = real + sine_imag, imag - sine_real
                    else:
                        real, imag = real - sine_imag, imag + sine_real
                gain_real, gain_imag = gains[c : c + 1], gains[ch + c : ch + c + 1]
                store(
                    first + index,
                    c,
                    gain_real * real - gain_imag * imag,
                    gain_real * imag + gain_imag * real,
                )


def levels_of(words):
    return [
        ((words >> 4) - 8).astype(jnp.float32).astype(jnp.bfloat16),
        ((words & 15) - 8).astype(jnp.float32).astype(jnp.bfloat16),
    ]


def own_kernel(main_ref, next_ref, gains_ref, weights_ref, *refs):
    out_ref, zero_ref, held = refs[-3:]
    step = pl.program_id(0)
    ch = out_ref.shape[0]
    zero_ref[...] = jnp.zeros_like(zero_ref)
    words = jnp.concatenate([main_ref[...], next_ref[...]], axis=0)

    def store(b, c, real, imag):
        held[c, b * 2 * STEP : (b + 1) * 2 * STEP, :] = jnp.concatenate([real, imag], axis=0).astype(held.dtype)

    spectra_of(weights_ref, levels_of(words), gains_ref[...], ch, store)
    for c in range(ch):
        out_ref[c, step] = held[c].T


def own_spectra(words, gains, weights, ch, spectra, after):
    count = words.shape[1]
    main = STEPS * STEP * ch
    steps = spectra // (STEPS * STEP)
    return pl.pallas_call(
        own_kernel,
        grid=(steps,),
        in_specs=[
            pl.BlockSpec((main, count), lambda i: (i, 0)),
            pl.BlockSpec((STEP * ch, count), lambda i: ((i + 1) * STEPS, 0)),
            pl.BlockSpec(gains.shape, lambda i: (0, 0)),
            pl.BlockSpec(weights.shape, lambda i: (0, 0)),
        ]
        + [pl.BlockSpec(memory_space=pl.ANY)] * len(after),
        out_specs=[
            pl.BlockSpec(memory_space=pltpu.VMEM),
            pl.BlockSpec((16, LANES), lambda i: (0, 0)),
        ],
        out_shape=[
            jax.ShapeDtypeStruct((ch, steps, count, 2 * STEPS * STEP), jnp.bfloat16),
            jax.ShapeDtypeStruct((16, LANES), jnp.bfloat16),
        ],
        scratch_shapes=[
            pltpu.VMEM((ch, 2 * STEPS * STEP, count), jnp.bfloat16),
        ],
        compiler_params=pltpu.CompilerParams(vmem_limit_bytes=12 << 20),
        cost_estimate=pl.CostEstimate(
            flops=4 * spectra * ch * 2 * SPAN * ch * count,
            bytes_accessed=4 * words.size + 4 * ch * spectra * count,
            transcendentals=0,
        ),
        name="own_spectra",
    )(words, words, gains, weights, *after)


def select_kernel(block, place_ref, slots_ref, words_ref, gains_ref, *refs):
    lines, count = words_ref.shape
    outs, sends = refs[: len(refs) // 2], refs[len(refs) // 2 :]
    rows, size = len(outs) * LANES, sends[0].shape[0]
    place = lax.broadcasted_iota(jnp.int32, (count, rows), 0) + place_ref[0] * count
    slots = jnp.concatenate([slots_ref[index : index + 1, :] for index in range(len(outs))], axis=1)
    choice = jnp.where(slots == place, 1.0, 0.0).astype(jnp.bfloat16)

    def store(first, taken):
        half = first // size
        spot = slice(first - half * size, first - half * size + taken.shape[0])
        for index, out_ref in enumerate(outs):
            out_ref[first : first + taken.shape[0], :] = taken[:, index * LANES : (index + 1) * LANES]

        @pl.when(place_ref[0] % 2 != half)
        def _():
            for index, send_ref in enumerate(sends):
                send_ref[spot, :] = taken[:, index * LANES : (index + 1) * LANES]

    def put(first, values):
        values = values.astype(jnp.float32).astype(jnp.bfloat16)
        store(first, jnp.dot(values, choice, preferred_element_type=jnp.float32).astype(outs[0].dtype))

    for first in range(0, lines, block):
        put(first, words_ref[first : min(first + block, lines), :])
    gains = gains_ref[...]
    put(lines, jnp.concatenate([gains >> 4, gains & 15], axis=0))
    first = lines + 2 * gains.shape[0]
    store(first, jnp.zeros((2 * size - first, rows), outs[0].dtype))


def at_hand(value):
    return pltpu.with_memory_space_constraint(value, pltpu.HBM)


def select_rows(place, words, gains, slots, rows, total):
    pieces = rows // LANES
    outs = pl.pallas_call(
        functools.partial(select_kernel, total // STEPS),
        grid=(1,),
        in_specs=[
            pl.BlockSpec(memory_space=pltpu.SMEM),
            pl.BlockSpec((8, LANES), lambda i: (0, 0)),
            pl.BlockSpec(memory_space=pltpu.VMEM),
            pl.BlockSpec(gains.shape, lambda i: (0, 0)),
        ],
        out_specs=[pl.BlockSpec(memory_space=pltpu.VMEM)] * (2 * pieces),
        out_shape=[jax.ShapeDtypeStruct((total, LANES), jnp.bfloat16)] * pieces
        + [jax.ShapeDtypeStruct((total // 2, LANES), jnp.bfloat16)] * pieces,
        compiler_params=pltpu.CompilerParams(vmem_limit_bytes=12 << 20),
        name="select_rows",
    )(place, at_hand(slots), words, at_hand(gains))
    return outs[:pieces], outs[pieces:]


def swap(value, bit):
    pairs = [(index, index ^ bit) for index in range(lax.axis_size("feed"))]
    return lax.ppermute(value, "feed", pairs)


def side(bit):
    return lax.axis_index("feed") // bit % 2


def reduce_half(value, bit):
    size = value.shape[0] // 2
    keep = lax.dynamic_slice_in_dim(value, side(bit) * size, size, 0)
    send = lax.dynamic_slice_in_dim(value, (1 - side(bit)) * size, size, 0)
    return keep + swap(send, bit)


def add_kernel(place_ref, value_ref, other_ref, out_ref):
    size = out_ref.shape[0]
    block = size // STEPS
    start = place_ref[0] % 2 * size

    @pl.loop(0, STEPS)
    def _(step):
        mine = value_ref[pl.ds(pl.multiple_of(start + step * block, 16), block), :]
        spot = pl.ds(pl.multiple_of(step * block, 16), block)
        out_ref[spot, :] = mine + other_ref[spot, :]


def reduce_core(place, value, send):
    return pl.pallas_call(
        add_kernel,
        grid=(1,),
        in_specs=[pl.BlockSpec(memory_space=pltpu.SMEM)] + [pl.BlockSpec(memory_space=pltpu.VMEM)] * 2,
        out_specs=pl.BlockSpec(memory_space=pltpu.VMEM),
        out_shape=jax.ShapeDtypeStruct(send.shape, value.dtype),
        compiler_params=pltpu.CompilerParams(vmem_limit_bytes=4 << 20),
        name="add_halves",
    )(place, value, swap(send, 1))


def gather_half(value, bit, buffer):
    size = value.shape[0]
    other = swap(value, bit)
    buffer = lax.dynamic_update_slice_in_dim(buffer, value, side(bit) * size, 0)
    return lax.dynamic_update_slice_in_dim(buffer, other, (1 - side(bit)) * size, 0)


def quarters(half):
    size = half.shape[0] // 2
    left, right = half[:size], half[size:]
    left_1, right_1 = reduce_half(left, 2), reduce_half(right, 4)
    return (left, right), (left_1, right_1)


def eighths(first):
    return reduce_half(first[0], 4), reduce_half(first[1], 2)


def cross(second):
    return [value + swap(value, 8) for value in second]


def gathered(half, first, third):
    left_1, right_1 = gather_half(third[0], 4, first[0]), gather_half(third[1], 2, first[1])
    left, right = gather_half(left_1, 2, half[0]), gather_half(right_1, 4, half[1])
    return jnp.concatenate([left, right], axis=0)


def rows_kernel(words_ref, parts_ref, weights_ref, out_ref):
    ch, rows = out_ref.shape[0], words_ref.shape[1]
    width = 2 * STEPS * STEP
    main = STEPS * STEP * ch
    parts = parts_ref[...].astype(jnp.float32)
    gains = parts[: 2 * ch] * 16.0 + parts[2 * ch :]

    @pl.loop(0, out_ref.shape[1] // width)
    def _(step):
        words = words_ref[pl.ds(pl.multiple_of(step * main, main), main + STEP * ch), :]
        words = words.astype(jnp.float32).astype(jnp.int32)

        def store(b, c, real, imag):
            spot = pl.ds(pl.multiple_of(step * width, width) + b * 2 * STEP, 2 * STEP)
            out_ref[c, spot, :rows] = jnp.concatenate([real, imag], axis=0).astype(out_ref.dtype)
            out_ref[c, spot, rows:] = jnp.concatenate([imag, -real], axis=0).astype(out_ref.dtype)

        spectra_of(weights_ref, levels_of(words), gains, ch, store)


def row_spectra(words, parts, weights, ch, spectra):
    rows = words.shape[1]
    return pl.pallas_call(
        rows_kernel,
        grid=(1,),
        in_specs=[
            pl.BlockSpec(memory_space=pltpu.VMEM),
            pl.BlockSpec(parts.shape, lambda i: (0, 0)),
            pl.BlockSpec(weights.shape, lambda i: (0, 0)),
        ],
        out_specs=pl.BlockSpec(memory_space=pltpu.VMEM),
        out_shape=jax.ShapeDtypeStruct((ch, 2 * spectra, 2 * rows), jnp.bfloat16),
        compiler_params=pltpu.CompilerParams(vmem_limit_bytes=8 << 20),
        cost_estimate=pl.CostEstimate(
            flops=8 * spectra * ch * SPAN * ch * rows,
            bytes_accessed=2 * words.size + 8 * ch * spectra * rows,
            transcendentals=0,
        ),
        name="row_spectra",
    )(words, parts, weights)


def products_kernel(own_ref, left_ref, *refs):
    out_ref, done_ref = refs[-2:]
    done_ref[...] = jnp.zeros_like(done_ref)
    each, steps = out_ref.shape[0], own_ref.shape[1]
    for index in range(each):
        c = pl.program_id(0) * each + index
        spectra = jnp.concatenate([own_ref[c, part] for part in range(steps)], axis=1)
        products = jnp.dot(spectra, left_ref[c], preferred_element_type=jnp.float32)
        count = products.shape[0]
        largest = jnp.maximum(jnp.max(jnp.abs(products), axis=0, keepdims=True), 2.0**-60)
        power = jnp.floor(jnp.log2(largest))
        coded = jnp.round(products * (jnp.exp2(RANGE - power) * FIT))
        out_ref[index, :count, :] = coded.astype(jnp.int32).astype(jnp.int16)
        line = jnp.broadcast_to(power, (out_ref.shape[1] - count, power.shape[1]))
        out_ref[index, count:, :] = line.astype(jnp.int32).astype(jnp.int16)


def row_products(own, left, after):
    ch, steps, count, width = own.shape
    columns = left.shape[2]
    each = 4
    return pl.pallas_call(
        products_kernel,
        grid=(ch // each,),
        in_specs=[pl.BlockSpec(memory_space=pltpu.VMEM)] * 2 + [pl.BlockSpec(memory_space=pl.ANY)] * len(after),
        out_specs=[
            pl.BlockSpec((each, count + EXTRA, columns), lambda i: (i, 0, 0)),
            pl.BlockSpec((16, LANES), lambda i: (0, 0)),
        ],
        out_shape=[
            pltpu.HBM((ch, count + EXTRA, columns), jnp.int16),
            jax.ShapeDtypeStruct((16, LANES), jnp.bfloat16),
        ],
        compiler_params=pltpu.CompilerParams(vmem_limit_bytes=10 << 20),
        cost_estimate=pl.CostEstimate(
            flops=2 * left.size * count, bytes_accessed=2 * left.size + 2 * own.size, transcendentals=0
        ),
        name="row_products",
    )(own, left, *after)


def finish_kernel(scale, slot_ref, coded_ref, *refs):
    out_ref, products, tile, mixed = refs[-4:]
    step = pl.program_id(0)
    sources, lines, width = coded_ref.shape
    count = lines - EXTRA
    pieces = width // LANES
    together = 8 // pieces

    @pl.when(step == 0)
    def _():
        for source in range(sources):
            power = coded_ref[source, count:, :][:1].astype(jnp.float32)
            values = coded_ref[source, :count, :].astype(jnp.float32) * (jnp.exp2(power - RANGE) * (scale / FIT))
            for piece in range(pieces):
                products[pl.ds(source * count * pieces + piece, count, stride=pieces), :] = values[
                    :, piece * LANES : (piece + 1) * LANES
                ]

    tiles = out_ref.shape[1] // 8

    @pl.loop(0, tiles)
    def _(j):
        for part in range(together):
            for i in range(LANES):
                line = slot_ref[((step * tiles + j) * together + part) * LANES + i]
                tile[i * pieces : (i + 1) * pieces, :] = products[pl.ds(pl.multiple_of(line, pieces), pieces), :]
            for piece in range(pieces):
                turned = tile[pl.ds(piece, LANES, stride=pieces), :].T
                mixed[pl.ds(part * pieces + piece, LANES, stride=8), :] = turned
        out_ref[:, pl.ds(pl.multiple_of(j * 8, 8), 8), :] = mixed[...].reshape(out_ref.shape[0], 8, LANES)


def finish(coded, places, index, pieces, scale, before):
    sources, lines, width = coded.shape
    rows = width // 2
    feeds = sources * (lines - EXTRA)
    columns = 2 * (feeds // LANES)
    earlier = [] if before is None else [before]
    return pl.pallas_call(
        functools.partial(finish_kernel, scale),
        grid=(columns // 16,),
        in_specs=[
            pl.BlockSpec(memory_space=pltpu.SMEM),
            pl.BlockSpec(memory_space=pltpu.VMEM),
        ]
        + [pl.BlockSpec(memory_space=pl.ANY)] * len(earlier),
        out_specs=pl.BlockSpec((rows, 16, LANES), lambda i: (index, i, 0)),
        out_shape=jax.ShapeDtypeStruct((pieces * rows, columns, LANES), jnp.float32),
        scratch_shapes=[
            pltpu.VMEM((feeds * width // LANES, LANES), jnp.float32),
            pltpu.VMEM((width, LANES), jnp.float32),
            pltpu.VMEM((8 * LANES, LANES), jnp.float32),
        ],
        input_output_aliases={2: 0} if earlier else {},
        compiler_params=pltpu.CompilerParams(vmem_limit_bytes=14 << 20),
        name="finish",
    )(places, coded, *earlier)


def through_rows(samples, gains, feed_slot):
    count, ch, frames = samples.shape
    spectra = frames - TAPS + 1
    pieces = ROWS // LANES
    lines = frames * ch
    unit = 16 * STEPS * 2
    total = pl.cdiv(lines + 4 * ch, unit) * unit
    words = jnp.transpose(samples, (2, 1, 0)).reshape(lines, count)
    scales = gains.reshape(2 * ch, count)
    weights = jnp.asarray(filter_weights(ch))
    place = lax.axis_index("feed").reshape(1)
    picked, sent = select_rows(place, words, scales, feed_slot.reshape(-1, LANES), ROWS, total)
    halves, firsts = zip(*[quarters(reduce_core(place, *pair)) for pair in zip(picked, sent)])
    seconds = [eighths(first) for first in firsts]
    own, zero = own_spectra(words, scales.astype(jnp.float32), weights, ch, spectra, sum(seconds, ()))
    thirds = [cross(second) for second in seconds]
    thirds[0][0] = thirds[0][0] + zero[0, 0]
    ends = [gathered(*parts) for parts in zip(halves, firsts, thirds)]
    out, after = None, [ends[-1]]
    for index in range(pieces):
        rows = gather_half(ends[index], 1, picked[index])
        parts = rows[lines : lines + 4 * ch]
        left = row_spectra(rows, parts, weights, ch, spectra)
        coded, done = row_products(own, left, after)
        after = [done]
        moved = lax.all_to_all(coded, "feed", split_axis=0, concat_axis=0, tiled=True)
        out = finish(moved, feed_slot * 2, index, pieces, 1.0 / spectra, out)
    feeds = feed_slot.shape[0]
    out = out.reshape(ROWS, feeds // LANES, 2, LANES)
    return jnp.transpose(out, (0, 2, 1, 3)).reshape(ROWS, 2, feeds)


def body(samples, gains, feed_slot):
    count, ch, frames = samples.shape
    spectra = frames - TAPS + 1
    even = count % LANES == 0 and spectra % (STEPS * STEP) == 0 and ch % STEPS == 0
    if lax.axis_size("feed") == ch == 16 and even:
        return through_rows(samples, gains, feed_slot)
    return through_spectra(samples, gains, feed_slot)


def solution(mesh):
    return jax.shard_map(
        body,
        mesh=mesh,
        in_specs=(P(("band", "feed"), None, None), P(None, "band", "feed"), P()),
        out_specs=P(("band", "feed"), None, None),
        check_vma=False,
    )
```
